32 devices in a mesh: rep: 4 (over z), ep: 8 (over y, x, core).
Axes of the slice: x: 2, y: 2, z: 4, core: 2. Of those that a mesh axis runs over, the one named last changes fastest.
Arguments:
- hidden_in: bfloat16 [32, 256, 2048], P(('rep', 'ep')), may hold values from -6 to 6
- out_grad: bfloat16 [32, 256, 2048], P(('rep', 'ep')), may hold values from -6 to 6
- attn_gain: bfloat16 [2048], P(('rep', 'ep')), may hold values from 0.5 to 1.5
- w_q: bfloat16 [2048, 4096], P(('rep', 'ep')), may hold values from -0.125 to 0.125
- key_weight: bfloat16 [2048, 512], P(('rep', 'ep')), may hold values from -0.125 to 0.125
- value_weight: bfloat16 [2048, 512], P(('rep', 'ep')), may hold values from -0.125 to 0.125
- w_o: bfloat16 [4096, 2048], P(('rep', 'ep')), may hold values from -0.375 to 0.375
- ffn_gain: bfloat16 [2048], P(('rep', 'ep')), may hold values from 0.5 to 1.5
- router_w: bfloat16 [2048, 16], P(('rep', 'ep')), may hold values from -0.0625 to 0.0625
- qk_gains: bfloat16 [2, 128], replicated, may hold values from 0.5 to 1.5
- w_gate: bfloat16 [16, 2048, 768], P('ep'), may hold values from -0.125 to 0.125
- w_up: bfloat16 [16, 2048, 768], P('ep'), may hold values from -0.125 to 0.125
- w_down: bfloat16 [16, 768, 2048], P('ep'), may hold values from -0.625 to 0.625
- lengths: int32 [32], replicated, may hold values from 64 to 256, as said below
- routes: int32 [32, 256, 8], P(('rep', 'ep')), may hold values from 0 to 15, all different within a row; in each aligned block of 256 rows (0 to 255, 256 to 511, ..., all dimensions but the last counted through in order) at most 160 rows name the same one
- order: int32 [32, 2048], P(('rep', 'ep')), may hold values from 0 to 2047, each once within a row
Outputs:
- layer_out: float32 [32, 256, 2048], P(('rep', 'ep'))
- grad_in: float32 [32, 256, 2048], P(('rep', 'ep'))
- grad_attn_gain: float32 [2048], P(('rep', 'ep'))
- grad_w_q: float32 [2048, 4096], P(('rep', 'ep'))
- grad_w_k: float32 [2048, 512], P(('rep', 'ep'))
- grad_w_v: float32 [2048, 512], P(('rep', 'ep'))
- grad_w_o: float32 [4096, 2048], P(('rep', 'ep'))
- grad_ffn_gain: float32 [2048], P(('rep', 'ep'))
- grad_router: float32 [2048, 16], P(('rep', 'ep'))
- grad_qk_gains: float32 [2, 128], replicated
- grad_w_gate: float32 [16, 2048, 768], P('ep', 'rep')
- grad_w_up: float32 [16, 2048, 768], P('ep', 'rep')
- grad_w_down: float32 [16, 768, 2048], P('ep', 'rep')
The draws below stay inside these ranges and needn't reach their ends.
Inputs may be any that keep to these rules, and one draw needn't show every extreme that they name: `lengths`: one sequence has exactly 256 live tokens and one exactly 64. `routes`: each token names 8 different experts; in the 256 rows of one sequence no expert is named by more than 160 tokens. `order`: each row holds every pair index once.
All inputs are finite; a program needn't handle non-finite values.
Results may differ from the reference program's by a relative error of at most 0.015.
Values may be sent and summed in bfloat16 or wider, within the bound.
A program may use at most 320 MiB of HBM per device.

```python
import math
import jax
import jax.numpy as jnp
import numpy as np
from jax import lax

MODEL_DIM = 2048
QUERY_HEADS = 32
KEY_VALUE_HEADS = 4
HEAD_DIM = 128
FFE = 768
TOPK = 8
SEQ = 256
E = 16
MOST = 160
SEQS = 32
N_REP = 4
N_EP = 8


def draw_lengths(key, part):
    first, second, third = jax.random.split(key, 3)
    drawn = jax.random.randint(first, (SEQS,), SEQ // 4, SEQ + 1)
    full_pos = jax.random.randint(second, (), 0, SEQS)
    short_pos = (full_pos + 1 + jax.random.randint(third, (), 0, SEQS - 1)) % SEQS
    position = jnp.arange(SEQS)
    drawn = jnp.where(position == full_pos, SEQ, jnp.where(position == short_pos, SEQ // 4, drawn))
    return drawn.astype(jnp.int32)


def levels(own_key, shape, shards, smallest, top_value):
    def one(dim, shards_of):
        heights = jax.random.uniform(jax.random.fold_in(jax.random.fold_in(own_key, 6), dim), (shards_of,), jnp.float32, smallest / len(shards), top_value / len(shards))
        return jnp.repeat(jnp.exp(heights), shape[dim] // shards_of).reshape((-1,) + (1,) * (len(shape) - dim - 1))

    factor_of = one(*shards[0])
    for cut in shards[1:]:
        factor_of = factor_of * one(*cut)
    return factor_of


def shared_out(stream_key, own, number, rows, amount, top, reach, lean):
    order = jax.random.permutation(stream_key, amount)
    crowded, common = load_shares(amount, rows * top, reach, lean, True), load_shares(amount, rows * top, reach, lean, False)
    places = jnp.arange(amount)

    def named(sizes, turn):
        used = int((sizes > 0).sum())
        fixed = max(1, used // 4)
        moved = fixed + (places - fixed + turn * (used - fixed)) % max(1, amount - fixed)
        return jnp.zeros((amount,), jnp.int32).at[order[jnp.where(places < fixed, places, moved)]].set(jnp.asarray(sizes, jnp.int32))

    sizes = jnp.where(number % 4 == 0, named(crowded, number // 4), named(common, number - number // 4 - 1))
    mixed = jax.random.permutation(jax.random.fold_in(own, 3), amount)
    donor, receiver = mixed[0:amount // 2 * 2:2], mixed[1:amount // 2 * 2:2]
    slack = jnp.minimum(sizes[donor] - 1, reach - sizes[receiver]) // 2
    slack = jnp.where((donor == order[0]) | (receiver == order[0]) | (sizes[receiver] == 0), 0, jnp.maximum(slack, 0))
    moved = jax.random.randint(jax.random.fold_in(own, 4), (amount // 2,), 0, 1 << 20) % (slack + 1)
    sizes = sizes.at[donor].add(-moved).at[receiver].add(moved)
    labels = jnp.searchsorted(jnp.cumsum(sizes), jnp.arange(rows * top), side="right").astype(jnp.int32)
    table = labels.reshape(top, rows).T
    table = table[jax.random.permutation(jax.random.fold_in(own, 1), rows)]
    turn = jax.random.randint(jax.random.fold_in(own, 2), (rows, 1), 0, top)
    return jnp.take_along_axis(table, (jnp.arange(top)[None, :] + turn) % top, axis=1)


def load_shares(amount, total, most, slope, full):
    portions = [(1 << 20) // math.isqrt(standing ** slope) + 1 for standing in range(1, amount + 1)]
    largest = most if full else min(most, max(-(-total // amount), total * portions[0] // sum(portions)))
    least = 1 if total - largest >= amount - 1 else 0
    counts, surplus = [largest] + [least] * (amount - 1), total - largest - least * (amount - 1)
    while surplus > 0:
        free = [i for i in range(1, amount) if counts[i] < largest] or [i for i in range(1, amount) if counts[i] < most]
        mass, left = sum([portions[i] for i in free]), surplus
        for i in free:
            more = min(most - counts[i], max(1, left * portions[i] // mass), surplus)
            counts[i] = counts[i] + more
            surplus = surplus - more
    return np.array(counts)


def normal_values(rng, shape, width, most, cuts=(), kind=jnp.bfloat16):
    loudness = levels(rng, shape, cuts, -0.22, 0.18) if cuts else 1.0
    array = jax.random.normal(rng, shape, jnp.float32) * width * loudness
    return jnp.minimum(jnp.maximum(array, -most), most).astype(kind)


def setup_inputs(seed: int = 0) -> dict:
    key_list = jax.random.split(jax.random.key(seed), 17)
    hidden_in = normal_values(key_list[0], (SEQS, SEQ, MODEL_DIM), 1.0, 6.0, ((0, 32),))
    out_grad = normal_values(key_list[1], (SEQS, SEQ, MODEL_DIM), 1.0, 6.0, ((0, 32),))
    attn_gain = jnp.clip(1.0 + 0.1 * jax.random.normal(key_list[2], (MODEL_DIM,), jnp.float32), 0.5, 1.5).astype(jnp.bfloat16)
    w_q = normal_values(key_list[3], (MODEL_DIM, QUERY_HEADS * HEAD_DIM), MODEL_DIM ** -0.5, 0.125, ((0, 32),))
    key_weight = normal_values(key_list[4], (MODEL_DIM, KEY_VALUE_HEADS * HEAD_DIM), MODEL_DIM ** -0.5, 0.125, ((0, 32),))
    value_weight = normal_values(key_list[5], (MODEL_DIM, KEY_VALUE_HEADS * HEAD_DIM), MODEL_DIM ** -0.5, 0.125, ((0, 32),))
    w_o = normal_values(key_list[6], (QUERY_HEADS * HEAD_DIM, MODEL_DIM), (QUERY_HEADS * HEAD_DIM // 16) ** -0.5, 0.375, ((0, 32),))
    ffn_gain = jnp.clip(1.0 + 0.1 * jax.random.normal(key_list[7], (MODEL_DIM,), jnp.float32), 0.5, 1.5).astype(jnp.bfloat16)
    router_w = normal_values(key_list[8], (MODEL_DIM, E), (4 * MODEL_DIM) ** -0.5, 0.0625, ((0, 32),))
    qk_gains = jnp.clip(1.0 + 0.1 * jax.random.normal(key_list[9], (2, HEAD_DIM), jnp.float32), 0.5, 1.5).astype(jnp.bfloat16)
    w_gate = normal_values(key_list[10], (E, MODEL_DIM, FFE), MODEL_DIM ** -0.5, 0.125, ((0, 8),))
    w_up = normal_values(key_list[11], (E, MODEL_DIM, FFE), MODEL_DIM ** -0.5, 0.125, ((0, 8),))
    w_down = normal_values(key_list[12], (E, FFE, MODEL_DIM), (FFE // 8) ** -0.5, 0.625, ((0, 8),))
    lengths = draw_lengths(jax.random.fold_in(key_list[16], 71), 0)
    routes_keys = jax.random.split(jax.random.fold_in(key_list[14], 1), SEQS * SEQ // SEQ)
    routes_turns = jax.random.permutation(jax.random.fold_in(key_list[14], 3), SEQS * SEQ // SEQ)
    routes = jax.vmap(lambda own, number: shared_out(jax.random.fold_in(key_list[14], 2), own, number, SEQ, E, TOPK, MOST, 1))(routes_keys, routes_turns).reshape((SEQS, SEQ, TOPK))
    order = jax.vmap(lambda own: jax.random.permutation(own, SEQ * TOPK))(jax.random.split(key_list[15], SEQS)).reshape((SEQS, SEQ * TOPK)).astype(jnp.int32)
    return {"hidden_in": hidden_in, "out_grad": out_grad, "attn_gain": attn_gain, "w_q": w_q, "key_weight": key_weight, "value_weight": value_weight, "w_o": w_o, "ffn_gain": ffn_gain, "router_w": router_w, "qk_gains": qk_gains, "w_gate": w_gate, "w_up": w_up, "w_down": w_down, "lengths": lengths, "routes": routes, "order": order}


eps = 1e-06
rope_base = 1000000.0
top_precision = lax.Precision.HIGHEST

@jax.custom_vjp
def reduced_cast(v):
    return lax.optimization_barrier(v.astype(jnp.bfloat16)).astype(jnp.float32)

@jax.custom_vjp
def reduced_cast_back(v):
    return v

def low_keep(v):
    return (reduced_cast(v), None)

def low_pass(kept, grad):
    return (grad,)

def back_keep(v):
    return (v, None)

def back_low(kept, grad):
    return (reduced_cast(grad),)
reduced_cast.defvjp(low_keep, low_pass)
reduced_cast_back.defvjp(back_keep, back_low)

def apply_norm(value_rows):
    return value_rows * lax.rsqrt(lax.optimization_barrier(jnp.mean(value_rows * value_rows, axis=-1, keepdims=True)) + eps)

def rope_tables(count, head_size):
    half_size = head_size // 2
    freqs = rope_base ** (-2.0 * jnp.arange(half_size, dtype=jnp.float32) / head_size)
    angles = jnp.arange(count, dtype=jnp.float32)[:, None] * freqs[None, :]
    cosine_lookup = jnp.concatenate([jnp.cos(angles), jnp.cos(angles)], axis=1)
    sine_lookup = jnp.concatenate([jnp.sin(angles), jnp.sin(angles)], axis=1)
    return (cosine_lookup, sine_lookup)

def apply_rotation(value_rows, cosine_lookup, sine_lookup):
    half_size = value_rows.shape[-1] // 2
    turned = jnp.concatenate([-value_rows[..., half_size:], value_rows[..., :half_size]], axis=-1)
    return value_rows * cosine_lookup[:, None, :] + turned * sine_lookup[:, None, :]

def local_routes(route_rows, order_row, length, experts):
    pair_expert = route_rows.reshape(-1)
    pair_total = pair_expert.shape[0]
    top_count = route_rows.shape[1]
    pair_index = jnp.arange(pair_total, dtype=jnp.int32)
    live_pair = pair_index // top_count < length
    inverse = jnp.zeros((pair_total,), jnp.int32).at[order_row].set(pair_index)
    ordered_expert = pair_expert[inverse]
    ordered_live = live_pair[inverse]
    expert_iota = jnp.arange(experts, dtype=jnp.int32)
    same_expert = (ordered_expert[:, None] == expert_iota[None, :]).astype(jnp.int32)
    live_hot = same_expert * ordered_live[:, None].astype(jnp.int32)
    before = jnp.cumsum(live_hot, axis=0) - live_hot
    ordered_rank = lax.optimization_barrier(jnp.sum(before * same_expert, axis=1))
    pair_rank = ordered_rank[order_row]
    expert_loads = lax.optimization_barrier(jnp.sum(live_hot, axis=0))
    return (pair_expert, live_pair, pair_rank, expert_loads)

def sequence_forward(params, inputs, length, token_rows, valid_rows, pair_slots, pair_keep, route_rows):
    gain_a, mat_q, key_matrix, value_matrix, mat_o, gain_f, mat_r, query_key_gain, mat_gate, mat_up, mat_down = params
    sequence_length = inputs.shape[0]
    positions = jnp.arange(sequence_length, dtype=jnp.int32)
    live_rows = (positions < length).astype(jnp.float32)
    hidden_first = reduced_cast(apply_norm(inputs) * gain_a)
    query_projected = reduced_cast_back(jnp.dot(hidden_first, mat_q, precision=top_precision)).reshape(sequence_length, QUERY_HEADS, HEAD_DIM)
    key_projected = reduced_cast_back(jnp.dot(hidden_first, key_matrix, precision=top_precision)).reshape(sequence_length, KEY_VALUE_HEADS, HEAD_DIM)
    value_rows = reduced_cast(reduced_cast_back(jnp.dot(hidden_first, value_matrix, precision=top_precision))).reshape(sequence_length, KEY_VALUE_HEADS, HEAD_DIM)
    cosine_lookup, sine_lookup = rope_tables(sequence_length, HEAD_DIM)
    query_rows = reduced_cast(apply_rotation(apply_norm(query_projected) * query_key_gain[0], cosine_lookup, sine_lookup)).reshape(sequence_length, KEY_VALUE_HEADS, QUERY_HEADS // KEY_VALUE_HEADS, HEAD_DIM)
    keys = reduced_cast(apply_rotation(apply_norm(key_projected) * query_key_gain[1], cosine_lookup, sine_lookup))
    scores = reduced_cast_back(jnp.einsum('tkgd,ukd->kgtu', query_rows, keys, precision=top_precision) * HEAD_DIM ** (-0.5))
    allowed = (positions[None, :] <= positions[:, None]) & (positions[None, :] < length)
    scores = jnp.where(allowed, scores, -1e+30)
    attn_probs = jax.nn.softmax(scores, axis=-1)
    attended = jnp.einsum('kgtu,ukd->tkgd', reduced_cast(attn_probs), value_rows, precision=top_precision).reshape(sequence_length, QUERY_HEADS * HEAD_DIM)
    attended = reduced_cast(reduced_cast_back(attended))
    middle = inputs + reduced_cast_back(jnp.dot(attended, mat_o, precision=top_precision))
    h_two = reduced_cast(apply_norm(middle) * gain_f)
    logits = jnp.dot(h_two, mat_r, precision=top_precision)
    chosen = jnp.take_along_axis(logits, route_rows, axis=1)
    route_gates = jax.nn.softmax(chosen, axis=-1)
    expert_rows = (reduced_cast_back(h_two[token_rows]) * valid_rows[:, None]).reshape(E, MOST, MODEL_DIM)
    gate_act = reduced_cast_back(jnp.einsum('emd,edf->emf', expert_rows, mat_gate, precision=top_precision))
    up_act = reduced_cast_back(jnp.einsum('emd,edf->emf', expert_rows, mat_up, precision=top_precision))
    hidden = reduced_cast(jax.nn.silu(gate_act) * up_act)
    expert_out = reduced_cast(reduced_cast_back(jnp.einsum('emf,efd->emd', hidden, mat_down, precision=top_precision))).reshape(E * MOST, MODEL_DIM)
    picked = expert_out[pair_slots].reshape(sequence_length, TOPK, MODEL_DIM)
    pair_weight = route_gates * pair_keep.reshape(sequence_length, TOPK)
    moe_output = lax.optimization_barrier(jnp.sum(pair_weight[..., None] * picked, axis=1))
    return live_rows[:, None] * (middle + moe_output)

def reference(hidden_in, out_grad, attn_gain, w_q, key_weight, value_weight, w_o, ffn_gain, router_w, qk_gains, w_gate, w_up, w_down, lengths, routes, order):

    def route_one(route_rows, order_row, length):
        return local_routes(route_rows, order_row, length, E)
    pair_expert, live_pair, pair_rank, expert_loads = jax.vmap(route_one)(routes, order, lengths)
    grouped = expert_loads.reshape(N_REP, N_EP, E)
    load_prefix = (jnp.cumsum(grouped, axis=1) - grouped).reshape(SEQS, E)
    group_total = lax.optimization_barrier(jnp.sum(lengths.reshape(N_REP, N_EP), axis=1))
    capacity = jnp.repeat(9 * TOPK * group_total // (8 * E), N_EP)
    offsets = jnp.take_along_axis(load_prefix, pair_expert, axis=1)
    kept_pairs = live_pair & (offsets + pair_rank < capacity[:, None])
    slot_count = E * MOST
    dest_slot = pair_expert * MOST + pair_rank
    slot_index = jnp.where(kept_pairs, dest_slot, slot_count).astype(jnp.int32)
    pair_index = jnp.arange(SEQ * TOPK, dtype=jnp.int32)

    def token_table(where_to):
        return jnp.zeros((slot_count,), jnp.int32).at[where_to].set(pair_index // TOPK, mode='drop')

    def valid_table(where_to):
        return jnp.zeros((slot_count,), jnp.float32).at[where_to].set(1.0, mode='drop')
    token_of = jax.vmap(token_table)(slot_index)
    slot_valid = jax.vmap(valid_table)(slot_index)
    safe_slot = jnp.minimum(dest_slot, slot_count - 1).astype(jnp.int32)
    kept_float = kept_pairs.astype(jnp.float32)
    params = (attn_gain.astype(jnp.float32), w_q.astype(jnp.float32), key_weight.astype(jnp.float32), value_weight.astype(jnp.float32), w_o.astype(jnp.float32), ffn_gain.astype(jnp.float32), router_w.astype(jnp.float32), qk_gains.astype(jnp.float32), w_gate.astype(jnp.float32), w_up.astype(jnp.float32), w_down.astype(jnp.float32))

    def forward(inputs_all, weights):

        def one_sequence(item):
            return sequence_forward(weights, *item)
        return lax.map(jax.checkpoint(one_sequence), (inputs_all, lengths, token_of, slot_valid, safe_slot, kept_float, routes))
    output, pullback = jax.vjp(forward, hidden_in.astype(jnp.float32), params)
    grad_input, grads = pullback(out_grad.astype(jnp.float32))
    return (output, grad_input, grads[0], grads[1], grads[2], grads[3], grads[4], grads[5], grads[6], grads[7], grads[8], grads[9], grads[10])
```

```python
import functools

import jax
import jax.numpy as jnp
from jax import lax
from jax.experimental import pallas as pl
from jax.experimental.pallas import tpu as pltpu
from jax.sharding import PartitionSpec as P

eps = 1e-06
rope_base = 1000000.0
top_precision = lax.Precision.HIGHEST
MESH = pl.DeviceIdType.MESH
f32, bf16 = jnp.float32, jnp.bfloat16
EXT = 128
UNIT = 16
TILE = 256
VMEM_BYTES = 58 * 1024 * 1024


def rms_parts(value_rows):
    inverse = lax.rsqrt(jnp.mean(value_rows * value_rows, axis=-1, keepdims=True) + eps)
    return (value_rows * inverse, inverse)


def rms_back(grad_norm, normed, inverse):
    return inverse * (grad_norm - normed * jnp.mean(grad_norm * normed, axis=-1, keepdims=True))


def rope_tables(count, head_size):
    half_size = head_size // 2
    freqs = rope_base ** (-2.0 * jnp.arange(half_size, dtype=f32) / head_size)
    angles = jnp.arange(count, dtype=f32)[:, None] * freqs[None, :]
    cosine_lookup = jnp.concatenate([jnp.cos(angles), jnp.cos(angles)], axis=1)
    sine_lookup = jnp.concatenate([jnp.sin(angles), jnp.sin(angles)], axis=1)
    return (cosine_lookup, sine_lookup)


def apply_rotation(value_rows, cosine_lookup, sine_lookup):
    half_size = value_rows.shape[-1] // 2
    turned = jnp.concatenate([-value_rows[..., half_size:], value_rows[..., :half_size]], axis=-1)
    return value_rows * cosine_lookup[:, None, :] + turned * sine_lookup[:, None, :]


def rotate_back(grads, cosine_lookup, sine_lookup):
    half_size = grads.shape[-1] // 2
    scaled = grads * sine_lookup[:, None, :]
    turned = jnp.concatenate([scaled[..., half_size:], -scaled[..., :half_size]], axis=-1)
    return grads * cosine_lookup[:, None, :] + turned


def bits_of(count):
    return count.bit_length() - 1


def gather_orders(count):
    bits = bits_of(count)
    up = list(range(1, bits)) + [0]
    down = list(range(bits - 1, 0, -1)) + [0]
    return (up, down)


def spans(bits):
    masks = [0]
    for bit in bits:
        masks = masks + [m | (1 << bit) for m in masks]
    return masks


def meet(peers):
    barrier = pltpu.get_barrier_semaphore()
    for peer in peers:
        pl.semaphore_signal(barrier, inc=1, device_id=peer, device_id_type=MESH)
    pl.semaphore_wait(barrier, len(peers))


def token_gather_kernel(count, x_ref, out_ref, send_sem, recv_sem, local_sem):
    rep, me = lax.axis_index("rep"), lax.axis_index("ep")
    bits = bits_of(count)
    half = x_ref.shape[0] // 2
    meet([(rep, me ^ (1 << b)) for b in range(bits)])
    local = pltpu.make_async_copy(x_ref, out_ref.at[me], local_sem)
    local.start()
    orders = gather_orders(count)
    copies = []

    def send(h, mask, bit):
        rows = pl.ds(h * half, half)
        source = x_ref.at[rows] if mask == 0 else out_ref.at[me ^ mask, rows]
        there = mask | (1 << bit)
        copy = pltpu.make_async_remote_copy(
            src_ref=source,
            dst_ref=out_ref.at[me ^ mask, rows],
            send_sem=send_sem.at[h, there],
            recv_sem=recv_sem.at[h, there],
            device_id=(rep, me ^ (1 << bit)),
            device_id_type=MESH,
        )
        copy.start()
        copies.append(copy)

    def arrived(h, mask):
        rows = pl.ds(h * half, half)
        pltpu.make_async_copy(
            x_ref.at[rows], out_ref.at[me ^ mask, rows], recv_sem.at[h, mask]
        ).wait()

    for stage in range(bits):
        for h in range(2):
            send(h, 0, orders[h][stage])
    for stage in range(bits):
        for low in spans(orders[0][:stage]):
            index = spans(orders[0][:stage]).index(low)
            for h in range(2):
                mask = spans(orders[h][:stage])[index] | (1 << orders[h][stage])
                arrived(h, mask)
                for later in range(stage + 1, bits):
                    send(h, mask, orders[h][later])
    for copy in copies:
        copy.wait_send()
    local.wait()


def gather_tokens(x, count, collective_id):
    return pl.pallas_call(
        functools.partial(token_gather_kernel, count),
        out_shape=jax.ShapeDtypeStruct((count,) + x.shape, x.dtype),
        in_specs=[pl.BlockSpec(memory_space=pl.ANY)],
        out_specs=pl.BlockSpec(memory_space=pl.ANY),
        scratch_shapes=[
            pltpu.SemaphoreType.DMA((2, count)),
            pltpu.SemaphoreType.DMA((2, count)),
            pltpu.SemaphoreType.DMA,
        ],
        compiler_params=pltpu.CompilerParams(collective_id=collective_id, has_side_effects=True),
        name="token_gather",
    )(x)


def token_sum_kernel(count, widths, y_ref, out_ref, *scratch):
    bits = bits_of(count)
    own, got = scratch[:2], scratch[2:4]
    send_sem, recv_sem, own_sem, out_sem = scratch[4:8]
    result = scratch[8:10]
    rep, me = lax.axis_index("rep"), lax.axis_index("ep")
    meet([(rep, me ^ (1 << b)) for b in range(bits)])
    orders = [list(reversed(o)) for o in gather_orders(count)]
    columns = (pl.ds(0, widths[0]), pl.ds(widths[0], widths[1]))
    sends = []
    firsts = [list(reversed(spans(o[1:]))) for o in orders]
    slot_of = []
    for h in range(2):
        table, base = {}, 0
        for stage in range(bits):
            for place, mask in enumerate(reversed(spans(orders[h][stage + 1 :]))):
                table[(stage, mask)] = base + place
            base += 1 << (bits - 1 - stage)
        slot_of.append(table)
    seat = [{mask: i for i, mask in enumerate(firsts[h])} for h in range(2)]

    def send(h, stage, mask):
        bit = 1 << orders[h][stage]
        slot = slot_of[h][(stage, mask)]
        source = y_ref.at[me ^ bit ^ mask, :, columns[h]] if stage == 0 else own[h].at[seat[h][bit | mask]]
        copy = pltpu.make_async_remote_copy(
            src_ref=source,
            dst_ref=got[h].at[slot],
            send_sem=send_sem.at[h, slot],
            recv_sem=recv_sem.at[h, slot],
            device_id=(rep, me ^ bit),
            device_id_type=MESH,
        )
        copy.start()
        sends.append(copy)

    loads = [{}, {}]
    for i in range(len(firsts[0])):
        for h in range(2):
            mask = firsts[h][i]
            send(h, 0, mask)
            load = pltpu.make_async_copy(
                y_ref.at[me ^ mask, :, columns[h]], own[h].at[seat[h][mask]], own_sem.at[h, i]
            )
            load.start()
            loads[h][mask] = load

    rows_total = y_ref.shape[1]
    step = 32

    def add(h, stage, mask):
        slot = slot_of[h][(stage, mask)]
        if stage == 0:
            loads[h][mask].wait()
        pltpu.make_async_copy(got[h].at[slot], got[h].at[slot], recv_sem.at[h, slot]).wait()
        last = stage == bits - 1

        def body(i, carry):
            rows = pl.ds(pl.multiple_of(i * step, step), step)
            total = own[h][seat[h][mask], rows, :].astype(f32) + got[h][slot, rows, :].astype(f32)
            if last:
                result[h][rows, :] = total
            else:
                own[h][seat[h][mask], rows, :] = total.astype(bf16)
            return carry

        lax.fori_loop(0, rows_total // step, body, 0)

    for stage in range(bits):
        masks = [list(reversed(spans(orders[h][stage + 1 :]))) for h in range(2)]
        for i in range(len(masks[0])):
            for h in range(2):
                mask = masks[h][i]
                add(h, stage, mask)
                if stage + 1 < bits:
                    following = 1 << orders[h][stage + 1]
                    if mask & following:
                        send(h, stage + 1, mask & ~following)
    outs = []
    for h in range(2):
        out = pltpu.make_async_copy(result[h], out_ref.at[:, columns[h]], out_sem.at[h])
        out.start()
        outs.append(out)
    for copy in sends:
        copy.wait_send()
    for out in outs:
        out.wait()


def sum_tokens(y, count, widths, collective_id):
    rows = y.shape[1]
    half = count // 2
    return pl.pallas_call(
        functools.partial(token_sum_kernel, count, widths),
        out_shape=jax.ShapeDtypeStruct(y.shape[1:], f32),
        in_specs=[pl.BlockSpec(memory_space=pl.ANY)],
        out_specs=pl.BlockSpec(memory_space=pl.ANY),
        scratch_shapes=[
            pltpu.VMEM((half, rows, widths[0]), bf16),
            pltpu.VMEM((half, rows, widths[1]), bf16),
            pltpu.VMEM((count - 1, rows, widths[0]), bf16),
            pltpu.VMEM((count - 1, rows, widths[1]), bf16),
            pltpu.SemaphoreType.DMA((2, count)),
            pltpu.SemaphoreType.DMA((2, count)),
            pltpu.SemaphoreType.DMA((2, half)),
            pltpu.SemaphoreType.DMA((2,)),
            pltpu.VMEM((rows, widths[0]), f32),
            pltpu.VMEM((rows, widths[1]), f32),
        ],
        compiler_params=pltpu.CompilerParams(
            collective_id=collective_id, has_side_effects=True, vmem_limit_bytes=VMEM_BYTES
        ),
        name="token_sum",
    )(y)


NT = (((1,), (1,)), ((), ()))
TN = (((0,), (0,)), ((), ()))


def expert_kernel(first, last, experts, width, *refs):
    (info, h_ref, g_ref, wg_ref, wu_ref, wd_ref) = refs[:6]
    rest = list(refs[6:])
    prev_ref = None if first else rest.pop(0)
    y_ref, gwg_ref, gwu_ref, gwd_ref = rest[:4]
    xs, gs, ds, hs, stage, prev_buf, wide, tall, in_sem, out_sem, prev_sem, grad_sem = rest[4:]
    hidden = wg_ref.shape[1]
    units = info[0]
    expert = info[1]
    table = 8
    per_tile = TILE // UNIT
    tiles = (units + per_tile - 1) // per_tile
    most = xs.shape[0] // TILE
    floor_tiles = min(4, most)

    def unit_in(u, slot):
        source = pl.ds(pl.multiple_of(info[table + u], UNIT), UNIT)
        target = pl.ds(pl.multiple_of(u * UNIT, UNIT), UNIT)
        return (
            pltpu.make_async_copy(h_ref.at[source], xs.at[target], in_sem.at[0, slot]),
            pltpu.make_async_copy(g_ref.at[source], gs.at[target], in_sem.at[1, slot]),
        )

    def begin(u, carry):
        for copy in unit_in(u, u // per_tile):
            copy.start()
        return carry

    lax.fori_loop(0, units, begin, 0)

    def blank(u, carry):
        target = pl.ds(pl.multiple_of(u * UNIT, UNIT), UNIT)
        xs[target, :] = jnp.zeros((UNIT, xs.shape[1]), bf16)
        gs[target, :] = jnp.zeros((UNIT, gs.shape[1]), bf16)
        return carry

    lax.fori_loop(units, jnp.maximum(tiles, floor_tiles) * per_tile, blank, 0)

    def blank_tile(i, carry):
        target = pl.ds(pl.multiple_of(i * TILE, TILE), TILE)
        ds[target, :] = jnp.zeros((TILE, ds.shape[1]), bf16)
        hs[target, :] = jnp.zeros((TILE, hs.shape[1]), bf16)
        return carry

    lax.fori_loop(tiles, floor_tiles, blank_tile, 0)

    def prev_copy(i):
        rows = pl.ds(pl.multiple_of(i * TILE, TILE), TILE)
        return pltpu.make_async_copy(prev_ref.at[rows], prev_buf.at[i % 2], prev_sem.at[i % 2])

    if not first:
        prev_copy(0).start()

    def unit_out(u):
        target = pl.ds(pl.multiple_of(info[table + u], UNIT), UNIT)
        tile = u // per_tile
        source = pl.ds(pl.multiple_of((u % per_tile) * UNIT, UNIT), UNIT)
        return pltpu.make_async_copy(stage.at[tile % 2, source], y_ref.at[target], out_sem.at[tile % 2])

    def out_start(i):
        if last:
            lax.fori_loop(
                i * per_tile,
                jnp.minimum((i + 1) * per_tile, units),
                lambda u, c: (unit_out(u).start(), c)[1],
                0,
            )
        else:
            rows = pl.ds(pl.multiple_of(i * TILE, TILE), TILE)
            pltpu.make_async_copy(stage.at[i % 2], y_ref.at[rows], out_sem.at[i % 2]).start()

    def out_wait(i):
        if last:
            lax.fori_loop(
                i * per_tile,
                jnp.minimum((i + 1) * per_tile, units),
                lambda u, c: (unit_out(u).wait(), c)[1],
                0,
            )
        else:
            rows = pl.ds(pl.multiple_of(i * TILE, TILE), TILE)
            pltpu.make_async_copy(stage.at[i % 2], y_ref.at[rows], out_sem.at[i % 2]).wait()

    lane = lax.broadcasted_iota(jnp.int32, (TILE, EXT), 1)
    weight_lanes = (lane == expert) | (lane == expert + experts) | (lane == expert + 2 * experts)

    def tile_step(i, carry):
        def landed(u, c):
            for copy in unit_in(u, i):
                copy.wait()
            return c

        lax.fori_loop(i * per_tile, jnp.minimum((i + 1) * per_tile, units), landed, 0)
        rows = pl.ds(pl.multiple_of(i * TILE, TILE), TILE)
        x = xs[rows, :width]
        g = gs[rows, :]
        extra = xs[rows, width:].astype(f32)
        weight = jnp.sum(jnp.where(weight_lanes, extra, 0.0), axis=1, keepdims=True)
        gate = jnp.dot(x, wg_ref[...], preferred_element_type=f32)
        up = jnp.dot(x, wu_ref[...], preferred_element_type=f32)
        d_plain = lax.dot_general(g, wd_ref[...], NT, preferred_element_type=f32)
        sig = 1.0 / (1.0 + jnp.exp(-gate))
        silu = gate * sig
        hid = silu * up
        d_weight = jnp.sum(hid.astype(bf16).astype(f32) * d_plain, axis=1, keepdims=True)
        hs[rows, :] = (hid * weight).astype(bf16)
        d_hidden = d_plain * weight
        ds[rows, :hidden] = (d_hidden * up * sig * (1.0 + gate * (1.0 - sig))).astype(bf16)
        ds[rows, hidden:] = (d_hidden * silu).astype(bf16)

        @pl.when(i >= 2)
        def _():
            out_wait(i - 2)

        if not first:

            @pl.when(i + 1 < tiles)
            def _():
                prev_copy(i + 1).start()

            prev_copy(i).wait()
        slot = i % 2
        high = d_weight.astype(bf16).astype(f32)
        low = d_weight - high
        note = jnp.where(lane == expert, high, 0.0) + jnp.where(lane == expert + experts, low, 0.0)
        d_row = lax.dot_general(ds[rows, :hidden], wg_ref[...], NT, preferred_element_type=f32)
        d_row += lax.dot_general(ds[rows, hidden:], wu_ref[...], NT, preferred_element_type=f32)
        if not first:
            d_row += prev_buf[slot, :, :width].astype(f32)
            note += prev_buf[slot, :, width : width + EXT].astype(f32)
        stage[slot, :, :width] = d_row.astype(bf16)
        stage[slot, :, width : width + EXT] = note.astype(bf16)
        out = jnp.dot(hs[rows, :], wd_ref[...], preferred_element_type=f32)
        if not first:
            out += prev_buf[slot, :, width + EXT :].astype(f32)
        stage[slot, :, width + EXT :] = out.astype(bf16)
        out_start(i)
        return carry

    lax.fori_loop(0, tiles, tile_step, 0)

    block = 256

    def grads(depth):
        def wide_copies(m):
            rows = pl.ds(pl.multiple_of(m * block, block), block)
            return (
                pltpu.make_async_copy(wide.at[m % 2, :, :hidden], gwg_ref.at[rows], grad_sem.at[0, m % 2]),
                pltpu.make_async_copy(wide.at[m % 2, :, hidden:], gwu_ref.at[rows], grad_sem.at[1, m % 2]),
            )

        def wide_step(m, carry):
            @pl.when(m >= 2)
            def _():
                for copy in wide_copies(m - 2):
                    copy.wait()

            columns = pl.ds(pl.multiple_of(m * block, block), block)
            wide[m % 2] = lax.dot_general(
                xs[:depth, columns], ds[:depth, :], TN, preferred_element_type=f32
            ).astype(bf16)
            for copy in wide_copies(m):
                copy.start()
            return carry

        count = width // block
        lax.fori_loop(0, count, wide_step, 0)
        for m in range(count - 2, count):
            for copy in wide_copies(m):
                copy.wait()

        def tall_copy(m):
            rows = pl.ds(pl.multiple_of(m * block, block), block)
            return pltpu.make_async_copy(tall.at[m % 2], gwd_ref.at[rows], grad_sem.at[0, m % 2])

        def tall_step(m, carry):
            @pl.when(m >= 2)
            def _():
                tall_copy(m - 2).wait()

            columns = pl.ds(pl.multiple_of(m * block, block), block)
            tall[m % 2] = lax.dot_general(
                hs[:depth, columns], gs[:depth, :], TN, preferred_element_type=f32
            ).astype(bf16)
            tall_copy(m).start()
            return carry

        count = hidden // block
        lax.fori_loop(0, count, tall_step, 0)
        for m in range(count - 2, count):
            tall_copy(m).wait()

    for choice in range(floor_tiles, most + 1):
        chosen = (tiles <= choice) if choice == floor_tiles else (tiles == choice)

        @pl.when(chosen)
        def _(choice=choice):
            grads(choice * TILE)

    @pl.when(tiles >= 2)
    def _():
        out_wait(tiles - 2)

    out_wait(tiles - 1)


def expert_pass(info, h_rows, g_rows, w_gate, w_up, w_down, prev, last, experts):
    tokens, width = g_rows.shape
    hidden = w_gate.shape[1]
    wide_row = width + EXT + width
    any_spec = pl.BlockSpec(memory_space=pl.ANY)
    vmem_spec = pl.BlockSpec(memory_space=pltpu.VMEM)
    first = prev is None
    operands = [info, h_rows, g_rows, w_gate, w_up, w_down] + ([] if first else [prev])
    specs = [pl.BlockSpec(memory_space=pltpu.SMEM), any_spec, any_spec, vmem_spec, vmem_spec, vmem_spec]
    specs += [] if first else [any_spec]
    return pl.pallas_call(
        functools.partial(expert_kernel, first, last, experts, width),
        out_shape=(
            jax.ShapeDtypeStruct((tokens, wide_row), bf16),
            jax.ShapeDtypeStruct((width, hidden), bf16),
            jax.ShapeDtypeStruct((width, hidden), bf16),
            jax.ShapeDtypeStruct((hidden, width), bf16),
        ),
        in_specs=specs,
        out_specs=(any_spec,) * 4,
        scratch_shapes=[
            pltpu.VMEM((tokens, width + EXT), bf16),
            pltpu.VMEM((tokens, width), bf16),
            pltpu.VMEM((tokens, 2 * hidden), bf16),
            pltpu.VMEM((tokens, hidden), bf16),
            pltpu.VMEM((2, TILE, wide_row), bf16),
            pltpu.VMEM((2, TILE, wide_row), bf16),
            pltpu.VMEM((2, 256, 2 * hidden), bf16),
            pltpu.VMEM((2, 256, width), bf16),
            pltpu.SemaphoreType.DMA((2, tokens // TILE)),
            pltpu.SemaphoreType.DMA((2,)),
            pltpu.SemaphoreType.DMA((2,)),
            pltpu.SemaphoreType.DMA((2, 2)),
        ],
        compiler_params=pltpu.CompilerParams(vmem_limit_bytes=VMEM_BYTES),
        cost_estimate=pl.CostEstimate(
            flops=18 * tokens * width * hidden, bytes_accessed=12 * tokens * width, transcendentals=0
        ),
        name="experts",
    )(*operands)


def unit_table(lengths):
    per_sequence = TILE // UNIT
    counts = (lengths + UNIT - 1) // UNIT
    unit = jnp.arange(lengths.shape[0] * per_sequence, dtype=jnp.int32)
    live = (unit % per_sequence) < jnp.repeat(counts, per_sequence)
    place = jnp.cumsum(live.astype(jnp.int32)) - 1
    hit = (place[None, :] == unit[:, None]) & live[None, :]
    rows = jnp.sum(jnp.where(hit, unit[None, :] * UNIT, 0), axis=1)
    return (jnp.sum(counts), rows)


def split_three(value):
    high = lax.reduce_precision(value, 8, 7)
    rest = value - high
    middle = lax.reduce_precision(rest, 8, 7)
    return jnp.concatenate([high, middle, rest - middle], axis=-1)


def per_device(
    hidden_in,
    out_grad,
    attn_gain,
    w_q,
    key_weight,
    value_weight,
    w_o,
    ffn_gain,
    router_w,
    qk_gains,
    w_gate,
    w_up,
    w_down,
    lengths,
    routes,
    order,
):
    everywhere = ("rep", "ep")
    rep_count, ep_count = (lax.axis_size("rep"), lax.axis_size("ep"))
    rep_index, ep_index = (lax.axis_index("rep"), lax.axis_index("ep"))
    inputs = hidden_in[0].astype(f32)
    sequence_length, model_width = inputs.shape
    head_size = qk_gains.shape[1]
    wide_q, wide_kv = (w_q.shape[1], key_weight.shape[1])
    heads_q, heads_kv = (wide_q // head_size, wide_kv // head_size)
    groups = heads_q // heads_kv
    local_experts = w_gate.shape[0]
    experts = local_experts * ep_count
    top_count = routes.shape[2]
    score_scale = head_size ** (-0.5)
    group_lengths = lax.dynamic_slice_in_dim(lengths, rep_index * ep_count, ep_count)
    length = lax.dynamic_index_in_dim(group_lengths, ep_index, keepdims=False)
    positions = jnp.arange(sequence_length, dtype=jnp.int32)
    live = positions < length
    live_rows = live.astype(f32)

    expert_iota = jnp.arange(experts, dtype=jnp.int32)
    route_hot = routes[0][..., None] == expert_iota
    routed = jnp.any(route_hot, axis=1) & live[:, None]
    order_of = jnp.sum(
        jnp.where(route_hot, order[0].reshape(sequence_length, top_count)[..., None], 0), axis=1
    )
    sort_key = jnp.where(routed, order_of, sequence_length * top_count)
    loads = jnp.sum(routed.astype(jnp.int32), axis=0)
    rank = jnp.sum((sort_key[None, :, :] < sort_key[:, None, :]).astype(jnp.int32), axis=1)

    own_rows = w_q.shape[0]
    load_columns = -(-experts // own_rows)
    load_block = jnp.pad(loads, (0, load_columns * own_rows - experts)).reshape(load_columns, own_rows).T
    small = jnp.concatenate(
        [router_w, attn_gain[:, None], ffn_gain[:, None], load_block.astype(bf16)], axis=1
    )
    small = jnp.pad(small, ((0, 0), (0, EXT - small.shape[1])))
    pack = jnp.concatenate([w_q, key_weight, value_weight, small], axis=1)
    mat_qkv = lax.all_gather(pack, everywhere, axis=0, tiled=True)
    mat_o = lax.all_gather(w_o, everywhere, axis=0, tiled=True)
    grads_all = lax.all_gather(out_grad[0], "ep", axis=0, tiled=True)

    wide_all = wide_q + 2 * wide_kv
    small_all = mat_qkv[:, wide_all:]
    mat_router = small_all[:, :experts]
    gain_attn = small_all[:, experts].astype(f32)
    gain_ffn = small_all[:, experts + 1].astype(f32)
    loads_all = (
        small_all[:, experts + 2 : experts + 2 + load_columns]
        .reshape(rep_count, ep_count, own_rows, load_columns)
        .transpose(0, 1, 3, 2)
        .reshape(rep_count, ep_count, load_columns * own_rows)[:, :, :experts]
        .astype(jnp.int32)
    )
    group_loads = lax.dynamic_index_in_dim(loads_all, rep_index, keepdims=False)
    earlier = (jnp.arange(ep_count) < ep_index)[:, None]
    load_prefix = jnp.sum(jnp.where(earlier, group_loads, 0), axis=0)
    capacity = 9 * top_count * jnp.sum(group_lengths) // (8 * experts)
    kept = routed & (load_prefix[None, :] + rank < capacity)
    kept_float = kept.astype(f32)

    gain_q = qk_gains[0].astype(f32)
    gain_k = qk_gains[1].astype(f32)
    norm_one, inv_one = rms_parts(inputs)
    hidden_first = (norm_one * gain_attn).astype(bf16)
    projected = jnp.dot(hidden_first, mat_qkv, preferred_element_type=f32)
    query_projected = projected[:, :wide_q].reshape(sequence_length, heads_q, head_size)
    key_projected = projected[:, wide_q : wide_q + wide_kv].reshape(sequence_length, heads_kv, head_size)
    value_rows = (
        projected[:, wide_q + wide_kv : wide_all]
        .astype(bf16)
        .reshape(sequence_length, heads_kv, head_size)
    )
    cosine_lookup, sine_lookup = rope_tables(sequence_length, head_size)
    q_norm, q_inv = rms_parts(query_projected)
    k_norm, k_inv = rms_parts(key_projected)
    query_rows = (
        apply_rotation(q_norm * gain_q, cosine_lookup, sine_lookup)
        .astype(bf16)
        .reshape(sequence_length, heads_kv, groups, head_size)
    )
    keys = apply_rotation(k_norm * gain_k, cosine_lookup, sine_lookup).astype(bf16)
    scores = jnp.einsum("tkgd,ukd->kgtu", query_rows, keys, preferred_element_type=f32) * score_scale
    allowed = (positions[None, :] <= positions[:, None]) & (positions[None, :] < length)
    scores = jnp.where(allowed, scores, -1e30)
    attn_probs = jax.nn.softmax(scores, axis=-1)
    probs_low = attn_probs.astype(bf16)
    attended = (
        jnp.einsum("kgtu,ukd->tkgd", probs_low, value_rows, preferred_element_type=f32)
        .astype(bf16)
        .reshape(sequence_length, heads_q * head_size)
    )
    middle = inputs + jnp.dot(attended, mat_o, preferred_element_type=f32)
    norm_two, inv_two = rms_parts(middle)
    h_two = (norm_two * gain_ffn).astype(bf16)
    logits = jnp.dot(h_two, mat_router, preferred_element_type=f32)
    named = jnp.any(route_hot, axis=1)
    top_logit = jnp.max(jnp.where(named, logits, -jnp.inf), axis=1, keepdims=True)
    raised = jnp.where(named, jnp.exp(jnp.where(named, logits - top_logit, 0.0)), 0.0)
    route_gates = raised / jnp.sum(raised, axis=1, keepdims=True)
    pair_weight = route_gates * kept_float

    extra = split_three(pair_weight).astype(bf16)
    extra = jnp.pad(extra, ((0, 0), (0, EXT - extra.shape[1])))
    sent = jnp.concatenate([h_two, extra], axis=1)
    h_all = gather_tokens(sent, ep_count, 1)

    part = min(ep_count, 8)
    tokens = part * sequence_length
    sums = []
    y_parts = []
    for c in range(ep_count // part):
        live_units, unit_rows = unit_table(group_lengths[c * part : (c + 1) * part])
        h_rows = h_all[c * part : (c + 1) * part].reshape(tokens, model_width + EXT)
        g_rows = grads_all[c * tokens : (c + 1) * tokens]
        prev, found = None, []
        for local in range(local_experts):
            info = jnp.concatenate(
                [
                    jnp.stack([live_units, ep_index * local_experts + local]).astype(jnp.int32),
                    jnp.zeros((6,), jnp.int32),
                    unit_rows,
                ]
            )
            prev, *weight_grads = expert_pass(
                info,
                h_rows,
                g_rows,
                w_gate[local],
                w_up[local],
                w_down[local],
                prev,
                local == local_experts - 1,
                experts,
            )
            found.append(weight_grads)
        y_parts.append(prev.reshape(part, sequence_length, -1))
        sums.append(found)
    y_all = y_parts[0] if len(y_parts) == 1 else jnp.concatenate(y_parts, axis=0)
    expert_sums = []
    for which in range(3):
        pieces = []
        for local in range(local_experts):
            total = sums[0][local][which]
            for more in sums[1:]:
                total = (total.astype(f32) + more[local][which].astype(f32)).astype(bf16)
            pieces.append(lax.psum_scatter(total, "rep", scatter_dimension=0, tiled=True).astype(f32))
        expert_sums.append(jnp.stack(pieces))

    back = sum_tokens(y_all, ep_count, (model_width + EXT, model_width), 2)
    live_column = live[:, None]
    moe_output = jnp.where(live_column, back[:, model_width + EXT :], 0.0)
    layer_out = jnp.where(live_column, middle + moe_output, 0.0)
    grad_rows = out_grad[0].astype(f32) * live_rows[:, None]
    notes = back[:, model_width : model_width + 2 * experts]
    d_weight = jnp.where(live_column, notes[:, :experts] + notes[:, experts:], 0.0)
    d_gates = d_weight * kept_float
    d_logits = route_gates * (d_gates - jnp.sum(route_gates * d_gates, axis=-1, keepdims=True))

    router_float = mat_router.astype(f32)
    d_h_two = jnp.where(live_column, back[:, :model_width], 0.0)
    d_h_two = d_h_two + jnp.dot(d_logits, router_float.T, precision=top_precision)
    grad_router = jnp.dot(h_two.astype(f32).T, d_logits, precision=top_precision)
    grad_ffn = jnp.sum(d_h_two * norm_two, axis=0)
    d_middle = grad_rows + rms_back(d_h_two * gain_ffn, norm_two, inv_two)
    d_middle_low = d_middle.astype(bf16)
    grad_wo = jnp.einsum("tc,td->cd", attended, d_middle_low, preferred_element_type=f32)
    d_attended = (
        jnp.einsum("td,cd->tc", d_middle_low, mat_o, preferred_element_type=f32)
        .astype(bf16)
        .reshape(sequence_length, heads_kv, groups, head_size)
    )
    d_probs = jnp.einsum("tkgd,ukd->kgtu", d_attended, value_rows, preferred_element_type=f32)
    d_values = (
        jnp.einsum("kgtu,tkgd->ukd", probs_low, d_attended, preferred_element_type=f32)
        .astype(bf16)
        .reshape(sequence_length, heads_kv * head_size)
    )
    d_scores = (attn_probs * (d_probs - jnp.sum(attn_probs * d_probs, axis=-1, keepdims=True))).astype(bf16)
    d_queries = (
        jnp.einsum("kgtu,ukd->tkgd", d_scores, keys, preferred_element_type=f32).reshape(
            sequence_length, heads_q, head_size
        )
        * score_scale
    )
    d_keys = jnp.einsum("kgtu,tkgd->ukd", d_scores, query_rows, preferred_element_type=f32) * score_scale
    d_q_scaled = rotate_back(d_queries, cosine_lookup, sine_lookup)
    d_k_scaled = rotate_back(d_keys, cosine_lookup, sine_lookup)
    grad_gain_q = jnp.sum(d_q_scaled * q_norm, axis=(0, 1))
    grad_gain_k = jnp.sum(d_k_scaled * k_norm, axis=(0, 1))
    d_q_proj = (
        rms_back(d_q_scaled * gain_q, q_norm, q_inv).astype(bf16).reshape(sequence_length, heads_q * head_size)
    )
    d_k_proj = (
        rms_back(d_k_scaled * gain_k, k_norm, k_inv).astype(bf16).reshape(sequence_length, heads_kv * head_size)
    )
    d_qkv = jnp.concatenate([d_q_proj, d_k_proj, d_values], axis=1)
    grad_qkv = jnp.einsum("tc,tf->cf", hidden_first, d_qkv, preferred_element_type=f32)
    d_h_one = jnp.einsum("tf,cf->tc", d_qkv, mat_qkv[:, :wide_all], preferred_element_type=f32)
    grad_attn = jnp.sum(d_h_one * norm_one, axis=0)
    grad_input = d_middle + rms_back(d_h_one * gain_attn, norm_one, inv_one)

    def dense_sum(value):
        blocks = value.astype(bf16).reshape(rep_count, ep_count, -1, value.shape[1])
        inner = lax.psum_scatter(blocks, "ep", scatter_dimension=1, tiled=False)
        return lax.psum_scatter(inner, "rep", scatter_dimension=0, tiled=False).astype(f32)

    small_grads = jnp.concatenate([grad_router, grad_attn[:, None], grad_ffn[:, None]], axis=1)
    small_grads = jnp.pad(small_grads, ((0, 0), (0, EXT - small_grads.shape[1])))
    sum_qkv = dense_sum(jnp.concatenate([grad_qkv.astype(bf16), small_grads.astype(bf16)], axis=1))
    sum_o = dense_sum(grad_wo)
    small_sum = sum_qkv[:, wide_all:]
    head_sums = lax.psum(jnp.stack([grad_gain_q, grad_gain_k]), everywhere)
    return (
        layer_out[None],
        grad_input[None],
        small_sum[:, experts],
        sum_qkv[:, :wide_q],
        sum_qkv[:, wide_q : wide_q + wide_kv],
        sum_qkv[:, wide_q + wide_kv : wide_all],
        sum_o,
        small_sum[:, experts + 1],
        small_sum[:, :experts],
        head_sums,
        expert_sums[0],
        expert_sums[1],
        expert_sums[2],
    )


def solution(mesh):
    both = ("rep", "ep")
    placed = (
        P(both, None, None),
        P(both, None, None),
        P(both),
        P(both, None),
        P(both, None),
        P(both, None),
        P(both, None),
        P(both),
        P(both, None),
        P(),
        P("ep", None, None),
        P("ep", None, None),
        P("ep", None, None),
        P(),
        P(both, None, None),
        P(both, None),
    )
    return jax.shard_map(
        per_device,
        mesh=mesh,
        in_specs=placed,
        out_specs=(
            P(both, None, None),
            P(both, None, None),
            P(both),
            P(both, None),
            P(both, None),
            P(both, None),
            P(both, None),
            P(both),
            P(both, None),
            P(),
            P("ep", "rep", None),
            P("ep", "rep", None),
            P("ep", "rep", None),
        ),
        check_vma=False,
    )
```

```python
import functools

import jax
import jax.numpy as jnp
from jax import lax
from jax.experimental import pallas as pl
from jax.experimental.pallas import tpu as pltpu
from jax.sharding import PartitionSpec as P

eps = 1e-06
rope_base = 1000000.0
top_precision = lax.Precision.HIGHEST
MESH = pl.DeviceIdType.MESH
f32, bf16 = jnp.float32, jnp.bfloat16
EXT = 128
UNIT = 16
TILE = 256
VMEM_BYTES = 58 * 1024 * 1024


def rms_parts(value_rows):
    inverse = lax.rsqrt(jnp.mean(value_rows * value_rows, axis=-1, keepdims=True) + eps)
    return (value_rows * inverse, inverse)


def rms_back(grad_norm, normed, inverse):
    return inverse * (grad_norm - normed * jnp.mean(grad_norm * normed, axis=-1, keepdims=True))


def rope_tables(count, head_size):
    half_size = head_size // 2
    freqs = rope_base ** (-2.0 * jnp.arange(half_size, dtype=f32) / head_size)
    angles = jnp.arange(count, dtype=f32)[:, None] * freqs[None, :]
    cosine_lookup = jnp.concatenate([jnp.cos(angles), jnp.cos(angles)], axis=1)
    sine_lookup = jnp.concatenate([jnp.sin(angles), jnp.sin(angles)], axis=1)
    return (cosine_lookup, sine_lookup)


def apply_rotation(value_rows, cosine_lookup, sine_lookup):
    half_size = value_rows.shape[-1] // 2
    turned = jnp.concatenate([-value_rows[..., half_size:], value_rows[..., :half_size]], axis=-1)
    return value_rows * cosine_lookup[:, None, :] + turned * sine_lookup[:, None, :]


def rotate_back(grads, cosine_lookup, sine_lookup):
    half_size = grads.shape[-1] // 2
    scaled = grads * sine_lookup[:, None, :]
    turned = jnp.concatenate([scaled[..., half_size:], -scaled[..., :half_size]], axis=-1)
    return grads * cosine_lookup[:, None, :] + turned


def bits_of(count):
    return count.bit_length() - 1


def gather_orders(count):
    bits = bits_of(count)
    up = list(range(1, bits)) + [0]
    down = list(range(bits - 1, 0, -1)) + [0]
    return (up, down)


def spans(bits):
    masks = [0]
    for bit in bits:
        masks = masks + [m | (1 << bit) for m in masks]
    return masks


def meet(peers):
    barrier = pltpu.get_barrier_semaphore()
    for peer in peers:
        pl.semaphore_signal(barrier, inc=1, device_id=peer, device_id_type=MESH)
    pl.semaphore_wait(barrier, len(peers))


def token_gather_kernel(count, x_ref, out_ref, send_sem, recv_sem, local_sem):
    rep, me = lax.axis_index("rep"), lax.axis_index("ep")
    bits = bits_of(count)
    half = x_ref.shape[0] // 2
    meet([(rep, me ^ (1 << b)) for b in range(bits)])
    local = pltpu.make_async_copy(x_ref, out_ref.at[me], local_sem)
    local.start()
    orders = gather_orders(count)
    copies = []

    def send(h, mask, bit):
        rows = pl.ds(h * half, half)
        source = x_ref.at[rows] if mask == 0 else out_ref.at[me ^ mask, rows]
        there = mask | (1 << bit)
        copy = pltpu.make_async_remote_copy(
            src_ref=source,
            dst_ref=out_ref.at[me ^ mask, rows],
            send_sem=send_sem.at[h, there],
            recv_sem=recv_sem.at[h, there],
            device_id=(rep, me ^ (1 << bit)),
            device_id_type=MESH,
        )
        copy.start()
        copies.append(copy)

    def arrived(h, mask):
        rows = pl.ds(h * half, half)
        pltpu.make_async_copy(
            x_ref.at[rows], out_ref.at[me ^ mask, rows], recv_sem.at[h, mask]
        ).wait()

    for stage in range(bits):
        for h in range(2):
            send(h, 0, orders[h][stage])
    for stage in range(bits):
        for low in spans(orders[0][:stage]):
            index = spans(orders[0][:stage]).index(low)
            for h in range(2):
                mask = spans(orders[h][:stage])[index] | (1 << orders[h][stage])
                arrived(h, mask)
                for later in range(stage + 1, bits):
                    send(h, mask, orders[h][later])
    for copy in copies:
        copy.wait_send()
    local.wait()


def gather_tokens(x, count, collective_id):
    return pl.pallas_call(
        functools.partial(token_gather_kernel, count),
        out_shape=jax.ShapeDtypeStruct((count,) + x.shape, x.dtype),
        in_specs=[pl.BlockSpec(memory_space=pl.ANY)],
        out_specs=pl.BlockSpec(memory_space=pl.ANY),
        scratch_shapes=[
            pltpu.SemaphoreType.DMA((2, count)),
            pltpu.SemaphoreType.DMA((2, count)),
            pltpu.SemaphoreType.DMA,
        ],
        compiler_params=pltpu.CompilerParams(collective_id=collective_id, has_side_effects=True),
        name="token_gather",
    )(x)


def token_sum_kernel(count, widths, y_ref, out_ref, *scratch):
    bits = bits_of(count)
    own, got = scratch[:2], scratch[2:4]
    send_sem, recv_sem, own_sem, out_sem = scratch[4:8]
    result = scratch[8:10]
    rep, me = lax.axis_index("rep"), lax.axis_index("ep")
    meet([(rep, me ^ (1 << b)) for b in range(bits)])
    orders = [list(reversed(o)) for o in gather_orders(count)]
    columns = (pl.ds(0, widths[0]), pl.ds(widths[0], widths[1]))
    sends = []
    firsts = [list(reversed(spans(o[1:]))) for o in orders]
    slot_of = []
    for h in range(2):
        table, base = {}, 0
        for stage in range(bits):
            for place, mask in enumerate(reversed(spans(orders[h][stage + 1 :]))):
                table[(stage, mask)] = base + place
            base += 1 << (bits - 1 - stage)
        slot_of.append(table)
    seat = [{mask: i for i, mask in enumerate(firsts[h])} for h in range(2)]

    def send(h, stage, mask):
        bit = 1 << orders[h][stage]
        slot = slot_of[h][(stage, mask)]
        source = y_ref.at[me ^ bit ^ mask, :, columns[h]] if stage == 0 else own[h].at[seat[h][bit | mask]]
        copy = pltpu.make_async_remote_copy(
            src_ref=source,
            dst_ref=got[h].at[slot],
            send_sem=send_sem.at[h, slot],
            recv_sem=recv_sem.at[h, slot],
            device_id=(rep, me ^ bit),
            device_id_type=MESH,
        )
        copy.start()
        sends.append(copy)

    loads = [{}, {}]
    for i in range(len(firsts[0])):
        for h in range(2):
            mask = firsts[h][i]
            send(h, 0, mask)
            load = pltpu.make_async_copy(
                y_ref.at[me ^ mask, :, columns[h]], own[h].at[seat[h][mask]], own_sem.at[h, i]
            )
            load.start()
            loads[h][mask] = load

    rows_total = y_ref.shape[1]
    step = 32

    def add(h, stage, mask):
        slot = slot_of[h][(stage, mask)]
        if stage == 0:
            loads[h][mask].wait()
        pltpu.make_async_copy(got[h].at[slot], got[h].at[slot], recv_sem.at[h, slot]).wait()
        last = stage == bits - 1

        def body(i, carry):
            rows = pl.ds(pl.multiple_of(i * step, step), step)
            total = own[h][seat[h][mask], rows, :].astype(f32) + got[h][slot, rows, :].astype(f32)
            if last:
                result[h][rows, :] = total
            else:
                own[h][seat[h][mask], rows, :] = total.astype(bf16)
            return carry

        lax.fori_loop(0, rows_total // step, body, 0)

    for stage in range(bits):
        masks = [list(reversed(spans(orders[h][stage + 1 :]))) for h in range(2)]
        for i in range(len(masks[0])):
            for h in range(2):
                mask = masks[h][i]
                add(h, stage, mask)
                if stage + 1 < bits:
                    following = 1 << orders[h][stage + 1]
                    if mask & following:
                        send(h, stage + 1, mask & ~following)
    outs = []
    for h in range(2):
        out = pltpu.make_async_copy(result[h], out_ref.at[:, columns[h]], out_sem.at[h])
        out.start()
        outs.append(out)
    for copy in sends:
        copy.wait_send()
    for out in outs:
        out.wait()


def sum_tokens(y, count, widths, collective_id):
    rows = y.shape[1]
    half = count // 2
    return pl.pallas_call(
        functools.partial(token_sum_kernel, count, widths),
        out_shape=jax.ShapeDtypeStruct(y.shape[1:], f32),
        in_specs=[pl.BlockSpec(memory_space=pl.ANY)],
        out_specs=pl.BlockSpec(memory_space=pl.ANY),
        scratch_shapes=[
            pltpu.VMEM((half, rows, widths[0]), bf16),
            pltpu.VMEM((half, rows, widths[1]), bf16),
            pltpu.VMEM((count - 1, rows, widths[0]), bf16),
            pltpu.VMEM((count - 1, rows, widths[1]), bf16),
            pltpu.SemaphoreType.DMA((2, count)),
            pltpu.SemaphoreType.DMA((2, count)),
            pltpu.SemaphoreType.DMA((2, half)),
            pltpu.SemaphoreType.DMA((2,)),
            pltpu.VMEM((rows, widths[0]), f32),
            pltpu.VMEM((rows, widths[1]), f32),
        ],
        compiler_params=pltpu.CompilerParams(
            collective_id=collective_id, has_side_effects=True, vmem_limit_bytes=VMEM_BYTES
        ),
        name="token_sum",
    )(y)


def dense_sum_kernel(n_rep, n_ep, rows, chunks, split, *refs):
    left_ref, right_ref, small_ref, head_ref, out_ref, head_out = refs[:6]
    rest = list(refs[6:])
    bits = bits_of(n_ep)
    wide = right_ref.shape[1] // (chunks - 1)
    half = wide // 2
    rep, me = lax.axis_index("rep"), lax.axis_index("ep")
    mine = [lax.rem(lax.div(me, 1 << b), 2) for b in range(bits)]
    part, got_core = rest[:2]
    acc = [None] + [rest[2 + 2 * k : 4 + 2 * k] for k in range(bits)]
    rest = rest[2 + 2 * bits :]
    got = [None] + [rest[2 * k : 2 * k + 2] for k in range(bits)]
    rest = rest[2 * bits :]
    head_own, head_got, head_rep = rest[:3]
    core_send, core_recv, step_send, step_recv, rep_send, rep_recv, head_send, head_recv, head_rs, head_rr = rest[3:]
    up = list(range(1, bits))
    orders = (up, up[::-1])
    left = [[sorted(set(up) - set(o[:k])) for k in range(bits)] for o in orders]
    lags = [0, 1]
    for _ in range(bits):
        lags.append(lags[-1] + 2)
    deep = 4
    others = [lax.rem(rep + d, n_rep) for d in range(1, n_rep)]
    meet([(rep, me ^ (1 << b)) for b in range(bits)] + [(other, me) for other in others])

    def core_copy(c):
        slot = lax.rem(c, 2)
        return pltpu.make_async_remote_copy(
            src_ref=part.at[slot, 1 - mine[0]],
            dst_ref=got_core.at[slot],
            send_sem=core_send.at[slot],
            recv_sem=core_recv.at[slot],
            device_id=(rep, me ^ 1),
            device_id_type=MESH,
        )

    def bit_copy(k, h, c):
        slot = lax.rem(c, deep)
        bit = orders[h][k - 1]
        place = left[h][k - 1].index(bit)
        return pltpu.make_async_remote_copy(
            src_ref=acc[k][h].at[(slot,) + (slice(None),) * place + (1 - mine[bit],)],
            dst_ref=got[k][h].at[slot],
            send_sem=step_send.at[k, h, slot],
            recv_sem=step_recv.at[k, h, slot],
            device_id=(rep, me ^ (1 << bit)),
            device_id_type=MESH,
        )

    def rep_copy(h, c, d):
        slot = lax.rem(c, deep)
        return pltpu.make_async_remote_copy(
            src_ref=acc[bits][h].at[slot, others[d]],
            dst_ref=got[bits][h].at[slot, n_rep - 2 - d],
            send_sem=rep_send.at[h, slot, d],
            recv_sem=rep_recv.at[h, slot, n_rep - 2 - d],
            device_id=(others[d], me),
            device_id_type=MESH,
        )

    corners = [()]
    for _ in up:
        corners = [c + (v,) for c in corners for v in range(2)]
    block = n_rep * rows
    side_rows = len(corners) * block

    def stage_make(c):
        slot = lax.rem(c, 2)

        @pl.when(c >= 2)
        def _():
            core_copy(c - 2).wait_send()

        @pl.when(c < chunks - 1)
        def _():
            which = jnp.where(c >= split[0], 1, 0) + jnp.where(c >= split[1], 1, 0)
            columns = pl.ds(pl.multiple_of(c * wide, wide), wide)
            weights = right_ref[:, columns]
            for side in (1, 0):
                which_side = 1 - mine[0] if side else mine[0]
                for n, corner in enumerate(corners):
                    start = (which * 2 + which_side) * side_rows + n * block
                    value = jnp.dot(
                        left_ref[pl.ds(pl.multiple_of(start, block), block), :],
                        weights,
                        preferred_element_type=f32,
                    )
                    part[(slot, which_side) + corner] = value.astype(bf16).reshape(n_rep, rows, wide)

        @pl.when(c == chunks - 1)
        def _():
            thin = small_ref.shape[1]
            for side in range(2):
                for n, corner in enumerate(corners):
                    value = small_ref[pl.ds(side * side_rows + n * block, block), :].reshape(n_rep, rows, thin)
                    blank = jnp.zeros((n_rep, rows, wide - thin), bf16)
                    part[(slot, side) + corner + (slice(None), slice(None), slice(0, thin))] = value
                    part[(slot, side) + corner + (slice(None), slice(None), slice(thin, wide))] = blank

        core_copy(c).start()

    def stage_core(c):
        slot, put = lax.rem(c, 2), lax.rem(c, deep)

        @pl.when(c >= deep)
        def _():
            for h in range(2):
                if bits > 1:
                    bit_copy(1, h, c - deep).wait_send()

        core_copy(c).wait_recv()
        for corner in corners:
            total = part[(slot, mine[0]) + corner].astype(f32) + got_core[(slot,) + corner].astype(f32)
            total = total.astype(bf16)
            for h in range(2):
                acc[1][h][(put,) + corner] = total[:, :, h * half : (h + 1) * half]
        for h in range(2):
            bit_copy(1, h, c).start()

    def stage_bit(k, c):
        slot = lax.rem(c, deep)
        for h in range(2):
            bit = orders[h][k - 2]
            place = left[h][k - 2].index(bit)

            @pl.when(c >= deep)
            def _(h=h):
                if k < bits:
                    bit_copy(k, h, c - deep).wait_send()
                else:
                    for d in range(n_rep - 1):
                        rep_copy(h, c - deep, d).wait_send()

            bit_copy(k - 1, h, c).wait_recv()
            small_corners = [()]
            for _ in left[h][k - 1]:
                small_corners = [q + (v,) for q in small_corners for v in range(2)]
            for corner in small_corners:
                full = corner[:place] + (mine[bit],) + corner[place:]
                total = acc[k - 1][h][(slot,) + full].astype(f32) + got[k - 1][h][(slot,) + corner].astype(f32)
                acc[k][h][(slot,) + corner] = total.astype(bf16)
            if k < bits:
                bit_copy(k, h, c).start()
            else:
                for d in range(n_rep - 1):
                    rep_copy(h, c, d).start()

    def stage_end(c):
        slot = lax.rem(c, deep)
        for h in range(2):
            total = acc[bits][h][slot, rep].astype(f32)
            for d in range(n_rep - 1):
                rep_copy(h, c, d).wait_recv()
            for d in range(n_rep - 1):
                total += got[bits][h][slot, d].astype(f32)
            out_ref[:, pl.ds(pl.multiple_of(c * wide + h * half, half), half)] = total

    def head_copy(t):
        return pltpu.make_async_remote_copy(
            src_ref=head_own.at[t],
            dst_ref=head_got.at[t],
            send_sem=head_send.at[t],
            recv_sem=head_recv.at[t],
            device_id=(rep, me ^ (1 << t)),
            device_id_type=MESH,
        )

    def head_rep_copy(d):
        return pltpu.make_async_remote_copy(
            src_ref=head_own.at[bits],
            dst_ref=head_rep.at[rep],
            send_sem=head_rs.at[d],
            recv_sem=head_rr.at[n_rep - 2 - d],
            device_id=(others[d], me),
            device_id_type=MESH,
        )

    def head_step(t):
        if t == 0:
            head_own[0] = head_ref[...]
            head_copy(0).start()
        elif t <= bits:
            head_copy(t - 1).wait_recv()
            head_own[t] = head_own[t - 1] + head_got[t - 1]
            if t < bits:
                head_copy(t).start()
            else:
                for d in range(n_rep - 1):
                    head_rep_copy(d).start()
                head_rep[rep] = head_own[bits]
        else:
            for d in range(n_rep - 1):
                head_rep_copy(d).wait_recv()
            total = head_rep[0]
            for r in range(1, n_rep):
                total = total + head_rep[r]
            head_out[...] = total

    def step(i, carry):
        for stage in reversed(range(len(lags))):
            c = i - lags[stage]

            @pl.when((c >= 0) & (c < chunks))
            def _(stage=stage, c=c):
                if stage == 0:
                    stage_make(c)
                elif stage == 1:
                    stage_core(c)
                elif stage <= bits:
                    stage_bit(stage, c)
                else:
                    stage_end(c)

        for t in range(bits + 2):

            @pl.when(i == t)
            def _(t=t):
                head_step(t)

        return carry

    lax.fori_loop(0, chunks + lags[-1], step, 0)
    for c in range(chunks - 2, chunks):
        core_copy(c).wait_send()
    for c in range(chunks - deep, chunks):
        for h in range(2):
            for k in range(1, bits):
                bit_copy(k, h, c).wait_send()
            for d in range(n_rep - 1):
                rep_copy(h, c, d).wait_send()
    for t in range(bits):
        head_copy(t).wait_send()
    for d in range(n_rep - 1):
        head_rep_copy(d).wait_send()


def dense_sum(left, right, small, head, n_rep, n_ep, split, collective_id):
    chunk = 512
    chunks = right.shape[1] // chunk + 1
    bits = bits_of(n_ep)
    rows = left.shape[0] // (3 * n_rep * n_ep)
    deep = 4
    half = chunk // 2
    vmem = pl.BlockSpec(memory_space=pltpu.VMEM)
    inner = (n_rep, rows)
    scratch = [
        pltpu.VMEM((2, 2) + (2,) * (bits - 1) + inner + (chunk,), bf16),
        pltpu.VMEM((2,) + (2,) * (bits - 1) + inner + (chunk,), bf16),
    ]
    for k in range(1, bits + 1):
        scratch += [pltpu.VMEM((deep,) + (2,) * (bits - k) + inner + (half,), bf16)] * 2
    for k in range(1, bits):
        scratch += [pltpu.VMEM((deep,) + (2,) * (bits - 1 - k) + inner + (half,), bf16)] * 2
    scratch += [pltpu.VMEM((deep, n_rep - 1, rows, half), bf16)] * 2
    scratch += [
        pltpu.VMEM((bits + 1,) + head.shape, f32),
        pltpu.VMEM((bits,) + head.shape, f32),
        pltpu.VMEM((n_rep,) + head.shape, f32),
        pltpu.SemaphoreType.DMA((2,)),
        pltpu.SemaphoreType.DMA((2,)),
        pltpu.SemaphoreType.DMA((bits, 2, deep)),
        pltpu.SemaphoreType.DMA((bits, 2, deep)),
        pltpu.SemaphoreType.DMA((2, deep, n_rep - 1)),
        pltpu.SemaphoreType.DMA((2, deep, n_rep - 1)),
        pltpu.SemaphoreType.DMA((bits,)),
        pltpu.SemaphoreType.DMA((bits,)),
        pltpu.SemaphoreType.DMA((n_rep - 1,)),
        pltpu.SemaphoreType.DMA((n_rep - 1,)),
    ]
    return pl.pallas_call(
        functools.partial(dense_sum_kernel, n_rep, n_ep, rows, chunks, split),
        out_shape=(
            jax.ShapeDtypeStruct((rows, chunks * chunk), f32),
            jax.ShapeDtypeStruct(head.shape, f32),
        ),
        in_specs=[vmem] * 4,
        out_specs=(vmem, vmem),
        scratch_shapes=scratch,
        compiler_params=pltpu.CompilerParams(
            collective_id=collective_id, has_side_effects=True, vmem_limit_bytes=VMEM_BYTES
        ),
        cost_estimate=pl.CostEstimate(
            flops=2 * left.shape[0] * left.shape[1] * right.shape[1],
            bytes_accessed=600_000_000,
            transcendentals=0,
        ),
        name="dense_sum",
    )(left, right, small, head)


NT = (((1,), (1,)), ((), ()))
TN = (((0,), (0,)), ((), ()))


def expert_kernel(first, last, experts, width, *refs):
    (info, h_ref, g_ref, wg_ref, wu_ref, wd_ref) = refs[:6]
    rest = list(refs[6:])
    prev_ref = None if first else rest.pop(0)
    y_ref, gwg_ref, gwu_ref, gwd_ref = rest[:4]
    xs, gs, ds, hs, stage, prev_buf, wide, tall, in_sem, out_sem, prev_sem, grad_sem = rest[4:]
    hidden = wg_ref.shape[1]
    units = info[0]
    expert = info[1]
    table = 8
    per_tile = TILE // UNIT
    tiles = (units + per_tile - 1) // per_tile
    most = xs.shape[0] // TILE
    floor_tiles = min(4, most)

    def unit_in(u, slot):
        source = pl.ds(pl.multiple_of(info[table + u], UNIT), UNIT)
        target = pl.ds(pl.multiple_of(u * UNIT, UNIT), UNIT)
        return (
            pltpu.make_async_copy(h_ref.at[source], xs.at[target], in_sem.at[0, slot]),
            pltpu.make_async_copy(g_ref.at[source], gs.at[target], in_sem.at[1, slot]),
        )

    def begin(u, carry):
        for copy in unit_in(u, u // per_tile):
            copy.start()
        return carry

    lax.fori_loop(0, units, begin, 0)

    def blank(u, carry):
        target = pl.ds(pl.multiple_of(u * UNIT, UNIT), UNIT)
        xs[target, :] = jnp.zeros((UNIT, xs.shape[1]), bf16)
        gs[target, :] = jnp.zeros((UNIT, gs.shape[1]), bf16)
        return carry

    lax.fori_loop(units, jnp.maximum(tiles, floor_tiles) * per_tile, blank, 0)

    def blank_tile(i, carry):
        target = pl.ds(pl.multiple_of(i * TILE, TILE), TILE)
        ds[target, :] = jnp.zeros((TILE, ds.shape[1]), bf16)
        hs[target, :] = jnp.zeros((TILE, hs.shape[1]), bf16)
        return carry

    lax.fori_loop(tiles, floor_tiles, blank_tile, 0)

    def prev_copy(i):
        rows = pl.ds(pl.multiple_of(i * TILE, TILE), TILE)
        return pltpu.make_async_copy(prev_ref.at[rows], prev_buf.at[i % 2], prev_sem.at[i % 2])

    if not first:
        prev_copy(0).start()

    def unit_out(u):
        target = pl.ds(pl.multiple_of(info[table + u], UNIT), UNIT)
        tile = u // per_tile
        source = pl.ds(pl.multiple_of((u % per_tile) * UNIT, UNIT), UNIT)
        return pltpu.make_async_copy(stage.at[tile % 2, source], y_ref.at[target], out_sem.at[tile % 2])

    def out_start(i):
        if last:
            lax.fori_loop(
                i * per_tile,
                jnp.minimum((i + 1) * per_tile, units),
                lambda u, c: (unit_out(u).start(), c)[1],
                0,
            )
        else:
            rows = pl.ds(pl.multiple_of(i * TILE, TILE), TILE)
            pltpu.make_async_copy(stage.at[i % 2], y_ref.at[rows], out_sem.at[i % 2]).start()

    def out_wait(i):
        if last:
            lax.fori_loop(
                i * per_tile,
                jnp.minimum((i + 1) * per_tile, units),
                lambda u, c: (unit_out(u).wait(), c)[1],
                0,
            )
        else:
            rows = pl.ds(pl.multiple_of(i * TILE, TILE), TILE)
            pltpu.make_async_copy(stage.at[i % 2], y_ref.at[rows], out_sem.at[i % 2]).wait()

    lane = lax.broadcasted_iota(jnp.int32, (TILE, EXT), 1)
    weight_lanes = (lane == expert) | (lane == expert + experts) | (lane == expert + 2 * experts)

    def tile_step(i, carry):
        def landed(u, c):
            for copy in unit_in(u, i):
                copy.wait()
            return c

        lax.fori_loop(i * per_tile, jnp.minimum((i + 1) * per_tile, units), landed, 0)
        rows = pl.ds(pl.multiple_of(i * TILE, TILE), TILE)
        x = xs[rows, :width]
        g = gs[rows, :]
        extra = xs[rows, width:].astype(f32)
        weight = jnp.sum(jnp.where(weight_lanes, extra, 0.0), axis=1, keepdims=True)
        gate = jnp.dot(x, wg_ref[...], preferred_element_type=f32)
        up = jnp.dot(x, wu_ref[...], preferred_element_type=f32)
        d_plain = lax.dot_general(g, wd_ref[...], NT, preferred_element_type=f32)
        sig = 1.0 / (1.0 + jnp.exp(-gate))
        silu = gate * sig
        hid = silu * up
        d_weight = jnp.sum(hid.astype(bf16).astype(f32) * d_plain, axis=1, keepdims=True)
        hs[rows, :] = (hid * weight).astype(bf16)
        d_hidden = d_plain * weight
        ds[rows, :hidden] = (d_hidden * up * sig * (1.0 + gate * (1.0 - sig))).astype(bf16)
        ds[rows, hidden:] = (d_hidden * silu).astype(bf16)

        @pl.when(i >= 2)
        def _():
            out_wait(i - 2)

        if not first:

            @pl.when(i + 1 < tiles)
            def _():
                prev_copy(i + 1).start()

            prev_copy(i).wait()
        slot = i % 2
        high = d_weight.astype(bf16).astype(f32)
        low = d_weight - high
        note = jnp.where(lane == expert, high, 0.0) + jnp.where(lane == expert + experts, low, 0.0)
        d_row = lax.dot_general(ds[rows, :hidden], wg_ref[...], NT, preferred_element_type=f32)
        d_row += lax.dot_general(ds[rows, hidden:], wu_ref[...], NT, preferred_element_type=f32)
        if not first:
            d_row += prev_buf[slot, :, :width].astype(f32)
            note += prev_buf[slot, :, width : width + EXT].astype(f32)
        stage[slot, :, :width] = d_row.astype(bf16)
        stage[slot, :, width : width + EXT] = note.astype(bf16)
        out = jnp.dot(hs[rows, :], wd_ref[...], preferred_element_type=f32)
        if not first:
            out += prev_buf[slot, :, width + EXT :].astype(f32)
        stage[slot, :, width + EXT :] = out.astype(bf16)
        out_start(i)
        return carry

    lax.fori_loop(0, tiles, tile_step, 0)

    block = 256

    def grads(depth):
        def wide_copies(m):
            rows = pl.ds(pl.multiple_of(m * block, block), block)
            return (
                pltpu.make_async_copy(wide.at[m % 2, :, :hidden], gwg_ref.at[rows], grad_sem.at[0, m % 2]),
                pltpu.make_async_copy(wide.at[m % 2, :, hidden:], gwu_ref.at[rows], grad_sem.at[1, m % 2]),
            )

        def wide_step(m, carry):
            @pl.when(m >= 2)
            def _():
                for copy in wide_copies(m - 2):
                    copy.wait()

            columns = pl.ds(pl.multiple_of(m * block, block), block)
            wide[m % 2] = lax.dot_general(
                xs[:depth, columns], ds[:depth, :], TN, preferred_element_type=f32
            ).astype(bf16)
            for copy in wide_copies(m):
                copy.start()
            return carry

        count = width // block
        lax.fori_loop(0, count, wide_step, 0)
        for m in range(count - 2, count):
            for copy in wide_copies(m):
                copy.wait()

        def tall_copy(m):
            rows = pl.ds(pl.multiple_of(m * block, block), block)
            return pltpu.make_async_copy(tall.at[m % 2], gwd_ref.at[rows], grad_sem.at[0, m % 2])

        def tall_step(m, carry):
            @pl.when(m >= 2)
            def _():
                tall_copy(m - 2).wait()

            columns = pl.ds(pl.multiple_of(m * block, block), block)
            tall[m % 2] = lax.dot_general(
                hs[:depth, columns], gs[:depth, :], TN, preferred_element_type=f32
            ).astype(bf16)
            tall_copy(m).start()
            return carry

        count = hidden // block
        lax.fori_loop(0, count, tall_step, 0)
        for m in range(count - 2, count):
            tall_copy(m).wait()

    for choice in range(floor_tiles, most + 1):
        chosen = (tiles <= choice) if choice == floor_tiles else (tiles == choice)

        @pl.when(chosen)
        def _(choice=choice):
            grads(choice * TILE)

    @pl.when(tiles >= 2)
    def _():
        out_wait(tiles - 2)

    out_wait(tiles - 1)


def expert_pass(info, h_rows, g_rows, w_gate, w_up, w_down, prev, last, experts):
    tokens, width = g_rows.shape
    hidden = w_gate.shape[1]
    wide_row = width + EXT + width
    any_spec = pl.BlockSpec(memory_space=pl.ANY)
    vmem_spec = pl.BlockSpec(memory_space=pltpu.VMEM)
    first = prev is None
    operands = [info, h_rows, g_rows, w_gate, w_up, w_down] + ([] if first else [prev])
    specs = [pl.BlockSpec(memory_space=pltpu.SMEM), any_spec, any_spec, vmem_spec, vmem_spec, vmem_spec]
    specs += [] if first else [any_spec]
    return pl.pallas_call(
        functools.partial(expert_kernel, first, last, experts, width),
        out_shape=(
            jax.ShapeDtypeStruct((tokens, wide_row), bf16),
            jax.ShapeDtypeStruct((width, hidden), bf16),
            jax.ShapeDtypeStruct((width, hidden), bf16),
            jax.ShapeDtypeStruct((hidden, width), bf16),
        ),
        in_specs=specs,
        out_specs=(any_spec,) * 4,
        scratch_shapes=[
            pltpu.VMEM((tokens, width + EXT), bf16),
            pltpu.VMEM((tokens, width), bf16),
            pltpu.VMEM((tokens, 2 * hidden), bf16),
            pltpu.VMEM((tokens, hidden), bf16),
            pltpu.VMEM((2, TILE, wide_row), bf16),
            pltpu.VMEM((2, TILE, wide_row), bf16),
            pltpu.VMEM((2, 256, 2 * hidden), bf16),
            pltpu.VMEM((2, 256, width), bf16),
            pltpu.SemaphoreType.DMA((2, tokens // TILE)),
            pltpu.SemaphoreType.DMA((2,)),
            pltpu.SemaphoreType.DMA((2,)),
            pltpu.SemaphoreType.DMA((2, 2)),
        ],
        compiler_params=pltpu.CompilerParams(vmem_limit_bytes=VMEM_BYTES),
        cost_estimate=pl.CostEstimate(
            flops=18 * tokens * width * hidden, bytes_accessed=12 * tokens * width, transcendentals=0
        ),
        name="experts",
    )(*operands)


def unit_table(lengths):
    per_sequence = TILE // UNIT
    counts = (lengths + UNIT - 1) // UNIT
    unit = jnp.arange(lengths.shape[0] * per_sequence, dtype=jnp.int32)
    live = (unit % per_sequence) < jnp.repeat(counts, per_sequence)
    place = jnp.cumsum(live.astype(jnp.int32)) - 1
    hit = (place[None, :] == unit[:, None]) & live[None, :]
    rows = jnp.sum(jnp.where(hit, unit[None, :] * UNIT, 0), axis=1)
    return (jnp.sum(counts), rows)


def split_three(value):
    high = lax.reduce_precision(value, 8, 7)
    rest = value - high
    middle = lax.reduce_precision(rest, 8, 7)
    return jnp.concatenate([high, middle, rest - middle], axis=-1)


def per_device(
    hidden_in,
    out_grad,
    attn_gain,
    w_q,
    key_weight,
    value_weight,
    w_o,
    ffn_gain,
    router_w,
    qk_gains,
    w_gate,
    w_up,
    w_down,
    lengths,
    routes,
    order,
):
    everywhere = ("rep", "ep")
    rep_count, ep_count = (lax.axis_size("rep"), lax.axis_size("ep"))
    rep_index, ep_index = (lax.axis_index("rep"), lax.axis_index("ep"))
    inputs = hidden_in[0].astype(f32)
    sequence_length, model_width = inputs.shape
    head_size = qk_gains.shape[1]
    wide_q, wide_kv = (w_q.shape[1], key_weight.shape[1])
    heads_q, heads_kv = (wide_q // head_size, wide_kv // head_size)
    groups = heads_q // heads_kv
    local_experts = w_gate.shape[0]
    experts = local_experts * ep_count
    top_count = routes.shape[2]
    score_scale = head_size ** (-0.5)
    group_lengths = lax.dynamic_slice_in_dim(lengths, rep_index * ep_count, ep_count)
    length = lax.dynamic_index_in_dim(group_lengths, ep_index, keepdims=False)
    positions = jnp.arange(sequence_length, dtype=jnp.int32)
    live = positions < length
    live_rows = live.astype(f32)

    expert_iota = jnp.arange(experts, dtype=jnp.int32)
    route_hot = routes[0][..., None] == expert_iota
    routed = jnp.any(route_hot, axis=1) & live[:, None]
    order_of = jnp.sum(
        jnp.where(route_hot, order[0].reshape(sequence_length, top_count)[..., None], 0), axis=1
    )
    sort_key = jnp.where(routed, order_of, sequence_length * top_count)
    loads = jnp.sum(routed.astype(jnp.int32), axis=0)
    rank = jnp.sum((sort_key[None, :, :] < sort_key[:, None, :]).astype(jnp.int32), axis=1)

    own_rows = w_q.shape[0]
    load_columns = -(-experts // own_rows)
    load_block = jnp.pad(loads, (0, load_columns * own_rows - experts)).reshape(load_columns, own_rows).T
    small = jnp.concatenate(
        [router_w, attn_gain[:, None], ffn_gain[:, None], load_block.astype(bf16)], axis=1
    )
    small = jnp.pad(small, ((0, 0), (0, EXT - small.shape[1])))
    pack = jnp.concatenate([w_q, key_weight, value_weight, small], axis=1)
    mat_qkv = lax.all_gather(pack, everywhere, axis=0, tiled=True)
    mat_o = lax.all_gather(w_o, everywhere, axis=0, tiled=True)
    grads_all = lax.all_gather(out_grad[0], "ep", axis=0, tiled=True)

    wide_all = wide_q + 2 * wide_kv
    small_all = mat_qkv[:, wide_all:]
    mat_router = small_all[:, :experts]
    gain_attn = small_all[:, experts].astype(f32)
    gain_ffn = small_all[:, experts + 1].astype(f32)
    loads_all = (
        small_all[:, experts + 2 : experts + 2 + load_columns]
        .reshape(rep_count, ep_count, own_rows, load_columns)
        .transpose(0, 1, 3, 2)
        .reshape(rep_count, ep_count, load_columns * own_rows)[:, :, :experts]
        .astype(jnp.int32)
    )
    group_loads = lax.dynamic_index_in_dim(loads_all, rep_index, keepdims=False)
    earlier = (jnp.arange(ep_count) < ep_index)[:, None]
    load_prefix = jnp.sum(jnp.where(earlier, group_loads, 0), axis=0)
    capacity = 9 * top_count * jnp.sum(group_lengths) // (8 * experts)
    kept = routed & (load_prefix[None, :] + rank < capacity)
    kept_float = kept.astype(f32)

    gain_q = qk_gains[0].astype(f32)
    gain_k = qk_gains[1].astype(f32)
    norm_one, inv_one = rms_parts(inputs)
    hidden_first = (norm_one * gain_attn).astype(bf16)
    projected = jnp.dot(hidden_first, mat_qkv, preferred_element_type=f32)
    query_projected = projected[:, :wide_q].reshape(sequence_length, heads_q, head_size)
    key_projected = projected[:, wide_q : wide_q + wide_kv].reshape(sequence_length, heads_kv, head_size)
    value_rows = (
        projected[:, wide_q + wide_kv : wide_all]
        .astype(bf16)
        .reshape(sequence_length, heads_kv, head_size)
    )
    cosine_lookup, sine_lookup = rope_tables(sequence_length, head_size)
    q_norm, q_inv = rms_parts(query_projected)
    k_norm, k_inv = rms_parts(key_projected)
    query_rows = (
        apply_rotation(q_norm * gain_q, cosine_lookup, sine_lookup)
        .astype(bf16)
        .reshape(sequence_length, heads_kv, groups, head_size)
    )
    keys = apply_rotation(k_norm * gain_k, cosine_lookup, sine_lookup).astype(bf16)
    scores = jnp.einsum("tkgd,ukd->kgtu", query_rows, keys, preferred_element_type=f32) * score_scale
    allowed = (positions[None, :] <= positions[:, None]) & (positions[None, :] < length)
    scores = jnp.where(allowed, scores, -1e30)
    attn_probs = jax.nn.softmax(scores, axis=-1)
    probs_low = attn_probs.astype(bf16)
    attended = (
        jnp.einsum("kgtu,ukd->tkgd", probs_low, value_rows, preferred_element_type=f32)
        .astype(bf16)
        .reshape(sequence_length, heads_q * head_size)
    )
    middle = inputs + jnp.dot(attended, mat_o, preferred_element_type=f32)
    norm_two, inv_two = rms_parts(middle)
    h_two = (norm_two * gain_ffn).astype(bf16)
    logits = jnp.dot(h_two, mat_router, preferred_element_type=f32)
    named = jnp.any(route_hot, axis=1)
    top_logit = jnp.max(jnp.where(named, logits, -jnp.inf), axis=1, keepdims=True)
    raised = jnp.where(named, jnp.exp(jnp.where(named, logits - top_logit, 0.0)), 0.0)
    route_gates = raised / jnp.sum(raised, axis=1, keepdims=True)
    pair_weight = route_gates * kept_float

    extra = split_three(pair_weight).astype(bf16)
    extra = jnp.pad(extra, ((0, 0), (0, EXT - extra.shape[1])))
    sent = jnp.concatenate([h_two, extra], axis=1)
    h_all = gather_tokens(sent, ep_count, 1)

    part = min(ep_count, 8)
    tokens = part * sequence_length
    sums = []
    y_parts = []
    for c in range(ep_count // part):
        live_units, unit_rows = unit_table(group_lengths[c * part : (c + 1) * part])
        h_rows = h_all[c * part : (c + 1) * part].reshape(tokens, model_width + EXT)
        g_rows = grads_all[c * tokens : (c + 1) * tokens]
        prev, found = None, []
        for local in range(local_experts):
            info = jnp.concatenate(
                [
                    jnp.stack([live_units, ep_index * local_experts + local]).astype(jnp.int32),
                    jnp.zeros((6,), jnp.int32),
                    unit_rows,
                ]
            )
            prev, *weight_grads = expert_pass(
                info,
                h_rows,
                g_rows,
                w_gate[local],
                w_up[local],
                w_down[local],
                prev,
                local == local_experts - 1,
                experts,
            )
            found.append(weight_grads)
        y_parts.append(prev.reshape(part, sequence_length, -1))
        sums.append(found)
    y_all = y_parts[0] if len(y_parts) == 1 else jnp.concatenate(y_parts, axis=0)
    expert_sums = []
    for which in range(3):
        pieces = []
        for local in range(local_experts):
            total = sums[0][local][which]
            for more in sums[1:]:
                total = (total.astype(f32) + more[local][which].astype(f32)).astype(bf16)
            pieces.append(lax.psum_scatter(total, "rep", scatter_dimension=0, tiled=True).astype(f32))
        expert_sums.append(jnp.stack(pieces))

    back = sum_tokens(y_all, ep_count, (model_width + EXT, model_width), 2)
    live_column = live[:, None]
    moe_output = jnp.where(live_column, back[:, model_width + EXT :], 0.0)
    layer_out = jnp.where(live_column, middle + moe_output, 0.0)
    grad_rows = out_grad[0].astype(f32) * live_rows[:, None]
    notes = back[:, model_width : model_width + 2 * experts]
    d_weight = jnp.where(live_column, notes[:, :experts] + notes[:, experts:], 0.0)
    d_gates = d_weight * kept_float
    d_logits = route_gates * (d_gates - jnp.sum(route_gates * d_gates, axis=-1, keepdims=True))

    router_float = mat_router.astype(f32)
    d_h_two = jnp.where(live_column, back[:, :model_width], 0.0)
    d_h_two = d_h_two + jnp.dot(d_logits, router_float.T, precision=top_precision)
    grad_router = jnp.dot(h_two.astype(f32).T, d_logits, precision=top_precision)
    grad_ffn = jnp.sum(d_h_two * norm_two, axis=0)
    d_middle = grad_rows + rms_back(d_h_two * gain_ffn, norm_two, inv_two)
    d_middle_low = d_middle.astype(bf16)
    d_attended = (
        jnp.einsum("td,cd->tc", d_middle_low, mat_o, preferred_element_type=f32)
        .astype(bf16)
        .reshape(sequence_length, heads_kv, groups, head_size)
    )
    d_probs = jnp.einsum("tkgd,ukd->kgtu", d_attended, value_rows, preferred_element_type=f32)
    d_values = (
        jnp.einsum("kgtu,tkgd->ukd", probs_low, d_attended, preferred_element_type=f32)
        .astype(bf16)
        .reshape(sequence_length, heads_kv * head_size)
    )
    d_scores = (attn_probs * (d_probs - jnp.sum(attn_probs * d_probs, axis=-1, keepdims=True))).astype(bf16)
    d_queries = (
        jnp.einsum("kgtu,ukd->tkgd", d_scores, keys, preferred_element_type=f32).reshape(
            sequence_length, heads_q, head_size
        )
        * score_scale
    )
    d_keys = jnp.einsum("kgtu,tkgd->ukd", d_scores, query_rows, preferred_element_type=f32) * score_scale
    d_q_scaled = rotate_back(d_queries, cosine_lookup, sine_lookup)
    d_k_scaled = rotate_back(d_keys, cosine_lookup, sine_lookup)
    grad_gain_q = jnp.sum(d_q_scaled * q_norm, axis=(0, 1))
    grad_gain_k = jnp.sum(d_k_scaled * k_norm, axis=(0, 1))
    d_q_proj = (
        rms_back(d_q_scaled * gain_q, q_norm, q_inv).astype(bf16).reshape(sequence_length, heads_q * head_size)
    )
    d_k_proj = (
        rms_back(d_k_scaled * gain_k, k_norm, k_inv).astype(bf16).reshape(sequence_length, heads_kv * head_size)
    )
    d_qkv = jnp.concatenate([d_q_proj, d_k_proj, d_values], axis=1)
    d_h_one = jnp.einsum("tf,cf->tc", d_qkv, mat_qkv[:, :wide_all], preferred_element_type=f32)
    grad_attn = jnp.sum(d_h_one * norm_one, axis=0)
    grad_input = d_middle + rms_back(d_h_one * gain_attn, norm_one, inv_one)

    small_grads = jnp.concatenate([grad_router, grad_attn[:, None], grad_ffn[:, None]], axis=1)
    small_grads = jnp.pad(small_grads, ((0, 0), (0, EXT - small_grads.shape[1]))).astype(bf16)
    ep_bits = bits_of(ep_count)

    def owner_order(value, parts):
        shape = (rep_count,) + (2,) * ep_bits + (parts, own_rows, value.shape[1])
        axes = (ep_bits + 1,) + tuple(range(ep_bits, 0, -1)) + (0, ep_bits + 2, ep_bits + 3)
        return value.reshape(shape).transpose(axes).reshape(value.shape)

    left = jnp.concatenate([owner_order(hidden_first.T, 1), owner_order(attended.T, 2)], axis=0)
    right = jnp.concatenate([d_qkv, d_middle_low, d_middle_low], axis=1)
    head = jnp.pad(jnp.stack([grad_gain_q, grad_gain_k]), ((0, 6), (0, 0)))
    splits = (wide_all // 512, (wide_all + model_width) // 512)
    sums_all, head_sum = dense_sum(
        left, right, owner_order(small_grads, 1), head, rep_count, ep_count, splits, 3
    )
    sum_o = jnp.concatenate(
        [sums_all[:, wide_all : wide_all + model_width], sums_all[:, wide_all + model_width : wide_all + 2 * model_width]],
        axis=0,
    )
    small_sum = sums_all[:, wide_all + 2 * model_width :]
    return (
        layer_out[None],
        grad_input[None],
        small_sum[:, experts],
        sums_all[:, :wide_q],
        sums_all[:, wide_q : wide_q + wide_kv],
        sums_all[:, wide_q + wide_kv : wide_all],
        sum_o,
        small_sum[:, experts + 1],
        small_sum[:, :experts],
        head_sum[:2],
        expert_sums[0],
        expert_sums[1],
        expert_sums[2],
    )


def solution(mesh):
    both = ("rep", "ep")
    placed = (
        P(both, None, None),
        P(both, None, None),
        P(both),
        P(both, None),
        P(both, None),
        P(both, None),
        P(both, None),
        P(both),
        P(both, None),
        P(),
        P("ep", None, None),
        P("ep", None, None),
        P("ep", None, None),
        P(),
        P(both, None, None),
        P(both, None),
    )
    return jax.shard_map(
        per_device,
        mesh=mesh,
        in_specs=placed,
        out_specs=(
            P(both, None, None),
            P(both, None, None),
            P(both),
            P(both, None),
            P(both, None),
            P(both, None),
            P(both, None),
            P(both),
            P(both, None),
            P(),
            P("ep", "rep", None),
            P("ep", "rep", None),
            P("ep", "rep", None),
        ),
        check_vma=False,
    )
```

```python
import functools

import jax
import jax.numpy as jnp
from jax import lax
from jax.experimental import pallas as pl
from jax.experimental.pallas import tpu as pltpu
from jax.sharding import PartitionSpec as P

eps = 1e-06
rope_base = 1000000.0
top_precision = lax.Precision.HIGHEST
MESH = pl.DeviceIdType.MESH
f32, bf16 = jnp.float32, jnp.bfloat16
EXT = 128
UNIT = 16
TILE = 256
VMEM_BYTES = 58 * 1024 * 1024


def rms_parts(value_rows):
    inverse = lax.rsqrt(jnp.mean(value_rows * value_rows, axis=-1, keepdims=True) + eps)
    return (value_rows * inverse, inverse)


def rms_back(grad_norm, normed, inverse):
    return inverse * (grad_norm - normed * jnp.mean(grad_norm * normed, axis=-1, keepdims=True))


def rope_tables(count, head_size):
    half_size = head_size // 2
    freqs = rope_base ** (-2.0 * jnp.arange(half_size, dtype=f32) / head_size)
    angles = jnp.arange(count, dtype=f32)[:, None] * freqs[None, :]
    cosine_lookup = jnp.concatenate([jnp.cos(angles), jnp.cos(angles)], axis=1)
    sine_lookup = jnp.concatenate([jnp.sin(angles), jnp.sin(angles)], axis=1)
    return (cosine_lookup, sine_lookup)


def apply_rotation(value_rows, cosine_lookup, sine_lookup):
    half_size = value_rows.shape[-1] // 2
    turned = jnp.concatenate([-value_rows[..., half_size:], value_rows[..., :half_size]], axis=-1)
    return value_rows * cosine_lookup[:, None, :] + turned * sine_lookup[:, None, :]


def rotate_back(grads, cosine_lookup, sine_lookup):
    half_size = grads.shape[-1] // 2
    scaled = grads * sine_lookup[:, None, :]
    turned = jnp.concatenate([scaled[..., half_size:], -scaled[..., :half_size]], axis=-1)
    return grads * cosine_lookup[:, None, :] + turned


def bits_of(count):
    return count.bit_length() - 1


def gather_orders(count):
    bits = bits_of(count)
    up = list(range(1, bits)) + [0]
    down = list(range(bits - 1, 0, -1)) + [0]
    return (up, down)


def spans(bits):
    masks = [0]
    for bit in bits:
        masks = masks + [m | (1 << bit) for m in masks]
    return masks


def meet(peers):
    barrier = pltpu.get_barrier_semaphore()
    for peer in peers:
        pl.semaphore_signal(barrier, inc=1, device_id=peer, device_id_type=MESH)
    pl.semaphore_wait(barrier, len(peers))


def token_gather_kernel(count, x_ref, out_ref, send_sem, recv_sem, local_sem):
    rep, me = lax.axis_index("rep"), lax.axis_index("ep")
    bits = bits_of(count)
    half = x_ref.shape[0] // 2
    meet([(rep, me ^ (1 << b)) for b in range(bits)])
    local = pltpu.make_async_copy(x_ref, out_ref.at[me], local_sem)
    local.start()
    orders = gather_orders(count)
    copies = []

    def send(h, mask, bit):
        rows = pl.ds(h * half, half)
        source = x_ref.at[rows] if mask == 0 else out_ref.at[me ^ mask, rows]
        there = mask | (1 << bit)
        copy = pltpu.make_async_remote_copy(
            src_ref=source,
            dst_ref=out_ref.at[me ^ mask, rows],
            send_sem=send_sem.at[h, there],
            recv_sem=recv_sem.at[h, there],
            device_id=(rep, me ^ (1 << bit)),
            device_id_type=MESH,
        )
        copy.start()
        copies.append(copy)

    def arrived(h, mask):
        rows = pl.ds(h * half, half)
        pltpu.make_async_copy(
            x_ref.at[rows], out_ref.at[me ^ mask, rows], recv_sem.at[h, mask]
        ).wait()

    for stage in range(bits):
        for h in range(2):
            send(h, 0, orders[h][stage])
    for stage in range(bits):
        for low in spans(orders[0][:stage]):
            index = spans(orders[0][:stage]).index(low)
            for h in range(2):
                mask = spans(orders[h][:stage])[index] | (1 << orders[h][stage])
                arrived(h, mask)
                for later in range(stage + 1, bits):
                    send(h, mask, orders[h][later])
    for copy in copies:
        copy.wait_send()
    local.wait()


def gather_tokens(x, count, collective_id):
    return pl.pallas_call(
        functools.partial(token_gather_kernel, count),
        out_shape=jax.ShapeDtypeStruct((count,) + x.shape, x.dtype),
        in_specs=[pl.BlockSpec(memory_space=pl.ANY)],
        out_specs=pl.BlockSpec(memory_space=pl.ANY),
        scratch_shapes=[
            pltpu.SemaphoreType.DMA((2, count)),
            pltpu.SemaphoreType.DMA((2, count)),
            pltpu.SemaphoreType.DMA,
        ],
        compiler_params=pltpu.CompilerParams(collective_id=collective_id, has_side_effects=True),
        name="token_gather",
    )(x)


def weight_gather_kernel(n_rep, n_ep, split, x_ref, out_ref, send_sem, recv_sem, local_sem):
    rep, me = lax.axis_index("rep"), lax.axis_index("ep")
    bits = bits_of(n_ep)
    columns = (pl.ds(0, split), pl.ds(split, x_ref.shape[1] - split))
    meet([(rep, me ^ (1 << b)) for b in range(bits)] + [(rep ^ d, me) for d in range(1, n_rep)])
    local = pltpu.make_async_copy(x_ref, out_ref.at[rep, me], local_sem)
    local.start()
    orders = gather_orders(n_ep)
    copies = []

    def block(d, h, mask):
        if d == 0 and mask == 0:
            return x_ref.at[:, columns[h]]
        return out_ref.at[rep ^ d, me ^ mask, :, columns[h]]

    def copy_to(d, h, mask, there_d, there_mask, device):
        copy = pltpu.make_async_remote_copy(
            src_ref=block(d, h, mask),
            dst_ref=out_ref.at[rep ^ d, me ^ mask, :, columns[h]],
            send_sem=send_sem.at[there_d, h, there_mask],
            recv_sem=recv_sem.at[there_d, h, there_mask],
            device_id=device,
            device_id_type=MESH,
        )
        copy.start()
        copies.append(copy)

    def send(d, h, mask, bit):
        copy_to(d, h, mask, d, mask | (1 << bit), (rep, me ^ (1 << bit)))

    def arrived(d, h, mask):
        target = out_ref.at[rep ^ d, me ^ mask, :, columns[h]]
        pltpu.make_async_copy(target, target, recv_sem.at[d, h, mask]).wait()

    def spread(d):
        for stage in range(bits):
            for h in range(2):
                send(d, h, 0, orders[h][stage])

    def relay(d):
        for stage in range(bits):
            for index in range(1 << stage):
                for h in range(2):
                    mask = spans(orders[h][:stage])[index] | (1 << orders[h][stage])
                    arrived(d, h, mask)
                    for later in range(stage + 1, bits):
                        send(d, h, mask, orders[h][later])

    for d in range(1, n_rep):
        for h in range(2):
            copy_to(0, h, 0, d, 0, (rep ^ d, me))
    spread(0)
    for d in range(1, n_rep):
        for h in range(2):
            arrived(d, h, 0)
        spread(d)
        relay(d - 1)
    relay(n_rep - 1)
    for copy in copies:
        copy.wait_send()
    local.wait()


def gather_weights(x, n_rep, n_ep, collective_id):
    split = -(-x.shape[1] // 256) * 128
    return pl.pallas_call(
        functools.partial(weight_gather_kernel, n_rep, n_ep, split),
        out_shape=jax.ShapeDtypeStruct((n_rep, n_ep) + x.shape, x.dtype),
        in_specs=[pl.BlockSpec(memory_space=pl.ANY)],
        out_specs=pl.BlockSpec(memory_space=pl.ANY),
        scratch_shapes=[
            pltpu.SemaphoreType.DMA((n_rep, 2, n_ep)),
            pltpu.SemaphoreType.DMA((n_rep, 2, n_ep)),
            pltpu.SemaphoreType.DMA,
        ],
        compiler_params=pltpu.CompilerParams(collective_id=collective_id, has_side_effects=True),
        name="weight_gather",
    )(x)


def token_sum_kernel(count, widths, y_ref, out_ref, *scratch):
    bits = bits_of(count)
    own, got = scratch[:2], scratch[2:4]
    send_sem, recv_sem, own_sem, out_sem = scratch[4:8]
    result = scratch[8:10]
    rep, me = lax.axis_index("rep"), lax.axis_index("ep")
    meet([(rep, me ^ (1 << b)) for b in range(bits)])
    orders = [list(reversed(o)) for o in gather_orders(count)]
    columns = (pl.ds(0, widths[0]), pl.ds(widths[0], widths[1]))
    sends = []
    firsts = [list(reversed(spans(o[1:]))) for o in orders]
    slot_of = []
    for h in range(2):
        table, base = {}, 0
        for stage in range(bits):
            for place, mask in enumerate(reversed(spans(orders[h][stage + 1 :]))):
                table[(stage, mask)] = base + place
            base += 1 << (bits - 1 - stage)
        slot_of.append(table)
    seat = [{mask: i for i, mask in enumerate(firsts[h])} for h in range(2)]

    def send(h, stage, mask):
        bit = 1 << orders[h][stage]
        slot = slot_of[h][(stage, mask)]
        source = y_ref.at[me ^ bit ^ mask, :, columns[h]] if stage == 0 else own[h].at[seat[h][bit | mask]]
        copy = pltpu.make_async_remote_copy(
            src_ref=source,
            dst_ref=got[h].at[slot],
            send_sem=send_sem.at[h, slot],
            recv_sem=recv_sem.at[h, slot],
            device_id=(rep, me ^ bit),
            device_id_type=MESH,
        )
        copy.start()
        sends.append(copy)

    loads = [{}, {}]
    for i in range(len(firsts[0])):
        for h in range(2):
            mask = firsts[h][i]
            send(h, 0, mask)
            load = pltpu.make_async_copy(
                y_ref.at[me ^ mask, :, columns[h]], own[h].at[seat[h][mask]], own_sem.at[h, i]
            )
            load.start()
            loads[h][mask] = load

    rows_total = y_ref.shape[1]
    step = 32

    def add(h, stage, mask):
        slot = slot_of[h][(stage, mask)]
        if stage == 0:
            loads[h][mask].wait()
        pltpu.make_async_copy(got[h].at[slot], got[h].at[slot], recv_sem.at[h, slot]).wait()
        last = stage == bits - 1

        def body(i, carry):
            rows = pl.ds(pl.multiple_of(i * step, step), step)
            total = own[h][seat[h][mask], rows, :].astype(f32) + got[h][slot, rows, :].astype(f32)
            if last:
                result[h][rows, :] = total
            else:
                own[h][seat[h][mask], rows, :] = total.astype(bf16)
            return carry

        lax.fori_loop(0, rows_total // step, body, 0)

    for stage in range(bits):
        masks = [list(reversed(spans(orders[h][stage + 1 :]))) for h in range(2)]
        for i in range(len(masks[0])):
            for h in range(2):
                mask = masks[h][i]
                add(h, stage, mask)
                if stage + 1 < bits:
                    following = 1 << orders[h][stage + 1]
                    if mask & following:
                        send(h, stage + 1, mask & ~following)
    outs = []
    for h in range(2):
        out = pltpu.make_async_copy(result[h], out_ref.at[:, columns[h]], out_sem.at[h])
        out.start()
        outs.append(out)
    for copy in sends:
        copy.wait_send()
    for out in outs:
        out.wait()


def sum_tokens(y, count, widths, collective_id):
    rows = y.shape[1]
    half = count // 2
    return pl.pallas_call(
        functools.partial(token_sum_kernel, count, widths),
        out_shape=jax.ShapeDtypeStruct(y.shape[1:], f32),
        in_specs=[pl.BlockSpec(memory_space=pl.ANY)],
        out_specs=pl.BlockSpec(memory_space=pl.ANY),
        scratch_shapes=[
            pltpu.VMEM((half, rows, widths[0]), bf16),
            pltpu.VMEM((half, rows, widths[1]), bf16),
            pltpu.VMEM((count - 1, rows, widths[0]), bf16),
            pltpu.VMEM((count - 1, rows, widths[1]), bf16),
            pltpu.SemaphoreType.DMA((2, count)),
            pltpu.SemaphoreType.DMA((2, count)),
            pltpu.SemaphoreType.DMA((2, half)),
            pltpu.SemaphoreType.DMA((2,)),
            pltpu.VMEM((rows, widths[0]), f32),
            pltpu.VMEM((rows, widths[1]), f32),
        ],
        compiler_params=pltpu.CompilerParams(
            collective_id=collective_id, has_side_effects=True, vmem_limit_bytes=VMEM_BYTES
        ),
        name="token_sum",
    )(y)


def dense_sum_kernel(n_rep, n_ep, rows, chunks, split, *refs):
    left_ref, right_ref, small_ref, head_ref, out_ref, head_out = refs[:6]
    rest = list(refs[6:])
    bits = bits_of(n_ep)
    wide = right_ref.shape[1] // (chunks - 1)
    half = wide // 2
    rep, me = lax.axis_index("rep"), lax.axis_index("ep")
    mine = [lax.rem(lax.div(me, 1 << b), 2) for b in range(bits)]
    part, got_core = rest[:2]
    acc = [None] + [rest[2 + 2 * k : 4 + 2 * k] for k in range(bits)]
    rest = rest[2 + 2 * bits :]
    got = [None] + [rest[2 * k : 2 * k + 2] for k in range(bits)]
    rest = rest[2 * bits :]
    head_own, head_got, head_rep = rest[:3]
    core_send, core_recv, step_send, step_recv, rep_send, rep_recv, head_send, head_recv, head_rs, head_rr = rest[3:]
    up = list(range(1, bits))
    orders = (up, up[::-1])
    left = [[sorted(set(up) - set(o[:k])) for k in range(bits)] for o in orders]
    lags = [0, 1]
    for _ in range(bits):
        lags.append(lags[-1] + 2)
    deep = 4
    others = [lax.rem(rep + d, n_rep) for d in range(1, n_rep)]
    meet([(rep, me ^ (1 << b)) for b in range(bits)] + [(other, me) for other in others])

    def core_copy(c):
        slot = lax.rem(c, 2)
        return pltpu.make_async_remote_copy(
            src_ref=part.at[slot, 1 - mine[0]],
            dst_ref=got_core.at[slot],
            send_sem=core_send.at[slot],
            recv_sem=core_recv.at[slot],
            device_id=(rep, me ^ 1),
            device_id_type=MESH,
        )

    def bit_copy(k, h, c):
        slot = lax.rem(c, deep)
        bit = orders[h][k - 1]
        place = left[h][k - 1].index(bit)
        return pltpu.make_async_remote_copy(
            src_ref=acc[k][h].at[(slot,) + (slice(None),) * place + (1 - mine[bit],)],
            dst_ref=got[k][h].at[slot],
            send_sem=step_send.at[k, h, slot],
            recv_sem=step_recv.at[k, h, slot],
            device_id=(rep, me ^ (1 << bit)),
            device_id_type=MESH,
        )

    def rep_copy(h, c, d):
        slot = lax.rem(c, deep)
        return pltpu.make_async_remote_copy(
            src_ref=acc[bits][h].at[slot, others[d]],
            dst_ref=got[bits][h].at[slot, n_rep - 2 - d],
            send_sem=rep_send.at[h, slot, d],
            recv_sem=rep_recv.at[h, slot, n_rep - 2 - d],
            device_id=(others[d], me),
            device_id_type=MESH,
        )

    corners = [()]
    for _ in up:
        corners = [c + (v,) for c in corners for v in range(2)]
    block = n_rep * rows
    side_rows = len(corners) * block

    def stage_make(c):
        slot = lax.rem(c, 2)

        @pl.when(c >= 2)
        def _():
            core_copy(c - 2).wait_send()

        @pl.when(c < chunks - 1)
        def _():
            which = jnp.where(c >= split[0], 1, 0) + jnp.where(c >= split[1], 1, 0)
            columns = pl.ds(pl.multiple_of(c * wide, wide), wide)
            weights = right_ref[:, columns]
            for side in (1, 0):
                which_side = 1 - mine[0] if side else mine[0]
                for n, corner in enumerate(corners):
                    start = (which * 2 + which_side) * side_rows + n * block
                    value = jnp.dot(
                        left_ref[pl.ds(pl.multiple_of(start, block), block), :],
                        weights,
                        preferred_element_type=f32,
                    )
                    part[(slot, which_side) + corner] = value.astype(bf16).reshape(n_rep, rows, wide)

        @pl.when(c == chunks - 1)
        def _():
            thin = small_ref.shape[1]
            for side in range(2):
                for n, corner in enumerate(corners):
                    value = small_ref[pl.ds(side * side_rows + n * block, block), :].reshape(n_rep, rows, thin)
                    blank = jnp.zeros((n_rep, rows, wide - thin), bf16)
                    part[(slot, side) + corner + (slice(None), slice(None), slice(0, thin))] = value
                    part[(slot, side) + corner + (slice(None), slice(None), slice(thin, wide))] = blank

        core_copy(c).start()

    def stage_core(c):
        slot, put = lax.rem(c, 2), lax.rem(c, deep)

        @pl.when(c >= deep)
        def _():
            for h in range(2):
                if bits > 1:
                    bit_copy(1, h, c - deep).wait_send()

        core_copy(c).wait_recv()
        for corner in corners:
            total = part[(slot, mine[0]) + corner].astype(f32) + got_core[(slot,) + corner].astype(f32)
            total = total.astype(bf16)
            for h in range(2):
                acc[1][h][(put,) + corner] = total[:, :, h * half : (h + 1) * half]
        for h in range(2):
            bit_copy(1, h, c).start()

    def stage_bit(k, c):
        slot = lax.rem(c, deep)
        for h in range(2):
            bit = orders[h][k - 2]
            place = left[h][k - 2].index(bit)

            @pl.when(c >= deep)
            def _(h=h):
                if k < bits:
                    bit_copy(k, h, c - deep).wait_send()
                else:
                    for d in range(n_rep - 1):
                        rep_copy(h, c - deep, d).wait_send()

            bit_copy(k - 1, h, c).wait_recv()
            small_corners = [()]
            for _ in left[h][k - 1]:
                small_corners = [q + (v,) for q in small_corners for v in range(2)]
            for corner in small_corners:
                full = corner[:place] + (mine[bit],) + corner[place:]
                total = acc[k - 1][h][(slot,) + full].astype(f32) + got[k - 1][h][(slot,) + corner].astype(f32)
                acc[k][h][(slot,) + corner] = total.astype(bf16)
            if k < bits:
                bit_copy(k, h, c).start()
            else:
                for d in range(n_rep - 1):
                    rep_copy(h, c, d).start()

    def stage_end(c):
        slot = lax.rem(c, deep)
        for h in range(2):
            total = acc[bits][h][slot, rep].astype(f32)
            for d in range(n_rep - 1):
                rep_copy(h, c, d).wait_recv()
            for d in range(n_rep - 1):
                total += got[bits][h][slot, d].astype(f32)
            out_ref[:, pl.ds(pl.multiple_of(c * wide + h * half, half), half)] = total

    def head_copy(t):
        return pltpu.make_async_remote_copy(
            src_ref=head_own.at[t],
            dst_ref=head_got.at[t],
            send_sem=head_send.at[t],
            recv_sem=head_recv.at[t],
            device_id=(rep, me ^ (1 << t)),
            device_id_type=MESH,
        )

    def head_rep_copy(d):
        return pltpu.make_async_remote_copy(
            src_ref=head_own.at[bits],
            dst_ref=head_rep.at[rep],
            send_sem=head_rs.at[d],
            recv_sem=head_rr.at[n_rep - 2 - d],
            device_id=(others[d], me),
            device_id_type=MESH,
        )

    def head_step(t):
        if t == 0:
            head_own[0] = head_ref[...]
            head_copy(0).start()
        elif t <= bits:
            head_copy(t - 1).wait_recv()
            head_own[t] = head_own[t - 1] + head_got[t - 1]
            if t < bits:
                head_copy(t).start()
            else:
                for d in range(n_rep - 1):
                    head_rep_copy(d).start()
                head_rep[rep] = head_own[bits]
        else:
            for d in range(n_rep - 1):
                head_rep_copy(d).wait_recv()
            total = head_rep[0]
            for r in range(1, n_rep):
                total = total + head_rep[r]
            head_out[...] = total

    def step(i, carry):
        for stage in reversed(range(len(lags))):
            c = i - lags[stage]

            @pl.when((c >= 0) & (c < chunks))
            def _(stage=stage, c=c):
                if stage == 0:
                    stage_make(c)
                elif stage == 1:
                    stage_core(c)
                elif stage <= bits:
                    stage_bit(stage, c)
                else:
                    stage_end(c)

        for t in range(bits + 2):

            @pl.when(i == t)
            def _(t=t):
                head_step(t)

        return carry

    lax.fori_loop(0, chunks + lags[-1], step, 0)
    for c in range(chunks - 2, chunks):
        core_copy(c).wait_send()
    for c in range(chunks - deep, chunks):
        for h in range(2):
            for k in range(1, bits):
                bit_copy(k, h, c).wait_send()
            for d in range(n_rep - 1):
                rep_copy(h, c, d).wait_send()
    for t in range(bits):
        head_copy(t).wait_send()
    for d in range(n_rep - 1):
        head_rep_copy(d).wait_send()


def dense_sum(left, right, small, head, n_rep, n_ep, split, collective_id):
    chunk = 512
    chunks = right.shape[1] // chunk + 1
    bits = bits_of(n_ep)
    rows = left.shape[0] // (3 * n_rep * n_ep)
    deep = 4
    half = chunk // 2
    vmem = pl.BlockSpec(memory_space=pltpu.VMEM)
    inner = (n_rep, rows)
    scratch = [
        pltpu.VMEM((2, 2) + (2,) * (bits - 1) + inner + (chunk,), bf16),
        pltpu.VMEM((2,) + (2,) * (bits - 1) + inner + (chunk,), bf16),
    ]
    for k in range(1, bits + 1):
        scratch += [pltpu.VMEM((deep,) + (2,) * (bits - k) + inner + (half,), bf16)] * 2
    for k in range(1, bits):
        scratch += [pltpu.VMEM((deep,) + (2,) * (bits - 1 - k) + inner + (half,), bf16)] * 2
    scratch += [pltpu.VMEM((deep, n_rep - 1, rows, half), bf16)] * 2
    scratch += [
        pltpu.VMEM((bits + 1,) + head.shape, f32),
        pltpu.VMEM((bits,) + head.shape, f32),
        pltpu.VMEM((n_rep,) + head.shape, f32),
        pltpu.SemaphoreType.DMA((2,)),
        pltpu.SemaphoreType.DMA((2,)),
        pltpu.SemaphoreType.DMA((bits, 2, deep)),
        pltpu.SemaphoreType.DMA((bits, 2, deep)),
        pltpu.SemaphoreType.DMA((2, deep, n_rep - 1)),
        pltpu.SemaphoreType.DMA((2, deep, n_rep - 1)),
        pltpu.SemaphoreType.DMA((bits,)),
        pltpu.SemaphoreType.DMA((bits,)),
        pltpu.SemaphoreType.DMA((n_rep - 1,)),
        pltpu.SemaphoreType.DMA((n_rep - 1,)),
    ]
    return pl.pallas_call(
        functools.partial(dense_sum_kernel, n_rep, n_ep, rows, chunks, split),
        out_shape=(
            jax.ShapeDtypeStruct((rows, chunks * chunk), f32),
            jax.ShapeDtypeStruct(head.shape, f32),
        ),
        in_specs=[vmem] * 4,
        out_specs=(vmem, vmem),
        scratch_shapes=scratch,
        compiler_params=pltpu.CompilerParams(
            collective_id=collective_id, has_side_effects=True, vmem_limit_bytes=VMEM_BYTES
        ),
        cost_estimate=pl.CostEstimate(flops=1000, bytes_accessed=1000, transcendentals=0),
        name="dense_sum",
    )(left, right, small, head)


NT = (((1,), (1,)), ((), ()))
TN = (((0,), (0,)), ((), ()))


def expert_kernel(first, last, experts, width, *refs):
    (info, h_ref, g_ref, wg_ref, wu_ref, wd_ref) = refs[:6]
    rest = list(refs[6:])
    prev_ref = None if first else rest.pop(0)
    y_ref, gwide_ref, gwd_ref = rest[:3]
    xs, gs, ds, hs, stage, prev_buf, wide, tall, in_sem, out_sem, prev_sem, grad_sem = rest[3:]
    hidden = wg_ref.shape[1]
    units = info[0]
    expert = info[1]
    table = 8
    per_tile = TILE // UNIT
    tiles = (units + per_tile - 1) // per_tile
    most = xs.shape[0] // TILE
    floor_tiles = min(4, most)

    def unit_in(u, slot):
        source = pl.ds(pl.multiple_of(info[table + u], UNIT), UNIT)
        target = pl.ds(pl.multiple_of(u * UNIT, UNIT), UNIT)
        return (
            pltpu.make_async_copy(h_ref.at[source], xs.at[target], in_sem.at[0, slot]),
            pltpu.make_async_copy(g_ref.at[source], gs.at[target], in_sem.at[1, slot]),
        )

    def begin(u, carry):
        for copy in unit_in(u, u // per_tile):
            copy.start()
        return carry

    lax.fori_loop(0, units, begin, 0)

    def blank(u, carry):
        target = pl.ds(pl.multiple_of(u * UNIT, UNIT), UNIT)
        xs[target, :] = jnp.zeros((UNIT, xs.shape[1]), bf16)
        gs[target, :] = jnp.zeros((UNIT, gs.shape[1]), bf16)
        return carry

    lax.fori_loop(units, jnp.maximum(tiles, floor_tiles) * per_tile, blank, 0)

    def blank_tile(i, carry):
        target = pl.ds(pl.multiple_of(i * TILE, TILE), TILE)
        ds[target, :] = jnp.zeros((TILE, ds.shape[1]), bf16)
        hs[target, :] = jnp.zeros((TILE, hs.shape[1]), bf16)
        return carry

    lax.fori_loop(tiles, floor_tiles, blank_tile, 0)

    def prev_copy(i):
        rows = pl.ds(pl.multiple_of(i * TILE, TILE), TILE)
        return pltpu.make_async_copy(prev_ref.at[rows], prev_buf.at[i % 2], prev_sem.at[i % 2])

    if not first:
        prev_copy(0).start()

    def unit_out(u):
        target = pl.ds(pl.multiple_of(info[table + u], UNIT), UNIT)
        tile = u // per_tile
        source = pl.ds(pl.multiple_of((u % per_tile) * UNIT, UNIT), UNIT)
        return pltpu.make_async_copy(stage.at[tile % 2, source], y_ref.at[target], out_sem.at[tile % 2])

    def out_start(i):
        if last:
            lax.fori_loop(
                i * per_tile,
                jnp.minimum((i + 1) * per_tile, units),
                lambda u, c: (unit_out(u).start(), c)[1],
                0,
            )
        else:
            rows = pl.ds(pl.multiple_of(i * TILE, TILE), TILE)
            pltpu.make_async_copy(stage.at[i % 2], y_ref.at[rows], out_sem.at[i % 2]).start()

    def out_wait(i):
        if last:
            lax.fori_loop(
                i * per_tile,
                jnp.minimum((i + 1) * per_tile, units),
                lambda u, c: (unit_out(u).wait(), c)[1],
                0,
            )
        else:
            rows = pl.ds(pl.multiple_of(i * TILE, TILE), TILE)
            pltpu.make_async_copy(stage.at[i % 2], y_ref.at[rows], out_sem.at[i % 2]).wait()

    lane = lax.broadcasted_iota(jnp.int32, (TILE, EXT), 1)
    weight_lanes = (lane == expert) | (lane == expert + experts) | (lane == expert + 2 * experts)

    def tile_step(i, carry):
        def landed(u, c):
            for copy in unit_in(u, i):
                copy.wait()
            return c

        lax.fori_loop(i * per_tile, jnp.minimum((i + 1) * per_tile, units), landed, 0)
        rows = pl.ds(pl.multiple_of(i * TILE, TILE), TILE)
        x = xs[rows, :width]
        g = gs[rows, :]
        extra = xs[rows, width:].astype(f32)
        weight = jnp.sum(jnp.where(weight_lanes, extra, 0.0), axis=1, keepdims=True)
        gate = jnp.dot(x, wg_ref[...], preferred_element_type=f32)
        up = jnp.dot(x, wu_ref[...], preferred_element_type=f32)
        d_plain = lax.dot_general(g, wd_ref[...], NT, preferred_element_type=f32)
        sig = 1.0 / (1.0 + jnp.exp(-gate))
        silu = gate * sig
        hid = silu * up
        d_weight = jnp.sum(hid.astype(bf16).astype(f32) * d_plain, axis=1, keepdims=True)
        hs[rows, :] = (hid * weight).astype(bf16)
        d_hidden = d_plain * weight
        ds[rows, :hidden] = (d_hidden * up * sig * (1.0 + gate * (1.0 - sig))).astype(bf16)
        ds[rows, hidden:] = (d_hidden * silu).astype(bf16)

        @pl.when(i >= 2)
        def _():
            out_wait(i - 2)

        if not first:

            @pl.when(i + 1 < tiles)
            def _():
                prev_copy(i + 1).start()

            prev_copy(i).wait()
        slot = i % 2
        high = d_weight.astype(bf16).astype(f32)
        low = d_weight - high
        note = jnp.where(lane == expert, high, 0.0) + jnp.where(lane == expert + experts, low, 0.0)
        d_row = lax.dot_general(ds[rows, :hidden], wg_ref[...], NT, preferred_element_type=f32)
        d_row += lax.dot_general(ds[rows, hidden:], wu_ref[...], NT, preferred_element_type=f32)
        if not first:
            d_row += prev_buf[slot, :, :width].astype(f32)
            note += prev_buf[slot, :, width : width + EXT].astype(f32)
        stage[slot, :, :width] = d_row.astype(bf16)
        stage[slot, :, width : width + EXT] = note.astype(bf16)
        out = jnp.dot(hs[rows, :], wd_ref[...], preferred_element_type=f32)
        if not first:
            out += prev_buf[slot, :, width + EXT :].astype(f32)
        stage[slot, :, width + EXT :] = out.astype(bf16)
        out_start(i)
        return carry

    lax.fori_loop(0, tiles, tile_step, 0)

    block = 256

    def grads(depth):
        def wide_copies(m):
            per = gwide_ref.shape[2] // block
            rows = pl.ds(pl.multiple_of((m % per) * block, block), block)
            return tuple(
                pltpu.make_async_copy(
                    wide.at[m % 2, :, p * hidden : (p + 1) * hidden],
                    gwide_ref.at[m // per, p, rows],
                    grad_sem.at[p, m % 2],
                )
                for p in range(2)
            )

        def wide_step(m, carry):
            @pl.when(m >= 2)
            def _():
                for copy in wide_copies(m - 2):
                    copy.wait()

            columns = pl.ds(pl.multiple_of(m * block, block), block)
            wide[m % 2] = lax.dot_general(
                xs[:depth, columns], ds[:depth, :], TN, preferred_element_type=f32
            ).astype(bf16)
            for copy in wide_copies(m):
                copy.start()
            return carry

        count = width // block
        lax.fori_loop(0, count, wide_step, 0)
        for m in range(count - 2, count):
            for copy in wide_copies(m):
                copy.wait()

        def tall_copy(m):
            rows = pl.ds(pl.multiple_of(m * block, block), block)
            return pltpu.make_async_copy(tall.at[m % 2], gwd_ref.at[rows], grad_sem.at[0, m % 2])

        def tall_step(m, carry):
            @pl.when(m >= 2)
            def _():
                tall_copy(m - 2).wait()

            columns = pl.ds(pl.multiple_of(m * block, block), block)
            tall[m % 2] = lax.dot_general(
                hs[:depth, columns], gs[:depth, :], TN, preferred_element_type=f32
            ).astype(bf16)
            tall_copy(m).start()
            return carry

        count = hidden // block
        lax.fori_loop(0, count, tall_step, 0)
        for m in range(count - 2, count):
            tall_copy(m).wait()

    for choice in range(floor_tiles, most + 1):
        chosen = (tiles <= choice) if choice == floor_tiles else (tiles == choice)

        @pl.when(chosen)
        def _(choice=choice):
            grads(choice * TILE)

    @pl.when(tiles >= 2)
    def _():
        out_wait(tiles - 2)

    out_wait(tiles - 1)


def expert_pass(info, h_rows, g_rows, w_gate, w_up, w_down, prev, last, experts, shares):
    tokens, width = g_rows.shape
    hidden = w_gate.shape[1]
    wide_row = width + EXT + width
    any_spec = pl.BlockSpec(memory_space=pl.ANY)
    vmem_spec = pl.BlockSpec(memory_space=pltpu.VMEM)
    first = prev is None
    operands = [info, h_rows, g_rows, w_gate, w_up, w_down] + ([] if first else [prev])
    specs = [pl.BlockSpec(memory_space=pltpu.SMEM), any_spec, any_spec, vmem_spec, vmem_spec, vmem_spec]
    specs += [] if first else [any_spec]
    return pl.pallas_call(
        functools.partial(expert_kernel, first, last, experts, width),
        out_shape=(
            jax.ShapeDtypeStruct((tokens, wide_row), bf16),
            jax.ShapeDtypeStruct((shares, 2, width // shares, hidden), bf16),
            jax.ShapeDtypeStruct((hidden, width), bf16),
        ),
        in_specs=specs,
        out_specs=(any_spec,) * 3,
        scratch_shapes=[
            pltpu.VMEM((tokens, width + EXT), bf16),
            pltpu.VMEM((tokens, width), bf16),
            pltpu.VMEM((tokens, 2 * hidden), bf16),
            pltpu.VMEM((tokens, hidden), bf16),
            pltpu.VMEM((2, TILE, wide_row), bf16),
            pltpu.VMEM((2, TILE, wide_row), bf16),
            pltpu.VMEM((2, 256, 2 * hidden), bf16),
            pltpu.VMEM((2, 256, width), bf16),
            pltpu.SemaphoreType.DMA((2, tokens // TILE)),
            pltpu.SemaphoreType.DMA((2,)),
            pltpu.SemaphoreType.DMA((2,)),
            pltpu.SemaphoreType.DMA((2, 2)),
        ],
        compiler_params=pltpu.CompilerParams(vmem_limit_bytes=VMEM_BYTES),
        cost_estimate=pl.CostEstimate(flops=1000, bytes_accessed=1000, transcendentals=0),
        name="experts",
    )(*operands)


def unit_table(lengths):
    per_sequence = TILE // UNIT
    counts = (lengths + UNIT - 1) // UNIT
    unit = jnp.arange(lengths.shape[0] * per_sequence, dtype=jnp.int32)
    live = (unit % per_sequence) < jnp.repeat(counts, per_sequence)
    place = jnp.cumsum(live.astype(jnp.int32)) - 1
    hit = (place[None, :] == unit[:, None]) & live[None, :]
    rows = jnp.sum(jnp.where(hit, unit[None, :] * UNIT, 0), axis=1)
    return (jnp.sum(counts), rows)


def split_three(value):
    high = lax.reduce_precision(value, 8, 7)
    rest = value - high
    middle = lax.reduce_precision(rest, 8, 7)
    return jnp.concatenate([high, middle, rest - middle], axis=-1)


def per_device(
    hidden_in,
    out_grad,
    attn_gain,
    w_q,
    key_weight,
    value_weight,
    w_o,
    ffn_gain,
    router_w,
    qk_gains,
    w_gate,
    w_up,
    w_down,
    lengths,
    routes,
    order,
):
    everywhere = ("rep", "ep")
    rep_count, ep_count = (lax.axis_size("rep"), lax.axis_size("ep"))
    rep_index, ep_index = (lax.axis_index("rep"), lax.axis_index("ep"))
    inputs = hidden_in[0].astype(f32)
    sequence_length, model_width = inputs.shape
    head_size = qk_gains.shape[1]
    wide_q, wide_kv = (w_q.shape[1], key_weight.shape[1])
    heads_q, heads_kv = (wide_q // head_size, wide_kv // head_size)
    groups = heads_q // heads_kv
    local_experts = w_gate.shape[0]
    experts = local_experts * ep_count
    top_count = routes.shape[2]
    score_scale = head_size ** (-0.5)
    group_lengths = lax.dynamic_slice_in_dim(lengths, rep_index * ep_count, ep_count)
    length = lax.dynamic_index_in_dim(group_lengths, ep_index, keepdims=False)
    positions = jnp.arange(sequence_length, dtype=jnp.int32)
    live = positions < length
    live_rows = live.astype(f32)

    expert_iota = jnp.arange(experts, dtype=jnp.int32)
    route_hot = routes[0][..., None] == expert_iota
    routed = jnp.any(route_hot, axis=1) & live[:, None]
    order_of = jnp.sum(
        jnp.where(route_hot, order[0].reshape(sequence_length, top_count)[..., None], 0), axis=1
    )
    sort_key = jnp.where(routed, order_of, sequence_length * top_count)
    loads = jnp.sum(routed.astype(jnp.int32), axis=0)
    rank = jnp.sum((sort_key[None, :, :] < sort_key[:, None, :]).astype(jnp.int32), axis=1)

    own_rows = w_q.shape[0]
    load_columns = -(-experts // own_rows)
    load_block = jnp.pad(loads, (0, load_columns * own_rows - experts)).reshape(load_columns, own_rows).T
    small = jnp.concatenate(
        [router_w, attn_gain[:, None], ffn_gain[:, None], load_block.astype(bf16)], axis=1
    )
    small = jnp.pad(small, ((0, 0), (0, EXT - small.shape[1])))
    pack = jnp.concatenate([w_q, key_weight, value_weight, small], axis=1)
    mat_o = lax.all_gather(w_o, everywhere, axis=0, tiled=True)
    mat_qkv = gather_weights(pack, rep_count, ep_count, 4).reshape(-1, pack.shape[1])
    grads_all = lax.all_gather(out_grad[0], "ep", axis=0, tiled=True)

    wide_all = wide_q + 2 * wide_kv
    small_all = mat_qkv[:, wide_all:]
    mat_router = small_all[:, :experts]
    gain_attn = small_all[:, experts].astype(f32)
    gain_ffn = small_all[:, experts + 1].astype(f32)
    loads_all = (
        small_all[:, experts + 2 : experts + 2 + load_columns]
        .reshape(rep_count, ep_count, own_rows, load_columns)
        .transpose(0, 1, 3, 2)
        .reshape(rep_count, ep_count, load_columns * own_rows)[:, :, :experts]
        .astype(jnp.int32)
    )
    group_loads = lax.dynamic_index_in_dim(loads_all, rep_index, keepdims=False)
    earlier = (jnp.arange(ep_count) < ep_index)[:, None]
    load_prefix = jnp.sum(jnp.where(earlier, group_loads, 0), axis=0)
    capacity = 9 * top_count * jnp.sum(group_lengths) // (8 * experts)
    kept = routed & (load_prefix[None, :] + rank < capacity)
    kept_float = kept.astype(f32)

    gain_q = qk_gains[0].astype(f32)
    gain_k = qk_gains[1].astype(f32)
    norm_one, inv_one = rms_parts(inputs)
    hidden_first = (norm_one * gain_attn).astype(bf16)
    projected = jnp.dot(hidden_first, mat_qkv, preferred_element_type=f32)
    query_projected = projected[:, :wide_q].reshape(sequence_length, heads_q, head_size)
    key_projected = projected[:, wide_q : wide_q + wide_kv].reshape(sequence_length, heads_kv, head_size)
    value_rows = (
        projected[:, wide_q + wide_kv : wide_all]
        .astype(bf16)
        .reshape(sequence_length, heads_kv, head_size)
    )
    cosine_lookup, sine_lookup = rope_tables(sequence_length, head_size)
    q_norm, q_inv = rms_parts(query_projected)
    k_norm, k_inv = rms_parts(key_projected)
    query_rows = (
        apply_rotation(q_norm * gain_q, cosine_lookup, sine_lookup)
        .astype(bf16)
        .reshape(sequence_length, heads_kv, groups, head_size)
    )
    keys = apply_rotation(k_norm * gain_k, cosine_lookup, sine_lookup).astype(bf16)
    scores = jnp.einsum("tkgd,ukd->kgtu", query_rows, keys, preferred_element_type=f32) * score_scale
    allowed = (positions[None, :] <= positions[:, None]) & (positions[None, :] < length)
    scores = jnp.where(allowed, scores, -1e30)
    attn_probs = jax.nn.softmax(scores, axis=-1)
    probs_low = attn_probs.astype(bf16)
    attended = (
        jnp.einsum("kgtu,ukd->tkgd", probs_low, value_rows, preferred_element_type=f32)
        .astype(bf16)
        .reshape(sequence_length, heads_q * head_size)
    )
    middle = inputs + jnp.dot(attended, mat_o, preferred_element_type=f32)
    norm_two, inv_two = rms_parts(middle)
    h_two = (norm_two * gain_ffn).astype(bf16)
    logits = jnp.dot(h_two, mat_router, preferred_element_type=f32)
    named = jnp.any(route_hot, axis=1)
    top_logit = jnp.max(jnp.where(named, logits, -jnp.inf), axis=1, keepdims=True)
    raised = jnp.where(named, jnp.exp(jnp.where(named, logits - top_logit, 0.0)), 0.0)
    route_gates = raised / jnp.sum(raised, axis=1, keepdims=True)
    pair_weight = route_gates * kept_float

    extra = split_three(pair_weight).astype(bf16)
    extra = jnp.pad(extra, ((0, 0), (0, EXT - extra.shape[1])))
    sent = jnp.concatenate([h_two, extra], axis=1)
    h_all = gather_tokens(sent, ep_count, 1)

    part = min(ep_count, 8)
    tokens = part * sequence_length
    sums = []
    y_parts = []
    for c in range(ep_count // part):
        live_units, unit_rows = unit_table(group_lengths[c * part : (c + 1) * part])
        h_rows = h_all[c * part : (c + 1) * part].reshape(tokens, model_width + EXT)
        g_rows = grads_all[c * tokens : (c + 1) * tokens]
        prev, found = None, []
        for local in range(local_experts):
            info = jnp.concatenate(
                [
                    jnp.stack([live_units, ep_index * local_experts + local]).astype(jnp.int32),
                    jnp.zeros((6,), jnp.int32),
                    unit_rows,
                ]
            )
            prev, *weight_grads = expert_pass(
                info,
                h_rows,
                g_rows,
                w_gate[local],
                w_up[local],
                w_down[local],
                prev,
                local == local_experts - 1,
                experts,
                rep_count,
            )
            found.append(weight_grads)
        y_parts.append(prev.reshape(part, sequence_length, -1))
        sums.append(found)
    y_all = y_parts[0] if len(y_parts) == 1 else jnp.concatenate(y_parts, axis=0)
    wide_sums, tall_sums = [], []
    for local in range(local_experts):
        for which, kind in enumerate((wide_sums, tall_sums)):
            total = sums[0][local][which]
            for more in sums[1:]:
                total = (total.astype(f32) + more[local][which].astype(f32)).astype(bf16)
            kind.append(lax.psum_scatter(total, "rep", scatter_dimension=0, tiled=True).astype(f32))
    wide_sums = jnp.concatenate(wide_sums, axis=0)
    expert_sums = (wide_sums[:, 0], wide_sums[:, 1], jnp.stack(tall_sums))

    back = sum_tokens(y_all, ep_count, (model_width + EXT, model_width), 2)
    live_column = live[:, None]
    moe_output = jnp.where(live_column, back[:, model_width + EXT :], 0.0)
    layer_out = jnp.where(live_column, middle + moe_output, 0.0)
    grad_rows = out_grad[0].astype(f32) * live_rows[:, None]
    notes = back[:, model_width : model_width + 2 * experts]
    d_weight = jnp.where(live_column, notes[:, :experts] + notes[:, experts:], 0.0)
    d_gates = d_weight * kept_float
    d_logits = route_gates * (d_gates - jnp.sum(route_gates * d_gates, axis=-1, keepdims=True))

    router_float = mat_router.astype(f32)
    d_h_two = jnp.where(live_column, back[:, :model_width], 0.0)
    d_h_two = d_h_two + jnp.dot(d_logits, router_float.T, precision=top_precision)
    grad_router = jnp.dot(h_two.astype(f32).T, d_logits, precision=top_precision)
    grad_ffn = jnp.sum(d_h_two * norm_two, axis=0)
    d_middle = grad_rows + rms_back(d_h_two * gain_ffn, norm_two, inv_two)
    d_middle_low = d_middle.astype(bf16)
    d_attended = (
        jnp.einsum("td,cd->tc", d_middle_low, mat_o, preferred_element_type=f32)
        .astype(bf16)
        .reshape(sequence_length, heads_kv, groups, head_size)
    )
    d_probs = jnp.einsum("tkgd,ukd->kgtu", d_attended, value_rows, preferred_element_type=f32)
    d_values = (
        jnp.einsum("kgtu,tkgd->ukd", probs_low, d_attended, preferred_element_type=f32)
        .astype(bf16)
        .reshape(sequence_length, heads_kv * head_size)
    )
    d_scores = (attn_probs * (d_probs - jnp.sum(attn_probs * d_probs, axis=-1, keepdims=True))).astype(bf16)
    d_queries = (
        jnp.einsum("kgtu,ukd->tkgd", d_scores, keys, preferred_element_type=f32).reshape(
            sequence_length, heads_q, head_size
        )
        * score_scale
    )
    d_keys = jnp.einsum("kgtu,tkgd->ukd", d_scores, query_rows, preferred_element_type=f32) * score_scale
    d_q_scaled = rotate_back(d_queries, cosine_lookup, sine_lookup)
    d_k_scaled = rotate_back(d_keys, cosine_lookup, sine_lookup)
    grad_gain_q = jnp.sum(d_q_scaled * q_norm, axis=(0, 1))
    grad_gain_k = jnp.sum(d_k_scaled * k_norm, axis=(0, 1))
    d_q_proj = (
        rms_back(d_q_scaled * gain_q, q_norm, q_inv).astype(bf16).reshape(sequence_length, heads_q * head_size)
    )
    d_k_proj = (
        rms_back(d_k_scaled * gain_k, k_norm, k_inv).astype(bf16).reshape(sequence_length, heads_kv * head_size)
    )
    d_qkv = jnp.concatenate([d_q_proj, d_k_proj, d_values], axis=1)
    d_h_one = jnp.einsum("tf,cf->tc", d_qkv, mat_qkv[:, :wide_all], preferred_element_type=f32)
    grad_attn = jnp.sum(d_h_one * norm_one, axis=0)
    grad_input = d_middle + rms_back(d_h_one * gain_attn, norm_one, inv_one)

    small_grads = jnp.concatenate([grad_router, grad_attn[:, None], grad_ffn[:, None]], axis=1)
    small_grads = jnp.pad(small_grads, ((0, 0), (0, EXT - small_grads.shape[1]))).astype(bf16)
    ep_bits = bits_of(ep_count)

    def owner_order(value, parts):
        shape = (rep_count,) + (2,) * ep_bits + (parts, own_rows, value.shape[1])
        axes = (ep_bits + 1,) + tuple(range(ep_bits, 0, -1)) + (0, ep_bits + 2, ep_bits + 3)
        return value.reshape(shape).transpose(axes).reshape(value.shape)

    left = jnp.concatenate([owner_order(hidden_first.T, 1), owner_order(attended.T, 2)], axis=0)
    right = jnp.concatenate([d_qkv, d_middle_low, d_middle_low], axis=1)
    head = jnp.pad(jnp.stack([grad_gain_q, grad_gain_k]), ((0, 6), (0, 0)))
    splits = (wide_all // 512, (wide_all + model_width) // 512)
    sums_all, head_sum = dense_sum(
        left, right, owner_order(small_grads, 1), head, rep_count, ep_count, splits, 3
    )
    sum_o = jnp.concatenate(
        [sums_all[:, wide_all : wide_all + model_width], sums_all[:, wide_all + model_width : wide_all + 2 * model_width]],
        axis=0,
    )
    small_sum = sums_all[:, wide_all + 2 * model_width :]
    return (
        layer_out[None],
        grad_input[None],
        small_sum[:, experts],
        sums_all[:, :wide_q],
        sums_all[:, wide_q : wide_q + wide_kv],
        sums_all[:, wide_q + wide_kv : wide_all],
        sum_o,
        small_sum[:, experts + 1],
        small_sum[:, :experts],
        head_sum[:2],
        expert_sums[0],
        expert_sums[1],
        expert_sums[2],
    )


def solution(mesh):
    both = ("rep", "ep")
    placed = (
        P(both, None, None),
        P(both, None, None),
        P(both),
        P(both, None),
        P(both, None),
        P(both, None),
        P(both, None),
        P(both),
        P(both, None),
        P(),
        P("ep", None, None),
        P("ep", None, None),
        P("ep", None, None),
        P(),
        P(both, None, None),
        P(both, None),
    )
    return jax.shard_map(
        per_device,
        mesh=mesh,
        in_specs=placed,
        out_specs=(
            P(both, None, None),
            P(both, None, None),
            P(both),
            P(both, None),
            P(both, None),
            P(both, None),
            P(both, None),
            P(both),
            P(both, None),
            P(),
            P("ep", "rep", None),
            P("ep", "rep", None),
            P("ep", "rep", None),
        ),
        check_vma=False,
    )
```

```python
import functools
import math

import jax
import jax.numpy as jnp
from jax import lax
from jax.experimental import pallas as pl
from jax.experimental.pallas import tpu as pltpu
from jax.sharding import PartitionSpec as P

eps = 1e-06
rope_base = 1000000.0
top_precision = lax.Precision.HIGHEST
MESH = pl.DeviceIdType.MESH
f32, bf16 = jnp.float32, jnp.bfloat16
EXT = 128
UNIT = 16
LANES = 256
TILE = 256
VMEM_BYTES = 58 * 1024 * 1024


def rms_parts(value_rows):
    inverse = lax.rsqrt(jnp.mean(value_rows * value_rows, axis=-1, keepdims=True) + eps)
    return (value_rows * inverse, inverse)


def rms_back(grad_norm, normed, inverse):
    return inverse * (grad_norm - normed * jnp.mean(grad_norm * normed, axis=-1, keepdims=True))


def rope_tables(count, head_size):
    half_size = head_size // 2
    freqs = rope_base ** (-2.0 * jnp.arange(half_size, dtype=f32) / head_size)
    angles = jnp.arange(count, dtype=f32)[:, None] * freqs[None, :]
    cosine_lookup = jnp.concatenate([jnp.cos(angles), jnp.cos(angles)], axis=1)
    sine_lookup = jnp.concatenate([jnp.sin(angles), jnp.sin(angles)], axis=1)
    return (cosine_lookup, sine_lookup)


def apply_rotation(value_rows, cosine_lookup, sine_lookup):
    half_size = value_rows.shape[-1] // 2
    turned = jnp.concatenate([-value_rows[..., half_size:], value_rows[..., :half_size]], axis=-1)
    return value_rows * cosine_lookup[:, None, :] + turned * sine_lookup[:, None, :]


def rotate_back(grads, cosine_lookup, sine_lookup):
    half_size = grads.shape[-1] // 2
    scaled = grads * sine_lookup[:, None, :]
    turned = jnp.concatenate([scaled[..., half_size:], -scaled[..., :half_size]], axis=-1)
    return grads * cosine_lookup[:, None, :] + turned


def bits_of(count):
    return count.bit_length() - 1


def gather_orders(count):
    bits = bits_of(count)
    up = list(range(1, bits)) + [0]
    down = list(range(bits - 1, 0, -1)) + [0]
    return (up, down)


def spans(bits):
    masks = [0]
    for bit in bits:
        masks = masks + [m | (1 << bit) for m in masks]
    return masks


def meet(peers):
    barrier = pltpu.get_barrier_semaphore()
    for peer in peers:
        pl.semaphore_signal(barrier, inc=1, device_id=peer, device_id_type=MESH)
    pl.semaphore_wait(barrier, len(peers))


def token_gather_kernel(count, x_ref, out_ref, send_sem, recv_sem, local_sem):
    rep, me = lax.axis_index("rep"), lax.axis_index("ep")
    bits = bits_of(count)
    half = x_ref.shape[0] // 2
    meet([(rep, me ^ (1 << b)) for b in range(bits)])
    local = pltpu.make_async_copy(x_ref, out_ref.at[me], local_sem)
    local.start()
    orders = gather_orders(count)
    copies = []

    def send(h, mask, bit):
        rows = pl.ds(h * half, half)
        source = x_ref.at[rows] if mask == 0 else out_ref.at[me ^ mask, rows]
        there = mask | (1 << bit)
        copy = pltpu.make_async_remote_copy(
            src_ref=source,
            dst_ref=out_ref.at[me ^ mask, rows],
            send_sem=send_sem.at[h, there],
            recv_sem=recv_sem.at[h, there],
            device_id=(rep, me ^ (1 << bit)),
            device_id_type=MESH,
        )
        copy.start()
        copies.append(copy)

    def arrived(h, mask):
        rows = pl.ds(h * half, half)
        pltpu.make_async_copy(
            x_ref.at[rows], out_ref.at[me ^ mask, rows], recv_sem.at[h, mask]
        ).wait()

    for stage in range(bits):
        for h in range(2):
            send(h, 0, orders[h][stage])
    for stage in range(bits):
        for low in spans(orders[0][:stage]):
            index = spans(orders[0][:stage]).index(low)
            for h in range(2):
                mask = spans(orders[h][:stage])[index] | (1 << orders[h][stage])
                arrived(h, mask)
                for later in range(stage + 1, bits):
                    send(h, mask, orders[h][later])
    for copy in copies:
        copy.wait_send()
    local.wait()


def gather_tokens(x, count, collective_id):
    return pl.pallas_call(
        functools.partial(token_gather_kernel, count),
        out_shape=jax.ShapeDtypeStruct((count,) + x.shape, x.dtype),
        in_specs=[pl.BlockSpec(memory_space=pl.ANY)],
        out_specs=pl.BlockSpec(memory_space=pl.ANY),
        scratch_shapes=[
            pltpu.SemaphoreType.DMA((2, count)),
            pltpu.SemaphoreType.DMA((2, count)),
            pltpu.SemaphoreType.DMA,
        ],
        compiler_params=pltpu.CompilerParams(collective_id=collective_id, has_side_effects=True),
        name="token_gather",
    )(x)


def weight_gather_kernel(n_rep, n_ep, split, x_ref, out_ref, send_sem, recv_sem, local_sem):
    rep, me = lax.axis_index("rep"), lax.axis_index("ep")
    bits = bits_of(n_ep)
    columns = (pl.ds(0, split), pl.ds(split, x_ref.shape[1] - split))
    meet([(rep, me ^ (1 << b)) for b in range(bits)] + [(rep ^ d, me) for d in range(1, n_rep)])
    local = pltpu.make_async_copy(x_ref, out_ref.at[rep, me], local_sem)
    local.start()
    orders = gather_orders(n_ep)
    copies = []

    def block(d, h, mask):
        if d == 0 and mask == 0:
            return x_ref.at[:, columns[h]]
        return out_ref.at[rep ^ d, me ^ mask, :, columns[h]]

    def copy_to(d, h, mask, there_d, there_mask, device):
        copy = pltpu.make_async_remote_copy(
            src_ref=block(d, h, mask),
            dst_ref=out_ref.at[rep ^ d, me ^ mask, :, columns[h]],
            send_sem=send_sem.at[there_d, h, there_mask],
            recv_sem=recv_sem.at[there_d, h, there_mask],
            device_id=device,
            device_id_type=MESH,
        )
        copy.start()
        copies.append(copy)

    def send(d, h, mask, bit):
        copy_to(d, h, mask, d, mask | (1 << bit), (rep, me ^ (1 << bit)))

    def arrived(d, h, mask):
        target = out_ref.at[rep ^ d, me ^ mask, :, columns[h]]
        pltpu.make_async_copy(target, target, recv_sem.at[d, h, mask]).wait()

    def spread(d):
        for stage in range(bits):
            for h in range(2):
                send(d, h, 0, orders[h][stage])

    def relay(d):
        for stage in range(bits):
            for index in range(1 << stage):
                for h in range(2):
                    mask = spans(orders[h][:stage])[index] | (1 << orders[h][stage])
                    arrived(d, h, mask)
                    for later in range(stage + 1, bits):
                        send(d, h, mask, orders[h][later])

    for d in range(1, n_rep):
        for h in range(2):
            copy_to(0, h, 0, d, 0, (rep ^ d, me))
    spread(0)
    for d in range(1, n_rep):
        for h in range(2):
            arrived(d, h, 0)
        spread(d)
        relay(d - 1)
    relay(n_rep - 1)
    for copy in copies:
        copy.wait_send()
    local.wait()


def gather_weights(x, n_rep, n_ep, collective_id):
    split = -(-x.shape[1] // 256) * 128
    return pl.pallas_call(
        functools.partial(weight_gather_kernel, n_rep, n_ep, split),
        out_shape=jax.ShapeDtypeStruct((n_rep, n_ep) + x.shape, x.dtype),
        in_specs=[pl.BlockSpec(memory_space=pl.ANY)],
        out_specs=pl.BlockSpec(memory_space=pl.ANY),
        scratch_shapes=[
            pltpu.SemaphoreType.DMA((n_rep, 2, n_ep)),
            pltpu.SemaphoreType.DMA((n_rep, 2, n_ep)),
            pltpu.SemaphoreType.DMA,
        ],
        compiler_params=pltpu.CompilerParams(collective_id=collective_id, has_side_effects=True),
        name="weight_gather",
    )(x)


def token_sum_kernel(count, widths, y_ref, out_ref, *scratch):
    bits = bits_of(count)
    own, got = scratch[:2], scratch[2:4]
    send_sem, recv_sem, own_sem, out_sem = scratch[4:8]
    result = scratch[8:10]
    rep, me = lax.axis_index("rep"), lax.axis_index("ep")
    meet([(rep, me ^ (1 << b)) for b in range(bits)])
    orders = [list(reversed(o)) for o in gather_orders(count)]
    columns = (pl.ds(0, widths[0]), pl.ds(widths[0], widths[1]))
    sends = []
    firsts = [list(reversed(spans(o[1:]))) for o in orders]
    slot_of = []
    for h in range(2):
        table, base = {}, 0
        for stage in range(bits):
            for place, mask in enumerate(reversed(spans(orders[h][stage + 1 :]))):
                table[(stage, mask)] = base + place
            base += 1 << (bits - 1 - stage)
        slot_of.append(table)
    seat = [{mask: i for i, mask in enumerate(firsts[h])} for h in range(2)]

    def send(h, stage, mask):
        bit = 1 << orders[h][stage]
        slot = slot_of[h][(stage, mask)]
        source = y_ref.at[me ^ bit ^ mask, :, columns[h]] if stage == 0 else own[h].at[seat[h][bit | mask]]
        copy = pltpu.make_async_remote_copy(
            src_ref=source,
            dst_ref=got[h].at[slot],
            send_sem=send_sem.at[h, slot],
            recv_sem=recv_sem.at[h, slot],
            device_id=(rep, me ^ bit),
            device_id_type=MESH,
        )
        copy.start()
        sends.append(copy)

    loads = [{}, {}]
    for i in range(len(firsts[0])):
        for h in range(2):
            mask = firsts[h][i]
            send(h, 0, mask)
            load = pltpu.make_async_copy(
                y_ref.at[me ^ mask, :, columns[h]], own[h].at[seat[h][mask]], own_sem.at[h, i]
            )
            load.start()
            loads[h][mask] = load

    rows_total = y_ref.shape[1]
    step = 32

    def add(h, stage, mask):
        slot = slot_of[h][(stage, mask)]
        if stage == 0:
            loads[h][mask].wait()
        pltpu.make_async_copy(got[h].at[slot], got[h].at[slot], recv_sem.at[h, slot]).wait()
        last = stage == bits - 1

        def body(i, carry):
            rows = pl.ds(pl.multiple_of(i * step, step), step)
            total = own[h][seat[h][mask], rows, :].astype(f32) + got[h][slot, rows, :].astype(f32)
            if last:
                result[h][rows, :] = total
            else:
                own[h][seat[h][mask], rows, :] = total.astype(bf16)
            return carry

        lax.fori_loop(0, rows_total // step, body, 0)

    for stage in range(bits):
        masks = [list(reversed(spans(orders[h][stage + 1 :]))) for h in range(2)]
        for i in range(len(masks[0])):
            for h in range(2):
                mask = masks[h][i]
                add(h, stage, mask)
                if stage + 1 < bits:
                    following = 1 << orders[h][stage + 1]
                    if mask & following:
                        send(h, stage + 1, mask & ~following)
    outs = []
    for h in range(2):
        out = pltpu.make_async_copy(result[h], out_ref.at[:, columns[h]], out_sem.at[h])
        out.start()
        outs.append(out)
    for copy in sends:
        copy.wait_send()
    for out in outs:
        out.wait()


def sum_tokens(y, count, widths, collective_id):
    rows = y.shape[1]
    half = count // 2
    return pl.pallas_call(
        functools.partial(token_sum_kernel, count, widths),
        out_shape=jax.ShapeDtypeStruct(y.shape[1:], f32),
        in_specs=[pl.BlockSpec(memory_space=pl.ANY)],
        out_specs=pl.BlockSpec(memory_space=pl.ANY),
        scratch_shapes=[
            pltpu.VMEM((half, rows, widths[0]), bf16),
            pltpu.VMEM((half, rows, widths[1]), bf16),
            pltpu.VMEM((count - 1, rows, widths[0]), bf16),
            pltpu.VMEM((count - 1, rows, widths[1]), bf16),
            pltpu.SemaphoreType.DMA((2, count)),
            pltpu.SemaphoreType.DMA((2, count)),
            pltpu.SemaphoreType.DMA((2, half)),
            pltpu.SemaphoreType.DMA((2,)),
            pltpu.VMEM((rows, widths[0]), f32),
            pltpu.VMEM((rows, widths[1]), f32),
        ],
        compiler_params=pltpu.CompilerParams(
            collective_id=collective_id, has_side_effects=True, vmem_limit_bytes=VMEM_BYTES
        ),
        name="token_sum",
    )(y)


def dense_sum_kernel(n_rep, n_ep, rows, chunks, split, *refs):
    left_ref, right_ref, small_ref, head_ref, out_ref, head_out = refs[:6]
    rest = list(refs[6:])
    bits = bits_of(n_ep)
    wide = right_ref.shape[1] // (chunks - 1)
    half = wide // 2
    rep, me = lax.axis_index("rep"), lax.axis_index("ep")
    mine = [lax.rem(lax.div(me, 1 << b), 2) for b in range(bits)]
    part, got_core = rest[:2]
    acc = [None] + [rest[2 + 2 * k : 4 + 2 * k] for k in range(bits)]
    rest = rest[2 + 2 * bits :]
    got = [None] + [rest[2 * k : 2 * k + 2] for k in range(bits)]
    rest = rest[2 * bits :]
    head_own, head_got, head_rep = rest[:3]
    core_send, core_recv, step_send, step_recv, rep_send, rep_recv, head_send, head_recv, head_rs, head_rr = rest[3:]
    up = list(range(1, bits))
    orders = (up, up[::-1])
    left = [[sorted(set(up) - set(o[:k])) for k in range(bits)] for o in orders]
    lags = [0, 1]
    for _ in range(bits):
        lags.append(lags[-1] + 2)
    deep = 4
    others = [lax.rem(rep + d, n_rep) for d in range(1, n_rep)]
    meet([(rep, me ^ (1 << b)) for b in range(bits)] + [(other, me) for other in others])

    def core_copy(c):
        slot = lax.rem(c, 2)
        return pltpu.make_async_remote_copy(
            src_ref=part.at[slot, 1 - mine[0]],
            dst_ref=got_core.at[slot],
            send_sem=core_send.at[slot],
            recv_sem=core_recv.at[slot],
            device_id=(rep, me ^ 1),
            device_id_type=MESH,
        )

    def bit_copy(k, h, c):
        slot = lax.rem(c, deep)
        bit = orders[h][k - 1]
        place = left[h][k - 1].index(bit)
        return pltpu.make_async_remote_copy(
            src_ref=acc[k][h].at[(slot,) + (slice(None),) * place + (1 - mine[bit],)],
            dst_ref=got[k][h].at[slot],
            send_sem=step_send.at[k, h, slot],
            recv_sem=step_recv.at[k, h, slot],
            device_id=(rep, me ^ (1 << bit)),
            device_id_type=MESH,
        )

    def rep_copy(h, c, d):
        slot = lax.rem(c, deep)
        return pltpu.make_async_remote_copy(
            src_ref=acc[bits][h].at[slot, others[d]],
            dst_ref=got[bits][h].at[slot, n_rep - 2 - d],
            send_sem=rep_send.at[h, slot, d],
            recv_sem=rep_recv.at[h, slot, n_rep - 2 - d],
            device_id=(others[d], me),
            device_id_type=MESH,
        )

    corners = [()]
    for _ in up:
        corners = [c + (v,) for c in corners for v in range(2)]
    block = n_rep * rows
    side_rows = len(corners) * block

    def stage_make(c):
        slot = lax.rem(c, 2)

        @pl.when(c >= 2)
        def _():
            core_copy(c - 2).wait_send()

        @pl.when(c < chunks - 1)
        def _():
            which = jnp.where(c >= split[0], 1, 0) + jnp.where(c >= split[1], 1, 0)
            columns = pl.ds(pl.multiple_of(c * wide, wide), wide)
            weights = right_ref[:, columns]
            for side in (1, 0):
                which_side = 1 - mine[0] if side else mine[0]
                for n, corner in enumerate(corners):
                    start = (which * 2 + which_side) * side_rows + n * block
                    value = jnp.dot(
                        left_ref[pl.ds(pl.multiple_of(start, block), block), :],
                        weights,
                        preferred_element_type=f32,
                    )
                    part[(slot, which_side) + corner] = value.astype(bf16).reshape(n_rep, rows, wide)

        @pl.when(c == chunks - 1)
        def _():
            thin = small_ref.shape[1]
            for side in range(2):
                for n, corner in enumerate(corners):
                    value = small_ref[pl.ds(side * side_rows + n * block, block), :].reshape(n_rep, rows, thin)
                    blank = jnp.zeros((n_rep, rows, wide - thin), bf16)
                    part[(slot, side) + corner + (slice(None), slice(None), slice(0, thin))] = value
                    part[(slot, side) + corner + (slice(None), slice(None), slice(thin, wide))] = blank

        core_copy(c).start()

    def stage_core(c):
        slot, put = lax.rem(c, 2), lax.rem(c, deep)

        @pl.when(c >= deep)
        def _():
            for h in range(2):
                if bits > 1:
                    bit_copy(1, h, c - deep).wait_send()

        core_copy(c).wait_recv()
        for corner in corners:
            total = part[(slot, mine[0]) + corner].astype(f32) + got_core[(slot,) + corner].astype(f32)
            total = total.astype(bf16)
            for h in range(2):
                acc[1][h][(put,) + corner] = total[:, :, h * half : (h + 1) * half]
        for h in range(2):
            bit_copy(1, h, c).start()

    def stage_bit(k, c):
        slot = lax.rem(c, deep)
        for h in range(2):
            bit = orders[h][k - 2]
            place = left[h][k - 2].index(bit)

            @pl.when(c >= deep)
            def _(h=h):
                if k < bits:
                    bit_copy(k, h, c - deep).wait_send()
                else:
                    for d in range(n_rep - 1):
                        rep_copy(h, c - deep, d).wait_send()

            bit_copy(k - 1, h, c).wait_recv()
            small_corners = [()]
            for _ in left[h][k - 1]:
                small_corners = [q + (v,) for q in small_corners for v in range(2)]
            for corner in small_corners:
                full = corner[:place] + (mine[bit],) + corner[place:]
                total = acc[k - 1][h][(slot,) + full].astype(f32) + got[k - 1][h][(slot,) + corner].astype(f32)
                acc[k][h][(slot,) + corner] = total.astype(bf16)
            if k < bits:
                bit_copy(k, h, c).start()
            else:
                for d in range(n_rep - 1):
                    rep_copy(h, c, d).start()

    def stage_end(c):
        slot = lax.rem(c, deep)
        for h in range(2):
            total = acc[bits][h][slot, rep].astype(f32)
            for d in range(n_rep - 1):
                rep_copy(h, c, d).wait_recv()
            for d in range(n_rep - 1):
                total += got[bits][h][slot, d].astype(f32)
            out_ref[:, pl.ds(pl.multiple_of(c * wide + h * half, half), half)] = total

    def head_copy(t):
        return pltpu.make_async_remote_copy(
            src_ref=head_own.at[t],
            dst_ref=head_got.at[t],
            send_sem=head_send.at[t],
            recv_sem=head_recv.at[t],
            device_id=(rep, me ^ (1 << t)),
            device_id_type=MESH,
        )

    def head_rep_copy(d):
        return pltpu.make_async_remote_copy(
            src_ref=head_own.at[bits],
            dst_ref=head_rep.at[rep],
            send_sem=head_rs.at[d],
            recv_sem=head_rr.at[n_rep - 2 - d],
            device_id=(others[d], me),
            device_id_type=MESH,
        )

    def head_step(t):
        if t == 0:
            head_own[0] = head_ref[...]
            head_copy(0).start()
        elif t <= bits:
            head_copy(t - 1).wait_recv()
            head_own[t] = head_own[t - 1] + head_got[t - 1]
            if t < bits:
                head_copy(t).start()
            else:
                for d in range(n_rep - 1):
                    head_rep_copy(d).start()
                head_rep[rep] = head_own[bits]
        else:
            for d in range(n_rep - 1):
                head_rep_copy(d).wait_recv()
            total = head_rep[0]
            for r in range(1, n_rep):
                total = total + head_rep[r]
            head_out[...] = total

    def step(i, carry):
        for stage in reversed(range(len(lags))):
            c = i - lags[stage]

            @pl.when((c >= 0) & (c < chunks))
            def _(stage=stage, c=c):
                if stage == 0:
                    stage_make(c)
                elif stage == 1:
                    stage_core(c)
                elif stage <= bits:
                    stage_bit(stage, c)
                else:
                    stage_end(c)

        for t in range(bits + 2):

            @pl.when(i == t)
            def _(t=t):
                head_step(t)

        return carry

    lax.fori_loop(0, chunks + lags[-1], step, 0)
    for c in range(chunks - 2, chunks):
        core_copy(c).wait_send()
    for c in range(chunks - deep, chunks):
        for h in range(2):
            for k in range(1, bits):
                bit_copy(k, h, c).wait_send()
            for d in range(n_rep - 1):
                rep_copy(h, c, d).wait_send()
    for t in range(bits):
        head_copy(t).wait_send()
    for d in range(n_rep - 1):
        head_rep_copy(d).wait_send()


def dense_sum(left, right, small, head, n_rep, n_ep, split, collective_id):
    chunk = 512
    chunks = right.shape[1] // chunk + 1
    bits = bits_of(n_ep)
    rows = left.shape[0] // (3 * n_rep * n_ep)
    deep = 4
    half = chunk // 2
    vmem = pl.BlockSpec(memory_space=pltpu.VMEM)
    inner = (n_rep, rows)
    scratch = [
        pltpu.VMEM((2, 2) + (2,) * (bits - 1) + inner + (chunk,), bf16),
        pltpu.VMEM((2,) + (2,) * (bits - 1) + inner + (chunk,), bf16),
    ]
    for k in range(1, bits + 1):
        scratch += [pltpu.VMEM((deep,) + (2,) * (bits - k) + inner + (half,), bf16)] * 2
    for k in range(1, bits):
        scratch += [pltpu.VMEM((deep,) + (2,) * (bits - 1 - k) + inner + (half,), bf16)] * 2
    scratch += [pltpu.VMEM((deep, n_rep - 1, rows, half), bf16)] * 2
    scratch += [
        pltpu.VMEM((bits + 1,) + head.shape, f32),
        pltpu.VMEM((bits,) + head.shape, f32),
        pltpu.VMEM((n_rep,) + head.shape, f32),
        pltpu.SemaphoreType.DMA((2,)),
        pltpu.SemaphoreType.DMA((2,)),
        pltpu.SemaphoreType.DMA((bits, 2, deep)),
        pltpu.SemaphoreType.DMA((bits, 2, deep)),
        pltpu.SemaphoreType.DMA((2, deep, n_rep - 1)),
        pltpu.SemaphoreType.DMA((2, deep, n_rep - 1)),
        pltpu.SemaphoreType.DMA((bits,)),
        pltpu.SemaphoreType.DMA((bits,)),
        pltpu.SemaphoreType.DMA((n_rep - 1,)),
        pltpu.SemaphoreType.DMA((n_rep - 1,)),
    ]
    return pl.pallas_call(
        functools.partial(dense_sum_kernel, n_rep, n_ep, rows, chunks, split),
        out_shape=(
            jax.ShapeDtypeStruct((rows, chunks * chunk), f32),
            jax.ShapeDtypeStruct(head.shape, f32),
        ),
        in_specs=[vmem] * 4,
        out_specs=(vmem, vmem),
        scratch_shapes=scratch,
        compiler_params=pltpu.CompilerParams(
            collective_id=collective_id, has_side_effects=True, vmem_limit_bytes=VMEM_BYTES
        ),
        cost_estimate=pl.CostEstimate(flops=1000, bytes_accessed=1000, transcendentals=0),
        name="dense_sum",
    )(left, right, small, head)


NT = (((1,), (1,)), ((), ()))
TN = (((0,), (0,)), ((), ()))


def expert_kernel(first, last, experts, width, hidden_of, *refs):
    (info, h_ref, g_ref, wg_ref, wu_ref, wd_ref) = refs[:6]
    rest = list(refs[6:])
    prev_ref = None if first else rest.pop(0)
    y_ref, grad_ref = rest[:2]
    xs, gs, ds, hs, stage, prev_buf, wide, tall, in_sem, out_sem, prev_sem, grad_sem = rest[2:]
    shares = grad_ref.shape[0]
    wide_share, tall_share = width // shares, hidden_of // shares
    hidden = wg_ref.shape[1]
    units = info[0]
    expert = info[1]
    table = 8
    per_tile = TILE // UNIT
    tiles = (units + per_tile - 1) // per_tile
    most = xs.shape[0] // TILE
    floor_tiles = min(4, most)

    def unit_in(u, slot):
        source = pl.ds(pl.multiple_of(info[table + u], UNIT), UNIT)
        target = pl.ds(pl.multiple_of(u * UNIT, UNIT), UNIT)
        return (
            pltpu.make_async_copy(h_ref.at[source], xs.at[target], in_sem.at[0, slot]),
            pltpu.make_async_copy(g_ref.at[source], gs.at[target], in_sem.at[1, slot]),
        )

    def begin(u, carry):
        for copy in unit_in(u, u // per_tile):
            copy.start()
        return carry

    lax.fori_loop(0, units, begin, 0)

    def blank(u, carry):
        target = pl.ds(pl.multiple_of(u * UNIT, UNIT), UNIT)
        xs[target, :] = jnp.zeros((UNIT, xs.shape[1]), bf16)
        gs[target, :] = jnp.zeros((UNIT, gs.shape[1]), bf16)
        return carry

    lax.fori_loop(units, jnp.maximum(tiles, floor_tiles) * per_tile, blank, 0)

    def blank_tile(i, carry):
        target = pl.ds(pl.multiple_of(i * TILE, TILE), TILE)
        ds[target, :] = jnp.zeros((TILE, ds.shape[1]), bf16)
        hs[target, :] = jnp.zeros((TILE, hs.shape[1]), bf16)
        return carry

    lax.fori_loop(tiles, floor_tiles, blank_tile, 0)

    def prev_copy(i):
        rows = pl.ds(pl.multiple_of(i * TILE, TILE), TILE)
        return pltpu.make_async_copy(prev_ref.at[rows], prev_buf.at[i % 2], prev_sem.at[i % 2])

    if not first:
        prev_copy(0).start()

    def unit_out(u):
        target = pl.ds(pl.multiple_of(info[table + u], UNIT), UNIT)
        tile = u // per_tile
        source = pl.ds(pl.multiple_of((u % per_tile) * UNIT, UNIT), UNIT)
        return pltpu.make_async_copy(stage.at[tile % 2, source], y_ref.at[target], out_sem.at[tile % 2])

    def out_start(i):
        if last:
            lax.fori_loop(
                i * per_tile,
                jnp.minimum((i + 1) * per_tile, units),
                lambda u, c: (unit_out(u).start(), c)[1],
                0,
            )
        else:
            rows = pl.ds(pl.multiple_of(i * TILE, TILE), TILE)
            pltpu.make_async_copy(stage.at[i % 2], y_ref.at[rows], out_sem.at[i % 2]).start()

    def out_wait(i):
        if last:
            lax.fori_loop(
                i * per_tile,
                jnp.minimum((i + 1) * per_tile, units),
                lambda u, c: (unit_out(u).wait(), c)[1],
                0,
            )
        else:
            rows = pl.ds(pl.multiple_of(i * TILE, TILE), TILE)
            pltpu.make_async_copy(stage.at[i % 2], y_ref.at[rows], out_sem.at[i % 2]).wait()

    lane = lax.broadcasted_iota(jnp.int32, (TILE, EXT), 1)
    weight_lanes = (lane == expert) | (lane == expert + experts) | (lane == expert + 2 * experts)

    def tile_step(i, carry):
        def landed(u, c):
            for copy in unit_in(u, i):
                copy.wait()
            return c

        lax.fori_loop(i * per_tile, jnp.minimum((i + 1) * per_tile, units), landed, 0)
        rows = pl.ds(pl.multiple_of(i * TILE, TILE), TILE)
        x = xs[rows, :width]
        g = gs[rows, :]
        extra = xs[rows, width:].astype(f32)
        weight = jnp.sum(jnp.where(weight_lanes, extra, 0.0), axis=1, keepdims=True)
        gate = jnp.dot(x, wg_ref[...], preferred_element_type=f32)
        up = jnp.dot(x, wu_ref[...], preferred_element_type=f32)
        d_plain = lax.dot_general(g, wd_ref[...], NT, preferred_element_type=f32)
        sig = 1.0 / (1.0 + jnp.exp(-gate))
        silu = gate * sig
        hid = silu * up
        d_weight = jnp.sum(hid.astype(bf16).astype(f32) * d_plain, axis=1, keepdims=True)
        hs[rows, :] = (hid * weight).astype(bf16)
        d_hidden = d_plain * weight
        ds[rows, :hidden] = (d_hidden * up * sig * (1.0 + gate * (1.0 - sig))).astype(bf16)
        ds[rows, hidden:] = (d_hidden * silu).astype(bf16)

        @pl.when(i >= 2)
        def _():
            out_wait(i - 2)

        if not first:

            @pl.when(i + 1 < tiles)
            def _():
                prev_copy(i + 1).start()

            prev_copy(i).wait()
        slot = i % 2
        high = d_weight.astype(bf16).astype(f32)
        low = d_weight - high
        note = jnp.where(lane == expert, high, 0.0) + jnp.where(lane == expert + experts, low, 0.0)
        d_row = lax.dot_general(ds[rows, :hidden], wg_ref[...], NT, preferred_element_type=f32)
        d_row += lax.dot_general(ds[rows, hidden:], wu_ref[...], NT, preferred_element_type=f32)
        if not first:
            d_row += prev_buf[slot, :, :width].astype(f32)
            note += prev_buf[slot, :, width : width + EXT].astype(f32)
        stage[slot, :, :width] = d_row.astype(bf16)
        stage[slot, :, width : width + EXT] = note.astype(bf16)
        out = jnp.dot(hs[rows, :], wd_ref[...], preferred_element_type=f32)
        if not first:
            out += prev_buf[slot, :, width + EXT :].astype(f32)
        stage[slot, :, width + EXT :] = out.astype(bf16)
        out_start(i)
        return carry

    lax.fori_loop(0, tiles, tile_step, 0)

    block = 256

    def grads(depth):
        def wide_copies(m):
            per = wide_share // block
            return tuple(
                pltpu.make_async_copy(
                    wide.at[m % 2, :, p * LANES : (p + 1) * LANES],
                    grad_ref.at[
                        m // per,
                        pl.ds(pl.multiple_of(p * wide_share + (m % per) * block, block), block),
                    ],
                    grad_sem.at[m % 2, p],
                )
                for p in range(2 * hidden // LANES)
            )

        def wide_step(m, carry):
            @pl.when(m >= 2)
            def _():
                for copy in wide_copies(m - 2):
                    copy.wait()

            columns = pl.ds(pl.multiple_of(m * block, block), block)
            wide[m % 2] = lax.dot_general(
                xs[:depth, columns], ds[:depth, :], TN, preferred_element_type=f32
            ).astype(bf16)
            for copy in wide_copies(m):
                copy.start()
            return carry

        count = width // block
        lax.fori_loop(0, count, wide_step, 0)
        for m in range(count - 2, count):
            for copy in wide_copies(m):
                copy.wait()

        piece = math.gcd(block, tall_share)
        base = 2 * hidden // LANES * wide_share

        def tall_copies(m):
            made = []
            for q in range(block // piece):
                first_row = m * block + q * piece
                share, inside = first_row // tall_share, first_row % tall_share
                for p in range(width // LANES):
                    rows = pl.ds(pl.multiple_of(base + p * tall_share + inside, piece), piece)
                    made.append(
                        pltpu.make_async_copy(
                            tall.at[m % 2, q * piece : (q + 1) * piece, p * LANES : (p + 1) * LANES],
                            grad_ref.at[share, rows],
                            grad_sem.at[m % 2, q * (width // LANES) + p],
                        )
                    )
            return made

        def tall_step(m, carry):
            @pl.when(m >= 2)
            def _():
                for copy in tall_copies(m - 2):
                    copy.wait()

            columns = pl.ds(pl.multiple_of(m * block, block), block)
            tall[m % 2] = lax.dot_general(
                hs[:depth, columns], gs[:depth, :], TN, preferred_element_type=f32
            ).astype(bf16)
            for copy in tall_copies(m):
                copy.start()
            return carry

        count = hidden // block
        lax.fori_loop(0, count, tall_step, 0)
        for m in range(count - 2, count):
            for copy in tall_copies(m):
                copy.wait()

    for choice in range(floor_tiles, most + 1):
        chosen = (tiles <= choice) if choice == floor_tiles else (tiles == choice)

        @pl.when(chosen)
        def _(choice=choice):
            grads(choice * TILE)

    @pl.when(tiles >= 2)
    def _():
        out_wait(tiles - 2)

    out_wait(tiles - 1)


def expert_pass(info, h_rows, g_rows, w_gate, w_up, w_down, prev, last, experts, shares):
    tokens, width = g_rows.shape
    hidden = w_gate.shape[1]
    wide_row = width + EXT + width
    any_spec = pl.BlockSpec(memory_space=pl.ANY)
    vmem_spec = pl.BlockSpec(memory_space=pltpu.VMEM)
    first = prev is None
    operands = [info, h_rows, g_rows, w_gate, w_up, w_down] + ([] if first else [prev])
    specs = [pl.BlockSpec(memory_space=pltpu.SMEM), any_spec, any_spec, vmem_spec, vmem_spec, vmem_spec]
    specs += [] if first else [any_spec]
    return pl.pallas_call(
        functools.partial(expert_kernel, first, last, experts, width, hidden),
        out_shape=(
            jax.ShapeDtypeStruct((tokens, wide_row), bf16),
            jax.ShapeDtypeStruct((shares, 3 * hidden * width // shares // LANES, LANES), bf16),
        ),
        in_specs=specs,
        out_specs=(any_spec,) * 2,
        scratch_shapes=[
            pltpu.VMEM((tokens, width + EXT), bf16),
            pltpu.VMEM((tokens, width), bf16),
            pltpu.VMEM((tokens, 2 * hidden), bf16),
            pltpu.VMEM((tokens, hidden), bf16),
            pltpu.VMEM((2, TILE, wide_row), bf16),
            pltpu.VMEM((2, TILE, wide_row), bf16),
            pltpu.VMEM((2, 256, 2 * hidden), bf16),
            pltpu.VMEM((2, 256, width), bf16),
            pltpu.SemaphoreType.DMA((2, tokens // TILE)),
            pltpu.SemaphoreType.DMA((2,)),
            pltpu.SemaphoreType.DMA((2,)),
            pltpu.SemaphoreType.DMA((2, max(2 * hidden // LANES, 256 // math.gcd(256, hidden // shares) * width // LANES))),
        ],
        compiler_params=pltpu.CompilerParams(vmem_limit_bytes=VMEM_BYTES),
        cost_estimate=pl.CostEstimate(flops=1000, bytes_accessed=1000, transcendentals=0),
        name="experts",
    )(*operands)


def unit_table(lengths):
    per_sequence = TILE // UNIT
    counts = (lengths + UNIT - 1) // UNIT
    unit = jnp.arange(lengths.shape[0] * per_sequence, dtype=jnp.int32)
    live = (unit % per_sequence) < jnp.repeat(counts, per_sequence)
    place = jnp.cumsum(live.astype(jnp.int32)) - 1
    hit = (place[None, :] == unit[:, None]) & live[None, :]
    rows = jnp.sum(jnp.where(hit, unit[None, :] * UNIT, 0), axis=1)
    return (jnp.sum(counts), rows)


def split_three(value):
    high = lax.reduce_precision(value, 8, 7)
    rest = value - high
    middle = lax.reduce_precision(rest, 8, 7)
    return jnp.concatenate([high, middle, rest - middle], axis=-1)


def per_device(
    hidden_in,
    out_grad,
    attn_gain,
    w_q,
    key_weight,
    value_weight,
    w_o,
    ffn_gain,
    router_w,
    qk_gains,
    w_gate,
    w_up,
    w_down,
    lengths,
    routes,
    order,
):
    everywhere = ("rep", "ep")
    rep_count, ep_count = (lax.axis_size("rep"), lax.axis_size("ep"))
    rep_index, ep_index = (lax.axis_index("rep"), lax.axis_index("ep"))
    inputs = hidden_in[0].astype(f32)
    sequence_length, model_width = inputs.shape
    head_size = qk_gains.shape[1]
    wide_q, wide_kv = (w_q.shape[1], key_weight.shape[1])
    heads_q, heads_kv = (wide_q // head_size, wide_kv // head_size)
    groups = heads_q // heads_kv
    local_experts = w_gate.shape[0]
    experts = local_experts * ep_count
    top_count = routes.shape[2]
    score_scale = head_size ** (-0.5)
    group_lengths = lax.dynamic_slice_in_dim(lengths, rep_index * ep_count, ep_count)
    length = lax.dynamic_index_in_dim(group_lengths, ep_index, keepdims=False)
    positions = jnp.arange(sequence_length, dtype=jnp.int32)
    live = positions < length
    live_rows = live.astype(f32)

    expert_iota = jnp.arange(experts, dtype=jnp.int32)
    route_hot = routes[0][..., None] == expert_iota
    routed = jnp.any(route_hot, axis=1) & live[:, None]
    order_of = jnp.sum(
        jnp.where(route_hot, order[0].reshape(sequence_length, top_count)[..., None], 0), axis=1
    )
    sort_key = jnp.where(routed, order_of, sequence_length * top_count)
    loads = jnp.sum(routed.astype(jnp.int32), axis=0)
    rank = jnp.sum((sort_key[None, :, :] < sort_key[:, None, :]).astype(jnp.int32), axis=1)

    own_rows = w_q.shape[0]
    load_columns = -(-experts // own_rows)
    load_block = jnp.pad(loads, (0, load_columns * own_rows - experts)).reshape(load_columns, own_rows).T
    small = jnp.concatenate(
        [router_w, attn_gain[:, None], ffn_gain[:, None], load_block.astype(bf16)], axis=1
    )
    small = jnp.pad(small, ((0, 0), (0, EXT - small.shape[1])))
    pack = jnp.concatenate([w_q, key_weight, value_weight, small], axis=1)
    mat_qkv = gather_weights(pack, rep_count, ep_count, 4)
    grads_all = lax.all_gather(out_grad[0], "ep", axis=0, tiled=True)
    if ep_count <= 8:
        w_o, mat_qkv, grads_all = lax.optimization_barrier((w_o, mat_qkv, grads_all))
    else:
        w_o, mat_qkv = lax.optimization_barrier((w_o, mat_qkv))
    mat_qkv = mat_qkv.reshape(-1, pack.shape[1])
    mat_o = lax.all_gather(w_o, everywhere, axis=0, tiled=True)

    wide_all = wide_q + 2 * wide_kv
    small_all = mat_qkv[:, wide_all:]
    mat_router = small_all[:, :experts]
    gain_attn = small_all[:, experts].astype(f32)
    gain_ffn = small_all[:, experts + 1].astype(f32)
    loads_all = (
        small_all[:, experts + 2 : experts + 2 + load_columns]
        .reshape(rep_count, ep_count, own_rows, load_columns)
        .transpose(0, 1, 3, 2)
        .reshape(rep_count, ep_count, load_columns * own_rows)[:, :, :experts]
        .astype(jnp.int32)
    )
    group_loads = lax.dynamic_index_in_dim(loads_all, rep_index, keepdims=False)
    earlier = (jnp.arange(ep_count) < ep_index)[:, None]
    load_prefix = jnp.sum(jnp.where(earlier, group_loads, 0), axis=0)
    capacity = 9 * top_count * jnp.sum(group_lengths) // (8 * experts)
    kept = routed & (load_prefix[None, :] + rank < capacity)
    kept_float = kept.astype(f32)

    gain_q = qk_gains[0].astype(f32)
    gain_k = qk_gains[1].astype(f32)
    norm_one, inv_one = rms_parts(inputs)
    hidden_first = (norm_one * gain_attn).astype(bf16)
    projected = jnp.dot(hidden_first, mat_qkv, preferred_element_type=f32)
    query_projected = projected[:, :wide_q].reshape(sequence_length, heads_q, head_size)
    key_projected = projected[:, wide_q : wide_q + wide_kv].reshape(sequence_length, heads_kv, head_size)
    value_rows = (
        projected[:, wide_q + wide_kv : wide_all]
        .astype(bf16)
        .reshape(sequence_length, heads_kv, head_size)
    )
    cosine_lookup, sine_lookup = rope_tables(sequence_length, head_size)
    q_norm, q_inv = rms_parts(query_projected)
    k_norm, k_inv = rms_parts(key_projected)
    query_rows = (
        apply_rotation(q_norm * gain_q, cosine_lookup, sine_lookup)
        .astype(bf16)
        .reshape(sequence_length, heads_kv, groups, head_size)
    )
    keys = apply_rotation(k_norm * gain_k, cosine_lookup, sine_lookup).astype(bf16)
    scores = jnp.einsum("tkgd,ukd->kgtu", query_rows, keys, preferred_element_type=f32) * score_scale
    allowed = (positions[None, :] <= positions[:, None]) & (positions[None, :] < length)
    scores = jnp.where(allowed, scores, -1e30)
    attn_probs = jax.nn.softmax(scores, axis=-1)
    probs_low = attn_probs.astype(bf16)
    attended = (
        jnp.einsum("kgtu,ukd->tkgd", probs_low, value_rows, preferred_element_type=f32)
        .astype(bf16)
        .reshape(sequence_length, heads_q * head_size)
    )
    middle = inputs + jnp.dot(attended, mat_o, preferred_element_type=f32)
    norm_two, inv_two = rms_parts(middle)
    h_two = (norm_two * gain_ffn).astype(bf16)
    logits = jnp.dot(h_two, mat_router, preferred_element_type=f32)
    named = jnp.any(route_hot, axis=1)
    top_logit = jnp.max(jnp.where(named, logits, -jnp.inf), axis=1, keepdims=True)
    raised = jnp.where(named, jnp.exp(jnp.where(named, logits - top_logit, 0.0)), 0.0)
    route_gates = raised / jnp.sum(raised, axis=1, keepdims=True)
    pair_weight = route_gates * kept_float

    extra = split_three(pair_weight).astype(bf16)
    extra = jnp.pad(extra, ((0, 0), (0, EXT - extra.shape[1])))
    sent = jnp.concatenate([h_two, extra], axis=1)
    h_all = gather_tokens(sent, ep_count, 1)

    part = min(ep_count, 8)
    tokens = part * sequence_length
    sums = []
    y_parts = []
    for c in range(ep_count // part):
        live_units, unit_rows = unit_table(group_lengths[c * part : (c + 1) * part])
        h_rows = h_all[c * part : (c + 1) * part].reshape(tokens, model_width + EXT)
        g_rows = grads_all[c * tokens : (c + 1) * tokens]
        prev, found = None, []
        for local in range(local_experts):
            info = jnp.concatenate(
                [
                    jnp.stack([live_units, ep_index * local_experts + local]).astype(jnp.int32),
                    jnp.zeros((6,), jnp.int32),
                    unit_rows,
                ]
            )
            prev, weight_grads = expert_pass(
                info,
                h_rows,
                g_rows,
                w_gate[local],
                w_up[local],
                w_down[local],
                prev,
                local == local_experts - 1,
                experts,
                rep_count,
            )
            found.append(weight_grads)
        y_parts.append(prev.reshape(part, sequence_length, -1))
        sums.append(found)
    y_all = y_parts[0] if len(y_parts) == 1 else jnp.concatenate(y_parts, axis=0)
    hidden_units = w_gate.shape[2]
    wide_share, tall_share = model_width // rep_count, hidden_units // rep_count
    found = []
    for local in range(local_experts):
        total = sums[0][local]
        for more in sums[1:]:
            total = (total.astype(f32) + more[local].astype(f32)).astype(bf16)
        found.append(lax.psum_scatter(total, "rep", scatter_dimension=0, tiled=True))
    found = jnp.concatenate(found, axis=0)

    def unpacked(start, rows, columns):
        blocks = found[:, start : start + rows * (columns // LANES)]
        blocks = blocks.reshape(local_experts, columns // LANES, rows, LANES)
        return blocks.transpose(0, 2, 1, 3).reshape(local_experts, rows, columns).astype(f32)

    wide_rows = wide_share * (hidden_units // LANES)
    expert_sums = (
        unpacked(0, wide_share, hidden_units),
        unpacked(wide_rows, wide_share, hidden_units),
        unpacked(2 * wide_rows, tall_share, model_width),
    )

    back = sum_tokens(y_all, ep_count, (model_width + EXT, model_width), 2)
    live_column = live[:, None]
    moe_output = jnp.where(live_column, back[:, model_width + EXT :], 0.0)
    layer_out = jnp.where(live_column, middle + moe_output, 0.0)
    grad_rows = out_grad[0].astype(f32) * live_rows[:, None]
    notes = back[:, model_width : model_width + 2 * experts]
    d_weight = jnp.where(live_column, notes[:, :experts] + notes[:, experts:], 0.0)
    d_gates = d_weight * kept_float
    d_logits = route_gates * (d_gates - jnp.sum(route_gates * d_gates, axis=-1, keepdims=True))

    router_float = mat_router.astype(f32)
    d_h_two = jnp.where(live_column, back[:, :model_width], 0.0)
    d_h_two = d_h_two + jnp.dot(d_logits, router_float.T, precision=top_precision)
    grad_router = jnp.dot(h_two.astype(f32).T, d_logits, precision=top_precision)
    grad_ffn = jnp.sum(d_h_two * norm_two, axis=0)
    d_middle = grad_rows + rms_back(d_h_two * gain_ffn, norm_two, inv_two)
    d_middle_low = d_middle.astype(bf16)
    d_attended = (
        jnp.einsum("td,cd->tc", d_middle_low, mat_o, preferred_element_type=f32)
        .astype(bf16)
        .reshape(sequence_length, heads_kv, groups, head_size)
    )
    d_probs = jnp.einsum("tkgd,ukd->kgtu", d_attended, value_rows, preferred_element_type=f32)
    d_values = (
        jnp.einsum("kgtu,tkgd->ukd", probs_low, d_attended, preferred_element_type=f32)
        .astype(bf16)
        .reshape(sequence_length, heads_kv * head_size)
    )
    d_scores = (attn_probs * (d_probs - jnp.sum(attn_probs * d_probs, axis=-1, keepdims=True))).astype(bf16)
    d_queries = (
        jnp.einsum("kgtu,ukd->tkgd", d_scores, keys, preferred_element_type=f32).reshape(
            sequence_length, heads_q, head_size
        )
        * score_scale
    )
    d_keys = jnp.einsum("kgtu,tkgd->ukd", d_scores, query_rows, preferred_element_type=f32) * score_scale
    d_q_scaled = rotate_back(d_queries, cosine_lookup, sine_lookup)
    d_k_scaled = rotate_back(d_keys, cosine_lookup, sine_lookup)
    grad_gain_q = jnp.sum(d_q_scaled * q_norm, axis=(0, 1))
    grad_gain_k = jnp.sum(d_k_scaled * k_norm, axis=(0, 1))
    d_q_proj = (
        rms_back(d_q_scaled * gain_q, q_norm, q_inv).astype(bf16).reshape(sequence_length, heads_q * head_size)
    )
    d_k_proj = (
        rms_back(d_k_scaled * gain_k, k_norm, k_inv).astype(bf16).reshape(sequence_length, heads_kv * head_size)
    )
    d_qkv = jnp.concatenate([d_q_proj, d_k_proj, d_values], axis=1)
    d_h_one = jnp.einsum("tf,cf->tc", d_qkv, mat_qkv[:, :wide_all], preferred_element_type=f32)
    grad_attn = jnp.sum(d_h_one * norm_one, axis=0)
    grad_input = d_middle + rms_back(d_h_one * gain_attn, norm_one, inv_one)

    small_grads = jnp.concatenate([grad_router, grad_attn[:, None], grad_ffn[:, None]], axis=1)
    small_grads = jnp.pad(small_grads, ((0, 0), (0, EXT - small_grads.shape[1]))).astype(bf16)
    ep_bits = bits_of(ep_count)

    def owner_order(value, parts):
        shape = (rep_count,) + (2,) * ep_bits + (parts, own_rows, value.shape[1])
        axes = (ep_bits + 1,) + tuple(range(ep_bits, 0, -1)) + (0, ep_bits + 2, ep_bits + 3)
        return value.reshape(shape).transpose(axes).reshape(value.shape)

    left = jnp.concatenate([owner_order(hidden_first.T, 1), owner_order(attended.T, 2)], axis=0)
    right = jnp.concatenate([d_qkv, d_middle_low, d_middle_low], axis=1)
    head = jnp.pad(jnp.stack([grad_gain_q, grad_gain_k]), ((0, 6), (0, 0)))
    splits = (wide_all // 512, (wide_all + model_width) // 512)
    sums_all, head_sum = dense_sum(
        left, right, owner_order(small_grads, 1), head, rep_count, ep_count, splits, 3
    )
    sum_o = jnp.concatenate(
        [sums_all[:, wide_all : wide_all + model_width], sums_all[:, wide_all + model_width : wide_all + 2 * model_width]],
        axis=0,
    )
    small_sum = sums_all[:, wide_all + 2 * model_width :]
    return (
        layer_out[None],
        grad_input[None],
        small_sum[:, experts],
        sums_all[:, :wide_q],
        sums_all[:, wide_q : wide_q + wide_kv],
        sums_all[:, wide_q + wide_kv : wide_all],
        sum_o,
        small_sum[:, experts + 1],
        small_sum[:, :experts],
        head_sum[:2],
        expert_sums[0],
        expert_sums[1],
        expert_sums[2],
    )


def solution(mesh):
    both = ("rep", "ep")
    placed = (
        P(both, None, None),
        P(both, None, None),
        P(both),
        P(both, None),
        P(both, None),
        P(both, None),
        P(both, None),
        P(both),
        P(both, None),
        P(),
        P("ep", None, None),
        P("ep", None, None),
        P("ep", None, None),
        P(),
        P(both, None, None),
        P(both, None),
    )
    return jax.shard_map(
        per_device,
        mesh=mesh,
        in_specs=placed,
        out_specs=(
            P(both, None, None),
            P(both, None, None),
            P(both),
            P(both, None),
            P(both, None),
            P(both, None),
            P(both, None),
            P(both),
            P(both, None),
            P(),
            P("ep", "rep", None),
            P("ep", "rep", None),
            P("ep", "rep", None),
        ),
        check_vma=False,
    )
```

```python
import functools
import math

import jax
import jax.numpy as jnp
from jax import lax
from jax.experimental import pallas as pl
from jax.experimental.pallas import tpu as pltpu
from jax.sharding import PartitionSpec as P

eps = 1e-06
rope_base = 1000000.0
top_precision = lax.Precision.HIGHEST
MESH = pl.DeviceIdType.MESH
f32, bf16 = jnp.float32, jnp.bfloat16
EXT = 128
UNIT = 16
LANES = 256
TILE = 256
VMEM_BYTES = 58 * 1024 * 1024
NT = (((1,), (1,)), ((), ()))
TN = (((0,), (0,)), ((), ()))


def rms_parts(value_rows):
    inverse = lax.rsqrt(jnp.mean(value_rows * value_rows, axis=-1, keepdims=True) + eps)
    return (value_rows * inverse, inverse)


def rms_back(grad_norm, normed, inverse):
    return inverse * (grad_norm - normed * jnp.mean(grad_norm * normed, axis=-1, keepdims=True))


def rope_tables(count, head_size):
    half_size = head_size // 2
    freqs = rope_base ** (-2.0 * jnp.arange(half_size, dtype=f32) / head_size)
    angles = jnp.arange(count, dtype=f32)[:, None] * freqs[None, :]
    cosine_lookup = jnp.concatenate([jnp.cos(angles), jnp.cos(angles)], axis=1)
    sine_lookup = jnp.concatenate([jnp.sin(angles), jnp.sin(angles)], axis=1)
    return (cosine_lookup, sine_lookup)


def apply_rotation(value_rows, cosine_lookup, sine_lookup):
    half_size = value_rows.shape[-1] // 2
    turned = jnp.concatenate([-value_rows[..., half_size:], value_rows[..., :half_size]], axis=-1)
    return value_rows * cosine_lookup[:, None, :] + turned * sine_lookup[:, None, :]


def rotate_back(grads, cosine_lookup, sine_lookup):
    half_size = grads.shape[-1] // 2
    scaled = grads * sine_lookup[:, None, :]
    turned = jnp.concatenate([scaled[..., half_size:], -scaled[..., :half_size]], axis=-1)
    return grads * cosine_lookup[:, None, :] + turned


def bits_of(count):
    return count.bit_length() - 1


def gather_orders(count):
    bits = bits_of(count)
    up = list(range(1, bits)) + [0]
    down = list(range(bits - 1, 0, -1)) + [0]
    return (up, down)


def spans(bits):
    masks = [0]
    for bit in bits:
        masks = masks + [m | (1 << bit) for m in masks]
    return masks


def meet(peers):
    barrier = pltpu.get_barrier_semaphore()
    for peer in peers:
        pl.semaphore_signal(barrier, inc=1, device_id=peer, device_id_type=MESH)
    pl.semaphore_wait(barrier, len(peers))


def token_gather_kernel(count, x_ref, out_ref, send_sem, recv_sem, local_sem):
    rep, me = lax.axis_index("rep"), lax.axis_index("ep")
    bits = bits_of(count)
    half = x_ref.shape[0] // 2
    meet([(rep, me ^ (1 << b)) for b in range(bits)])
    local = pltpu.make_async_copy(x_ref, out_ref.at[me], local_sem)
    local.start()
    orders = gather_orders(count)
    copies = []

    def send(h, mask, bit):
        rows = pl.ds(h * half, half)
        source = x_ref.at[rows] if mask == 0 else out_ref.at[me ^ mask, rows]
        there = mask | (1 << bit)
        copy = pltpu.make_async_remote_copy(
            src_ref=source,
            dst_ref=out_ref.at[me ^ mask, rows],
            send_sem=send_sem.at[h, there],
            recv_sem=recv_sem.at[h, there],
            device_id=(rep, me ^ (1 << bit)),
            device_id_type=MESH,
        )
        copy.start()
        copies.append(copy)

    def arrived(h, mask):
        rows = pl.ds(h * half, half)
        pltpu.make_async_copy(
            x_ref.at[rows], out_ref.at[me ^ mask, rows], recv_sem.at[h, mask]
        ).wait()

    for stage in range(bits):
        for h in range(2):
            send(h, 0, orders[h][stage])
    for stage in range(bits):
        for low in spans(orders[0][:stage]):
            index = spans(orders[0][:stage]).index(low)
            for h in range(2):
                mask = spans(orders[h][:stage])[index] | (1 << orders[h][stage])
                arrived(h, mask)
                for later in range(stage + 1, bits):
                    send(h, mask, orders[h][later])
    for copy in copies:
        copy.wait_send()
    local.wait()


def gather_tokens(x, count, collective_id):
    return pl.pallas_call(
        functools.partial(token_gather_kernel, count),
        out_shape=jax.ShapeDtypeStruct((count,) + x.shape, x.dtype),
        in_specs=[pl.BlockSpec(memory_space=pl.ANY)],
        out_specs=pl.BlockSpec(memory_space=pl.ANY),
        scratch_shapes=[
            pltpu.SemaphoreType.DMA((2, count)),
            pltpu.SemaphoreType.DMA((2, count)),
            pltpu.SemaphoreType.DMA,
        ],
        compiler_params=pltpu.CompilerParams(collective_id=collective_id, has_side_effects=True),
        name="token_gather",
    )(x)


def weight_gather_kernel(n_rep, n_ep, split, x_ref, out_ref, send_sem, recv_sem, local_sem):
    rep, me = lax.axis_index("rep"), lax.axis_index("ep")
    bits = bits_of(n_ep)
    columns = (pl.ds(0, split), pl.ds(split, x_ref.shape[1] - split))
    meet([(rep, me ^ (1 << b)) for b in range(bits)] + [(rep ^ d, me) for d in range(1, n_rep)])
    local = pltpu.make_async_copy(x_ref, out_ref.at[rep, me], local_sem)
    local.start()
    orders = gather_orders(n_ep)
    copies = []

    def block(d, h, mask):
        if d == 0 and mask == 0:
            return x_ref.at[:, columns[h]]
        return out_ref.at[rep ^ d, me ^ mask, :, columns[h]]

    def copy_to(d, h, mask, there_d, there_mask, device):
        copy = pltpu.make_async_remote_copy(
            src_ref=block(d, h, mask),
            dst_ref=out_ref.at[rep ^ d, me ^ mask, :, columns[h]],
            send_sem=send_sem.at[there_d, h, there_mask],
            recv_sem=recv_sem.at[there_d, h, there_mask],
            device_id=device,
            device_id_type=MESH,
        )
        copy.start()
        copies.append(copy)

    def send(d, h, mask, bit):
        copy_to(d, h, mask, d, mask | (1 << bit), (rep, me ^ (1 << bit)))

    def arrived(d, h, mask):
        target = out_ref.at[rep ^ d, me ^ mask, :, columns[h]]
        pltpu.make_async_copy(target, target, recv_sem.at[d, h, mask]).wait()

    def spread(d):
        for stage in range(bits):
            for h in range(2):
                send(d, h, 0, orders[h][stage])

    def relay(d):
        for stage in range(bits):
            for index in range(1 << stage):
                for h in range(2):
                    mask = spans(orders[h][:stage])[index] | (1 << orders[h][stage])
                    arrived(d, h, mask)
                    for later in range(stage + 1, bits):
                        send(d, h, mask, orders[h][later])

    for d in range(1, n_rep):
        for h in range(2):
            copy_to(0, h, 0, d, 0, (rep ^ d, me))
    spread(0)
    for d in range(1, n_rep):
        for h in range(2):
            arrived(d, h, 0)
        spread(d)
        relay(d - 1)
    relay(n_rep - 1)
    for copy in copies:
        copy.wait_send()
    local.wait()


def gather_weights(x, n_rep, n_ep, collective_id):
    split = -(-x.shape[1] // 256) * 128
    return pl.pallas_call(
        functools.partial(weight_gather_kernel, n_rep, n_ep, split),
        out_shape=jax.ShapeDtypeStruct((n_rep, n_ep) + x.shape, x.dtype),
        in_specs=[pl.BlockSpec(memory_space=pl.ANY)],
        out_specs=pl.BlockSpec(memory_space=pl.ANY),
        scratch_shapes=[
            pltpu.SemaphoreType.DMA((n_rep, 2, n_ep)),
            pltpu.SemaphoreType.DMA((n_rep, 2, n_ep)),
            pltpu.SemaphoreType.DMA,
        ],
        compiler_params=pltpu.CompilerParams(collective_id=collective_id, has_side_effects=True),
        name="weight_gather",
    )(x)


class TokenSum:
    def __init__(self, count, y_ref, starts, results, scratch):
        self.bits = bits_of(count)
        self.y_ref, self.results = y_ref, results
        self.own, self.got = scratch[:2], scratch[2:4]
        self.send_sem, self.recv_sem, self.own_sem = scratch[4:7]
        self.rep, self.me = lax.axis_index("rep"), lax.axis_index("ep")
        self.orders = [list(reversed(o)) for o in gather_orders(count)]
        self.columns = [pl.ds(s, o.shape[2]) for s, o in zip(starts, self.own)]
        self.masks = [
            [list(reversed(spans(self.orders[h][k + 1 :]))) for k in range(self.bits)] for h in range(2)
        ]
        self.slots, self.seats = [], []
        for h in range(2):
            table = {}
            for stage in range(self.bits):
                for mask in self.masks[h][stage]:
                    table[(stage, mask)] = len(table)
            self.slots.append(table)
            self.seats.append({mask: i for i, mask in enumerate(self.masks[h][0])})

    @staticmethod
    def scratch(count, rows, widths):
        half = count // 2
        return [
            pltpu.VMEM((half, rows, widths[0]), bf16),
            pltpu.VMEM((half, rows, widths[1]), bf16),
            pltpu.VMEM((count - 1, rows, widths[0]), bf16),
            pltpu.VMEM((count - 1, rows, widths[1]), bf16),
            pltpu.SemaphoreType.DMA((2, count)),
            pltpu.SemaphoreType.DMA((2, count)),
            pltpu.SemaphoreType.DMA((2, half)),
        ]

    def meet(self):
        meet([(self.rep, self.me ^ (1 << b)) for b in range(self.bits)])

    def copy(self, h, stage, mask):
        bit = 1 << self.orders[h][stage]
        slot = self.slots[h][(stage, mask)]
        if stage == 0:
            source = self.y_ref.at[self.me ^ bit ^ mask, :, self.columns[h]]
        else:
            source = self.own[h].at[self.seats[h][bit | mask]]
        return pltpu.make_async_remote_copy(
            src_ref=source,
            dst_ref=self.got[h].at[slot],
            send_sem=self.send_sem.at[h, slot],
            recv_sem=self.recv_sem.at[h, slot],
            device_id=(self.rep, self.me ^ bit),
            device_id_type=MESH,
        )

    def load(self, h, mask):
        seat = self.seats[h][mask]
        return pltpu.make_async_copy(
            self.y_ref.at[self.me ^ mask, :, self.columns[h]], self.own[h].at[seat], self.own_sem.at[h, seat]
        )

    def begin(self):
        for i in range(len(self.masks[0][0])):
            for h in range(2):
                self.copy(h, 0, self.masks[h][0][i]).start()
                self.load(h, self.masks[h][0][i]).start()

    def add(self, h, stage, mask):
        slot, seat = self.slots[h][(stage, mask)], self.seats[h][mask]
        own, got = self.own[h], self.got[h]
        if stage == 0:
            self.load(h, mask).wait()
        self.copy(h, stage, mask).wait_recv()
        step = 32

        def body(i, carry):
            rows = pl.ds(pl.multiple_of(i * step, step), step)
            total = own[seat, rows, :].astype(f32) + got[slot, rows, :].astype(f32)
            if stage == self.bits - 1:
                self.results[h][rows, :] = total
            else:
                own[seat, rows, :] = total.astype(bf16)
            return carry

        lax.fori_loop(0, own.shape[1] // step, body, 0)

    def stage(self, stage):
        for i in range(len(self.masks[0][stage])):
            for h in range(2):
                mask = self.masks[h][stage][i]
                self.add(h, stage, mask)
                if stage + 1 < self.bits:
                    following = 1 << self.orders[h][stage + 1]
                    if mask & following:
                        self.copy(h, stage + 1, mask & ~following).start()

    def end(self):
        for h in range(2):
            for stage, mask in self.slots[h]:
                self.copy(h, stage, mask).wait_send()


def token_sum_kernel(count, starts, y_ref, first_ref, second_ref, *scratch):
    total = TokenSum(count, y_ref, starts, (first_ref, second_ref), scratch)
    total.meet()
    total.begin()
    for stage in range(total.bits):
        total.stage(stage)
    total.end()


def sum_tokens(y, count, starts, widths, collective_id):
    rows = y.shape[1]
    return pl.pallas_call(
        functools.partial(token_sum_kernel, count, starts),
        out_shape=tuple(jax.ShapeDtypeStruct((rows, w), f32) for w in widths),
        in_specs=[pl.BlockSpec(memory_space=pl.ANY)],
        out_specs=(pl.BlockSpec(memory_space=pltpu.VMEM),) * 2,
        scratch_shapes=TokenSum.scratch(count, rows, widths),
        compiler_params=pltpu.CompilerParams(
            collective_id=collective_id, has_side_effects=True, vmem_limit_bytes=VMEM_BYTES
        ),
        cost_estimate=pl.CostEstimate(flops=1000, bytes_accessed=1000, transcendentals=0),
        name="token_sum",
    )(y)


QUAD = 4


def attention_back_kernel(count, starts, heads_kv, groups, scale, *refs):
    (length_ref, proj_ref, gains_ref, cos_ref, sin_ref, mid_ref, wo_ref, y_ref) = refs[:8]
    right_ref, head_ref, first_ref, second_ref = refs[8:12]
    wo_buf, wo_sem, k_low, v_low, k_norm, dk_sum, dv_sum = refs[12:19]
    total = TokenSum(count, y_ref, starts, (first_ref, second_ref), refs[19:])
    size = gains_ref.shape[1]
    tokens = proj_ref.shape[0]
    heads_q = heads_kv * groups
    wide_q, wide_kv = heads_q * size, heads_kv * size
    per_group = groups // QUAD
    turns = heads_q // QUAD

    def wo_copy(i):
        rows = pl.ds(pl.multiple_of(i * QUAD * size, QUAD * size), QUAD * size)
        return pltpu.make_async_copy(wo_ref.at[rows], wo_buf.at[i % 2], wo_sem.at[i % 2])

    wo_copy(0).start()
    total.meet()
    total.begin()
    head_ref[...] = jnp.zeros_like(head_ref)
    sent = right_ref.shape[1] - wide_q - 2 * wide_kv
    for n in range(sent // mid_ref.shape[1]):
        start = wide_q + 2 * wide_kv + n * mid_ref.shape[1]
        right_ref[:, start : start + mid_ref.shape[1]] = mid_ref[...]

    def rotate(value):
        return value * cos_ref[...] + pltpu.roll(value, size // 2, 1) * sin_ref[...]

    def rotate_back(value):
        return value * cos_ref[...] - pltpu.roll(value, size // 2, 1) * sin_ref[...]

    def norm_parts(value):
        inverse = lax.rsqrt(jnp.mean(value * value, axis=-1, keepdims=True) + eps)
        return value * inverse, inverse

    def project_back(gradient, normed, inverse, row):
        scaled = rotate_back(gradient)
        head_ref[row : row + 1, :] += jnp.sum(scaled * normed, axis=0, keepdims=True)
        lifted = scaled * gains_ref[row : row + 1, :]
        mean = jnp.mean(lifted * normed, axis=-1, keepdims=True)
        return (inverse * (lifted - normed * mean)).astype(bf16)

    key_pos = lax.broadcasted_iota(jnp.int32, (tokens, tokens), 0)
    query_pos = lax.broadcasted_iota(jnp.int32, (tokens, tokens), 1)
    allowed = (key_pos <= query_pos) & (key_pos < length_ref[0])

    def lanes(start):
        return pl.ds(pl.multiple_of(start, size), size)

    def turn(i, carry):
        group = i // per_group
        for stage, when in ((0, min(1, turns - 1)), (1, turns - 2)):

            @pl.when(i == when)
            def _(stage=stage):
                if stage < total.bits - 1:
                    total.stage(stage)

        @pl.when(i % per_group == 0)
        def _():
            normed, inverse = norm_parts(proj_ref[:, lanes(wide_q + group * size)])
            k_norm[:, :size] = normed
            k_norm[:, size:] = jnp.broadcast_to(inverse, normed.shape)
            k_low[...] = rotate(normed * gains_ref[1:2, :]).astype(bf16)
            v_low[...] = proj_ref[:, lanes(wide_q + wide_kv + group * size)].astype(bf16)
            dk_sum[...] = jnp.zeros_like(dk_sum)
            dv_sum[...] = jnp.zeros_like(dv_sum)

        @pl.when(i + 1 < turns)
        def _():
            wo_copy(i + 1).start()

        wo_copy(i).wait()
        d_att = lax.dot_general(mid_ref[...], wo_buf[i % 2], NT, preferred_element_type=f32).astype(bf16)
        keys, values = k_low[...], v_low[...]
        dk, dv = dk_sum[...], dv_sum[...]
        for n in range(QUAD):
            head = i * QUAD + n
            d_out = d_att[:, n * size : (n + 1) * size]
            normed, inverse = norm_parts(proj_ref[:, lanes(head * size)])
            query = rotate(normed * gains_ref[0:1, :]).astype(bf16)
            scores = lax.dot_general(keys, query, NT, preferred_element_type=f32) * scale
            scores = jnp.where(allowed, scores, -1e30)
            raised = jnp.exp(scores - jnp.max(scores, axis=0, keepdims=True))
            probs = raised * (1.0 / jnp.sum(raised, axis=0, keepdims=True))
            dv += jnp.dot(probs.astype(bf16), d_out, preferred_element_type=f32)
            d_probs = lax.dot_general(values, d_out, NT, preferred_element_type=f32)
            weighted = probs * d_probs
            d_scores = (weighted - probs * jnp.sum(weighted, axis=0, keepdims=True)).astype(bf16)
            dk += jnp.dot(d_scores, query, preferred_element_type=f32)
            d_query = lax.dot_general(d_scores, keys, TN, preferred_element_type=f32) * scale
            right_ref[:, lanes(head * size)] = project_back(d_query, normed, inverse, 0)
        dk_sum[...] = dk
        dv_sum[...] = dv

        @pl.when(i % per_group == per_group - 1)
        def _():
            right_ref[:, lanes(wide_q + group * size)] = project_back(
                dk_sum[...] * scale, k_norm[:, :size], k_norm[:, size:], 1
            )
            right_ref[:, lanes(wide_q + wide_kv + group * size)] = dv_sum[...].astype(bf16)

        return carry

    lax.fori_loop(0, turns, turn, 0)
    for stage in range(min(2, total.bits - 1), total.bits):
        total.stage(stage)
    total.end()


def attention_back(length, proj, gains, cos, sin, d_mid, mat_o, y, count, starts, widths, heads_kv, groups, collective_id):
    tokens, width = d_mid.shape
    size = gains.shape[1]
    vmem = pl.BlockSpec(memory_space=pltpu.VMEM)
    anywhere = pl.BlockSpec(memory_space=pl.ANY)
    columns = (heads_kv * groups + 2 * heads_kv) * size + 2 * width
    return pl.pallas_call(
        functools.partial(attention_back_kernel, count, starts, heads_kv, groups, size ** (-0.5)),
        out_shape=(
            jax.ShapeDtypeStruct((tokens, columns), bf16),
            jax.ShapeDtypeStruct((8, size), f32),
        )
        + tuple(jax.ShapeDtypeStruct((tokens, w), f32) for w in widths),
        in_specs=[pl.BlockSpec(memory_space=pltpu.SMEM)] + [vmem] * 5 + [anywhere] * 2,
        out_specs=(vmem,) * 4,
        scratch_shapes=[
            pltpu.VMEM((2, QUAD * size, width), bf16),
            pltpu.SemaphoreType.DMA((2,)),
            pltpu.VMEM((tokens, size), bf16),
            pltpu.VMEM((tokens, size), bf16),
            pltpu.VMEM((tokens, 2 * size), f32),
            pltpu.VMEM((tokens, size), f32),
            pltpu.VMEM((tokens, size), f32),
        ]
        + TokenSum.scratch(count, tokens, widths),
        compiler_params=pltpu.CompilerParams(
            collective_id=collective_id, has_side_effects=True, vmem_limit_bytes=VMEM_BYTES
        ),
        cost_estimate=pl.CostEstimate(flops=1000, bytes_accessed=1000, transcendentals=0),
        name="attention_back",
    )(length, proj, gains, cos, sin, d_mid, mat_o, y)


def dense_sum_kernel(n_rep, n_ep, rows, chunks, split, *refs):
    left_ref, right_ref, small_ref, head_ref, out_ref, head_out = refs[:6]
    rest = list(refs[6:])
    bits = bits_of(n_ep)
    wide = right_ref.shape[1] // (chunks - 1)
    half = wide // 2
    rep, me = lax.axis_index("rep"), lax.axis_index("ep")
    mine = [lax.rem(lax.div(me, 1 << b), 2) for b in range(bits)]
    part, got_core = rest[:2]
    acc = [None] + [rest[2 + 2 * k : 4 + 2 * k] for k in range(bits)]
    rest = rest[2 + 2 * bits :]
    got = [None] + [rest[2 * k : 2 * k + 2] for k in range(bits)]
    rest = rest[2 * bits :]
    head_own, head_got, head_rep = rest[:3]
    core_send, core_recv, step_send, step_recv, rep_send, rep_recv, head_send, head_recv, head_rs, head_rr = rest[3:]
    up = list(range(1, bits))
    orders = (up, up[::-1])
    left = [[sorted(set(up) - set(o[:k])) for k in range(bits)] for o in orders]
    lags = [0, 1]
    for _ in range(bits):
        lags.append(lags[-1] + 2)
    deep = 4
    others = [lax.rem(rep + d, n_rep) for d in range(1, n_rep)]
    meet([(rep, me ^ (1 << b)) for b in range(bits)] + [(other, me) for other in others])

    def core_copy(c):
        slot = lax.rem(c, 2)
        return pltpu.make_async_remote_copy(
            src_ref=part.at[slot, 1 - mine[0]],
            dst_ref=got_core.at[slot],
            send_sem=core_send.at[slot],
            recv_sem=core_recv.at[slot],
            device_id=(rep, me ^ 1),
            device_id_type=MESH,
        )

    def bit_copy(k, h, c):
        slot = lax.rem(c, deep)
        bit = orders[h][k - 1]
        place = left[h][k - 1].index(bit)
        return pltpu.make_async_remote_copy(
            src_ref=acc[k][h].at[(slot,) + (slice(None),) * place + (1 - mine[bit],)],
            dst_ref=got[k][h].at[slot],
            send_sem=step_send.at[k, h, slot],
            recv_sem=step_recv.at[k, h, slot],
            device_id=(rep, me ^ (1 << bit)),
            device_id_type=MESH,
        )

    def rep_copy(h, c, d):
        slot = lax.rem(c, deep)
        return pltpu.make_async_remote_copy(
            src_ref=acc[bits][h].at[slot, others[d]],
            dst_ref=got[bits][h].at[slot, n_rep - 2 - d],
            send_sem=rep_send.at[h, slot, d],
            recv_sem=rep_recv.at[h, slot, n_rep - 2 - d],
            device_id=(others[d], me),
            device_id_type=MESH,
        )

    corners = [()]
    for _ in up:
        corners = [c + (v,) for c in corners for v in range(2)]
    block = n_rep * rows
    side_rows = len(corners) * block

    def stage_make(c):
        slot = lax.rem(c, 2)

        @pl.when(c >= 2)
        def _():
            core_copy(c - 2).wait_send()

        @pl.when(c < chunks - 1)
        def _():
            which = jnp.where(c >= split[0], 1, 0) + jnp.where(c >= split[1], 1, 0)
            columns = pl.ds(pl.multiple_of(c * wide, wide), wide)
            weights = right_ref[:, columns]
            for side in (1, 0):
                which_side = 1 - mine[0] if side else mine[0]
                for n, corner in enumerate(corners):
                    start = (which * 2 + which_side) * side_rows + n * block
                    value = jnp.dot(
                        left_ref[pl.ds(pl.multiple_of(start, block), block), :],
                        weights,
                        preferred_element_type=f32,
                    )
                    part[(slot, which_side) + corner] = value.astype(bf16).reshape(n_rep, rows, wide)

        @pl.when(c == chunks - 1)
        def _():
            thin = small_ref.shape[1]
            for side in range(2):
                for n, corner in enumerate(corners):
                    value = small_ref[pl.ds(side * side_rows + n * block, block), :].reshape(n_rep, rows, thin)
                    blank = jnp.zeros((n_rep, rows, wide - thin), bf16)
                    part[(slot, side) + corner + (slice(None), slice(None), slice(0, thin))] = value
                    part[(slot, side) + corner + (slice(None), slice(None), slice(thin, wide))] = blank

        core_copy(c).start()

    def stage_core(c):
        slot, put = lax.rem(c, 2), lax.rem(c, deep)

        @pl.when(c >= deep)
        def _():
            for h in range(2):
                if bits > 1:
                    bit_copy(1, h, c - deep).wait_send()

        core_copy(c).wait_recv()
        for corner in corners:
            total = part[(slot, mine[0]) + corner].astype(f32) + got_core[(slot,) + corner].astype(f32)
            total = total.astype(bf16)
            for h in range(2):
                acc[1][h][(put,) + corner] = total[:, :, h * half : (h + 1) * half]
        for h in range(2):
            bit_copy(1, h, c).start()

    def stage_bit(k, c):
        slot = lax.rem(c, deep)
        for h in range(2):
            bit = orders[h][k - 2]
            place = left[h][k - 2].index(bit)

            @pl.when(c >= deep)
            def _(h=h):
                if k < bits:
                    bit_copy(k, h, c - deep).wait_send()
                else:
                    for d in range(n_rep - 1):
                        rep_copy(h, c - deep, d).wait_send()

            bit_copy(k - 1, h, c).wait_recv()
            small_corners = [()]
            for _ in left[h][k - 1]:
                small_corners = [q + (v,) for q in small_corners for v in range(2)]
            for corner in small_corners:
                full = corner[:place] + (mine[bit],) + corner[place:]
                total = acc[k - 1][h][(slot,) + full].astype(f32) + got[k - 1][h][(slot,) + corner].astype(f32)
                acc[k][h][(slot,) + corner] = total.astype(bf16)
            if k < bits:
                bit_copy(k, h, c).start()
            else:
                for d in range(n_rep - 1):
                    rep_copy(h, c, d).start()

    def stage_end(c):
        slot = lax.rem(c, deep)
        for h in range(2):
            total = acc[bits][h][slot, rep].astype(f32)
            for d in range(n_rep - 1):
                rep_copy(h, c, d).wait_recv()
            for d in range(n_rep - 1):
                total += got[bits][h][slot, d].astype(f32)
            out_ref[:, pl.ds(pl.multiple_of(c * wide + h * half, half), half)] = total

    def head_copy(t):
        return pltpu.make_async_remote_copy(
            src_ref=head_own.at[t],
            dst_ref=head_got.at[t],
            send_sem=head_send.at[t],
            recv_sem=head_recv.at[t],
            device_id=(rep, me ^ (1 << t)),
            device_id_type=MESH,
        )

    def head_rep_copy(d):
        return pltpu.make_async_remote_copy(
            src_ref=head_own.at[bits],
            dst_ref=head_rep.at[rep],
            send_sem=head_rs.at[d],
            recv_sem=head_rr.at[n_rep - 2 - d],
            device_id=(others[d], me),
            device_id_type=MESH,
        )

    def head_step(t):
        if t == 0:
            head_own[0] = head_ref[...]
            head_copy(0).start()
        elif t <= bits:
            head_copy(t - 1).wait_recv()
            head_own[t] = head_own[t - 1] + head_got[t - 1]
            if t < bits:
                head_copy(t).start()
            else:
                for d in range(n_rep - 1):
                    head_rep_copy(d).start()
                head_rep[rep] = head_own[bits]
        else:
            for d in range(n_rep - 1):
                head_rep_copy(d).wait_recv()
            total = head_rep[0]
            for r in range(1, n_rep):
                total = total + head_rep[r]
            head_out[...] = total

    def step(i, carry):
        for stage in reversed(range(len(lags))):
            c = i - lags[stage]

            @pl.when((c >= 0) & (c < chunks))
            def _(stage=stage, c=c):
                if stage == 0:
                    stage_make(c)
                elif stage == 1:
                    stage_core(c)
                elif stage <= bits:
                    stage_bit(stage, c)
                else:
                    stage_end(c)

        for t in range(bits + 2):

            @pl.when(i == t)
            def _(t=t):
                head_step(t)

        return carry

    lax.fori_loop(0, chunks + lags[-1], step, 0)
    for c in range(chunks - 2, chunks):
        core_copy(c).wait_send()
    for c in range(chunks - deep, chunks):
        for h in range(2):
            for k in range(1, bits):
                bit_copy(k, h, c).wait_send()
            for d in range(n_rep - 1):
                rep_copy(h, c, d).wait_send()
    for t in range(bits):
        head_copy(t).wait_send()
    for d in range(n_rep - 1):
        head_rep_copy(d).wait_send()


def dense_sum(left, right, small, head, n_rep, n_ep, split, collective_id):
    chunk = 512
    chunks = right.shape[1] // chunk + 1
    bits = bits_of(n_ep)
    rows = left.shape[0] // (3 * n_rep * n_ep)
    deep = 4
    half = chunk // 2
    vmem = pl.BlockSpec(memory_space=pltpu.VMEM)
    inner = (n_rep, rows)
    scratch = [
        pltpu.VMEM((2, 2) + (2,) * (bits - 1) + inner + (chunk,), bf16),
        pltpu.VMEM((2,) + (2,) * (bits - 1) + inner + (chunk,), bf16),
    ]
    for k in range(1, bits + 1):
        scratch += [pltpu.VMEM((deep,) + (2,) * (bits - k) + inner + (half,), bf16)] * 2
    for k in range(1, bits):
        scratch += [pltpu.VMEM((deep,) + (2,) * (bits - 1 - k) + inner + (half,), bf16)] * 2
    scratch += [pltpu.VMEM((deep, n_rep - 1, rows, half), bf16)] * 2
    scratch += [
        pltpu.VMEM((bits + 1,) + head.shape, f32),
        pltpu.VMEM((bits,) + head.shape, f32),
        pltpu.VMEM((n_rep,) + head.shape, f32),
        pltpu.SemaphoreType.DMA((2,)),
        pltpu.SemaphoreType.DMA((2,)),
        pltpu.SemaphoreType.DMA((bits, 2, deep)),
        pltpu.SemaphoreType.DMA((bits, 2, deep)),
        pltpu.SemaphoreType.DMA((2, deep, n_rep - 1)),
        pltpu.SemaphoreType.DMA((2, deep, n_rep - 1)),
        pltpu.SemaphoreType.DMA((bits,)),
        pltpu.SemaphoreType.DMA((bits,)),
        pltpu.SemaphoreType.DMA((n_rep - 1,)),
        pltpu.SemaphoreType.DMA((n_rep - 1,)),
    ]
    return pl.pallas_call(
        functools.partial(dense_sum_kernel, n_rep, n_ep, rows, chunks, split),
        out_shape=(
            jax.ShapeDtypeStruct((rows, chunks * chunk), f32),
            jax.ShapeDtypeStruct(head.shape, f32),
        ),
        in_specs=[vmem] * 4,
        out_specs=(vmem, vmem),
        scratch_shapes=scratch,
        compiler_params=pltpu.CompilerParams(
            collective_id=collective_id, has_side_effects=True, vmem_limit_bytes=VMEM_BYTES
        ),
        cost_estimate=pl.CostEstimate(flops=1000, bytes_accessed=1000, transcendentals=0),
        name="dense_sum",
    )(left, right, small, head)


def expert_kernel(first, last, experts, width, hidden_of, *refs):
    (info, h_ref, g_ref, wg_ref, wu_ref, wd_ref) = refs[:6]
    rest = list(refs[6:])
    prev_ref = None if first else rest.pop(0)
    y_ref, grad_ref = rest[:2]
    xs, gs, ds, hs, stage, prev_buf, wide, tall, in_sem, out_sem, prev_sem, grad_sem = rest[2:]
    shares = grad_ref.shape[0]
    wide_share, tall_share = width // shares, hidden_of // shares
    hidden = wg_ref.shape[1]
    units = info[0]
    expert = info[1]
    table = 8
    per_tile = TILE // UNIT
    tiles = (units + per_tile - 1) // per_tile
    most = xs.shape[0] // TILE
    floor_tiles = min(4, most)

    def unit_in(u, slot):
        source = pl.ds(pl.multiple_of(info[table + u], UNIT), UNIT)
        target = pl.ds(pl.multiple_of(u * UNIT, UNIT), UNIT)
        return (
            pltpu.make_async_copy(h_ref.at[source], xs.at[target], in_sem.at[0, slot]),
            pltpu.make_async_copy(g_ref.at[source], gs.at[target], in_sem.at[1, slot]),
        )

    def begin(u, carry):
        for copy in unit_in(u, u // per_tile):
            copy.start()
        return carry

    lax.fori_loop(0, units, begin, 0)

    def blank(u, carry):
        target = pl.ds(pl.multiple_of(u * UNIT, UNIT), UNIT)
        xs[target, :] = jnp.zeros((UNIT, xs.shape[1]), bf16)
        gs[target, :] = jnp.zeros((UNIT, gs.shape[1]), bf16)
        return carry

    lax.fori_loop(units, jnp.maximum(tiles, floor_tiles) * per_tile, blank, 0)

    def blank_tile(i, carry):
        target = pl.ds(pl.multiple_of(i * TILE, TILE), TILE)
        ds[target, :] = jnp.zeros((TILE, ds.shape[1]), bf16)
        hs[target, :] = jnp.zeros((TILE, hs.shape[1]), bf16)
        return carry

    lax.fori_loop(tiles, floor_tiles, blank_tile, 0)

    def prev_copy(i):
        rows = pl.ds(pl.multiple_of(i * TILE, TILE), TILE)
        return pltpu.make_async_copy(prev_ref.at[rows], prev_buf.at[i % 2], prev_sem.at[i % 2])

    if not first:
        prev_copy(0).start()

    def unit_out(u):
        target = pl.ds(pl.multiple_of(info[table + u], UNIT), UNIT)
        tile = u // per_tile
        source = pl.ds(pl.multiple_of((u % per_tile) * UNIT, UNIT), UNIT)
        return pltpu.make_async_copy(stage.at[tile % 2, source], y_ref.at[target], out_sem.at[tile % 2])

    def out_start(i):
        if last:
            lax.fori_loop(
                i * per_tile,
                jnp.minimum((i + 1) * per_tile, units),
                lambda u, c: (unit_out(u).start(), c)[1],
                0,
            )
        else:
            rows = pl.ds(pl.multiple_of(i * TILE, TILE), TILE)
            pltpu.make_async_copy(stage.at[i % 2], y_ref.at[rows], out_sem.at[i % 2]).start()

    def out_wait(i):
        if last:
            lax.fori_loop(
                i * per_tile,
                jnp.minimum((i + 1) * per_tile, units),
                lambda u, c: (unit_out(u).wait(), c)[1],
                0,
            )
        else:
            rows = pl.ds(pl.multiple_of(i * TILE, TILE), TILE)
            pltpu.make_async_copy(stage.at[i % 2], y_ref.at[rows], out_sem.at[i % 2]).wait()

    lane = lax.broadcasted_iota(jnp.int32, (TILE, EXT), 1)
    weight_lanes = (lane == expert) | (lane == expert + experts) | (lane == expert + 2 * experts)

    def tile_step(i, carry):
        def landed(u, c):
            for copy in unit_in(u, i):
                copy.wait()
            return c

        lax.fori_loop(i * per_tile, jnp.minimum((i + 1) * per_tile, units), landed, 0)
        rows = pl.ds(pl.multiple_of(i * TILE, TILE), TILE)
        x = xs[rows, :width]
        g = gs[rows, :]
        extra = xs[rows, width:].astype(f32)
        weight = jnp.sum(jnp.where(weight_lanes, extra, 0.0), axis=1, keepdims=True)
        gate = jnp.dot(x, wg_ref[...], preferred_element_type=f32)
        up = jnp.dot(x, wu_ref[...], preferred_element_type=f32)
        d_plain = lax.dot_general(g, wd_ref[...], NT, preferred_element_type=f32)
        sig = 1.0 / (1.0 + jnp.exp(-gate))
        silu = gate * sig
        hid = silu * up
        d_weight = jnp.sum(hid.astype(bf16).astype(f32) * d_plain, axis=1, keepdims=True)
        hs[rows, :] = (hid * weight).astype(bf16)
        d_hidden = d_plain * weight
        ds[rows, :hidden] = (d_hidden * up * sig * (1.0 + gate * (1.0 - sig))).astype(bf16)
        ds[rows, hidden:] = (d_hidden * silu).astype(bf16)

        @pl.when(i >= 2)
        def _():
            out_wait(i - 2)

        if not first:

            @pl.when(i + 1 < tiles)
            def _():
                prev_copy(i + 1).start()

            prev_copy(i).wait()
        slot = i % 2
        high = d_weight.astype(bf16).astype(f32)
        low = d_weight - high
        note = jnp.where(lane == expert, high, 0.0) + jnp.where(lane == expert + experts, low, 0.0)
        d_row = lax.dot_general(ds[rows, :hidden], wg_ref[...], NT, preferred_element_type=f32)
        d_row += lax.dot_general(ds[rows, hidden:], wu_ref[...], NT, preferred_element_type=f32)
        if not first:
            d_row += prev_buf[slot, :, :width].astype(f32)
            note += prev_buf[slot, :, width : width + EXT].astype(f32)
        stage[slot, :, :width] = d_row.astype(bf16)
        stage[slot, :, width : width + EXT] = note.astype(bf16)
        out = jnp.dot(hs[rows, :], wd_ref[...], preferred_element_type=f32)
        if not first:
            out += prev_buf[slot, :, width + EXT :].astype(f32)
        stage[slot, :, width + EXT :] = out.astype(bf16)
        out_start(i)
        return carry

    lax.fori_loop(0, tiles, tile_step, 0)

    block = 256

    def grads(depth):
        def wide_copies(m):
            per = wide_share // block
            return tuple(
                pltpu.make_async_copy(
                    wide.at[m % 2, :, p * LANES : (p + 1) * LANES],
                    grad_ref.at[
                        m // per,
                        pl.ds(pl.multiple_of(p * wide_share + (m % per) * block, block), block),
                    ],
                    grad_sem.at[m % 2, p],
                )
                for p in range(2 * hidden // LANES)
            )

        def wide_step(m, carry):
            @pl.when(m >= 2)
            def _():
                for copy in wide_copies(m - 2):
                    copy.wait()

            columns = pl.ds(pl.multiple_of(m * block, block), block)
            wide[m % 2] = lax.dot_general(
                xs[:depth, columns], ds[:depth, :], TN, preferred_element_type=f32
            ).astype(bf16)
            for copy in wide_copies(m):
                copy.start()
            return carry

        count = width // block
        lax.fori_loop(0, count, wide_step, 0)
        for m in range(count - 2, count):
            for copy in wide_copies(m):
                copy.wait()

        piece = math.gcd(block, tall_share)
        base = 2 * hidden // LANES * wide_share

        def tall_copies(m):
            made = []
            for q in range(block // piece):
                first_row = m * block + q * piece
                share, inside = first_row // tall_share, first_row % tall_share
                for p in range(width // LANES):
                    rows = pl.ds(pl.multiple_of(base + p * tall_share + inside, piece), piece)
                    made.append(
                        pltpu.make_async_copy(
                            tall.at[m % 2, q * piece : (q + 1) * piece, p * LANES : (p + 1) * LANES],
                            grad_ref.at[share, rows],
                            grad_sem.at[m % 2, q * (width // LANES) + p],
                        )
                    )
            return made

        def tall_step(m, carry):
            @pl.when(m >= 2)
            def _():
                for copy in tall_copies(m - 2):
                    copy.wait()

            columns = pl.ds(pl.multiple_of(m * block, block), block)
            tall[m % 2] = lax.dot_general(
                hs[:depth, columns], gs[:depth, :], TN, preferred_element_type=f32
            ).astype(bf16)
            for copy in tall_copies(m):
                copy.start()
            return carry

        count = hidden // block
        lax.fori_loop(0, count, tall_step, 0)
        for m in range(count - 2, count):
            for copy in tall_copies(m):
                copy.wait()

    for choice in range(floor_tiles, most + 1):
        chosen = (tiles <= choice) if choice == floor_tiles else (tiles == choice)

        @pl.when(chosen)
        def _(choice=choice):
            grads(choice * TILE)

    @pl.when(tiles >= 2)
    def _():
        out_wait(tiles - 2)

    out_wait(tiles - 1)


def expert_pass(info, h_rows, g_rows, w_gate, w_up, w_down, prev, last, experts, shares):
    tokens, width = g_rows.shape
    hidden = w_gate.shape[1]
    wide_row = width + EXT + width
    any_spec = pl.BlockSpec(memory_space=pl.ANY)
    vmem_spec = pl.BlockSpec(memory_space=pltpu.VMEM)
    first = prev is None
    operands = [info, h_rows, g_rows, w_gate, w_up, w_down] + ([] if first else [prev])
    specs = [pl.BlockSpec(memory_space=pltpu.SMEM), any_spec, any_spec, vmem_spec, vmem_spec, vmem_spec]
    specs += [] if first else [any_spec]
    return pl.pallas_call(
        functools.partial(expert_kernel, first, last, experts, width, hidden),
        out_shape=(
            jax.ShapeDtypeStruct((tokens, wide_row), bf16),
            jax.ShapeDtypeStruct((shares, 3 * hidden * width // shares // LANES, LANES), bf16),
        ),
        in_specs=specs,
        out_specs=(any_spec,) * 2,
        scratch_shapes=[
            pltpu.VMEM((tokens, width + EXT), bf16),
            pltpu.VMEM((tokens, width), bf16),
            pltpu.VMEM((tokens, 2 * hidden), bf16),
            pltpu.VMEM((tokens, hidden), bf16),
            pltpu.VMEM((2, TILE, wide_row), bf16),
            pltpu.VMEM((2, TILE, wide_row), bf16),
            pltpu.VMEM((2, 256, 2 * hidden), bf16),
            pltpu.VMEM((2, 256, width), bf16),
            pltpu.SemaphoreType.DMA((2, tokens // TILE)),
            pltpu.SemaphoreType.DMA((2,)),
            pltpu.SemaphoreType.DMA((2,)),
            pltpu.SemaphoreType.DMA((2, max(2 * hidden // LANES, 256 // math.gcd(256, hidden // shares) * width // LANES))),
        ],
        compiler_params=pltpu.CompilerParams(vmem_limit_bytes=VMEM_BYTES),
        cost_estimate=pl.CostEstimate(flops=1000, bytes_accessed=1000, transcendentals=0),
        name="experts",
    )(*operands)


def unit_table(lengths):
    per_sequence = TILE // UNIT
    counts = (lengths + UNIT - 1) // UNIT
    unit = jnp.arange(lengths.shape[0] * per_sequence, dtype=jnp.int32)
    live = (unit % per_sequence) < jnp.repeat(counts, per_sequence)
    place = jnp.cumsum(live.astype(jnp.int32)) - 1
    hit = (place[None, :] == unit[:, None]) & live[None, :]
    rows = jnp.sum(jnp.where(hit, unit[None, :] * UNIT, 0), axis=1)
    return (jnp.sum(counts), rows)


def split_three(value):
    high = lax.reduce_precision(value, 8, 7)
    rest = value - high
    middle = lax.reduce_precision(rest, 8, 7)
    return jnp.concatenate([high, middle, rest - middle], axis=-1)


def per_device(
    hidden_in,
    out_grad,
    attn_gain,
    w_q,
    key_weight,
    value_weight,
    w_o,
    ffn_gain,
    router_w,
    qk_gains,
    w_gate,
    w_up,
    w_down,
    lengths,
    routes,
    order,
):
    everywhere = ("rep", "ep")
    rep_count, ep_count = (lax.axis_size("rep"), lax.axis_size("ep"))
    rep_index, ep_index = (lax.axis_index("rep"), lax.axis_index("ep"))
    inputs = hidden_in[0].astype(f32)
    sequence_length, model_width = inputs.shape
    head_size = qk_gains.shape[1]
    wide_q, wide_kv = (w_q.shape[1], key_weight.shape[1])
    heads_q, heads_kv = (wide_q // head_size, wide_kv // head_size)
    groups = heads_q // heads_kv
    local_experts = w_gate.shape[0]
    experts = local_experts * ep_count
    top_count = routes.shape[2]
    score_scale = head_size ** (-0.5)
    group_lengths = lax.dynamic_slice_in_dim(lengths, rep_index * ep_count, ep_count)
    length = lax.dynamic_index_in_dim(group_lengths, ep_index, keepdims=False)
    positions = jnp.arange(sequence_length, dtype=jnp.int32)
    live = positions < length
    live_rows = live.astype(f32)

    expert_iota = jnp.arange(experts, dtype=jnp.int32)
    route_hot = routes[0][..., None] == expert_iota
    routed = jnp.any(route_hot, axis=1) & live[:, None]
    order_of = jnp.sum(
        jnp.where(route_hot, order[0].reshape(sequence_length, top_count)[..., None], 0), axis=1
    )
    sort_key = jnp.where(routed, order_of, sequence_length * top_count)
    loads = jnp.sum(routed.astype(jnp.int32), axis=0)
    rank = jnp.sum((sort_key[None, :, :] < sort_key[:, None, :]).astype(jnp.int32), axis=1)

    own_rows = w_q.shape[0]
    load_columns = -(-experts // own_rows)
    load_block = jnp.pad(loads, (0, load_columns * own_rows - experts)).reshape(load_columns, own_rows).T
    small = jnp.concatenate(
        [router_w, attn_gain[:, None], ffn_gain[:, None], load_block.astype(bf16)], axis=1
    )
    small = jnp.pad(small, ((0, 0), (0, EXT - small.shape[1])))
    pack = jnp.concatenate([w_q, key_weight, value_weight, small], axis=1)
    mat_qkv = gather_weights(pack, rep_count, ep_count, 4)
    grads_all = lax.all_gather(out_grad[0], "ep", axis=0, tiled=True)
    if ep_count <= 8:
        w_o, mat_qkv, grads_all = lax.optimization_barrier((w_o, mat_qkv, grads_all))
    else:
        w_o, mat_qkv = lax.optimization_barrier((w_o, mat_qkv))
    mat_qkv = mat_qkv.reshape(-1, pack.shape[1])
    mat_o = lax.all_gather(w_o, everywhere, axis=0, tiled=True)

    wide_all = wide_q + 2 * wide_kv
    small_all = mat_qkv[:, wide_all:]
    mat_router = small_all[:, :experts]
    gain_attn = small_all[:, experts].astype(f32)
    gain_ffn = small_all[:, experts + 1].astype(f32)
    loads_all = (
        small_all[:, experts + 2 : experts + 2 + load_columns]
        .reshape(rep_count, ep_count, own_rows, load_columns)
        .transpose(0, 1, 3, 2)
        .reshape(rep_count, ep_count, load_columns * own_rows)[:, :, :experts]
        .astype(jnp.int32)
    )
    group_loads = lax.dynamic_index_in_dim(loads_all, rep_index, keepdims=False)
    earlier = (jnp.arange(ep_count) < ep_index)[:, None]
    load_prefix = jnp.sum(jnp.where(earlier, group_loads, 0), axis=0)
    capacity = 9 * top_count * jnp.sum(group_lengths) // (8 * experts)
    kept = routed & (load_prefix[None, :] + rank < capacity)
    kept_float = kept.astype(f32)

    gain_q = qk_gains[0].astype(f32)
    gain_k = qk_gains[1].astype(f32)
    norm_one, inv_one = rms_parts(inputs)
    hidden_first = (norm_one * gain_attn).astype(bf16)
    projected = jnp.dot(hidden_first, mat_qkv, preferred_element_type=f32)
    query_projected = projected[:, :wide_q].reshape(sequence_length, heads_q, head_size)
    key_projected = projected[:, wide_q : wide_q + wide_kv].reshape(sequence_length, heads_kv, head_size)
    value_rows = (
        projected[:, wide_q + wide_kv : wide_all]
        .astype(bf16)
        .reshape(sequence_length, heads_kv, head_size)
    )
    cosine_lookup, sine_lookup = rope_tables(sequence_length, head_size)
    q_norm, q_inv = rms_parts(query_projected)
    k_norm, k_inv = rms_parts(key_projected)
    query_rows = (
        apply_rotation(q_norm * gain_q, cosine_lookup, sine_lookup)
        .astype(bf16)
        .reshape(sequence_length, heads_kv, groups, head_size)
    )
    keys = apply_rotation(k_norm * gain_k, cosine_lookup, sine_lookup).astype(bf16)
    scores = jnp.einsum("tkgd,ukd->kgtu", query_rows, keys, preferred_element_type=f32) * score_scale
    allowed = (positions[None, :] <= positions[:, None]) & (positions[None, :] < length)
    scores = jnp.where(allowed, scores, -1e30)
    attn_probs = jax.nn.softmax(scores, axis=-1)
    probs_low = attn_probs.astype(bf16)
    attended = (
        jnp.einsum("kgtu,ukd->tkgd", probs_low, value_rows, preferred_element_type=f32)
        .astype(bf16)
        .reshape(sequence_length, heads_q * head_size)
    )
    middle = inputs + jnp.dot(attended, mat_o, preferred_element_type=f32)
    norm_two, inv_two = rms_parts(middle)
    h_two = (norm_two * gain_ffn).astype(bf16)
    logits = jnp.dot(h_two, mat_router, preferred_element_type=f32)
    named = jnp.any(route_hot, axis=1)
    top_logit = jnp.max(jnp.where(named, logits, -jnp.inf), axis=1, keepdims=True)
    raised = jnp.where(named, jnp.exp(jnp.where(named, logits - top_logit, 0.0)), 0.0)
    route_gates = raised / jnp.sum(raised, axis=1, keepdims=True)
    pair_weight = route_gates * kept_float

    extra = split_three(pair_weight).astype(bf16)
    extra = jnp.pad(extra, ((0, 0), (0, EXT - extra.shape[1])))
    sent = jnp.concatenate([h_two, extra], axis=1)
    h_all = gather_tokens(sent, ep_count, 1)

    part = min(ep_count, 8)
    tokens = part * sequence_length
    sums = []
    y_parts = []
    for c in range(ep_count // part):
        live_units, unit_rows = unit_table(group_lengths[c * part : (c + 1) * part])
        h_rows = h_all[c * part : (c + 1) * part].reshape(tokens, model_width + EXT)
        g_rows = grads_all[c * tokens : (c + 1) * tokens]
        prev, found = None, []
        for local in range(local_experts):
            info = jnp.concatenate(
                [
                    jnp.stack([live_units, ep_index * local_experts + local]).astype(jnp.int32),
                    jnp.zeros((6,), jnp.int32),
                    unit_rows,
                ]
            )
            prev, weight_grads = expert_pass(
                info,
                h_rows,
                g_rows,
                w_gate[local],
                w_up[local],
                w_down[local],
                prev,
                local == local_experts - 1,
                experts,
                rep_count,
            )
            found.append(weight_grads)
        y_parts.append(prev.reshape(part, sequence_length, -1))
        sums.append(found)
    y_all = y_parts[0] if len(y_parts) == 1 else jnp.concatenate(y_parts, axis=0)
    hidden_units = w_gate.shape[2]
    wide_share, tall_share = model_width // rep_count, hidden_units // rep_count
    found = []
    for local in range(local_experts):
        total = sums[0][local]
        for more in sums[1:]:
            total = (total.astype(f32) + more[local].astype(f32)).astype(bf16)
        found.append(lax.psum_scatter(total, "rep", scatter_dimension=0, tiled=True))
    found = jnp.concatenate(found, axis=0)

    def unpacked(start, rows, columns):
        blocks = found[:, start : start + rows * (columns // LANES)]
        blocks = blocks.reshape(local_experts, columns // LANES, rows, LANES)
        return blocks.transpose(0, 2, 1, 3).reshape(local_experts, rows, columns).astype(f32)

    wide_rows = wide_share * (hidden_units // LANES)
    expert_sums = (
        unpacked(0, wide_share, hidden_units),
        unpacked(wide_rows, wide_share, hidden_units),
        unpacked(2 * wide_rows, tall_share, model_width),
    )

    half_width = model_width // 2
    row_first, row_second = sum_tokens(
        y_all, ep_count, (0, half_width), (half_width, half_width + EXT), 2
    )
    live_column = live[:, None]
    grad_rows = out_grad[0].astype(f32) * live_rows[:, None]
    notes = row_second[:, half_width : half_width + 2 * experts]
    d_weight = jnp.where(live_column, notes[:, :experts] + notes[:, experts:], 0.0)
    d_gates = d_weight * kept_float
    d_logits = route_gates * (d_gates - jnp.sum(route_gates * d_gates, axis=-1, keepdims=True))

    router_float = mat_router.astype(f32)
    d_h_two = jnp.concatenate([row_first, row_second[:, :half_width]], axis=1)
    d_h_two = jnp.where(live_column, d_h_two, 0.0)
    d_h_two = d_h_two + jnp.dot(d_logits, router_float.T, precision=top_precision)
    grad_router = jnp.dot(h_two.astype(f32).T, d_logits, precision=top_precision)
    grad_ffn = jnp.sum(d_h_two * norm_two, axis=0)
    d_middle = grad_rows + rms_back(d_h_two * gain_ffn, norm_two, inv_two)
    d_middle_low = d_middle.astype(bf16)
    sign = jnp.where(jnp.arange(head_size) < head_size // 2, -1.0, 1.0).astype(f32)
    right, head, out_first, out_second = attention_back(
        length.reshape(1),
        projected,
        qk_gains.astype(f32),
        cosine_lookup,
        sine_lookup * sign[None, :],
        d_middle_low,
        mat_o,
        y_all,
        ep_count,
        (model_width + EXT, model_width + EXT + half_width),
        (half_width, half_width),
        heads_kv,
        groups,
        5,
    )
    moe_output = jnp.where(live_column, jnp.concatenate([out_first, out_second], axis=1), 0.0)
    layer_out = jnp.where(live_column, middle + moe_output, 0.0)
    d_qkv = right[:, :wide_all]
    d_h_one = jnp.einsum("tf,cf->tc", d_qkv, mat_qkv[:, :wide_all], preferred_element_type=f32)
    grad_attn = jnp.sum(d_h_one * norm_one, axis=0)
    grad_input = d_middle + rms_back(d_h_one * gain_attn, norm_one, inv_one)

    small_grads = jnp.concatenate([grad_router, grad_attn[:, None], grad_ffn[:, None]], axis=1)
    small_grads = jnp.pad(small_grads, ((0, 0), (0, EXT - small_grads.shape[1]))).astype(bf16)
    ep_bits = bits_of(ep_count)

    def owner_order(value, parts):
        shape = (rep_count,) + (2,) * ep_bits + (parts, own_rows, value.shape[1])
        axes = (ep_bits + 1,) + tuple(range(ep_bits, 0, -1)) + (0, ep_bits + 2, ep_bits + 3)
        return value.reshape(shape).transpose(axes).reshape(value.shape)

    left = jnp.concatenate([owner_order(hidden_first.T, 1), owner_order(attended.T, 2)], axis=0)
    splits = (wide_all // 512, (wide_all + model_width) // 512)
    sums_all, head_sum = dense_sum(
        left, right, owner_order(small_grads, 1), head, rep_count, ep_count, splits, 3
    )
    sum_o = jnp.concatenate(
        [sums_all[:, wide_all : wide_all + model_width], sums_all[:, wide_all + model_width : wide_all + 2 * model_width]],
        axis=0,
    )
    small_sum = sums_all[:, wide_all + 2 * model_width :]
    return (
        layer_out[None],
        grad_input[None],
        small_sum[:, experts],
        sums_all[:, :wide_q],
        sums_all[:, wide_q : wide_q + wide_kv],
        sums_all[:, wide_q + wide_kv : wide_all],
        sum_o,
        small_sum[:, experts + 1],
        small_sum[:, :experts],
        head_sum[:2],
        expert_sums[0],
        expert_sums[1],
        expert_sums[2],
    )


def solution(mesh):
    both = ("rep", "ep")
    placed = (
        P(both, None, None),
        P(both, None, None),
        P(both),
        P(both, None),
        P(both, None),
        P(both, None),
        P(both, None),
        P(both),
        P(both, None),
        P(),
        P("ep", None, None),
        P("ep", None, None),
        P("ep", None, None),
        P(),
        P(both, None, None),
        P(both, None),
    )
    return jax.shard_map(
        per_device,
        mesh=mesh,
        in_specs=placed,
        out_specs=(
            P(both, None, None),
            P(both, None, None),
            P(both),
            P(both, None),
            P(both, None),
            P(both, None),
            P(both, None),
            P(both),
            P(both, None),
            P(),
            P("ep", "rep", None),
            P("ep", "rep", None),
            P("ep", "rep", None),
        ),
        check_vma=False,
    )
```

```python
import functools
import math

import jax
import jax.numpy as jnp
from jax import lax
from jax.experimental import pallas as pl
from jax.experimental.pallas import tpu as pltpu
from jax.sharding import PartitionSpec as P

eps = 1e-06
rope_base = 1000000.0
top_precision = lax.Precision.HIGHEST
MESH = pl.DeviceIdType.MESH
f32, bf16 = jnp.float32, jnp.bfloat16
EXT = 128
UNIT = 16
LANES = 256
TILE = 256
VMEM_BYTES = 58 * 1024 * 1024
NT = (((1,), (1,)), ((), ()))
TN = (((0,), (0,)), ((), ()))


def rms_parts(value_rows):
    inverse = lax.rsqrt(jnp.mean(value_rows * value_rows, axis=-1, keepdims=True) + eps)
    return (value_rows * inverse, inverse)


def rms_back(grad_norm, normed, inverse):
    return inverse * (grad_norm - normed * jnp.mean(grad_norm * normed, axis=-1, keepdims=True))


def rope_tables(count, head_size):
    half_size = head_size // 2
    freqs = rope_base ** (-2.0 * jnp.arange(half_size, dtype=f32) / head_size)
    angles = jnp.arange(count, dtype=f32)[:, None] * freqs[None, :]
    cosine_lookup = jnp.concatenate([jnp.cos(angles), jnp.cos(angles)], axis=1)
    sine_lookup = jnp.concatenate([jnp.sin(angles), jnp.sin(angles)], axis=1)
    return (cosine_lookup, sine_lookup)


def bits_of(count):
    return count.bit_length() - 1


def gather_orders(count):
    bits = bits_of(count)
    up = list(range(1, bits)) + [0]
    down = list(range(bits - 1, 0, -1)) + [0]
    return (up, down)


def spans(bits):
    masks = [0]
    for bit in bits:
        masks = masks + [m | (1 << bit) for m in masks]
    return masks


def meet(peers):
    barrier = pltpu.get_barrier_semaphore()
    for peer in peers:
        pl.semaphore_signal(barrier, inc=1, device_id=peer, device_id_type=MESH)
    pl.semaphore_wait(barrier, len(peers))


def token_gather_kernel(count, x_ref, out_ref, send_sem, recv_sem, local_sem):
    rep, me = lax.axis_index("rep"), lax.axis_index("ep")
    bits = bits_of(count)
    half = x_ref.shape[0] // 2
    meet([(rep, me ^ (1 << b)) for b in range(bits)])
    local = pltpu.make_async_copy(x_ref, out_ref.at[me], local_sem)
    local.start()
    orders = gather_orders(count)
    copies = []

    def send(h, mask, bit):
        rows = pl.ds(h * half, half)
        source = x_ref.at[rows] if mask == 0 else out_ref.at[me ^ mask, rows]
        there = mask | (1 << bit)
        copy = pltpu.make_async_remote_copy(
            src_ref=source,
            dst_ref=out_ref.at[me ^ mask, rows],
            send_sem=send_sem.at[h, there],
            recv_sem=recv_sem.at[h, there],
            device_id=(rep, me ^ (1 << bit)),
            device_id_type=MESH,
        )
        copy.start()
        copies.append(copy)

    def arrived(h, mask):
        rows = pl.ds(h * half, half)
        pltpu.make_async_copy(
            x_ref.at[rows], out_ref.at[me ^ mask, rows], recv_sem.at[h, mask]
        ).wait()

    for stage in range(bits):
        for h in range(2):
            send(h, 0, orders[h][stage])
    for stage in range(bits):
        for low in spans(orders[0][:stage]):
            index = spans(orders[0][:stage]).index(low)
            for h in range(2):
                mask = spans(orders[h][:stage])[index] | (1 << orders[h][stage])
                arrived(h, mask)
                for later in range(stage + 1, bits):
                    send(h, mask, orders[h][later])
    for copy in copies:
        copy.wait_send()
    local.wait()


def gather_tokens(x, count, collective_id):
    return pl.pallas_call(
        functools.partial(token_gather_kernel, count),
        out_shape=jax.ShapeDtypeStruct((count,) + x.shape, x.dtype),
        in_specs=[pl.BlockSpec(memory_space=pl.ANY)],
        out_specs=pl.BlockSpec(memory_space=pl.ANY),
        scratch_shapes=[
            pltpu.SemaphoreType.DMA((2, count)),
            pltpu.SemaphoreType.DMA((2, count)),
            pltpu.SemaphoreType.DMA,
        ],
        compiler_params=pltpu.CompilerParams(collective_id=collective_id, has_side_effects=True),
        name="token_gather",
    )(x)


class BlockGather:
    def __init__(self, n_rep, n_ep, x_ref, out_ref, sems):
        self.n_rep, self.bits = n_rep, bits_of(n_ep)
        self.x_ref, self.out_ref = x_ref, out_ref
        self.send_sem, self.recv_sem, self.local_sem = sems
        self.rep, self.me = lax.axis_index("rep"), lax.axis_index("ep")
        split = -(-x_ref.shape[1] // 256) * 128
        self.columns = (pl.ds(0, split), pl.ds(split, x_ref.shape[1] - split))
        self.orders = gather_orders(n_ep)
        self.made = []

    @staticmethod
    def sems(n_rep, n_ep):
        return [
            pltpu.SemaphoreType.DMA((n_rep, 2, n_ep)),
            pltpu.SemaphoreType.DMA((n_rep, 2, n_ep)),
            pltpu.SemaphoreType.DMA,
        ]

    def peers(self):
        return [(self.rep, self.me ^ (1 << b)) for b in range(self.bits)] + [
            (self.rep ^ d, self.me) for d in range(1, self.n_rep)
        ]

    def row(self, d):
        return 0 if self.n_rep == 1 else self.rep ^ d

    def place(self, d, h, mask):
        return self.out_ref.at[self.row(d), self.me ^ mask, :, self.columns[h]]

    def copy(self, d, h, mask, there_d, there_mask, device):
        return pltpu.make_async_remote_copy(
            src_ref=self.x_ref.at[:, self.columns[h]] if d == 0 and mask == 0 else self.place(d, h, mask),
            dst_ref=self.place(d, h, mask),
            send_sem=self.send_sem.at[there_d, h, there_mask],
            recv_sem=self.recv_sem.at[there_d, h, there_mask],
            device_id=device,
            device_id_type=MESH,
        )

    def hop(self, d, h, mask, bit):
        return self.copy(d, h, mask, d, mask | (1 << bit), (self.rep, self.me ^ (1 << bit)))

    def send(self, d, h, mask, bit):
        self.made.append((d, h, mask, bit))
        self.hop(d, h, mask, bit).start()

    def arrived(self, d, h, mask):
        target = self.place(d, h, mask)
        pltpu.make_async_copy(target, target, self.recv_sem.at[d, h, mask]).wait()

    def local(self):
        return pltpu.make_async_copy(self.x_ref, self.out_ref.at[self.row(0), self.me], self.local_sem)

    def far(self, d, h):
        return self.copy(0, h, 0, d, 0, (self.rep ^ d, self.me))

    def spread(self, d):
        for stage in range(self.bits):
            for h in range(2):
                self.send(d, h, 0, self.orders[h][stage])

    def begin(self):
        self.local().start()
        for d in range(1, self.n_rep):
            for h in range(2):
                self.far(d, h).start()
        self.spread(0)

    def from_rep(self, d):
        for h in range(2):
            self.arrived(d, h, 0)
        self.spread(d)

    def relay(self, d, h, mask, stage):
        self.arrived(d, h, mask)
        for later in range(stage + 1, self.bits):
            self.send(d, h, mask, self.orders[h][later])

    def events(self):
        steps = []
        for d in range(self.n_rep):
            if d + 1 < self.n_rep:
                steps.append(functools.partial(self.from_rep, d + 1))
            for stage in range(self.bits):
                for index in range(1 << stage):
                    for h in range(2):
                        mask = spans(self.orders[h][:stage])[index] | (1 << self.orders[h][stage])
                        steps.append(functools.partial(self.relay, d, h, mask, stage))
        return steps

    def end(self):
        for made in dict.fromkeys(self.made):
            self.hop(*made).wait_send()
        for d in range(1, self.n_rep):
            for h in range(2):
                self.far(d, h).wait_send()
        self.local().wait()


def weight_gather_kernel(n_rep, n_ep, x_ref, out_ref, *sems):
    gather = BlockGather(n_rep, n_ep, x_ref, out_ref, sems)
    meet(gather.peers())
    gather.begin()
    for event in gather.events():
        event()
    gather.end()


def gather_weights(x, n_rep, n_ep, collective_id):
    return pl.pallas_call(
        functools.partial(weight_gather_kernel, n_rep, n_ep),
        out_shape=jax.ShapeDtypeStruct((n_rep, n_ep) + x.shape, x.dtype),
        in_specs=[pl.BlockSpec(memory_space=pl.ANY)],
        out_specs=pl.BlockSpec(memory_space=pl.ANY),
        scratch_shapes=BlockGather.sems(n_rep, n_ep),
        compiler_params=pltpu.CompilerParams(collective_id=collective_id, has_side_effects=True),
        cost_estimate=pl.CostEstimate(flops=1000, bytes_accessed=1000, transcendentals=0),
        name="weight_gather",
    )(x)


COLUMNS = 512


def attention_front_kernel(n_rep, n_ep, heads_kv, groups, scale, *refs):
    (length_ref, x_ref, row_ref, gains_ref, cos_ref, sin_ref, mat_ref, wo_ref, own_g_ref) = refs[:9]
    h_ref, proj_ref, att_ref, wo_all, g_all = refs[9:14]
    mat_buf, mat_sem, k_low, v_low = refs[14:18]
    gather = BlockGather(n_rep, n_ep, wo_ref, wo_all, refs[18:21])
    extra = BlockGather(1, n_ep, own_g_ref, g_all, refs[21:24])
    size = gains_ref.shape[1]
    tokens = x_ref.shape[0]
    wide_q, wide_kv = heads_kv * groups * size, heads_kv * size
    chunks = (wide_q + 2 * wide_kv) // COLUMNS
    pairs = heads_kv * groups // 2
    turns = chunks + pairs

    def mat_copy(i):
        columns = pl.ds(pl.multiple_of(i * COLUMNS, COLUMNS), COLUMNS)
        return pltpu.make_async_copy(mat_ref.at[:, columns], mat_buf.at[i % 2], mat_sem.at[i % 2])

    mat_copy(0).start()
    meet(gather.peers())
    gather.begin()
    x = x_ref[...].astype(f32)
    x = x * lax.rsqrt(jnp.mean(x * x, axis=-1, keepdims=True) + eps)
    h_ref[...] = (x * row_ref[0:1, :]).astype(bf16)

    def rotate(value):
        return value * cos_ref[...] + pltpu.roll(value, size // 2, 1) * sin_ref[...]

    def normed(value):
        return value * lax.rsqrt(jnp.mean(value * value, axis=-1, keepdims=True) + eps)

    query_pos = lax.broadcasted_iota(jnp.int32, (tokens, tokens), 0)
    key_pos = lax.broadcasted_iota(jnp.int32, (tokens, tokens), 1)
    allowed = (key_pos <= query_pos) & (key_pos < length_ref[0])

    def lanes(start):
        return pl.ds(pl.multiple_of(start, size), size)

    events = gather.events() + [extra.begin] + extra.events()
    per_turn = -(-len(events) // (turns - 1))

    def turn(i, carry):
        @pl.when(i < chunks)
        def _():
            @pl.when(i + 1 < chunks)
            def _():
                mat_copy(i + 1).start()

            mat_copy(i).wait()
            columns = pl.ds(pl.multiple_of(i * COLUMNS, COLUMNS), COLUMNS)
            proj_ref[:, columns] = jnp.dot(h_ref[...], mat_buf[i % 2], preferred_element_type=f32)

        @pl.when(i >= chunks)
        def _():
            pair = i - chunks
            group = pair // (groups // 2)

            @pl.when(pair % (groups // 2) == 0)
            def _():
                key = normed(proj_ref[:, lanes(wide_q + group * size)])
                k_low[...] = rotate(key * gains_ref[1:2, :]).astype(bf16)
                v_low[...] = proj_ref[:, lanes(wide_q + wide_kv + group * size)].astype(bf16)

            for n in range(2):
                head = pair * 2 + n
                query = rotate(normed(proj_ref[:, lanes(head * size)]) * gains_ref[0:1, :]).astype(bf16)
                scores = lax.dot_general(query, k_low[...], NT, preferred_element_type=f32) * scale
                scores = jnp.where(allowed, scores, -1e30)
                raised = jnp.exp(scores - jnp.max(scores, axis=1, keepdims=True))
                probs = (raised * (1.0 / jnp.sum(raised, axis=1, keepdims=True))).astype(bf16)
                att_ref[:, lanes(head * size)] = jnp.dot(
                    probs, v_low[...], preferred_element_type=f32
                ).astype(bf16)

        for k in range(turns):
            mine = events[k * per_turn : (k + 1) * per_turn]
            if mine:

                @pl.when(i == k)
                def _(mine=mine):
                    for event in mine:
                        event()

        return carry

    lax.fori_loop(0, turns, turn, 0)
    gather.end()
    extra.end()


def attention_front(
    length, x, row_gain, gains, cos, sin, mat, w_o, own_g, n_rep, n_ep, heads_kv, groups, collective_id
):
    tokens, width = x.shape
    size = gains.shape[1]
    vmem = pl.BlockSpec(memory_space=pltpu.VMEM)
    anywhere = pl.BlockSpec(memory_space=pl.ANY)
    wide_q = heads_kv * groups * size
    wide_all = wide_q + 2 * heads_kv * size
    return pl.pallas_call(
        functools.partial(attention_front_kernel, n_rep, n_ep, heads_kv, groups, size ** (-0.5)),
        out_shape=(
            jax.ShapeDtypeStruct((tokens, width), bf16),
            jax.ShapeDtypeStruct((tokens, wide_all), f32),
            jax.ShapeDtypeStruct((tokens, wide_q), bf16),
            jax.ShapeDtypeStruct((n_rep, n_ep) + w_o.shape, bf16),
            jax.ShapeDtypeStruct((1, n_ep) + own_g.shape, bf16),
        ),
        in_specs=[pl.BlockSpec(memory_space=pltpu.SMEM)] + [vmem] * 5 + [anywhere] * 3,
        out_specs=(vmem,) * 3 + (anywhere,) * 2,
        scratch_shapes=[
            pltpu.VMEM((2, width, COLUMNS), bf16),
            pltpu.SemaphoreType.DMA((2,)),
            pltpu.VMEM((tokens, size), bf16),
            pltpu.VMEM((tokens, size), bf16),
        ]
        + BlockGather.sems(n_rep, n_ep)
        + BlockGather.sems(1, n_ep),
        compiler_params=pltpu.CompilerParams(
            collective_id=collective_id, has_side_effects=True, vmem_limit_bytes=VMEM_BYTES
        ),
        cost_estimate=pl.CostEstimate(flops=1000, bytes_accessed=1000, transcendentals=0),
        name="attention_front",
    )(length, x, row_gain, gains, cos, sin, mat, w_o, own_g)


class TokenSum:
    def __init__(self, count, y_ref, starts, results, scratch):
        self.bits = bits_of(count)
        self.y_ref, self.results = y_ref, results
        self.own, self.got = scratch[:2], scratch[2:4]
        self.send_sem, self.recv_sem, self.own_sem = scratch[4:7]
        self.rep, self.me = lax.axis_index("rep"), lax.axis_index("ep")
        self.orders = [list(reversed(o)) for o in gather_orders(count)]
        self.columns = [pl.ds(s, o.shape[2]) for s, o in zip(starts, self.own)]
        self.masks = [
            [list(reversed(spans(self.orders[h][k + 1 :]))) for k in range(self.bits)] for h in range(2)
        ]
        self.slots, self.seats = [], []
        for h in range(2):
            table = {}
            for stage in range(self.bits):
                for mask in self.masks[h][stage]:
                    table[(stage, mask)] = len(table)
            self.slots.append(table)
            self.seats.append({mask: i for i, mask in enumerate(self.masks[h][0])})

    @staticmethod
    def scratch(count, rows, widths):
        half = count // 2
        return [
            pltpu.VMEM((half, rows, widths[0]), bf16),
            pltpu.VMEM((half, rows, widths[1]), bf16),
            pltpu.VMEM((count - 1, rows, widths[0]), bf16),
            pltpu.VMEM((count - 1, rows, widths[1]), bf16),
            pltpu.SemaphoreType.DMA((2, count)),
            pltpu.SemaphoreType.DMA((2, count)),
            pltpu.SemaphoreType.DMA((2, half)),
        ]

    def meet(self):
        meet([(self.rep, self.me ^ (1 << b)) for b in range(self.bits)])

    def copy(self, h, stage, mask):
        bit = 1 << self.orders[h][stage]
        slot = self.slots[h][(stage, mask)]
        if stage == 0:
            source = self.y_ref.at[self.me ^ bit ^ mask, :, self.columns[h]]
        else:
            source = self.own[h].at[self.seats[h][bit | mask]]
        return pltpu.make_async_remote_copy(
            src_ref=source,
            dst_ref=self.got[h].at[slot],
            send_sem=self.send_sem.at[h, slot],
            recv_sem=self.recv_sem.at[h, slot],
            device_id=(self.rep, self.me ^ bit),
            device_id_type=MESH,
        )

    def load(self, h, mask):
        seat = self.seats[h][mask]
        return pltpu.make_async_copy(
            self.y_ref.at[self.me ^ mask, :, self.columns[h]], self.own[h].at[seat], self.own_sem.at[h, seat]
        )

    def begin(self):
        for i in range(len(self.masks[0][0])):
            for h in range(2):
                self.copy(h, 0, self.masks[h][0][i]).start()
                self.load(h, self.masks[h][0][i]).start()

    def add(self, h, stage, mask):
        slot, seat = self.slots[h][(stage, mask)], self.seats[h][mask]
        own, got = self.own[h], self.got[h]
        if stage == 0:
            self.load(h, mask).wait()
        self.copy(h, stage, mask).wait_recv()
        step = 32

        def body(i, carry):
            rows = pl.ds(pl.multiple_of(i * step, step), step)
            total = own[seat, rows, :].astype(f32) + got[slot, rows, :].astype(f32)
            if stage == self.bits - 1:
                self.results[h][rows, :] = total
            else:
                own[seat, rows, :] = total.astype(bf16)
            return carry

        lax.fori_loop(0, own.shape[1] // step, body, 0)

    def stage(self, stage):
        for i in range(len(self.masks[0][stage])):
            for h in range(2):
                mask = self.masks[h][stage][i]
                self.add(h, stage, mask)
                if stage + 1 < self.bits:
                    following = 1 << self.orders[h][stage + 1]
                    if mask & following:
                        self.copy(h, stage + 1, mask & ~following).start()

    def end(self):
        for h in range(2):
            for stage, mask in self.slots[h]:
                self.copy(h, stage, mask).wait_send()


def token_sum_kernel(count, starts, y_ref, first_ref, second_ref, *scratch):
    total = TokenSum(count, y_ref, starts, (first_ref, second_ref), scratch)
    total.meet()
    total.begin()
    for stage in range(total.bits):
        total.stage(stage)
    total.end()


def sum_tokens(y, count, starts, widths, collective_id):
    rows = y.shape[1]
    return pl.pallas_call(
        functools.partial(token_sum_kernel, count, starts),
        out_shape=tuple(jax.ShapeDtypeStruct((rows, w), f32) for w in widths),
        in_specs=[pl.BlockSpec(memory_space=pl.ANY)],
        out_specs=(pl.BlockSpec(memory_space=pltpu.VMEM),) * 2,
        scratch_shapes=TokenSum.scratch(count, rows, widths),
        compiler_params=pltpu.CompilerParams(
            collective_id=collective_id, has_side_effects=True, vmem_limit_bytes=VMEM_BYTES
        ),
        cost_estimate=pl.CostEstimate(flops=1000, bytes_accessed=1000, transcendentals=0),
        name="token_sum",
    )(y)


QUAD = 4


def attention_back_kernel(count, starts, heads_kv, groups, scale, *refs):
    (length_ref, proj_ref, gains_ref, cos_ref, sin_ref, mid_ref, wo_ref, y_ref) = refs[:8]
    right_ref, head_ref, first_ref, second_ref = refs[8:12]
    wo_buf, wo_sem, k_low, v_low, k_norm, dk_sum, dv_sum = refs[12:19]
    total = TokenSum(count, y_ref, starts, (first_ref, second_ref), refs[19:])
    size = gains_ref.shape[1]
    tokens = proj_ref.shape[0]
    heads_q = heads_kv * groups
    wide_q, wide_kv = heads_q * size, heads_kv * size
    per_group = groups // QUAD
    turns = heads_q // QUAD

    def wo_copy(i):
        rows = pl.ds(pl.multiple_of(i * QUAD * size, QUAD * size), QUAD * size)
        return pltpu.make_async_copy(wo_ref.at[rows], wo_buf.at[i % 2], wo_sem.at[i % 2])

    wo_copy(0).start()
    total.meet()
    total.begin()
    head_ref[...] = jnp.zeros_like(head_ref)
    sent = right_ref.shape[1] - wide_q - 2 * wide_kv
    for n in range(sent // mid_ref.shape[1]):
        start = wide_q + 2 * wide_kv + n * mid_ref.shape[1]
        right_ref[:, start : start + mid_ref.shape[1]] = mid_ref[...]

    def rotate(value):
        return value * cos_ref[...] + pltpu.roll(value, size // 2, 1) * sin_ref[...]

    def rotate_back(value):
        return value * cos_ref[...] - pltpu.roll(value, size // 2, 1) * sin_ref[...]

    def norm_parts(value):
        inverse = lax.rsqrt(jnp.mean(value * value, axis=-1, keepdims=True) + eps)
        return value * inverse, inverse

    def project_back(gradient, normed, inverse, row):
        scaled = rotate_back(gradient)
        head_ref[row : row + 1, :] += jnp.sum(scaled * normed, axis=0, keepdims=True)
        lifted = scaled * gains_ref[row : row + 1, :]
        mean = jnp.mean(lifted * normed, axis=-1, keepdims=True)
        return (inverse * (lifted - normed * mean)).astype(bf16)

    key_pos = lax.broadcasted_iota(jnp.int32, (tokens, tokens), 0)
    query_pos = lax.broadcasted_iota(jnp.int32, (tokens, tokens), 1)
    allowed = (key_pos <= query_pos) & (key_pos < length_ref[0])

    def lanes(start):
        return pl.ds(pl.multiple_of(start, size), size)

    def turn(i, carry):
        group = i // per_group
        for stage, when in ((0, min(1, turns - 1)), (1, turns - 2)):

            @pl.when(i == when)
            def _(stage=stage):
                if stage < total.bits - 1:
                    total.stage(stage)

        @pl.when(i % per_group == 0)
        def _():
            normed, inverse = norm_parts(proj_ref[:, lanes(wide_q + group * size)])
            k_norm[:, :size] = normed
            k_norm[:, size:] = jnp.broadcast_to(inverse, normed.shape)
            k_low[...] = rotate(normed * gains_ref[1:2, :]).astype(bf16)
            v_low[...] = proj_ref[:, lanes(wide_q + wide_kv + group * size)].astype(bf16)
            dk_sum[...] = jnp.zeros_like(dk_sum)
            dv_sum[...] = jnp.zeros_like(dv_sum)

        @pl.when(i + 1 < turns)
        def _():
            wo_copy(i + 1).start()

        wo_copy(i).wait()
        d_att = lax.dot_general(mid_ref[...], wo_buf[i % 2], NT, preferred_element_type=f32).astype(bf16)
        keys, values = k_low[...], v_low[...]
        dk, dv = dk_sum[...], dv_sum[...]
        for n in range(QUAD):
            head = i * QUAD + n
            d_out = d_att[:, n * size : (n + 1) * size]
            normed, inverse = norm_parts(proj_ref[:, lanes(head * size)])
            query = rotate(normed * gains_ref[0:1, :]).astype(bf16)
            scores = lax.dot_general(keys, query, NT, preferred_element_type=f32) * scale
            scores = jnp.where(allowed, scores, -1e30)
            raised = jnp.exp(scores - jnp.max(scores, axis=0, keepdims=True))
            probs = raised * (1.0 / jnp.sum(raised, axis=0, keepdims=True))
            dv += jnp.dot(probs.astype(bf16), d_out, preferred_element_type=f32)
            d_probs = lax.dot_general(values, d_out, NT, preferred_element_type=f32)
            weighted = probs * d_probs
            d_scores = (weighted - probs * jnp.sum(weighted, axis=0, keepdims=True)).astype(bf16)
            dk += jnp.dot(d_scores, query, preferred_element_type=f32)
            d_query = lax.dot_general(d_scores, keys, TN, preferred_element_type=f32) * scale
            right_ref[:, lanes(head * size)] = project_back(d_query, normed, inverse, 0)
        dk_sum[...] = dk
        dv_sum[...] = dv

        @pl.when(i % per_group == per_group - 1)
        def _():
            right_ref[:, lanes(wide_q + group * size)] = project_back(
                dk_sum[...] * scale, k_norm[:, :size], k_norm[:, size:], 1
            )
            right_ref[:, lanes(wide_q + wide_kv + group * size)] = dv_sum[...].astype(bf16)

        return carry

    lax.fori_loop(0, turns, turn, 0)
    for stage in range(min(2, total.bits - 1), total.bits):
        total.stage(stage)
    total.end()


def attention_back(length, proj, gains, cos, sin, d_mid, mat_o, y, count, starts, widths, heads_kv, groups, collective_id):
    tokens, width = d_mid.shape
    size = gains.shape[1]
    vmem = pl.BlockSpec(memory_space=pltpu.VMEM)
    anywhere = pl.BlockSpec(memory_space=pl.ANY)
    columns = (heads_kv * groups + 2 * heads_kv) * size + 2 * width
    return pl.pallas_call(
        functools.partial(attention_back_kernel, count, starts, heads_kv, groups, size ** (-0.5)),
        out_shape=(
            jax.ShapeDtypeStruct((tokens, columns), bf16),
            jax.ShapeDtypeStruct((8, size), f32),
        )
        + tuple(jax.ShapeDtypeStruct((tokens, w), f32) for w in widths),
        in_specs=[pl.BlockSpec(memory_space=pltpu.SMEM)] + [vmem] * 5 + [anywhere] * 2,
        out_specs=(vmem,) * 4,
        scratch_shapes=[
            pltpu.VMEM((2, QUAD * size, width), bf16),
            pltpu.SemaphoreType.DMA((2,)),
            pltpu.VMEM((tokens, size), bf16),
            pltpu.VMEM((tokens, size), bf16),
            pltpu.VMEM((tokens, 2 * size), f32),
            pltpu.VMEM((tokens, size), f32),
            pltpu.VMEM((tokens, size), f32),
        ]
        + TokenSum.scratch(count, tokens, widths),
        compiler_params=pltpu.CompilerParams(
            collective_id=collective_id, has_side_effects=True, vmem_limit_bytes=VMEM_BYTES
        ),
        cost_estimate=pl.CostEstimate(flops=1000, bytes_accessed=1000, transcendentals=0),
        name="attention_back",
    )(length, proj, gains, cos, sin, d_mid, mat_o, y)


def dense_sum_kernel(n_rep, n_ep, rows, chunks, split, *refs):
    left_ref, right_ref, small_ref, head_ref, out_ref, head_out = refs[:6]
    rest = list(refs[6:])
    bits = bits_of(n_ep)
    wide = right_ref.shape[1] // (chunks - 1)
    half = wide // 2
    rep, me = lax.axis_index("rep"), lax.axis_index("ep")
    mine = [lax.rem(lax.div(me, 1 << b), 2) for b in range(bits)]
    part, got_core = rest[:2]
    acc = [None] + [rest[2 + 2 * k : 4 + 2 * k] for k in range(bits)]
    rest = rest[2 + 2 * bits :]
    got = [None] + [rest[2 * k : 2 * k + 2] for k in range(bits)]
    rest = rest[2 * bits :]
    head_own, head_got, head_rep = rest[:3]
    core_send, core_recv, step_send, step_recv, rep_send, rep_recv, head_send, head_recv, head_rs, head_rr = rest[3:]
    up = list(range(1, bits))
    orders = (up, up[::-1])
    left = [[sorted(set(up) - set(o[:k])) for k in range(bits)] for o in orders]
    lags = [0, 1]
    for _ in range(bits):
        lags.append(lags[-1] + 2)
    deep = 4
    others = [lax.rem(rep + d, n_rep) for d in range(1, n_rep)]
    meet([(rep, me ^ (1 << b)) for b in range(bits)] + [(other, me) for other in others])

    def core_copy(c):
        slot = lax.rem(c, 2)
        return pltpu.make_async_remote_copy(
            src_ref=part.at[slot, 1 - mine[0]],
            dst_ref=got_core.at[slot],
            send_sem=core_send.at[slot],
            recv_sem=core_recv.at[slot],
            device_id=(rep, me ^ 1),
            device_id_type=MESH,
        )

    def bit_copy(k, h, c):
        slot = lax.rem(c, deep)
        bit = orders[h][k - 1]
        place = left[h][k - 1].index(bit)
        return pltpu.make_async_remote_copy(
            src_ref=acc[k][h].at[(slot,) + (slice(None),) * place + (1 - mine[bit],)],
            dst_ref=got[k][h].at[slot],
            send_sem=step_send.at[k, h, slot],
            recv_sem=step_recv.at[k, h, slot],
            device_id=(rep, me ^ (1 << bit)),
            device_id_type=MESH,
        )

    def rep_copy(h, c, d):
        slot = lax.rem(c, deep)
        return pltpu.make_async_remote_copy(
            src_ref=acc[bits][h].at[slot, others[d]],
            dst_ref=got[bits][h].at[slot, n_rep - 2 - d],
            send_sem=rep_send.at[h, slot, d],
            recv_sem=rep_recv.at[h, slot, n_rep - 2 - d],
            device_id=(others[d], me),
            device_id_type=MESH,
        )

    corners = [()]
    for _ in up:
        corners = [c + (v,) for c in corners for v in range(2)]
    block = n_rep * rows
    side_rows = len(corners) * block

    def stage_make(c):
        slot = lax.rem(c, 2)

        @pl.when(c >= 2)
        def _():
            core_copy(c - 2).wait_send()

        @pl.when(c < chunks - 1)
        def _():
            which = jnp.where(c >= split[0], 1, 0) + jnp.where(c >= split[1], 1, 0)
            columns = pl.ds(pl.multiple_of(c * wide, wide), wide)
            weights = right_ref[:, columns]
            for side in (1, 0):
                which_side = 1 - mine[0] if side else mine[0]
                for n, corner in enumerate(corners):
                    start = (which * 2 + which_side) * side_rows + n * block
                    value = jnp.dot(
                        left_ref[pl.ds(pl.multiple_of(start, block), block), :],
                        weights,
                        preferred_element_type=f32,
                    )
                    part[(slot, which_side) + corner] = value.astype(bf16).reshape(n_rep, rows, wide)

        @pl.when(c == chunks - 1)
        def _():
            thin = small_ref.shape[1]
            for side in range(2):
                for n, corner in enumerate(corners):
                    value = small_ref[pl.ds(side * side_rows + n * block, block), :].reshape(n_rep, rows, thin)
                    blank = jnp.zeros((n_rep, rows, wide - thin), bf16)
                    part[(slot, side) + corner + (slice(None), slice(None), slice(0, thin))] = value
                    part[(slot, side) + corner + (slice(None), slice(None), slice(thin, wide))] = blank

        core_copy(c).start()

    def stage_core(c):
        slot, put = lax.rem(c, 2), lax.rem(c, deep)

        @pl.when(c >= deep)
        def _():
            for h in range(2):
                if bits > 1:
                    bit_copy(1, h, c - deep).wait_send()

        core_copy(c).wait_recv()
        for corner in corners:
            total = part[(slot, mine[0]) + corner].astype(f32) + got_core[(slot,) + corner].astype(f32)
            total = total.astype(bf16)
            for h in range(2):
                acc[1][h][(put,) + corner] = total[:, :, h * half : (h + 1) * half]
        for h in range(2):
            bit_copy(1, h, c).start()

    def stage_bit(k, c):
        slot = lax.rem(c, deep)
        for h in range(2):
            bit = orders[h][k - 2]
            place = left[h][k - 2].index(bit)

            @pl.when(c >= deep)
            def _(h=h):
                if k < bits:
                    bit_copy(k, h, c - deep).wait_send()
                else:
                    for d in range(n_rep - 1):
                        rep_copy(h, c - deep, d).wait_send()

            bit_copy(k - 1, h, c).wait_recv()
            small_corners = [()]
            for _ in left[h][k - 1]:
                small_corners = [q + (v,) for q in small_corners for v in range(2)]
            for corner in small_corners:
                full = corner[:place] + (mine[bit],) + corner[place:]
                total = acc[k - 1][h][(slot,) + full].astype(f32) + got[k - 1][h][(slot,) + corner].astype(f32)
                acc[k][h][(slot,) + corner] = total.astype(bf16)
            if k < bits:
                bit_copy(k, h, c).start()
            else:
                for d in range(n_rep - 1):
                    rep_copy(h, c, d).start()

    def stage_end(c):
        slot = lax.rem(c, deep)
        for h in range(2):
            total = acc[bits][h][slot, rep].astype(f32)
            for d in range(n_rep - 1):
                rep_copy(h, c, d).wait_recv()
            for d in range(n_rep - 1):
                total += got[bits][h][slot, d].astype(f32)
            out_ref[:, pl.ds(pl.multiple_of(c * wide + h * half, half), half)] = total

    def head_copy(t):
        return pltpu.make_async_remote_copy(
            src_ref=head_own.at[t],
            dst_ref=head_got.at[t],
            send_sem=head_send.at[t],
            recv_sem=head_recv.at[t],
            device_id=(rep, me ^ (1 << t)),
            device_id_type=MESH,
        )

    def head_rep_copy(d):
        return pltpu.make_async_remote_copy(
            src_ref=head_own.at[bits],
            dst_ref=head_rep.at[rep],
            send_sem=head_rs.at[d],
            recv_sem=head_rr.at[n_rep - 2 - d],
            device_id=(others[d], me),
            device_id_type=MESH,
        )

    def head_step(t):
        if t == 0:
            head_own[0] = head_ref[...]
            head_copy(0).start()
        elif t <= bits:
            head_copy(t - 1).wait_recv()
            head_own[t] = head_own[t - 1] + head_got[t - 1]
            if t < bits:
                head_copy(t).start()
            else:
                for d in range(n_rep - 1):
                    head_rep_copy(d).start()
                head_rep[rep] = head_own[bits]
        else:
            for d in range(n_rep - 1):
                head_rep_copy(d).wait_recv()
            total = head_rep[0]
            for r in range(1, n_rep):
                total = total + head_rep[r]
            head_out[...] = total

    def step(i, carry):
        for stage in reversed(range(len(lags))):
            c = i - lags[stage]

            @pl.when((c >= 0) & (c < chunks))
            def _(stage=stage, c=c):
                if stage == 0:
                    stage_make(c)
                elif stage == 1:
                    stage_core(c)
                elif stage <= bits:
                    stage_bit(stage, c)
                else:
                    stage_end(c)

        for t in range(bits + 2):

            @pl.when(i == t)
            def _(t=t):
                head_step(t)

        return carry

    lax.fori_loop(0, chunks + lags[-1], step, 0)
    for c in range(chunks - 2, chunks):
        core_copy(c).wait_send()
    for c in range(chunks - deep, chunks):
        for h in range(2):
            for k in range(1, bits):
                bit_copy(k, h, c).wait_send()
            for d in range(n_rep - 1):
                rep_copy(h, c, d).wait_send()
    for t in range(bits):
        head_copy(t).wait_send()
    for d in range(n_rep - 1):
        head_rep_copy(d).wait_send()


def dense_sum(left, right, small, head, n_rep, n_ep, split, collective_id):
    chunk = 512
    chunks = right.shape[1] // chunk + 1
    bits = bits_of(n_ep)
    rows = left.shape[0] // (3 * n_rep * n_ep)
    deep = 4
    half = chunk // 2
    vmem = pl.BlockSpec(memory_space=pltpu.VMEM)
    inner = (n_rep, rows)
    scratch = [
        pltpu.VMEM((2, 2) + (2,) * (bits - 1) + inner + (chunk,), bf16),
        pltpu.VMEM((2,) + (2,) * (bits - 1) + inner + (chunk,), bf16),
    ]
    for k in range(1, bits + 1):
        scratch += [pltpu.VMEM((deep,) + (2,) * (bits - k) + inner + (half,), bf16)] * 2
    for k in range(1, bits):
        scratch += [pltpu.VMEM((deep,) + (2,) * (bits - 1 - k) + inner + (half,), bf16)] * 2
    scratch += [pltpu.VMEM((deep, n_rep - 1, rows, half), bf16)] * 2
    scratch += [
        pltpu.VMEM((bits + 1,) + head.shape, f32),
        pltpu.VMEM((bits,) + head.shape, f32),
        pltpu.VMEM((n_rep,) + head.shape, f32),
        pltpu.SemaphoreType.DMA((2,)),
        pltpu.SemaphoreType.DMA((2,)),
        pltpu.SemaphoreType.DMA((bits, 2, deep)),
        pltpu.SemaphoreType.DMA((bits, 2, deep)),
        pltpu.SemaphoreType.DMA((2, deep, n_rep - 1)),
        pltpu.SemaphoreType.DMA((2, deep, n_rep - 1)),
        pltpu.SemaphoreType.DMA((bits,)),
        pltpu.SemaphoreType.DMA((bits,)),
        pltpu.SemaphoreType.DMA((n_rep - 1,)),
        pltpu.SemaphoreType.DMA((n_rep - 1,)),
    ]
    return pl.pallas_call(
        functools.partial(dense_sum_kernel, n_rep, n_ep, rows, chunks, split),
        out_shape=(
            jax.ShapeDtypeStruct((rows, chunks * chunk), f32),
            jax.ShapeDtypeStruct(head.shape, f32),
        ),
        in_specs=[vmem] * 4,
        out_specs=(vmem, vmem),
        scratch_shapes=scratch,
        compiler_params=pltpu.CompilerParams(
            collective_id=collective_id, has_side_effects=True, vmem_limit_bytes=VMEM_BYTES
        ),
        cost_estimate=pl.CostEstimate(flops=1000, bytes_accessed=1000, transcendentals=0),
        name="dense_sum",
    )(left, right, small, head)


def expert_kernel(local, first, last, experts, width, hidden_of, *refs):
    (info, h_ref, g_ref, wg_all, wu_all, wd_all) = refs[:6]
    rest = list(refs[6:])
    prev_ref = None if first else rest.pop(0)
    y_ref, grad_ref = rest[:2]
    xs, gs, ds, hs, stage, prev_buf, wide, tall, in_sem, out_sem, prev_sem, grad_sem = rest[2:14]
    wg_ref, wu_ref, wd_ref, weight_sem = rest[14:]
    weights = [
        pltpu.make_async_copy(source.at[local], target, weight_sem.at[n])
        for n, (source, target) in enumerate(((wg_all, wg_ref), (wu_all, wu_ref), (wd_all, wd_ref)))
    ]
    for copy in weights:
        copy.start()
    shares = grad_ref.shape[0]
    wide_share, tall_share = width // shares, hidden_of // shares
    hidden = wg_ref.shape[1]
    units = info[0]
    expert = info[1]
    table = 8
    per_tile = TILE // UNIT
    tiles = (units + per_tile - 1) // per_tile
    most = xs.shape[0] // TILE
    floor_tiles = min(4, most)

    def unit_in(u, slot):
        source = pl.ds(pl.multiple_of(info[table + u], UNIT), UNIT)
        target = pl.ds(pl.multiple_of(u * UNIT, UNIT), UNIT)
        return (
            pltpu.make_async_copy(h_ref.at[source], xs.at[target], in_sem.at[0, slot]),
            pltpu.make_async_copy(g_ref.at[source], gs.at[target], in_sem.at[1, slot]),
        )

    def begin(u, carry):
        for copy in unit_in(u, u // per_tile):
            copy.start()
        return carry

    lax.fori_loop(0, units, begin, 0)

    def blank(u, carry):
        target = pl.ds(pl.multiple_of(u * UNIT, UNIT), UNIT)
        xs[target, :] = jnp.zeros((UNIT, xs.shape[1]), bf16)
        gs[target, :] = jnp.zeros((UNIT, gs.shape[1]), bf16)
        return carry

    lax.fori_loop(units, jnp.maximum(tiles, floor_tiles) * per_tile, blank, 0)

    def blank_tile(i, carry):
        target = pl.ds(pl.multiple_of(i * TILE, TILE), TILE)
        ds[target, :] = jnp.zeros((TILE, ds.shape[1]), bf16)
        hs[target, :] = jnp.zeros((TILE, hs.shape[1]), bf16)
        return carry

    lax.fori_loop(tiles, floor_tiles, blank_tile, 0)

    def prev_copy(i):
        rows = pl.ds(pl.multiple_of(i * TILE, TILE), TILE)
        return pltpu.make_async_copy(prev_ref.at[rows], prev_buf.at[i % 2], prev_sem.at[i % 2])

    if not first:
        prev_copy(0).start()

    def unit_out(u):
        target = pl.ds(pl.multiple_of(info[table + u], UNIT), UNIT)
        tile = u // per_tile
        source = pl.ds(pl.multiple_of((u % per_tile) * UNIT, UNIT), UNIT)
        return pltpu.make_async_copy(stage.at[tile % 2, source], y_ref.at[target], out_sem.at[tile % 2])

    def out_start(i):
        if last:
            lax.fori_loop(
                i * per_tile,
                jnp.minimum((i + 1) * per_tile, units),
                lambda u, c: (unit_out(u).start(), c)[1],
                0,
            )
        else:
            rows = pl.ds(pl.multiple_of(i * TILE, TILE), TILE)
            pltpu.make_async_copy(stage.at[i % 2], y_ref.at[rows], out_sem.at[i % 2]).start()

    def out_wait(i):
        if last:
            lax.fori_loop(
                i * per_tile,
                jnp.minimum((i + 1) * per_tile, units),
                lambda u, c: (unit_out(u).wait(), c)[1],
                0,
            )
        else:
            rows = pl.ds(pl.multiple_of(i * TILE, TILE), TILE)
            pltpu.make_async_copy(stage.at[i % 2], y_ref.at[rows], out_sem.at[i % 2]).wait()

    lane = lax.broadcasted_iota(jnp.int32, (TILE, EXT), 1)
    weight_lanes = (lane == expert) | (lane == expert + experts) | (lane == expert + 2 * experts)

    def tile_step(i, carry):
        def landed(u, c):
            for copy in unit_in(u, i):
                copy.wait()
            return c

        lax.fori_loop(i * per_tile, jnp.minimum((i + 1) * per_tile, units), landed, 0)
        rows = pl.ds(pl.multiple_of(i * TILE, TILE), TILE)
        x = xs[rows, :width]
        g = gs[rows, :]
        extra = xs[rows, width:].astype(f32)
        weight = jnp.sum(jnp.where(weight_lanes, extra, 0.0), axis=1, keepdims=True)
        gate = jnp.dot(x, wg_ref[...], preferred_element_type=f32)
        up = jnp.dot(x, wu_ref[...], preferred_element_type=f32)
        d_plain = lax.dot_general(g, wd_ref[...], NT, preferred_element_type=f32)
        sig = 1.0 / (1.0 + jnp.exp(-gate))
        silu = gate * sig
        hid = silu * up
        d_weight = jnp.sum(hid.astype(bf16).astype(f32) * d_plain, axis=1, keepdims=True)
        hs[rows, :] = (hid * weight).astype(bf16)
        d_hidden = d_plain * weight
        ds[rows, :hidden] = (d_hidden * up * sig * (1.0 + gate * (1.0 - sig))).astype(bf16)
        ds[rows, hidden:] = (d_hidden * silu).astype(bf16)

        @pl.when(i >= 2)
        def _():
            out_wait(i - 2)

        if not first:

            @pl.when(i + 1 < tiles)
            def _():
                prev_copy(i + 1).start()

            prev_copy(i).wait()
        slot = i % 2
        high = d_weight.astype(bf16).astype(f32)
        low = d_weight - high
        note = jnp.where(lane == expert, high, 0.0) + jnp.where(lane == expert + experts, low, 0.0)
        d_row = lax.dot_general(ds[rows, :hidden], wg_ref[...], NT, preferred_element_type=f32)
        d_row += lax.dot_general(ds[rows, hidden:], wu_ref[...], NT, preferred_element_type=f32)
        if not first:
            d_row += prev_buf[slot, :, :width].astype(f32)
            note += prev_buf[slot, :, width : width + EXT].astype(f32)
        stage[slot, :, :width] = d_row.astype(bf16)
        stage[slot, :, width : width + EXT] = note.astype(bf16)
        out = jnp.dot(hs[rows, :], wd_ref[...], preferred_element_type=f32)
        if not first:
            out += prev_buf[slot, :, width + EXT :].astype(f32)
        stage[slot, :, width + EXT :] = out.astype(bf16)
        out_start(i)
        return carry

    for copy in weights:
        copy.wait()
    lax.fori_loop(0, tiles, tile_step, 0)

    block = 256

    def grads(depth):
        def wide_copies(m):
            per = wide_share // block
            return tuple(
                pltpu.make_async_copy(
                    wide.at[m % 2, :, p * LANES : (p + 1) * LANES],
                    grad_ref.at[
                        m // per,
                        pl.ds(pl.multiple_of(p * wide_share + (m % per) * block, block), block),
                    ],
                    grad_sem.at[m % 2, p],
                )
                for p in range(2 * hidden // LANES)
            )

        def wide_step(m, carry):
            @pl.when(m >= 2)
            def _():
                for copy in wide_copies(m - 2):
                    copy.wait()

            columns = pl.ds(pl.multiple_of(m * block, block), block)
            wide[m % 2] = lax.dot_general(
                xs[:depth, columns], ds[:depth, :], TN, preferred_element_type=f32
            ).astype(bf16)
            for copy in wide_copies(m):
                copy.start()
            return carry

        count = width // block
        lax.fori_loop(0, count, wide_step, 0)
        for m in range(count - 2, count):
            for copy in wide_copies(m):
                copy.wait()

        piece = math.gcd(block, tall_share)
        base = 2 * hidden // LANES * wide_share

        def tall_copies(m):
            made = []
            for q in range(block // piece):
                first_row = m * block + q * piece
                share, inside = first_row // tall_share, first_row % tall_share
                for p in range(width // LANES):
                    rows = pl.ds(pl.multiple_of(base + p * tall_share + inside, piece), piece)
                    made.append(
                        pltpu.make_async_copy(
                            tall.at[m % 2, q * piece : (q + 1) * piece, p * LANES : (p + 1) * LANES],
                            grad_ref.at[share, rows],
                            grad_sem.at[m % 2, q * (width // LANES) + p],
                        )
                    )
            return made

        def tall_step(m, carry):
            @pl.when(m >= 2)
            def _():
                for copy in tall_copies(m - 2):
                    copy.wait()

            columns = pl.ds(pl.multiple_of(m * block, block), block)
            tall[m % 2] = lax.dot_general(
                hs[:depth, columns], gs[:depth, :], TN, preferred_element_type=f32
            ).astype(bf16)
            for copy in tall_copies(m):
                copy.start()
            return carry

        count = hidden // block
        lax.fori_loop(0, count, tall_step, 0)
        for m in range(count - 2, count):
            for copy in tall_copies(m):
                copy.wait()

    for choice in range(floor_tiles, most + 1):
        chosen = (tiles <= choice) if choice == floor_tiles else (tiles == choice)

        @pl.when(chosen)
        def _(choice=choice):
            grads(choice * TILE)

    @pl.when(tiles >= 2)
    def _():
        out_wait(tiles - 2)

    out_wait(tiles - 1)


def expert_pass(info, h_rows, g_rows, w_gate, w_up, w_down, local, prev, last, experts, shares):
    tokens, width = g_rows.shape
    hidden = w_gate.shape[2]
    wide_row = width + EXT + width
    any_spec = pl.BlockSpec(memory_space=pl.ANY)
    first = prev is None
    operands = [info, h_rows, g_rows, w_gate, w_up, w_down] + ([] if first else [prev])
    specs = [pl.BlockSpec(memory_space=pltpu.SMEM), any_spec, any_spec, any_spec, any_spec, any_spec]
    specs += [] if first else [any_spec]
    return pl.pallas_call(
        functools.partial(expert_kernel, local, first, last, experts, width, hidden),
        out_shape=(
            jax.ShapeDtypeStruct((tokens, wide_row), bf16),
            jax.ShapeDtypeStruct((shares, 3 * hidden * width // shares // LANES, LANES), bf16),
        ),
        in_specs=specs,
        out_specs=(any_spec,) * 2,
        scratch_shapes=[
            pltpu.VMEM((tokens, width + EXT), bf16),
            pltpu.VMEM((tokens, width), bf16),
            pltpu.VMEM((tokens, 2 * hidden), bf16),
            pltpu.VMEM((tokens, hidden), bf16),
            pltpu.VMEM((2, TILE, wide_row), bf16),
            pltpu.VMEM((2, TILE, wide_row), bf16),
            pltpu.VMEM((2, 256, 2 * hidden), bf16),
            pltpu.VMEM((2, 256, width), bf16),
            pltpu.SemaphoreType.DMA((2, tokens // TILE)),
            pltpu.SemaphoreType.DMA((2,)),
            pltpu.SemaphoreType.DMA((2,)),
            pltpu.SemaphoreType.DMA((2, max(2 * hidden // LANES, 256 // math.gcd(256, hidden // shares) * width // LANES))),
            pltpu.VMEM((width, hidden), bf16),
            pltpu.VMEM((width, hidden), bf16),
            pltpu.VMEM((hidden, width), bf16),
            pltpu.SemaphoreType.DMA((3,)),
        ],
        compiler_params=pltpu.CompilerParams(vmem_limit_bytes=VMEM_BYTES),
        cost_estimate=pl.CostEstimate(flops=1000, bytes_accessed=1000, transcendentals=0),
        name="experts",
    )(*operands)


def unit_table(lengths):
    per_sequence = TILE // UNIT
    counts = (lengths + UNIT - 1) // UNIT
    unit = jnp.arange(lengths.shape[0] * per_sequence, dtype=jnp.int32)
    live = (unit % per_sequence) < jnp.repeat(counts, per_sequence)
    place = jnp.cumsum(live.astype(jnp.int32)) - 1
    hit = (place[None, :] == unit[:, None]) & live[None, :]
    rows = jnp.sum(jnp.where(hit, unit[None, :] * UNIT, 0), axis=1)
    return (jnp.sum(counts), rows)


def split_three(value):
    high = lax.reduce_precision(value, 8, 7)
    rest = value - high
    middle = lax.reduce_precision(rest, 8, 7)
    return jnp.concatenate([high, middle, rest - middle], axis=-1)


def per_device(
    hidden_in,
    out_grad,
    attn_gain,
    w_q,
    key_weight,
    value_weight,
    w_o,
    ffn_gain,
    router_w,
    qk_gains,
    w_gate,
    w_up,
    w_down,
    lengths,
    routes,
    order,
):
    everywhere = ("rep", "ep")
    rep_count, ep_count = (lax.axis_size("rep"), lax.axis_size("ep"))
    rep_index, ep_index = (lax.axis_index("rep"), lax.axis_index("ep"))
    inputs = hidden_in[0].astype(f32)
    sequence_length, model_width = inputs.shape
    head_size = qk_gains.shape[1]
    wide_q, wide_kv = (w_q.shape[1], key_weight.shape[1])
    heads_q, heads_kv = (wide_q // head_size, wide_kv // head_size)
    groups = heads_q // heads_kv
    local_experts = w_gate.shape[0]
    experts = local_experts * ep_count
    top_count = routes.shape[2]
    score_scale = head_size ** (-0.5)
    group_lengths = lax.dynamic_slice_in_dim(lengths, rep_index * ep_count, ep_count)
    length = lax.dynamic_index_in_dim(group_lengths, ep_index, keepdims=False)
    positions = jnp.arange(sequence_length, dtype=jnp.int32)
    live = positions < length
    live_rows = live.astype(f32)

    expert_iota = jnp.arange(experts, dtype=jnp.int32)
    route_hot = routes[0][..., None] == expert_iota
    routed = jnp.any(route_hot, axis=1) & live[:, None]
    order_of = jnp.sum(
        jnp.where(route_hot, order[0].reshape(sequence_length, top_count)[..., None], 0), axis=1
    )
    sort_key = jnp.where(routed, order_of, sequence_length * top_count)
    loads = jnp.sum(routed.astype(jnp.int32), axis=0)
    rank = jnp.sum((sort_key[None, :, :] < sort_key[:, None, :]).astype(jnp.int32), axis=1)

    own_rows = w_q.shape[0]
    load_columns = -(-experts // own_rows)
    load_block = jnp.pad(loads, (0, load_columns * own_rows - experts)).reshape(load_columns, own_rows).T
    small = jnp.concatenate(
        [router_w, attn_gain[:, None], ffn_gain[:, None], load_block.astype(bf16)], axis=1
    )
    small = jnp.pad(small, ((0, 0), (0, EXT - small.shape[1])))
    pack = jnp.concatenate([w_q, key_weight, value_weight, small], axis=1)
    mat_qkv = gather_weights(pack, rep_count, ep_count, 4).reshape(-1, pack.shape[1])

    wide_all = wide_q + 2 * wide_kv
    small_all = mat_qkv[:, wide_all:]
    mat_router = small_all[:, :experts]
    picks = (jnp.arange(EXT)[None, :] == experts + jnp.arange(8)[:, None]).astype(bf16)
    row_gain = lax.dot_general(picks, small_all, NT, preferred_element_type=f32)
    gain_attn, gain_ffn = (row_gain[0], row_gain[1])
    loads_all = (
        small_all[:, experts + 2 : experts + 2 + load_columns]
        .reshape(rep_count, ep_count, own_rows, load_columns)
        .transpose(0, 1, 3, 2)
        .reshape(rep_count, ep_count, load_columns * own_rows)[:, :, :experts]
        .astype(jnp.int32)
    )
    group_loads = lax.dynamic_index_in_dim(loads_all, rep_index, keepdims=False)
    earlier = (jnp.arange(ep_count) < ep_index)[:, None]
    load_prefix = jnp.sum(jnp.where(earlier, group_loads, 0), axis=0)
    capacity = 9 * top_count * jnp.sum(group_lengths) // (8 * experts)
    kept = routed & (load_prefix[None, :] + rank < capacity)
    kept_float = kept.astype(f32)

    cosine_lookup, sine_lookup = rope_tables(sequence_length, head_size)
    sign = jnp.where(jnp.arange(head_size) < head_size // 2, -1.0, 1.0).astype(f32)
    turned_sine = sine_lookup * sign[None, :]
    hidden_first, projected, attended, mat_o, grads_all = attention_front(
        length.reshape(1),
        hidden_in[0],
        row_gain,
        qk_gains.astype(f32),
        cosine_lookup,
        turned_sine,
        mat_qkv,
        w_o,
        out_grad[0],
        rep_count,
        ep_count,
        heads_kv,
        groups,
        6,
    )
    mat_o = mat_o.reshape(-1, model_width)
    grads_all = grads_all.reshape(-1, model_width)
    norm_one, inv_one = rms_parts(inputs)
    middle = inputs + jnp.dot(attended, mat_o, preferred_element_type=f32)
    norm_two, inv_two = rms_parts(middle)
    h_two = (norm_two * gain_ffn).astype(bf16)
    logits = jnp.dot(h_two, mat_router, preferred_element_type=f32)
    named = jnp.any(route_hot, axis=1)
    top_logit = jnp.max(jnp.where(named, logits, -jnp.inf), axis=1, keepdims=True)
    raised = jnp.where(named, jnp.exp(jnp.where(named, logits - top_logit, 0.0)), 0.0)
    route_gates = raised / jnp.sum(raised, axis=1, keepdims=True)
    pair_weight = route_gates * kept_float

    extra = split_three(pair_weight).astype(bf16)
    extra = jnp.pad(extra, ((0, 0), (0, EXT - extra.shape[1])))
    sent = jnp.concatenate([h_two, extra], axis=1)
    h_all = gather_tokens(sent, ep_count, 1)

    part = min(ep_count, 8)
    tokens = part * sequence_length
    sums = []
    y_parts = []
    for c in range(ep_count // part):
        live_units, unit_rows = unit_table(group_lengths[c * part : (c + 1) * part])
        h_rows = h_all[c * part : (c + 1) * part].reshape(tokens, model_width + EXT)
        g_rows = grads_all[c * tokens : (c + 1) * tokens]
        prev, found = None, []
        for local in range(local_experts):
            info = jnp.concatenate(
                [
                    jnp.stack([live_units, ep_index * local_experts + local]).astype(jnp.int32),
                    jnp.zeros((6,), jnp.int32),
                    unit_rows,
                ]
            )
            prev, weight_grads = expert_pass(
                info,
                h_rows,
                g_rows,
                w_gate,
                w_up,
                w_down,
                local,
                prev,
                local == local_experts - 1,
                experts,
                rep_count,
            )
            found.append(weight_grads)
        y_parts.append(prev.reshape(part, sequence_length, -1))
        sums.append(found)
    y_all = y_parts[0] if len(y_parts) == 1 else jnp.concatenate(y_parts, axis=0)
    hidden_units = w_gate.shape[2]
    wide_share, tall_share = model_width // rep_count, hidden_units // rep_count
    found = []
    for local in range(local_experts):
        total = sums[0][local]
        for more in sums[1:]:
            total = (total.astype(f32) + more[local].astype(f32)).astype(bf16)
        found.append(lax.psum_scatter(total, "rep", scatter_dimension=0, tiled=True))
    found = jnp.concatenate(found, axis=0)

    def unpacked(start, rows, columns):
        blocks = found[:, start : start + rows * (columns // LANES)]
        blocks = blocks.reshape(local_experts, columns // LANES, rows, LANES)
        return blocks.transpose(0, 2, 1, 3).reshape(local_experts, rows, columns).astype(f32)

    wide_rows = wide_share * (hidden_units // LANES)
    expert_sums = (
        unpacked(0, wide_share, hidden_units),
        unpacked(wide_rows, wide_share, hidden_units),
        unpacked(2 * wide_rows, tall_share, model_width),
    )

    half_width = model_width // 2
    row_first, row_second = sum_tokens(
        y_all, ep_count, (0, half_width), (half_width, half_width + EXT), 2
    )
    live_column = live[:, None]
    grad_rows = out_grad[0].astype(f32) * live_rows[:, None]
    notes = row_second[:, half_width : half_width + 2 * experts]
    d_weight = jnp.where(live_column, notes[:, :experts] + notes[:, experts:], 0.0)
    d_gates = d_weight * kept_float
    d_logits = route_gates * (d_gates - jnp.sum(route_gates * d_gates, axis=-1, keepdims=True))

    router_float = mat_router.astype(f32)
    d_h_two = jnp.concatenate([row_first, row_second[:, :half_width]], axis=1)
    d_h_two = jnp.where(live_column, d_h_two, 0.0)
    d_h_two = d_h_two + jnp.dot(d_logits, router_float.T, precision=top_precision)
    grad_router = jnp.dot(h_two.astype(f32).T, d_logits, precision=top_precision)
    grad_ffn = jnp.sum(d_h_two * norm_two, axis=0)
    d_middle = grad_rows + rms_back(d_h_two * gain_ffn, norm_two, inv_two)
    d_middle_low = d_middle.astype(bf16)
    right, head, out_first, out_second = attention_back(
        length.reshape(1),
        projected,
        qk_gains.astype(f32),
        cosine_lookup,
        turned_sine,
        d_middle_low,
        mat_o,
        y_all,
        ep_count,
        (model_width + EXT, model_width + EXT + half_width),
        (half_width, half_width),
        heads_kv,
        groups,
        5,
    )
    moe_output = jnp.where(live_column, jnp.concatenate([out_first, out_second], axis=1), 0.0)
    layer_out = jnp.where(live_column, middle + moe_output, 0.0)
    d_qkv = right[:, :wide_all]
    d_h_one = jnp.einsum("tf,cf->tc", d_qkv, mat_qkv[:, :wide_all], preferred_element_type=f32)
    grad_attn = jnp.sum(d_h_one * norm_one, axis=0)
    grad_input = d_middle + rms_back(d_h_one * gain_attn, norm_one, inv_one)

    small_grads = jnp.concatenate([grad_router, grad_attn[:, None], grad_ffn[:, None]], axis=1)
    small_grads = jnp.pad(small_grads, ((0, 0), (0, EXT - small_grads.shape[1]))).astype(bf16)
    ep_bits = bits_of(ep_count)

    def owner_order(value, parts):
        shape = (rep_count,) + (2,) * ep_bits + (parts, own_rows, value.shape[1])
        axes = (ep_bits + 1,) + tuple(range(ep_bits, 0, -1)) + (0, ep_bits + 2, ep_bits + 3)
        return value.reshape(shape).transpose(axes).reshape(value.shape)

    left = jnp.concatenate([owner_order(hidden_first.T, 1), owner_order(attended.T, 2)], axis=0)
    splits = (wide_all // 512, (wide_all + model_width) // 512)
    sums_all, head_sum = dense_sum(
        left, right, owner_order(small_grads, 1), head, rep_count, ep_count, splits, 3
    )
    sum_o = jnp.concatenate(
        [sums_all[:, wide_all : wide_all + model_width], sums_all[:, wide_all + model_width : wide_all + 2 * model_width]],
        axis=0,
    )
    small_sum = sums_all[:, wide_all + 2 * model_width :]
    return (
        layer_out[None],
        grad_input[None],
        small_sum[:, experts],
        sums_all[:, :wide_q],
        sums_all[:, wide_q : wide_q + wide_kv],
        sums_all[:, wide_q + wide_kv : wide_all],
        sum_o,
        small_sum[:, experts + 1],
        small_sum[:, :experts],
        head_sum[:2],
        expert_sums[0],
        expert_sums[1],
        expert_sums[2],
    )


def solution(mesh):
    both = ("rep", "ep")
    placed = (
        P(both, None, None),
        P(both, None, None),
        P(both),
        P(both, None),
        P(both, None),
        P(both, None),
        P(both, None),
        P(both),
        P(both, None),
        P(),
        P("ep", None, None),
        P("ep", None, None),
        P("ep", None, None),
        P(),
        P(both, None, None),
        P(both, None),
    )
    return jax.shard_map(
        per_device,
        mesh=mesh,
        in_specs=placed,
        out_specs=(
            P(both, None, None),
            P(both, None, None),
            P(both),
            P(both, None),
            P(both, None),
            P(both, None),
            P(both, None),
            P(both),
            P(both, None),
            P(),
            P("ep", "rep", None),
            P("ep", "rep", None),
            P("ep", "rep", None),
        ),
        check_vma=False,
    )
```

```python
import functools
import math

import jax
import jax.numpy as jnp
from jax import lax
from jax.experimental import pallas as pl
from jax.experimental.pallas import tpu as pltpu
from jax.sharding import PartitionSpec as P

eps = 1e-06
rope_base = 1000000.0
top_precision = lax.Precision.HIGHEST
MESH = pl.DeviceIdType.MESH
f32, bf16 = jnp.float32, jnp.bfloat16
EXT = 128
UNIT = 16
LANES = 256
TILE = 256
VMEM_BYTES = 58 * 1024 * 1024
NT = (((1,), (1,)), ((), ()))
TN = (((0,), (0,)), ((), ()))


def rms_parts(value_rows):
    inverse = lax.rsqrt(jnp.mean(value_rows * value_rows, axis=-1, keepdims=True) + eps)
    return (value_rows * inverse, inverse)


def rms_back(grad_norm, normed, inverse):
    return inverse * (grad_norm - normed * jnp.mean(grad_norm * normed, axis=-1, keepdims=True))


def rope_tables(count, head_size):
    half_size = head_size // 2
    freqs = rope_base ** (-2.0 * jnp.arange(half_size, dtype=f32) / head_size)
    angles = jnp.arange(count, dtype=f32)[:, None] * freqs[None, :]
    cosine_lookup = jnp.concatenate([jnp.cos(angles), jnp.cos(angles)], axis=1)
    sine_lookup = jnp.concatenate([jnp.sin(angles), jnp.sin(angles)], axis=1)
    return (cosine_lookup, sine_lookup)


def bits_of(count):
    return count.bit_length() - 1


def gather_orders(count):
    bits = bits_of(count)
    up = list(range(1, bits)) + [0]
    down = list(range(bits - 1, 0, -1)) + [0]
    return (up, down)


def spans(bits):
    masks = [0]
    for bit in bits:
        masks = masks + [m | (1 << bit) for m in masks]
    return masks


def meet(peers):
    barrier = pltpu.get_barrier_semaphore()
    for peer in peers:
        pl.semaphore_signal(barrier, inc=1, device_id=peer, device_id_type=MESH)
    pl.semaphore_wait(barrier, len(peers))


def token_gather_kernel(count, x_ref, out_ref, send_sem, recv_sem, local_sem):
    rep, me = lax.axis_index("rep"), lax.axis_index("ep")
    bits = bits_of(count)
    half = x_ref.shape[0] // 2
    meet([(rep, me ^ (1 << b)) for b in range(bits)])
    local = pltpu.make_async_copy(x_ref, out_ref.at[me], local_sem)
    local.start()
    orders = gather_orders(count)
    copies = []

    def send(h, mask, bit):
        rows = pl.ds(h * half, half)
        source = x_ref.at[rows] if mask == 0 else out_ref.at[me ^ mask, rows]
        there = mask | (1 << bit)
        copy = pltpu.make_async_remote_copy(
            src_ref=source,
            dst_ref=out_ref.at[me ^ mask, rows],
            send_sem=send_sem.at[h, there],
            recv_sem=recv_sem.at[h, there],
            device_id=(rep, me ^ (1 << bit)),
            device_id_type=MESH,
        )
        copy.start()
        copies.append(copy)

    def arrived(h, mask):
        rows = pl.ds(h * half, half)
        pltpu.make_async_copy(
            x_ref.at[rows], out_ref.at[me ^ mask, rows], recv_sem.at[h, mask]
        ).wait()

    for stage in range(bits):
        for h in range(2):
            send(h, 0, orders[h][stage])
    for stage in range(bits):
        for low in spans(orders[0][:stage]):
            index = spans(orders[0][:stage]).index(low)
            for h in range(2):
                mask = spans(orders[h][:stage])[index] | (1 << orders[h][stage])
                arrived(h, mask)
                for later in range(stage + 1, bits):
                    send(h, mask, orders[h][later])
    for copy in copies:
        copy.wait_send()
    local.wait()


def gather_tokens(x, count, collective_id):
    return pl.pallas_call(
        functools.partial(token_gather_kernel, count),
        out_shape=jax.ShapeDtypeStruct((count,) + x.shape, x.dtype),
        in_specs=[pl.BlockSpec(memory_space=pl.ANY)],
        out_specs=pl.BlockSpec(memory_space=pl.ANY),
        scratch_shapes=[
            pltpu.SemaphoreType.DMA((2, count)),
            pltpu.SemaphoreType.DMA((2, count)),
            pltpu.SemaphoreType.DMA,
        ],
        compiler_params=pltpu.CompilerParams(collective_id=collective_id, has_side_effects=True),
        name="token_gather",
    )(x)


class BlockGather:
    def __init__(self, n_rep, n_ep, x_ref, out_ref, sems):
        self.n_rep, self.bits = n_rep, bits_of(n_ep)
        self.x_ref, self.out_ref = x_ref, out_ref
        self.send_sem, self.recv_sem, self.up_sem, self.down_sem, self.local_sem = sems
        self.rep, self.me = lax.axis_index("rep"), lax.axis_index("ep")
        split = -(-x_ref.shape[1] // 256) * 128
        self.columns = (pl.ds(0, split), pl.ds(split, x_ref.shape[1] - split))
        self.orders = gather_orders(n_ep)
        self.entries = [(0, 0)]
        for s in range(1, n_rep):
            self.entries += [(s, -1), (s, 1)]

    @staticmethod
    def sems(n_rep, n_ep):
        return [
            pltpu.SemaphoreType.DMA((2 * n_rep - 1, 2, n_ep)),
            pltpu.SemaphoreType.DMA((2 * n_rep - 1, 2, n_ep)),
            pltpu.SemaphoreType.DMA((n_rep, 2)),
            pltpu.SemaphoreType.DMA((n_rep, 2)),
            pltpu.SemaphoreType.DMA,
        ]

    def meet(self):
        barrier = pltpu.get_barrier_semaphore()
        peers = [(self.rep, self.me ^ (1 << b)) for b in range(self.bits)]
        for peer in peers:
            pl.semaphore_signal(barrier, inc=1, device_id=peer, device_id_type=MESH)
        if self.n_rep > 1:
            for side in (-1, 1):

                @pl.when(self.reaches(side))
                def _(side=side):
                    pl.semaphore_signal(barrier, inc=1, device_id=(self.rep + side, self.me), device_id_type=MESH)

        count = len(peers)
        if self.n_rep > 1:
            count = count + jnp.where(self.reaches(-1), 1, 0) + jnp.where(self.reaches(1), 1, 0)
        pl.semaphore_wait(barrier, count)

    def reaches(self, side):
        return self.rep > 0 if side < 0 else self.rep < self.n_rep - 1

    def active(self, k):
        steps, side = self.entries[k]
        return self.rep >= steps if side < 0 else self.rep + steps < self.n_rep

    def guarded(self, k, action):
        if k == 0:
            action()
        else:
            pl.when(self.active(k))(action)

    def row(self, k):
        steps, side = self.entries[k]
        return 0 if self.n_rep == 1 else lax.rem(self.rep + side * steps + self.n_rep, self.n_rep)

    def place(self, k, h, mask):
        return self.out_ref.at[self.row(k), self.me ^ mask, :, self.columns[h]]

    def source(self, k, h, mask):
        return self.x_ref.at[:, self.columns[h]] if k == 0 and mask == 0 else self.place(k, h, mask)

    def hop(self, k, h, mask, bit):
        there = mask | (1 << bit)
        return pltpu.make_async_remote_copy(
            src_ref=self.source(k, h, mask),
            dst_ref=self.place(k, h, mask),
            send_sem=self.send_sem.at[k, h, there],
            recv_sem=self.recv_sem.at[k, h, there],
            device_id=(self.rep, self.me ^ (1 << bit)),
            device_id_type=MESH,
        )

    def along(self, k, h, side):
        steps = self.entries[k][0]
        lane = (steps * 2 if side > 0 else steps * 2 + 1)
        return pltpu.make_async_remote_copy(
            src_ref=self.source(k, h, 0),
            dst_ref=self.place(k, h, 0),
            send_sem=(self.up_sem if side > 0 else self.down_sem).at[steps, h],
            recv_sem=self.recv_sem.at[lane + 1, h, 0],
            device_id=(self.rep + side, self.me),
            device_id_type=MESH,
        )

    def arrived(self, k, h, mask):
        target = self.place(k, h, mask)
        pltpu.make_async_copy(target, target, self.recv_sem.at[k, h, mask]).wait()

    def local(self):
        return pltpu.make_async_copy(self.x_ref, self.out_ref.at[self.row(0), self.me], self.local_sem)

    def spread(self, k):
        for stage in range(self.bits):
            for h in range(2):
                self.hop(k, h, 0, self.orders[h][stage]).start()

    def onward(self, k, act):
        sides = (-1, 1) if k == 0 else (-self.entries[k][1],)
        if self.n_rep == 1 or self.entries[k][0] == self.n_rep - 1:
            return
        for side in sides:

            @pl.when(self.reaches(side))
            def _(side=side):
                for h in range(2):
                    act(self.along(k, h, side))

    def begin(self):
        self.local().start()
        self.onward(0, lambda copy: copy.start())
        self.spread(0)

    def from_rep(self, k):
        def action():
            for h in range(2):
                self.arrived(k, h, 0)
            self.onward(k, lambda copy: copy.start())
            self.spread(k)

        self.guarded(k, action)

    def relay(self, k, h, mask, stage):
        def action():
            self.arrived(k, h, mask)
            for later in range(stage + 1, self.bits):
                self.hop(k, h, mask, self.orders[h][later]).start()

        self.guarded(k, action)

    def tree(self):
        for stage in range(self.bits):
            for index in range(1 << stage):
                for h in range(2):
                    yield h, spans(self.orders[h][:stage])[index] | (1 << self.orders[h][stage]), stage

    def events(self):
        due = []
        for k, (steps, _) in enumerate(self.entries):
            if k:
                due.append((16 * steps, len(due), functools.partial(self.from_rep, k)))
            for h, mask, stage in self.tree():
                when = 16 * steps + 15 + 10 * stage if stage < self.bits - 1 else 1000 + steps
                due.append((when, len(due), functools.partial(self.relay, k, h, mask, stage)))
        return [step for _, _, step in sorted(due, key=lambda entry: entry[:2])]

    def end(self):
        for k in range(len(self.entries)):

            def action(k=k):
                for stage in range(self.bits):
                    for h in range(2):
                        self.hop(k, h, 0, self.orders[h][stage]).wait_send()
                for h, mask, stage in self.tree():
                    for later in range(stage + 1, self.bits):
                        self.hop(k, h, mask, self.orders[h][later]).wait_send()
                self.onward(k, lambda copy: copy.wait_send())

            self.guarded(k, action)


def weight_gather_kernel(n_rep, n_ep, x_ref, out_ref, *sems):
    gather = BlockGather(n_rep, n_ep, x_ref, out_ref, sems)
    gather.meet()
    gather.begin()
    for event in gather.events():
        event()
    gather.end()
    gather.local().wait()


def gather_weights(x, n_rep, n_ep, collective_id):
    return pl.pallas_call(
        functools.partial(weight_gather_kernel, n_rep, n_ep),
        out_shape=jax.ShapeDtypeStruct((n_rep, n_ep) + x.shape, x.dtype),
        in_specs=[pl.BlockSpec(memory_space=pl.ANY)],
        out_specs=pl.BlockSpec(memory_space=pl.ANY),
        scratch_shapes=BlockGather.sems(n_rep, n_ep),
        compiler_params=pltpu.CompilerParams(collective_id=collective_id, has_side_effects=True),
        cost_estimate=pl.CostEstimate(flops=1000, bytes_accessed=1000, transcendentals=0),
        name="weight_gather",
    )(x)


COLUMNS = 512


def attention_front_kernel(n_rep, n_ep, experts, heads_kv, groups, scale, *refs):
    (length_ref, x_ref, small_ref, gains_ref, cos_ref, sin_ref, key_ref, turned_ref) = refs[:8]
    (mat_ref, wo_ref, own_g_ref) = refs[8:11]
    h_ref, proj_ref, att_ref, middle_ref, second_ref, logit_ref, row_ref, rank_ref, wo_all, g_all = refs[11:21]
    mat_buf, mat_sem, k_low, v_low, wo_buf, wo_sem = refs[21:27]
    gather = BlockGather(n_rep, n_ep, wo_ref, wo_all, refs[27:32])
    extra = BlockGather(1, n_ep, own_g_ref, g_all, refs[32:37])
    size = gains_ref.shape[1]
    tokens, width = x_ref.shape
    wide_q, wide_kv = heads_kv * groups * size, heads_kv * size
    chunks = (wide_q + 2 * wide_kv) // COLUMNS
    pairs = heads_kv * groups // 2
    group_blocks = n_ep // 2
    block_rows = wo_ref.shape[0]
    deep = group_blocks * block_rows
    early = chunks + pairs
    turns = early + n_rep * 2

    def mat_copy(i):
        columns = pl.ds(pl.multiple_of(i * COLUMNS, COLUMNS), COLUMNS)
        return pltpu.make_async_copy(mat_ref.at[:, columns], mat_buf.at[i % 2], mat_sem.at[i % 2])

    def wo_copy(n):
        blocks = pl.ds((n % 2) * group_blocks, group_blocks)
        return pltpu.make_async_copy(wo_all.at[n // 2, blocks], wo_buf.at[n % 2], wo_sem.at[n % 2])

    mat_copy(0).start()
    gather.meet()
    gather.begin()
    pick = lax.broadcasted_iota(jnp.int32, (8, EXT), 0) + experts == lax.broadcasted_iota(jnp.int32, (8, EXT), 1)
    picks = jnp.where(pick, 1.0, 0.0).astype(bf16)
    row_ref[...] = lax.dot_general(picks, small_ref[...], NT, preferred_element_type=f32)
    x = x_ref[...].astype(f32)
    x = x * lax.rsqrt(jnp.mean(x * x, axis=-1, keepdims=True) + eps)
    h_ref[...] = (x * row_ref[0:1, :]).astype(bf16)
    for e in range(experts):
        smaller = key_ref[:, e : e + 1] < turned_ref[e : e + 1, :]
        rank_ref[e : e + 1, :] = jnp.sum(jnp.where(smaller, 1.0, 0.0), axis=0, keepdims=True)

    def rotate(value):
        return value * cos_ref[...] + pltpu.roll(value, size // 2, 1) * sin_ref[...]

    def normed(value):
        return value * lax.rsqrt(jnp.mean(value * value, axis=-1, keepdims=True) + eps)

    query_pos = lax.broadcasted_iota(jnp.int32, (tokens, tokens), 0)
    key_pos = lax.broadcasted_iota(jnp.int32, (tokens, tokens), 1)
    allowed = (key_pos <= query_pos) & (key_pos < length_ref[0])

    def lanes(start):
        return pl.ds(pl.multiple_of(start, size), size)

    first = gather.events()
    first.insert(len(first) - len(first) // 6, extra.begin)
    second = extra.events()

    def shares(events, start, stop):
        each = -(-len(events) // (stop - start))
        return {start + n: events[n * each : (n + 1) * each] for n in range(stop - start)}

    plan = {**shares(first, 0, early), **shares(second, early, turns)}

    def turn(i, carry):
        @pl.when(i < chunks)
        def _():
            @pl.when(i + 1 < chunks)
            def _():
                mat_copy(i + 1).start()

            mat_copy(i).wait()
            columns = pl.ds(pl.multiple_of(i * COLUMNS, COLUMNS), COLUMNS)
            proj_ref[:, columns] = jnp.dot(h_ref[...], mat_buf[i % 2], preferred_element_type=f32)

        @pl.when((i >= chunks) & (i < early))
        def _():
            pair = i - chunks
            group = pair // (groups // 2)

            @pl.when(pair % (groups // 2) == 0)
            def _():
                key = normed(proj_ref[:, lanes(wide_q + group * size)])
                k_low[...] = rotate(key * gains_ref[1:2, :]).astype(bf16)
                v_low[...] = proj_ref[:, lanes(wide_q + wide_kv + group * size)].astype(bf16)

            for n in range(2):
                head = pair * 2 + n
                query = rotate(normed(proj_ref[:, lanes(head * size)]) * gains_ref[0:1, :]).astype(bf16)
                scores = lax.dot_general(query, k_low[...], NT, preferred_element_type=f32) * scale
                scores = jnp.where(allowed, scores, -1e30)
                raised = jnp.exp(scores - jnp.max(scores, axis=1, keepdims=True))
                probs = (raised * (1.0 / jnp.sum(raised, axis=1, keepdims=True))).astype(bf16)
                att_ref[:, lanes(head * size)] = jnp.dot(
                    probs, v_low[...], preferred_element_type=f32
                ).astype(bf16)

        @pl.when(i >= early)
        def _():
            n = i - early

            @pl.when(n == 0)
            def _():
                gather.local().wait()
                wo_copy(0).start()
                middle_ref[...] = x_ref[...].astype(f32)

            @pl.when(i + 1 < turns)
            def _():
                wo_copy(n + 1).start()

            wo_copy(n).wait()
            columns = pl.ds(pl.multiple_of(n * deep, deep), deep)
            middle_ref[...] += jnp.dot(
                att_ref[:, columns], wo_buf[n % 2].reshape(deep, width), preferred_element_type=f32
            )

        for k, mine in plan.items():
            if mine:

                @pl.when(i == k)
                def _(mine=mine):
                    for event in mine:
                        event()

        return carry

    lax.fori_loop(0, turns, turn, 0)
    step = 64
    for r in range(0, tokens, step):
        low = (normed(middle_ref[r : r + step, :]) * row_ref[1:2, :]).astype(bf16)
        second_ref[r : r + step, :] = low
    logit_ref[...] = jnp.dot(second_ref[...], small_ref[...], preferred_element_type=f32)
    gather.end()
    extra.end()
    extra.local().wait()


def attention_front(
    length, x, small, gains, cos, sin, key, mat, w_o, own_g, n_rep, n_ep, heads_kv, groups, collective_id
):
    tokens, width = x.shape
    size = gains.shape[1]
    experts = key.shape[1]
    vmem = pl.BlockSpec(memory_space=pltpu.VMEM)
    anywhere = pl.BlockSpec(memory_space=pl.ANY)
    wide_q = heads_kv * groups * size
    wide_all = wide_q + 2 * heads_kv * size
    return pl.pallas_call(
        functools.partial(attention_front_kernel, n_rep, n_ep, experts, heads_kv, groups, size ** (-0.5)),
        out_shape=(
            jax.ShapeDtypeStruct((tokens, width), bf16),
            jax.ShapeDtypeStruct((tokens, wide_all), f32),
            jax.ShapeDtypeStruct((tokens, wide_q), bf16),
            jax.ShapeDtypeStruct((tokens, width), f32),
            jax.ShapeDtypeStruct((tokens, width), bf16),
            jax.ShapeDtypeStruct((tokens, EXT), f32),
            jax.ShapeDtypeStruct((8, width), f32),
            jax.ShapeDtypeStruct((experts, tokens), f32),
            jax.ShapeDtypeStruct((n_rep, n_ep) + w_o.shape, bf16),
            jax.ShapeDtypeStruct((1, n_ep) + own_g.shape, bf16),
        ),
        in_specs=[pl.BlockSpec(memory_space=pltpu.SMEM)] + [vmem] * 7 + [anywhere] * 3,
        out_specs=(vmem,) * 8 + (anywhere,) * 2,
        scratch_shapes=[
            pltpu.VMEM((2, width, COLUMNS), bf16),
            pltpu.SemaphoreType.DMA((2,)),
            pltpu.VMEM((tokens, size), bf16),
            pltpu.VMEM((tokens, size), bf16),
            pltpu.VMEM((2, n_ep // 2) + w_o.shape, bf16),
            pltpu.SemaphoreType.DMA((2,)),
        ]
        + BlockGather.sems(n_rep, n_ep)
        + BlockGather.sems(1, n_ep),
        compiler_params=pltpu.CompilerParams(
            collective_id=collective_id, has_side_effects=True, vmem_limit_bytes=VMEM_BYTES
        ),
        cost_estimate=pl.CostEstimate(flops=1000, bytes_accessed=1000, transcendentals=0),
        name="attention_front",
    )(length, x, small, gains, cos, sin, key, key.T, mat, w_o, own_g)


def unpack_kernel(shares, *refs):
    packs, outs = refs[: len(refs) - 3], refs[len(refs) - 3 :]
    for local, pack in enumerate(packs):
        start = 0
        for out, rows in zip(outs, shares):
            for p in range(out.shape[2] // LANES):
                out[local, :, p * LANES : (p + 1) * LANES] = pack[0, start : start + rows, :].astype(f32)
                start += rows


def unpack(packs, wide_share, tall_share, width, hidden):
    count = len(packs)
    vmem = pl.BlockSpec(memory_space=pltpu.VMEM)
    return pl.pallas_call(
        functools.partial(unpack_kernel, (wide_share, wide_share, tall_share)),
        out_shape=(
            jax.ShapeDtypeStruct((count, wide_share, hidden), f32),
            jax.ShapeDtypeStruct((count, wide_share, hidden), f32),
            jax.ShapeDtypeStruct((count, tall_share, width), f32),
        ),
        in_specs=[vmem] * count,
        out_specs=(vmem,) * 3,
        compiler_params=pltpu.CompilerParams(vmem_limit_bytes=VMEM_BYTES),
        cost_estimate=pl.CostEstimate(flops=1000, bytes_accessed=1000, transcendentals=0),
        name="unpack",
    )(*packs)


class TokenSum:
    def __init__(self, count, y_ref, starts, results, scratch):
        self.bits = bits_of(count)
        self.y_ref, self.results = y_ref, results
        self.own, self.got = scratch[:2], scratch[2:4]
        self.send_sem, self.recv_sem, self.own_sem = scratch[4:7]
        self.rep, self.me = lax.axis_index("rep"), lax.axis_index("ep")
        self.orders = [list(reversed(o)) for o in gather_orders(count)]
        self.columns = [pl.ds(s, o.shape[2]) for s, o in zip(starts, self.own)]
        self.masks = [
            [list(reversed(spans(self.orders[h][k + 1 :]))) for k in range(self.bits)] for h in range(2)
        ]
        self.slots, self.seats = [], []
        for h in range(2):
            table = {}
            for stage in range(self.bits):
                for mask in self.masks[h][stage]:
                    table[(stage, mask)] = len(table)
            self.slots.append(table)
            self.seats.append({mask: i for i, mask in enumerate(self.masks[h][0])})

    @staticmethod
    def scratch(count, rows, widths):
        half = count // 2
        return [
            pltpu.VMEM((half, rows, widths[0]), bf16),
            pltpu.VMEM((half, rows, widths[1]), bf16),
            pltpu.VMEM((count - 1, rows, widths[0]), bf16),
            pltpu.VMEM((count - 1, rows, widths[1]), bf16),
            pltpu.SemaphoreType.DMA((2, count)),
            pltpu.SemaphoreType.DMA((2, count)),
            pltpu.SemaphoreType.DMA((2, half)),
        ]

    def meet(self):
        meet([(self.rep, self.me ^ (1 << b)) for b in range(self.bits)])

    def copy(self, h, stage, mask):
        bit = 1 << self.orders[h][stage]
        slot = self.slots[h][(stage, mask)]
        if stage == 0:
            source = self.y_ref.at[self.me ^ bit ^ mask, :, self.columns[h]]
        else:
            source = self.own[h].at[self.seats[h][bit | mask]]
        return pltpu.make_async_remote_copy(
            src_ref=source,
            dst_ref=self.got[h].at[slot],
            send_sem=self.send_sem.at[h, slot],
            recv_sem=self.recv_sem.at[h, slot],
            device_id=(self.rep, self.me ^ bit),
            device_id_type=MESH,
        )

    def load(self, h, mask):
        seat = self.seats[h][mask]
        return pltpu.make_async_copy(
            self.y_ref.at[self.me ^ mask, :, self.columns[h]], self.own[h].at[seat], self.own_sem.at[h, seat]
        )

    def begin(self):
        for i in range(len(self.masks[0][0])):
            for h in range(2):
                self.copy(h, 0, self.masks[h][0][i]).start()
                self.load(h, self.masks[h][0][i]).start()

    def add(self, h, stage, mask):
        slot, seat = self.slots[h][(stage, mask)], self.seats[h][mask]
        own, got = self.own[h], self.got[h]
        if stage == 0:
            self.load(h, mask).wait()
        self.copy(h, stage, mask).wait_recv()
        step = 32

        def body(i, carry):
            rows = pl.ds(pl.multiple_of(i * step, step), step)
            total = own[seat, rows, :].astype(f32) + got[slot, rows, :].astype(f32)
            if stage == self.bits - 1:
                self.results[h][rows, :] = total
            else:
                own[seat, rows, :] = total.astype(bf16)
            return carry

        lax.fori_loop(0, own.shape[1] // step, body, 0)

    def stage(self, stage):
        for i in range(len(self.masks[0][stage])):
            for h in range(2):
                mask = self.masks[h][stage][i]
                self.add(h, stage, mask)
                if stage + 1 < self.bits:
                    following = 1 << self.orders[h][stage + 1]
                    if mask & following:
                        self.copy(h, stage + 1, mask & ~following).start()

    def end(self):
        for h in range(2):
            for stage, mask in self.slots[h]:
                self.copy(h, stage, mask).wait_send()


def token_sum_kernel(count, starts, y_ref, first_ref, second_ref, *scratch):
    total = TokenSum(count, y_ref, starts, (first_ref, second_ref), scratch)
    total.meet()
    total.begin()
    for stage in range(total.bits):
        total.stage(stage)
    total.end()


def sum_tokens(y, count, starts, widths, collective_id):
    rows = y.shape[1]
    return pl.pallas_call(
        functools.partial(token_sum_kernel, count, starts),
        out_shape=tuple(jax.ShapeDtypeStruct((rows, w), f32) for w in widths),
        in_specs=[pl.BlockSpec(memory_space=pl.ANY)],
        out_specs=(pl.BlockSpec(memory_space=pltpu.VMEM),) * 2,
        scratch_shapes=TokenSum.scratch(count, rows, widths),
        compiler_params=pltpu.CompilerParams(
            collective_id=collective_id, has_side_effects=True, vmem_limit_bytes=VMEM_BYTES
        ),
        cost_estimate=pl.CostEstimate(flops=1000, bytes_accessed=1000, transcendentals=0),
        name="token_sum",
    )(y)


QUAD = 4


def attention_back_kernel(count, starts, heads_kv, groups, scale, *refs):
    (length_ref, proj_ref, gains_ref, cos_ref, sin_ref, mid_ref, wo_ref, y_ref) = refs[:8]
    right_ref, head_ref, first_ref, second_ref = refs[8:12]
    wo_buf, wo_sem, k_low, v_low, k_norm, dk_sum, dv_sum = refs[12:19]
    total = TokenSum(count, y_ref, starts, (first_ref, second_ref), refs[19:])
    size = gains_ref.shape[1]
    tokens = proj_ref.shape[0]
    heads_q = heads_kv * groups
    wide_q, wide_kv = heads_q * size, heads_kv * size
    per_group = groups // QUAD
    turns = heads_q // QUAD

    def wo_copy(i):
        rows = pl.ds(pl.multiple_of(i * QUAD * size, QUAD * size), QUAD * size)
        return pltpu.make_async_copy(wo_ref.at[rows], wo_buf.at[i % 2], wo_sem.at[i % 2])

    wo_copy(0).start()
    total.meet()
    total.begin()
    head_ref[...] = jnp.zeros_like(head_ref)
    sent = right_ref.shape[1] - wide_q - 2 * wide_kv
    for n in range(sent // mid_ref.shape[1]):
        start = wide_q + 2 * wide_kv + n * mid_ref.shape[1]
        right_ref[:, start : start + mid_ref.shape[1]] = mid_ref[...]

    def rotate(value):
        return value * cos_ref[...] + pltpu.roll(value, size // 2, 1) * sin_ref[...]

    def rotate_back(value):
        return value * cos_ref[...] - pltpu.roll(value, size // 2, 1) * sin_ref[...]

    def norm_parts(value):
        inverse = lax.rsqrt(jnp.mean(value * value, axis=-1, keepdims=True) + eps)
        return value * inverse, inverse

    def project_back(gradient, normed, inverse, row):
        scaled = rotate_back(gradient)
        head_ref[row : row + 1, :] += jnp.sum(scaled * normed, axis=0, keepdims=True)
        lifted = scaled * gains_ref[row : row + 1, :]
        mean = jnp.mean(lifted * normed, axis=-1, keepdims=True)
        return (inverse * (lifted - normed * mean)).astype(bf16)

    key_pos = lax.broadcasted_iota(jnp.int32, (tokens, tokens), 0)
    query_pos = lax.broadcasted_iota(jnp.int32, (tokens, tokens), 1)
    allowed = (key_pos <= query_pos) & (key_pos < length_ref[0])

    def lanes(start):
        return pl.ds(pl.multiple_of(start, size), size)

    def turn(i, carry):
        group = i // per_group
        for stage, when in ((0, min(1, turns - 1)), (1, turns - 2)):

            @pl.when(i == when)
            def _(stage=stage):
                if stage < total.bits - 1:
                    total.stage(stage)

        @pl.when(i % per_group == 0)
        def _():
            normed, inverse = norm_parts(proj_ref[:, lanes(wide_q + group * size)])
            k_norm[:, :size] = normed
            k_norm[:, size:] = jnp.broadcast_to(inverse, normed.shape)
            k_low[...] = rotate(normed * gains_ref[1:2, :]).astype(bf16)
            v_low[...] = proj_ref[:, lanes(wide_q + wide_kv + group * size)].astype(bf16)
            dk_sum[...] = jnp.zeros_like(dk_sum)
            dv_sum[...] = jnp.zeros_like(dv_sum)

        @pl.when(i + 1 < turns)
        def _():
            wo_copy(i + 1).start()

        wo_copy(i).wait()
        d_att = lax.dot_general(mid_ref[...], wo_buf[i % 2], NT, preferred_element_type=f32).astype(bf16)
        keys, values = k_low[...], v_low[...]
        dk, dv = dk_sum[...], dv_sum[...]
        for n in range(QUAD):
            head = i * QUAD + n
            d_out = d_att[:, n * size : (n + 1) * size]
            normed, inverse = norm_parts(proj_ref[:, lanes(head * size)])
            query = rotate(normed * gains_ref[0:1, :]).astype(bf16)
            scores = lax.dot_general(keys, query, NT, preferred_element_type=f32) * scale
            scores = jnp.where(allowed, scores, -1e30)
            raised = jnp.exp(scores - jnp.max(scores, axis=0, keepdims=True))
            probs = raised * (1.0 / jnp.sum(raised, axis=0, keepdims=True))
            dv += jnp.dot(probs.astype(bf16), d_out, preferred_element_type=f32)
            d_probs = lax.dot_general(values, d_out, NT, preferred_element_type=f32)
            weighted = probs * d_probs
            d_scores = (weighted - probs * jnp.sum(weighted, axis=0, keepdims=True)).astype(bf16)
            dk += jnp.dot(d_scores, query, preferred_element_type=f32)
            d_query = lax.dot_general(d_scores, keys, TN, preferred_element_type=f32) * scale
            right_ref[:, lanes(head * size)] = project_back(d_query, normed, inverse, 0)
        dk_sum[...] = dk
        dv_sum[...] = dv

        @pl.when(i % per_group == per_group - 1)
        def _():
            right_ref[:, lanes(wide_q + group * size)] = project_back(
                dk_sum[...] * scale, k_norm[:, :size], k_norm[:, size:], 1
            )
            right_ref[:, lanes(wide_q + wide_kv + group * size)] = dv_sum[...].astype(bf16)

        return carry

    lax.fori_loop(0, turns, turn, 0)
    for stage in range(min(2, total.bits - 1), total.bits):
        total.stage(stage)
    total.end()


def attention_back(length, proj, gains, cos, sin, d_mid, mat_o, y, count, starts, widths, heads_kv, groups, collective_id):
    tokens, width = d_mid.shape
    size = gains.shape[1]
    vmem = pl.BlockSpec(memory_space=pltpu.VMEM)
    anywhere = pl.BlockSpec(memory_space=pl.ANY)
    columns = (heads_kv * groups + 2 * heads_kv) * size + 2 * width
    return pl.pallas_call(
        functools.partial(attention_back_kernel, count, starts, heads_kv, groups, size ** (-0.5)),
        out_shape=(
            jax.ShapeDtypeStruct((tokens, columns), bf16),
            jax.ShapeDtypeStruct((8, size), f32),
        )
        + tuple(jax.ShapeDtypeStruct((tokens, w), f32) for w in widths),
        in_specs=[pl.BlockSpec(memory_space=pltpu.SMEM)] + [vmem] * 5 + [anywhere] * 2,
        out_specs=(vmem,) * 4,
        scratch_shapes=[
            pltpu.VMEM((2, QUAD * size, width), bf16),
            pltpu.SemaphoreType.DMA((2,)),
            pltpu.VMEM((tokens, size), bf16),
            pltpu.VMEM((tokens, size), bf16),
            pltpu.VMEM((tokens, 2 * size), f32),
            pltpu.VMEM((tokens, size), f32),
            pltpu.VMEM((tokens, size), f32),
        ]
        + TokenSum.scratch(count, tokens, widths),
        compiler_params=pltpu.CompilerParams(
            collective_id=collective_id, has_side_effects=True, vmem_limit_bytes=VMEM_BYTES
        ),
        cost_estimate=pl.CostEstimate(flops=1000, bytes_accessed=1000, transcendentals=0),
        name="attention_back",
    )(length, proj, gains, cos, sin, d_mid, mat_o, y)


def dense_sum_kernel(n_rep, n_ep, rows, chunks, split, *refs):
    left_ref, right_ref, small_ref, head_ref, out_ref, head_out = refs[:6]
    rest = list(refs[6:])
    bits = bits_of(n_ep)
    wide = right_ref.shape[1] // (chunks - 1)
    half = wide // 2
    rep, me = lax.axis_index("rep"), lax.axis_index("ep")
    mine = [lax.rem(lax.div(me, 1 << b), 2) for b in range(bits)]
    part, got_core = rest[:2]
    acc = [None] + [rest[2 + 2 * k : 4 + 2 * k] for k in range(bits)]
    rest = rest[2 + 2 * bits :]
    got = [None] + [rest[2 * k : 2 * k + 2] for k in range(bits)]
    rest = rest[2 * bits :]
    head_own, head_got, head_rep = rest[:3]
    core_send, core_recv, step_send, step_recv, rep_send, rep_recv, head_send, head_recv, head_rs, head_rr = rest[3:]
    up = list(range(1, bits))
    orders = (up, up[::-1])
    left = [[sorted(set(up) - set(o[:k])) for k in range(bits)] for o in orders]
    lags = [0, 1]
    for _ in range(bits):
        lags.append(lags[-1] + 2)
    deep = 4
    others = [lax.rem(rep + d, n_rep) for d in range(1, n_rep)]
    meet([(rep, me ^ (1 << b)) for b in range(bits)] + [(other, me) for other in others])

    def core_copy(c):
        slot = lax.rem(c, 2)
        return pltpu.make_async_remote_copy(
            src_ref=part.at[slot, 1 - mine[0]],
            dst_ref=got_core.at[slot],
            send_sem=core_send.at[slot],
            recv_sem=core_recv.at[slot],
            device_id=(rep, me ^ 1),
            device_id_type=MESH,
        )

    def bit_copy(k, h, c):
        slot = lax.rem(c, deep)
        bit = orders[h][k - 1]
        place = left[h][k - 1].index(bit)
        return pltpu.make_async_remote_copy(
            src_ref=acc[k][h].at[(slot,) + (slice(None),) * place + (1 - mine[bit],)],
            dst_ref=got[k][h].at[slot],
            send_sem=step_send.at[k, h, slot],
            recv_sem=step_recv.at[k, h, slot],
            device_id=(rep, me ^ (1 << bit)),
            device_id_type=MESH,
        )

    def rep_copy(h, c, d):
        slot = lax.rem(c, deep)
        return pltpu.make_async_remote_copy(
            src_ref=acc[bits][h].at[slot, others[d]],
            dst_ref=got[bits][h].at[slot, n_rep - 2 - d],
            send_sem=rep_send.at[h, slot, d],
            recv_sem=rep_recv.at[h, slot, n_rep - 2 - d],
            device_id=(others[d], me),
            device_id_type=MESH,
        )

    corners = [()]
    for _ in up:
        corners = [c + (v,) for c in corners for v in range(2)]
    block = n_rep * rows
    side_rows = len(corners) * block

    def stage_make(c):
        slot = lax.rem(c, 2)

        @pl.when(c >= 2)
        def _():
            core_copy(c - 2).wait_send()

        @pl.when(c < chunks - 1)
        def _():
            which = jnp.where(c >= split[0], 1, 0) + jnp.where(c >= split[1], 1, 0)
            columns = pl.ds(pl.multiple_of(c * wide, wide), wide)
            weights = right_ref[:, columns]
            for side in (1, 0):
                which_side = 1 - mine[0] if side else mine[0]
                for n, corner in enumerate(corners):
                    start = (which * 2 + which_side) * side_rows + n * block
                    value = jnp.dot(
                        left_ref[pl.ds(pl.multiple_of(start, block), block), :],
                        weights,
                        preferred_element_type=f32,
                    )
                    part[(slot, which_side) + corner] = value.astype(bf16).reshape(n_rep, rows, wide)

        @pl.when(c == chunks - 1)
        def _():
            thin = small_ref.shape[1]
            for side in range(2):
                for n, corner in enumerate(corners):
                    value = small_ref[pl.ds(side * side_rows + n * block, block), :].reshape(n_rep, rows, thin)
                    blank = jnp.zeros((n_rep, rows, wide - thin), bf16)
                    part[(slot, side) + corner + (slice(None), slice(None), slice(0, thin))] = value
                    part[(slot, side) + corner + (slice(None), slice(None), slice(thin, wide))] = blank

        core_copy(c).start()

    def stage_core(c):
        slot, put = lax.rem(c, 2), lax.rem(c, deep)

        @pl.when(c >= deep)
        def _():
            for h in range(2):
                if bits > 1:
                    bit_copy(1, h, c - deep).wait_send()

        core_copy(c).wait_recv()
        for corner in corners:
            total = part[(slot, mine[0]) + corner].astype(f32) + got_core[(slot,) + corner].astype(f32)
            total = total.astype(bf16)
            for h in range(2):
                acc[1][h][(put,) + corner] = total[:, :, h * half : (h + 1) * half]
        for h in range(2):
            bit_copy(1, h, c).start()

    def stage_bit(k, c):
        slot = lax.rem(c, deep)
        for h in range(2):
            bit = orders[h][k - 2]
            place = left[h][k - 2].index(bit)

            @pl.when(c >= deep)
            def _(h=h):
                if k < bits:
                    bit_copy(k, h, c - deep).wait_send()
                else:
                    for d in range(n_rep - 1):
                        rep_copy(h, c - deep, d).wait_send()

            bit_copy(k - 1, h, c).wait_recv()
            small_corners = [()]
            for _ in left[h][k - 1]:
                small_corners = [q + (v,) for q in small_corners for v in range(2)]
            for corner in small_corners:
                full = corner[:place] + (mine[bit],) + corner[place:]
                total = acc[k - 1][h][(slot,) + full].astype(f32) + got[k - 1][h][(slot,) + corner].astype(f32)
                acc[k][h][(slot,) + corner] = total.astype(bf16)
            if k < bits:
                bit_copy(k, h, c).start()
            else:
                for d in range(n_rep - 1):
                    rep_copy(h, c, d).start()

    def stage_end(c):
        slot = lax.rem(c, deep)
        for h in range(2):
            total = acc[bits][h][slot, rep].astype(f32)
            for d in range(n_rep - 1):
                rep_copy(h, c, d).wait_recv()
            for d in range(n_rep - 1):
                total += got[bits][h][slot, d].astype(f32)
            out_ref[:, pl.ds(pl.multiple_of(c * wide + h * half, half), half)] = total

    def head_copy(t):
        return pltpu.make_async_remote_copy(
            src_ref=head_own.at[t],
            dst_ref=head_got.at[t],
            send_sem=head_send.at[t],
            recv_sem=head_recv.at[t],
            device_id=(rep, me ^ (1 << t)),
            device_id_type=MESH,
        )

    def head_rep_copy(d):
        return pltpu.make_async_remote_copy(
            src_ref=head_own.at[bits],
            dst_ref=head_rep.at[rep],
            send_sem=head_rs.at[d],
            recv_sem=head_rr.at[n_rep - 2 - d],
            device_id=(others[d], me),
            device_id_type=MESH,
        )

    def head_step(t):
        if t == 0:
            head_own[0] = head_ref[...]
            head_copy(0).start()
        elif t <= bits:
            head_copy(t - 1).wait_recv()
            head_own[t] = head_own[t - 1] + head_got[t - 1]
            if t < bits:
                head_copy(t).start()
            else:
                for d in range(n_rep - 1):
                    head_rep_copy(d).start()
                head_rep[rep] = head_own[bits]
        else:
            for d in range(n_rep - 1):
                head_rep_copy(d).wait_recv()
            total = head_rep[0]
            for r in range(1, n_rep):
                total = total + head_rep[r]
            head_out[...] = total

    def step(i, carry):
        for stage in reversed(range(len(lags))):
            c = i - lags[stage]

            @pl.when((c >= 0) & (c < chunks))
            def _(stage=stage, c=c):
                if stage == 0:
                    stage_make(c)
                elif stage == 1:
                    stage_core(c)
                elif stage <= bits:
                    stage_bit(stage, c)
                else:
                    stage_end(c)

        for t in range(bits + 2):

            @pl.when(i == t)
            def _(t=t):
                head_step(t)

        return carry

    lax.fori_loop(0, chunks + lags[-1], step, 0)
    for c in range(chunks - 2, chunks):
        core_copy(c).wait_send()
    for c in range(chunks - deep, chunks):
        for h in range(2):
            for k in range(1, bits):
                bit_copy(k, h, c).wait_send()
            for d in range(n_rep - 1):
                rep_copy(h, c, d).wait_send()
    for t in range(bits):
        head_copy(t).wait_send()
    for d in range(n_rep - 1):
        head_rep_copy(d).wait_send()


def dense_sum(left, right, small, head, n_rep, n_ep, split, collective_id):
    chunk = 512
    chunks = right.shape[1] // chunk + 1
    bits = bits_of(n_ep)
    rows = left.shape[0] // (3 * n_rep * n_ep)
    deep = 4
    half = chunk // 2
    vmem = pl.BlockSpec(memory_space=pltpu.VMEM)
    inner = (n_rep, rows)
    scratch = [
        pltpu.VMEM((2, 2) + (2,) * (bits - 1) + inner + (chunk,), bf16),
        pltpu.VMEM((2,) + (2,) * (bits - 1) + inner + (chunk,), bf16),
    ]
    for k in range(1, bits + 1):
        scratch += [pltpu.VMEM((deep,) + (2,) * (bits - k) + inner + (half,), bf16)] * 2
    for k in range(1, bits):
        scratch += [pltpu.VMEM((deep,) + (2,) * (bits - 1 - k) + inner + (half,), bf16)] * 2
    scratch += [pltpu.VMEM((deep, n_rep - 1, rows, half), bf16)] * 2
    scratch += [
        pltpu.VMEM((bits + 1,) + head.shape, f32),
        pltpu.VMEM((bits,) + head.shape, f32),
        pltpu.VMEM((n_rep,) + head.shape, f32),
        pltpu.SemaphoreType.DMA((2,)),
        pltpu.SemaphoreType.DMA((2,)),
        pltpu.SemaphoreType.DMA((bits, 2, deep)),
        pltpu.SemaphoreType.DMA((bits, 2, deep)),
        pltpu.SemaphoreType.DMA((2, deep, n_rep - 1)),
        pltpu.SemaphoreType.DMA((2, deep, n_rep - 1)),
        pltpu.SemaphoreType.DMA((bits,)),
        pltpu.SemaphoreType.DMA((bits,)),
        pltpu.SemaphoreType.DMA((n_rep - 1,)),
        pltpu.SemaphoreType.DMA((n_rep - 1,)),
    ]
    return pl.pallas_call(
        functools.partial(dense_sum_kernel, n_rep, n_ep, rows, chunks, split),
        out_shape=(
            jax.ShapeDtypeStruct((rows, chunks * chunk), f32),
            jax.ShapeDtypeStruct(head.shape, f32),
        ),
        in_specs=[vmem] * 4,
        out_specs=(vmem, vmem),
        scratch_shapes=scratch,
        compiler_params=pltpu.CompilerParams(
            collective_id=collective_id, has_side_effects=True, vmem_limit_bytes=VMEM_BYTES
        ),
        cost_estimate=pl.CostEstimate(flops=1000, bytes_accessed=1000, transcendentals=0),
        name="dense_sum",
    )(left, right, small, head)


def expert_kernel(local, first, last, experts, width, hidden_of, *refs):
    (info, h_ref, g_ref, wg_all, wu_all, wd_all) = refs[:6]
    rest = list(refs[6:])
    prev_ref = None if first else rest.pop(0)
    y_ref, grad_ref = rest[:2]
    xs, gs, ds, hs, stage, prev_buf, wide, tall, in_sem, out_sem, prev_sem, grad_sem = rest[2:14]
    wg_ref, wu_ref, wd_ref, weight_sem = rest[14:]
    weights = [
        pltpu.make_async_copy(source.at[local], target, weight_sem.at[n])
        for n, (source, target) in enumerate(((wg_all, wg_ref), (wu_all, wu_ref), (wd_all, wd_ref)))
    ]
    for copy in weights:
        copy.start()
    shares = grad_ref.shape[0]
    wide_share, tall_share = width // shares, hidden_of // shares
    hidden = wg_ref.shape[1]
    units = info[0]
    expert = info[1]
    table = 8
    per_tile = TILE // UNIT
    tiles = (units + per_tile - 1) // per_tile
    most = xs.shape[0] // TILE
    floor_tiles = min(4, most)

    def unit_in(u, slot):
        source = pl.ds(pl.multiple_of(info[table + u], UNIT), UNIT)
        target = pl.ds(pl.multiple_of(u * UNIT, UNIT), UNIT)
        return (
            pltpu.make_async_copy(h_ref.at[source], xs.at[target], in_sem.at[0, slot]),
            pltpu.make_async_copy(g_ref.at[source], gs.at[target], in_sem.at[1, slot]),
        )

    def begin(u, carry):
        for copy in unit_in(u, u // per_tile):
            copy.start()
        return carry

    lax.fori_loop(0, units, begin, 0)

    def blank(u, carry):
        target = pl.ds(pl.multiple_of(u * UNIT, UNIT), UNIT)
        xs[target, :] = jnp.zeros((UNIT, xs.shape[1]), bf16)
        gs[target, :] = jnp.zeros((UNIT, gs.shape[1]), bf16)
        return carry

    lax.fori_loop(units, jnp.maximum(tiles, floor_tiles) * per_tile, blank, 0)

    def blank_tile(i, carry):
        target = pl.ds(pl.multiple_of(i * TILE, TILE), TILE)
        ds[target, :] = jnp.zeros((TILE, ds.shape[1]), bf16)
        hs[target, :] = jnp.zeros((TILE, hs.shape[1]), bf16)
        return carry

    lax.fori_loop(tiles, floor_tiles, blank_tile, 0)

    def prev_copy(i):
        rows = pl.ds(pl.multiple_of(i * TILE, TILE), TILE)
        return pltpu.make_async_copy(prev_ref.at[rows], prev_buf.at[i % 2], prev_sem.at[i % 2])

    if not first:
        prev_copy(0).start()

    def unit_out(u):
        target = pl.ds(pl.multiple_of(info[table + u], UNIT), UNIT)
        tile = u // per_tile
        source = pl.ds(pl.multiple_of((u % per_tile) * UNIT, UNIT), UNIT)
        return pltpu.make_async_copy(stage.at[tile % 2, source], y_ref.at[target], out_sem.at[tile % 2])

    def out_start(i):
        if last:
            lax.fori_loop(
                i * per_tile,
                jnp.minimum((i + 1) * per_tile, units),
                lambda u, c: (unit_out(u).start(), c)[1],
                0,
            )
        else:
            rows = pl.ds(pl.multiple_of(i * TILE, TILE), TILE)
            pltpu.make_async_copy(stage.at[i % 2], y_ref.at[rows], out_sem.at[i % 2]).start()

    def out_wait(i):
        if last:
            lax.fori_loop(
                i * per_tile,
                jnp.minimum((i + 1) * per_tile, units),
                lambda u, c: (unit_out(u).wait(), c)[1],
                0,
            )
        else:
            rows = pl.ds(pl.multiple_of(i * TILE, TILE), TILE)
            pltpu.make_async_copy(stage.at[i % 2], y_ref.at[rows], out_sem.at[i % 2]).wait()

    lane = lax.broadcasted_iota(jnp.int32, (TILE, EXT), 1)
    weight_lanes = (lane == expert) | (lane == expert + experts) | (lane == expert + 2 * experts)

    def tile_step(i, carry):
        def landed(u, c):
            for copy in unit_in(u, i):
                copy.wait()
            return c

        lax.fori_loop(i * per_tile, jnp.minimum((i + 1) * per_tile, units), landed, 0)
        rows = pl.ds(pl.multiple_of(i * TILE, TILE), TILE)
        x = xs[rows, :width]
        g = gs[rows, :]
        extra = xs[rows, width:].astype(f32)
        weight = jnp.sum(jnp.where(weight_lanes, extra, 0.0), axis=1, keepdims=True)
        gate = jnp.dot(x, wg_ref[...], preferred_element_type=f32)
        up = jnp.dot(x, wu_ref[...], preferred_element_type=f32)
        d_plain = lax.dot_general(g, wd_ref[...], NT, preferred_element_type=f32)
        sig = 1.0 / (1.0 + jnp.exp(-gate))
        silu = gate * sig
        hid = silu * up
        d_weight = jnp.sum(hid.astype(bf16).astype(f32) * d_plain, axis=1, keepdims=True)
        hs[rows, :] = (hid * weight).astype(bf16)
        d_hidden = d_plain * weight
        ds[rows, :hidden] = (d_hidden * up * sig * (1.0 + gate * (1.0 - sig))).astype(bf16)
        ds[rows, hidden:] = (d_hidden * silu).astype(bf16)

        @pl.when(i >= 2)
        def _():
            out_wait(i - 2)

        if not first:

            @pl.when(i + 1 < tiles)
            def _():
                prev_copy(i + 1).start()

            prev_copy(i).wait()
        slot = i % 2
        high = d_weight.astype(bf16).astype(f32)
        low = d_weight - high
        note = jnp.where(lane == expert, high, 0.0) + jnp.where(lane == expert + experts, low, 0.0)
        d_row = lax.dot_general(ds[rows, :hidden], wg_ref[...], NT, preferred_element_type=f32)
        d_row += lax.dot_general(ds[rows, hidden:], wu_ref[...], NT, preferred_element_type=f32)
        if not first:
            d_row += prev_buf[slot, :, :width].astype(f32)
            note += prev_buf[slot, :, width : width + EXT].astype(f32)
        stage[slot, :, :width] = d_row.astype(bf16)
        stage[slot, :, width : width + EXT] = note.astype(bf16)
        out = jnp.dot(hs[rows, :], wd_ref[...], preferred_element_type=f32)
        if not first:
            out += prev_buf[slot, :, width + EXT :].astype(f32)
        stage[slot, :, width + EXT :] = out.astype(bf16)
        out_start(i)
        return carry

    for copy in weights:
        copy.wait()
    lax.fori_loop(0, tiles, tile_step, 0)

    block = 256

    def grads(depth):
        def wide_copies(m):
            per = wide_share // block
            return tuple(
                pltpu.make_async_copy(
                    wide.at[m % 2, :, p * LANES : (p + 1) * LANES],
                    grad_ref.at[
                        m // per,
                        pl.ds(pl.multiple_of(p * wide_share + (m % per) * block, block), block),
                    ],
                    grad_sem.at[m % 2, p],
                )
                for p in range(2 * hidden // LANES)
            )

        def wide_step(m, carry):
            @pl.when(m >= 2)
            def _():
                for copy in wide_copies(m - 2):
                    copy.wait()

            columns = pl.ds(pl.multiple_of(m * block, block), block)
            wide[m % 2] = lax.dot_general(
                xs[:depth, columns], ds[:depth, :], TN, preferred_element_type=f32
            ).astype(bf16)
            for copy in wide_copies(m):
                copy.start()
            return carry

        count = width // block
        lax.fori_loop(0, count, wide_step, 0)
        for m in range(count - 2, count):
            for copy in wide_copies(m):
                copy.wait()

        piece = math.gcd(block, tall_share)
        base = 2 * hidden // LANES * wide_share

        def tall_copies(m):
            made = []
            for q in range(block // piece):
                first_row = m * block + q * piece
                share, inside = first_row // tall_share, first_row % tall_share
                for p in range(width // LANES):
                    rows = pl.ds(pl.multiple_of(base + p * tall_share + inside, piece), piece)
                    made.append(
                        pltpu.make_async_copy(
                            tall.at[m % 2, q * piece : (q + 1) * piece, p * LANES : (p + 1) * LANES],
                            grad_ref.at[share, rows],
                            grad_sem.at[m % 2, q * (width // LANES) + p],
                        )
                    )
            return made

        def tall_step(m, carry):
            @pl.when(m >= 2)
            def _():
                for copy in tall_copies(m - 2):
                    copy.wait()

            columns = pl.ds(pl.multiple_of(m * block, block), block)
            tall[m % 2] = lax.dot_general(
                hs[:depth, columns], gs[:depth, :], TN, preferred_element_type=f32
            ).astype(bf16)
            for copy in tall_copies(m):
                copy.start()
            return carry

        count = hidden // block
        lax.fori_loop(0, count, tall_step, 0)
        for m in range(count - 2, count):
            for copy in tall_copies(m):
                copy.wait()

    for choice in range(floor_tiles, most + 1):
        chosen = (tiles <= choice) if choice == floor_tiles else (tiles == choice)

        @pl.when(chosen)
        def _(choice=choice):
            grads(choice * TILE)

    @pl.when(tiles >= 2)
    def _():
        out_wait(tiles - 2)

    out_wait(tiles - 1)


def expert_pass(info, h_rows, g_rows, w_gate, w_up, w_down, local, prev, last, experts, shares):
    tokens, width = g_rows.shape
    hidden = w_gate.shape[2]
    wide_row = width + EXT + width
    any_spec = pl.BlockSpec(memory_space=pl.ANY)
    first = prev is None
    operands = [info, h_rows, g_rows, w_gate, w_up, w_down] + ([] if first else [prev])
    specs = [pl.BlockSpec(memory_space=pltpu.SMEM), any_spec, any_spec, any_spec, any_spec, any_spec]
    specs += [] if first else [any_spec]
    return pl.pallas_call(
        functools.partial(expert_kernel, local, first, last, experts, width, hidden),
        out_shape=(
            jax.ShapeDtypeStruct((tokens, wide_row), bf16),
            jax.ShapeDtypeStruct((shares, 3 * hidden * width // shares // LANES, LANES), bf16),
        ),
        in_specs=specs,
        out_specs=(any_spec,) * 2,
        scratch_shapes=[
            pltpu.VMEM((tokens, width + EXT), bf16),
            pltpu.VMEM((tokens, width), bf16),
            pltpu.VMEM((tokens, 2 * hidden), bf16),
            pltpu.VMEM((tokens, hidden), bf16),
            pltpu.VMEM((2, TILE, wide_row), bf16),
            pltpu.VMEM((2, TILE, wide_row), bf16),
            pltpu.VMEM((2, 256, 2 * hidden), bf16),
            pltpu.VMEM((2, 256, width), bf16),
            pltpu.SemaphoreType.DMA((2, tokens // TILE)),
            pltpu.SemaphoreType.DMA((2,)),
            pltpu.SemaphoreType.DMA((2,)),
            pltpu.SemaphoreType.DMA((2, max(2 * hidden // LANES, 256 // math.gcd(256, hidden // shares) * width // LANES))),
            pltpu.VMEM((width, hidden), bf16),
            pltpu.VMEM((width, hidden), bf16),
            pltpu.VMEM((hidden, width), bf16),
            pltpu.SemaphoreType.DMA((3,)),
        ],
        compiler_params=pltpu.CompilerParams(vmem_limit_bytes=VMEM_BYTES),
        cost_estimate=pl.CostEstimate(flops=1000, bytes_accessed=1000, transcendentals=0),
        name="experts",
    )(*operands)


def unit_table(lengths):
    per_sequence = TILE // UNIT
    counts = (lengths + UNIT - 1) // UNIT
    unit = jnp.arange(lengths.shape[0] * per_sequence, dtype=jnp.int32)
    live = (unit % per_sequence) < jnp.repeat(counts, per_sequence)
    place = jnp.cumsum(live.astype(jnp.int32)) - 1
    hit = (place[None, :] == unit[:, None]) & live[None, :]
    rows = jnp.sum(jnp.where(hit, unit[None, :] * UNIT, 0), axis=1)
    return (jnp.sum(counts), rows)


def split_three(value):
    high = lax.reduce_precision(value, 8, 7)
    rest = value - high
    middle = lax.reduce_precision(rest, 8, 7)
    return jnp.concatenate([high, middle, rest - middle], axis=-1)


def per_device(
    hidden_in,
    out_grad,
    attn_gain,
    w_q,
    key_weight,
    value_weight,
    w_o,
    ffn_gain,
    router_w,
    qk_gains,
    w_gate,
    w_up,
    w_down,
    lengths,
    routes,
    order,
):
    everywhere = ("rep", "ep")
    rep_count, ep_count = (lax.axis_size("rep"), lax.axis_size("ep"))
    rep_index, ep_index = (lax.axis_index("rep"), lax.axis_index("ep"))
    inputs = hidden_in[0].astype(f32)
    sequence_length, model_width = inputs.shape
    head_size = qk_gains.shape[1]
    wide_q, wide_kv = (w_q.shape[1], key_weight.shape[1])
    heads_q, heads_kv = (wide_q // head_size, wide_kv // head_size)
    groups = heads_q // heads_kv
    local_experts = w_gate.shape[0]
    experts = local_experts * ep_count
    top_count = routes.shape[2]
    score_scale = head_size ** (-0.5)
    group_lengths = lax.dynamic_slice_in_dim(lengths, rep_index * ep_count, ep_count)
    length = lax.dynamic_index_in_dim(group_lengths, ep_index, keepdims=False)
    positions = jnp.arange(sequence_length, dtype=jnp.int32)
    live = positions < length
    live_rows = live.astype(f32)

    expert_iota = jnp.arange(experts, dtype=jnp.int32)
    route_hot = routes[0][..., None] == expert_iota
    routed = jnp.any(route_hot, axis=1) & live[:, None]
    order_of = jnp.sum(
        jnp.where(route_hot, order[0].reshape(sequence_length, top_count)[..., None], 0), axis=1
    )
    sort_key = jnp.where(routed, order_of, sequence_length * top_count)
    loads = jnp.sum(routed.astype(jnp.int32), axis=0)

    own_rows = w_q.shape[0]
    load_columns = -(-experts // own_rows)
    load_block = jnp.pad(loads, (0, load_columns * own_rows - experts)).reshape(load_columns, own_rows).T
    small = jnp.concatenate(
        [router_w, attn_gain[:, None], ffn_gain[:, None], load_block.astype(bf16)], axis=1
    )
    small = jnp.pad(small, ((0, 0), (0, EXT - small.shape[1])))
    pack = jnp.concatenate([w_q, key_weight, value_weight, small], axis=1)
    mat_qkv = gather_weights(pack, rep_count, ep_count, 4).reshape(-1, pack.shape[1])

    wide_all = wide_q + 2 * wide_kv
    small_all = mat_qkv[:, wide_all:]
    mat_router = small_all[:, :experts]
    loads_all = (
        small_all[:, experts + 2 : experts + 2 + load_columns]
        .reshape(rep_count, ep_count, own_rows, load_columns)
        .transpose(0, 1, 3, 2)
        .reshape(rep_count, ep_count, load_columns * own_rows)[:, :, :experts]
        .astype(jnp.int32)
    )
    group_loads = lax.dynamic_index_in_dim(loads_all, rep_index, keepdims=False)
    earlier = (jnp.arange(ep_count) < ep_index)[:, None]
    load_prefix = jnp.sum(jnp.where(earlier, group_loads, 0), axis=0)
    capacity = 9 * top_count * jnp.sum(group_lengths) // (8 * experts)

    cosine_lookup, sine_lookup = rope_tables(sequence_length, head_size)
    sign = jnp.where(jnp.arange(head_size) < head_size // 2, -1.0, 1.0).astype(f32)
    turned_sine = sine_lookup * sign[None, :]
    (
        hidden_first,
        projected,
        attended,
        middle,
        h_two,
        logits,
        row_gain,
        rank,
        mat_o,
        grads_all,
    ) = attention_front(
        length.reshape(1),
        hidden_in[0],
        small_all,
        qk_gains.astype(f32),
        cosine_lookup,
        turned_sine,
        sort_key.astype(f32),
        mat_qkv,
        w_o,
        out_grad[0],
        rep_count,
        ep_count,
        heads_kv,
        groups,
        6,
    )
    logits = logits[:, :experts]
    gain_attn, gain_ffn = (row_gain[0], row_gain[1])
    mat_o = mat_o.reshape(-1, model_width)
    grads_all = grads_all.reshape(-1, model_width)
    norm_one, inv_one = rms_parts(inputs)
    norm_two, inv_two = rms_parts(middle)
    kept = routed & (load_prefix[None, :] + rank.T.astype(jnp.int32) < capacity)
    kept_float = kept.astype(f32)
    named = jnp.any(route_hot, axis=1)
    top_logit = jnp.max(jnp.where(named, logits, -jnp.inf), axis=1, keepdims=True)
    raised = jnp.where(named, jnp.exp(jnp.where(named, logits - top_logit, 0.0)), 0.0)
    route_gates = raised / jnp.sum(raised, axis=1, keepdims=True)
    pair_weight = route_gates * kept_float

    extra = split_three(pair_weight).astype(bf16)
    extra = jnp.pad(extra, ((0, 0), (0, EXT - extra.shape[1])))
    sent = jnp.concatenate([h_two, extra], axis=1)
    h_all = gather_tokens(sent, ep_count, 1)

    part = min(ep_count, 8)
    tokens = part * sequence_length
    sums = []
    y_parts = []
    for c in range(ep_count // part):
        live_units, unit_rows = unit_table(group_lengths[c * part : (c + 1) * part])
        h_rows = h_all[c * part : (c + 1) * part].reshape(tokens, model_width + EXT)
        g_rows = grads_all[c * tokens : (c + 1) * tokens]
        prev, found = None, []
        for local in range(local_experts):
            info = jnp.concatenate(
                [
                    jnp.stack([live_units, ep_index * local_experts + local]).astype(jnp.int32),
                    jnp.zeros((6,), jnp.int32),
                    unit_rows,
                ]
            )
            prev, weight_grads = expert_pass(
                info,
                h_rows,
                g_rows,
                w_gate,
                w_up,
                w_down,
                local,
                prev,
                local == local_experts - 1,
                experts,
                rep_count,
            )
            found.append(weight_grads)
        y_parts.append(prev.reshape(part, sequence_length, -1))
        sums.append(found)
    y_all = y_parts[0] if len(y_parts) == 1 else jnp.concatenate(y_parts, axis=0)
    hidden_units = w_gate.shape[2]
    wide_share, tall_share = model_width // rep_count, hidden_units // rep_count
    found = []
    for local in range(local_experts):
        total = sums[0][local]
        for more in sums[1:]:
            total = (total.astype(f32) + more[local].astype(f32)).astype(bf16)
        found.append(lax.psum_scatter(total, "rep", scatter_dimension=0, tiled=True))
    expert_sums = unpack(found, wide_share, tall_share, model_width, hidden_units)

    half_width = model_width // 2
    row_first, row_second = sum_tokens(
        y_all, ep_count, (0, half_width), (half_width, half_width + EXT), 2
    )
    live_column = live[:, None]
    grad_rows = out_grad[0].astype(f32) * live_rows[:, None]
    notes = row_second[:, half_width : half_width + 2 * experts]
    d_weight = jnp.where(live_column, notes[:, :experts] + notes[:, experts:], 0.0)
    d_gates = d_weight * kept_float
    d_logits = route_gates * (d_gates - jnp.sum(route_gates * d_gates, axis=-1, keepdims=True))

    router_float = mat_router.astype(f32)
    d_h_two = jnp.concatenate([row_first, row_second[:, :half_width]], axis=1)
    d_h_two = jnp.where(live_column, d_h_two, 0.0)
    d_h_two = d_h_two + jnp.dot(d_logits, router_float.T, precision=top_precision)
    grad_router = jnp.dot(h_two.astype(f32).T, d_logits, precision=top_precision)
    grad_ffn = jnp.sum(d_h_two * norm_two, axis=0)
    d_middle = grad_rows + rms_back(d_h_two * gain_ffn, norm_two, inv_two)
    d_middle_low = d_middle.astype(bf16)
    right, head, out_first, out_second = attention_back(
        length.reshape(1),
        projected,
        qk_gains.astype(f32),
        cosine_lookup,
        turned_sine,
        d_middle_low,
        mat_o,
        y_all,
        ep_count,
        (model_width + EXT, model_width + EXT + half_width),
        (half_width, half_width),
        heads_kv,
        groups,
        5,
    )
    moe_output = jnp.where(live_column, jnp.concatenate([out_first, out_second], axis=1), 0.0)
    layer_out = jnp.where(live_column, middle + moe_output, 0.0)
    d_qkv = right[:, :wide_all]
    d_h_one = jnp.einsum("tf,cf->tc", d_qkv, mat_qkv[:, :wide_all], preferred_element_type=f32)
    grad_attn = jnp.sum(d_h_one * norm_one, axis=0)
    grad_input = d_middle + rms_back(d_h_one * gain_attn, norm_one, inv_one)

    small_grads = jnp.concatenate([grad_router, grad_attn[:, None], grad_ffn[:, None]], axis=1)
    small_grads = jnp.pad(small_grads, ((0, 0), (0, EXT - small_grads.shape[1]))).astype(bf16)
    ep_bits = bits_of(ep_count)

    def owner_order(value, parts):
        shape = (rep_count,) + (2,) * ep_bits + (parts, own_rows, value.shape[1])
        axes = (ep_bits + 1,) + tuple(range(ep_bits, 0, -1)) + (0, ep_bits + 2, ep_bits + 3)
        return value.reshape(shape).transpose(axes).reshape(value.shape)

    left = jnp.concatenate([owner_order(hidden_first.T, 1), owner_order(attended.T, 2)], axis=0)
    splits = (wide_all // 512, (wide_all + model_width) // 512)
    sums_all, head_sum = dense_sum(
        left, right, owner_order(small_grads, 1), head, rep_count, ep_count, splits, 3
    )
    sum_o = jnp.concatenate(
        [sums_all[:, wide_all : wide_all + model_width], sums_all[:, wide_all + model_width : wide_all + 2 * model_width]],
        axis=0,
    )
    small_sum = sums_all[:, wide_all + 2 * model_width :]
    return (
        layer_out[None],
        grad_input[None],
        small_sum[:, experts],
        sums_all[:, :wide_q],
        sums_all[:, wide_q : wide_q + wide_kv],
        sums_all[:, wide_q + wide_kv : wide_all],
        sum_o,
        small_sum[:, experts + 1],
        small_sum[:, :experts],
        head_sum[:2],
        expert_sums[0],
        expert_sums[1],
        expert_sums[2],
    )


def solution(mesh):
    both = ("rep", "ep")
    placed = (
        P(both, None, None),
        P(both, None, None),
        P(both),
        P(both, None),
        P(both, None),
        P(both, None),
        P(both, None),
        P(both),
        P(both, None),
        P(),
        P("ep", None, None),
        P("ep", None, None),
        P("ep", None, None),
        P(),
        P(both, None, None),
        P(both, None),
    )
    return jax.shard_map(
        per_device,
        mesh=mesh,
        in_specs=placed,
        out_specs=(
            P(both, None, None),
            P(both, None, None),
            P(both),
            P(both, None),
            P(both, None),
            P(both, None),
            P(both, None),
            P(both),
            P(both, None),
            P(),
            P("ep", "rep", None),
            P("ep", "rep", None),
            P("ep", "rep", None),
        ),
        check_vma=False,
    )
```

```python
import functools
import math

import jax
import jax.numpy as jnp
from jax import lax
from jax.experimental import pallas as pl
from jax.experimental.pallas import tpu as pltpu
from jax.sharding import PartitionSpec as P

eps = 1e-06
rope_base = 1000000.0
top_precision = lax.Precision.HIGHEST
MESH = pl.DeviceIdType.MESH
f32, bf16 = jnp.float32, jnp.bfloat16
EXT = 128
UNIT = 16
LANES = 256
TILE = 256
VMEM_BYTES = 58 * 1024 * 1024
NT = (((1,), (1,)), ((), ()))
TN = (((0,), (0,)), ((), ()))


def rms_parts(value_rows):
    inverse = lax.rsqrt(jnp.mean(value_rows * value_rows, axis=-1, keepdims=True) + eps)
    return (value_rows * inverse, inverse)


def rms_back(grad_norm, normed, inverse):
    return inverse * (grad_norm - normed * jnp.mean(grad_norm * normed, axis=-1, keepdims=True))


def rope_tables(count, head_size):
    half_size = head_size // 2
    freqs = rope_base ** (-2.0 * jnp.arange(half_size, dtype=f32) / head_size)
    angles = jnp.arange(count, dtype=f32)[:, None] * freqs[None, :]
    cosine_lookup = jnp.concatenate([jnp.cos(angles), jnp.cos(angles)], axis=1)
    sine_lookup = jnp.concatenate([jnp.sin(angles), jnp.sin(angles)], axis=1)
    return (cosine_lookup, sine_lookup)


def bits_of(count):
    return count.bit_length() - 1


def gather_orders(count):
    bits = bits_of(count)
    up = list(range(1, bits)) + [0]
    down = list(range(bits - 1, 0, -1)) + [0]
    return (up, down)


def spans(bits):
    masks = [0]
    for bit in bits:
        masks = masks + [m | (1 << bit) for m in masks]
    return masks


def meet(peers):
    barrier = pltpu.get_barrier_semaphore()
    for peer in peers:
        pl.semaphore_signal(barrier, inc=1, device_id=peer, device_id_type=MESH)
    pl.semaphore_wait(barrier, len(peers))


def token_gather_kernel(count, x_ref, out_ref, send_sem, recv_sem, local_sem):
    rep, me = lax.axis_index("rep"), lax.axis_index("ep")
    bits = bits_of(count)
    half = x_ref.shape[0] // 2
    meet([(rep, me ^ (1 << b)) for b in range(bits)])
    local = pltpu.make_async_copy(x_ref, out_ref.at[me], local_sem)
    local.start()
    orders = gather_orders(count)
    copies = []

    def send(h, mask, bit):
        rows = pl.ds(h * half, half)
        source = x_ref.at[rows] if mask == 0 else out_ref.at[me ^ mask, rows]
        there = mask | (1 << bit)
        copy = pltpu.make_async_remote_copy(
            src_ref=source,
            dst_ref=out_ref.at[me ^ mask, rows],
            send_sem=send_sem.at[h, there],
            recv_sem=recv_sem.at[h, there],
            device_id=(rep, me ^ (1 << bit)),
            device_id_type=MESH,
        )
        copy.start()
        copies.append(copy)

    def arrived(h, mask):
        rows = pl.ds(h * half, half)
        pltpu.make_async_copy(
            x_ref.at[rows], out_ref.at[me ^ mask, rows], recv_sem.at[h, mask]
        ).wait()

    for stage in range(bits):
        for h in range(2):
            send(h, 0, orders[h][stage])
    for stage in range(bits):
        for low in spans(orders[0][:stage]):
            index = spans(orders[0][:stage]).index(low)
            for h in range(2):
                mask = spans(orders[h][:stage])[index] | (1 << orders[h][stage])
                arrived(h, mask)
                for later in range(stage + 1, bits):
                    send(h, mask, orders[h][later])
    for copy in copies:
        copy.wait_send()
    local.wait()


def gather_tokens(x, count, collective_id):
    return pl.pallas_call(
        functools.partial(token_gather_kernel, count),
        out_shape=jax.ShapeDtypeStruct((count,) + x.shape, x.dtype),
        in_specs=[pl.BlockSpec(memory_space=pl.ANY)],
        out_specs=pl.BlockSpec(memory_space=pl.ANY),
        scratch_shapes=[
            pltpu.SemaphoreType.DMA((2, count)),
            pltpu.SemaphoreType.DMA((2, count)),
            pltpu.SemaphoreType.DMA,
        ],
        compiler_params=pltpu.CompilerParams(collective_id=collective_id, has_side_effects=True),
        name="token_gather",
    )(x)


class BlockGather:
    def __init__(self, n_rep, n_ep, x_ref, out_ref, sems):
        self.n_rep, self.bits = n_rep, bits_of(n_ep)
        self.x_ref, self.out_ref = x_ref, out_ref
        self.send_sem, self.recv_sem, self.up_sem, self.down_sem, self.local_sem = sems
        self.rep, self.me = lax.axis_index("rep"), lax.axis_index("ep")
        split = -(-x_ref.shape[1] // 256) * 128
        self.columns = (pl.ds(0, split), pl.ds(split, x_ref.shape[1] - split))
        self.orders = gather_orders(n_ep)
        self.entries = [(0, 0)]
        for s in range(1, n_rep):
            self.entries += [(s, -1), (s, 1)]

    @staticmethod
    def sems(n_rep, n_ep):
        return [
            pltpu.SemaphoreType.DMA((2 * n_rep - 1, 2, n_ep)),
            pltpu.SemaphoreType.DMA((2 * n_rep - 1, 2, n_ep)),
            pltpu.SemaphoreType.DMA((n_rep, 2)),
            pltpu.SemaphoreType.DMA((n_rep, 2)),
            pltpu.SemaphoreType.DMA,
        ]

    def meet(self):
        barrier = pltpu.get_barrier_semaphore()
        peers = [(self.rep, self.me ^ (1 << b)) for b in range(self.bits)]
        for peer in peers:
            pl.semaphore_signal(barrier, inc=1, device_id=peer, device_id_type=MESH)
        if self.n_rep > 1:
            for side in (-1, 1):

                @pl.when(self.reaches(side))
                def _(side=side):
                    pl.semaphore_signal(barrier, inc=1, device_id=(self.rep + side, self.me), device_id_type=MESH)

        count = len(peers)
        if self.n_rep > 1:
            count = count + jnp.where(self.reaches(-1), 1, 0) + jnp.where(self.reaches(1), 1, 0)
        pl.semaphore_wait(barrier, count)

    def reaches(self, side):
        return self.rep > 0 if side < 0 else self.rep < self.n_rep - 1

    def active(self, k):
        steps, side = self.entries[k]
        return self.rep >= steps if side < 0 else self.rep + steps < self.n_rep

    def guarded(self, k, action):
        if k == 0:
            action()
        else:
            pl.when(self.active(k))(action)

    def row(self, k):
        steps, side = self.entries[k]
        return 0 if self.n_rep == 1 else lax.rem(self.rep + side * steps + self.n_rep, self.n_rep)

    def place(self, k, h, mask):
        return self.out_ref.at[self.row(k), self.me ^ mask, :, self.columns[h]]

    def source(self, k, h, mask):
        return self.x_ref.at[:, self.columns[h]] if k == 0 and mask == 0 else self.place(k, h, mask)

    def hop(self, k, h, mask, bit):
        there = mask | (1 << bit)
        return pltpu.make_async_remote_copy(
            src_ref=self.source(k, h, mask),
            dst_ref=self.place(k, h, mask),
            send_sem=self.send_sem.at[k, h, there],
            recv_sem=self.recv_sem.at[k, h, there],
            device_id=(self.rep, self.me ^ (1 << bit)),
            device_id_type=MESH,
        )

    def along(self, k, h, side):
        steps = self.entries[k][0]
        lane = (steps * 2 if side > 0 else steps * 2 + 1)
        return pltpu.make_async_remote_copy(
            src_ref=self.source(k, h, 0),
            dst_ref=self.place(k, h, 0),
            send_sem=(self.up_sem if side > 0 else self.down_sem).at[steps, h],
            recv_sem=self.recv_sem.at[lane + 1, h, 0],
            device_id=(self.rep + side, self.me),
            device_id_type=MESH,
        )

    def arrived(self, k, h, mask):
        target = self.place(k, h, mask)
        pltpu.make_async_copy(target, target, self.recv_sem.at[k, h, mask]).wait()

    def local(self):
        return pltpu.make_async_copy(self.x_ref, self.out_ref.at[self.row(0), self.me], self.local_sem)

    def spread(self, k):
        for stage in range(self.bits):
            for h in range(2):
                self.hop(k, h, 0, self.orders[h][stage]).start()

    def onward(self, k, act):
        sides = (-1, 1) if k == 0 else (-self.entries[k][1],)
        if self.n_rep == 1 or self.entries[k][0] == self.n_rep - 1:
            return
        for side in sides:

            @pl.when(self.reaches(side))
            def _(side=side):
                for h in range(2):
                    act(self.along(k, h, side))

    def begin(self):
        self.local().start()
        self.onward(0, lambda copy: copy.start())
        self.spread(0)

    def from_rep(self, k):
        def action():
            for h in range(2):
                self.arrived(k, h, 0)
            self.onward(k, lambda copy: copy.start())
            self.spread(k)

        self.guarded(k, action)

    def relay(self, k, h, mask, stage):
        def action():
            self.arrived(k, h, mask)
            for later in range(stage + 1, self.bits):
                self.hop(k, h, mask, self.orders[h][later]).start()

        self.guarded(k, action)

    def tree(self):
        for stage in range(self.bits):
            for index in range(1 << stage):
                for h in range(2):
                    yield h, spans(self.orders[h][:stage])[index] | (1 << self.orders[h][stage]), stage

    def events(self):
        due = []
        for k, (steps, _) in enumerate(self.entries):
            if k:
                due.append((16 * steps, len(due), functools.partial(self.from_rep, k)))
            for h, mask, stage in self.tree():
                when = 16 * steps + 15 + 10 * stage if stage < self.bits - 1 else 1000 + steps
                due.append((when, len(due), functools.partial(self.relay, k, h, mask, stage)))
        return [step for _, _, step in sorted(due, key=lambda entry: entry[:2])]

    def end(self):
        for k in range(len(self.entries)):

            def action(k=k):
                for stage in range(self.bits):
                    for h in range(2):
                        self.hop(k, h, 0, self.orders[h][stage]).wait_send()
                for h, mask, stage in self.tree():
                    for later in range(stage + 1, self.bits):
                        self.hop(k, h, mask, self.orders[h][later]).wait_send()
                self.onward(k, lambda copy: copy.wait_send())

            self.guarded(k, action)


def weight_gather_kernel(n_rep, n_ep, x_ref, out_ref, *sems):
    gather = BlockGather(n_rep, n_ep, x_ref, out_ref, sems)
    gather.meet()
    gather.begin()
    for event in gather.events():
        event()
    gather.end()
    gather.local().wait()


def gather_weights(x, n_rep, n_ep, collective_id):
    return pl.pallas_call(
        functools.partial(weight_gather_kernel, n_rep, n_ep),
        out_shape=jax.ShapeDtypeStruct((n_rep, n_ep) + x.shape, x.dtype),
        in_specs=[pl.BlockSpec(memory_space=pl.ANY)],
        out_specs=pl.BlockSpec(memory_space=pl.ANY),
        scratch_shapes=BlockGather.sems(n_rep, n_ep),
        compiler_params=pltpu.CompilerParams(collective_id=collective_id, has_side_effects=True),
        cost_estimate=pl.CostEstimate(flops=1000, bytes_accessed=1000, transcendentals=0),
        name="weight_gather",
    )(x)


COLUMNS = 512


def attention_front_kernel(n_rep, n_ep, experts, heads_kv, groups, scale, *refs):
    (length_ref, x_ref, small_ref, gains_ref, cos_ref, sin_ref, key_ref, turned_ref) = refs[:8]
    (mat_ref, wo_ref, own_g_ref) = refs[8:11]
    h_ref, proj_ref, att_ref, middle_ref, second_ref, logit_ref, row_ref, rank_ref, wo_all, g_all = refs[11:21]
    mat_buf, mat_sem, k_low, v_low, wo_buf, wo_sem = refs[21:27]
    gather = BlockGather(n_rep, n_ep, wo_ref, wo_all, refs[27:32])
    extra = BlockGather(1, n_ep, own_g_ref, g_all, refs[32:37])
    size = gains_ref.shape[1]
    tokens, width = x_ref.shape
    wide_q, wide_kv = heads_kv * groups * size, heads_kv * size
    chunks = (wide_q + 2 * wide_kv) // COLUMNS
    pairs = heads_kv * groups // 2
    group_blocks = n_ep // 2
    block_rows = wo_ref.shape[0]
    deep = group_blocks * block_rows
    early = chunks + pairs
    turns = early + n_rep * 2

    def mat_copy(i):
        columns = pl.ds(pl.multiple_of(i * COLUMNS, COLUMNS), COLUMNS)
        return pltpu.make_async_copy(mat_ref.at[:, columns], mat_buf.at[i % 2], mat_sem.at[i % 2])

    def wo_copy(n):
        blocks = pl.ds((n % 2) * group_blocks, group_blocks)
        return pltpu.make_async_copy(wo_all.at[n // 2, blocks], wo_buf.at[n % 2], wo_sem.at[n % 2])

    mat_copy(0).start()
    gather.meet()
    gather.begin()
    pick = lax.broadcasted_iota(jnp.int32, (8, EXT), 0) + experts == lax.broadcasted_iota(jnp.int32, (8, EXT), 1)
    picks = jnp.where(pick, 1.0, 0.0).astype(bf16)
    row_ref[...] = lax.dot_general(picks, small_ref[...], NT, preferred_element_type=f32)
    x = x_ref[...].astype(f32)
    x = x * lax.rsqrt(jnp.mean(x * x, axis=-1, keepdims=True) + eps)
    h_ref[...] = (x * row_ref[0:1, :]).astype(bf16)
    for e in range(experts):
        smaller = key_ref[:, e : e + 1] < turned_ref[e : e + 1, :]
        rank_ref[e : e + 1, :] = jnp.sum(jnp.where(smaller, 1.0, 0.0), axis=0, keepdims=True)

    def rotate(value):
        return value * cos_ref[...] + pltpu.roll(value, size // 2, 1) * sin_ref[...]

    def normed(value):
        return value * lax.rsqrt(jnp.mean(value * value, axis=-1, keepdims=True) + eps)

    query_pos = lax.broadcasted_iota(jnp.int32, (tokens, tokens), 0)
    key_pos = lax.broadcasted_iota(jnp.int32, (tokens, tokens), 1)
    allowed = (key_pos <= query_pos) & (key_pos < length_ref[0])

    def lanes(start):
        return pl.ds(pl.multiple_of(start, size), size)

    first = gather.events()
    first.insert(len(first) - len(first) // 6, extra.begin)
    second = extra.events()

    def shares(events, start, stop):
        each = -(-len(events) // (stop - start))
        return {start + n: events[n * each : (n + 1) * each] for n in range(stop - start)}

    plan = {**shares(first, 0, early), **shares(second, early, turns)}

    def turn(i, carry):
        @pl.when(i < chunks)
        def _():
            @pl.when(i + 1 < chunks)
            def _():
                mat_copy(i + 1).start()

            mat_copy(i).wait()
            columns = pl.ds(pl.multiple_of(i * COLUMNS, COLUMNS), COLUMNS)
            proj_ref[:, columns] = jnp.dot(h_ref[...], mat_buf[i % 2], preferred_element_type=f32)

        @pl.when((i >= chunks) & (i < early))
        def _():
            pair = i - chunks
            group = pair // (groups // 2)

            @pl.when(pair % (groups // 2) == 0)
            def _():
                key = normed(proj_ref[:, lanes(wide_q + group * size)])
                k_low[...] = rotate(key * gains_ref[1:2, :]).astype(bf16)
                v_low[...] = proj_ref[:, lanes(wide_q + wide_kv + group * size)].astype(bf16)

            for n in range(2):
                head = pair * 2 + n
                query = rotate(normed(proj_ref[:, lanes(head * size)]) * gains_ref[0:1, :]).astype(bf16)
                scores = lax.dot_general(query, k_low[...], NT, preferred_element_type=f32) * scale
                scores = jnp.where(allowed, scores, -1e30)
                raised = jnp.exp(scores - jnp.max(scores, axis=1, keepdims=True))
                probs = (raised * (1.0 / jnp.sum(raised, axis=1, keepdims=True))).astype(bf16)
                att_ref[:, lanes(head * size)] = jnp.dot(
                    probs, v_low[...], preferred_element_type=f32
                ).astype(bf16)

        @pl.when(i >= early)
        def _():
            n = i - early

            @pl.when(n == 0)
            def _():
                gather.local().wait()
                wo_copy(0).start()
                middle_ref[...] = x_ref[...].astype(f32)

            @pl.when(i + 1 < turns)
            def _():
                wo_copy(n + 1).start()

            wo_copy(n).wait()
            columns = pl.ds(pl.multiple_of(n * deep, deep), deep)
            middle_ref[...] += jnp.dot(
                att_ref[:, columns], wo_buf[n % 2].reshape(deep, width), preferred_element_type=f32
            )

        for k, mine in plan.items():
            if mine:

                @pl.when(i == k)
                def _(mine=mine):
                    for event in mine:
                        event()

        return carry

    lax.fori_loop(0, turns, turn, 0)
    step = 64
    for r in range(0, tokens, step):
        low = (normed(middle_ref[r : r + step, :]) * row_ref[1:2, :]).astype(bf16)
        second_ref[r : r + step, :] = low
    logit_ref[...] = jnp.dot(second_ref[...], small_ref[...], preferred_element_type=f32)
    gather.end()
    extra.end()
    extra.local().wait()


def attention_front(
    length, x, small, gains, cos, sin, key, mat, w_o, own_g, n_rep, n_ep, heads_kv, groups, collective_id
):
    tokens, width = x.shape
    size = gains.shape[1]
    experts = key.shape[1]
    vmem = pl.BlockSpec(memory_space=pltpu.VMEM)
    anywhere = pl.BlockSpec(memory_space=pl.ANY)
    wide_q = heads_kv * groups * size
    wide_all = wide_q + 2 * heads_kv * size
    return pl.pallas_call(
        functools.partial(attention_front_kernel, n_rep, n_ep, experts, heads_kv, groups, size ** (-0.5)),
        out_shape=(
            jax.ShapeDtypeStruct((tokens, width), bf16),
            jax.ShapeDtypeStruct((tokens, wide_all), f32),
            jax.ShapeDtypeStruct((tokens, wide_q), bf16),
            jax.ShapeDtypeStruct((tokens, width), f32),
            jax.ShapeDtypeStruct((tokens, width), bf16),
            jax.ShapeDtypeStruct((tokens, EXT), f32),
            jax.ShapeDtypeStruct((8, width), f32),
            jax.ShapeDtypeStruct((experts, tokens), f32),
            jax.ShapeDtypeStruct((n_rep, n_ep) + w_o.shape, bf16),
            jax.ShapeDtypeStruct((1, n_ep) + own_g.shape, bf16),
        ),
        in_specs=[pl.BlockSpec(memory_space=pltpu.SMEM)] + [vmem] * 7 + [anywhere] * 3,
        out_specs=(vmem,) * 8 + (anywhere,) * 2,
        scratch_shapes=[
            pltpu.VMEM((2, width, COLUMNS), bf16),
            pltpu.SemaphoreType.DMA((2,)),
            pltpu.VMEM((tokens, size), bf16),
            pltpu.VMEM((tokens, size), bf16),
            pltpu.VMEM((2, n_ep // 2) + w_o.shape, bf16),
            pltpu.SemaphoreType.DMA((2,)),
        ]
        + BlockGather.sems(n_rep, n_ep)
        + BlockGather.sems(1, n_ep),
        compiler_params=pltpu.CompilerParams(
            collective_id=collective_id, has_side_effects=True, vmem_limit_bytes=VMEM_BYTES
        ),
        cost_estimate=pl.CostEstimate(flops=1000, bytes_accessed=1000, transcendentals=0),
        name="attention_front",
    )(length, x, small, gains, cos, sin, key, key.T, mat, w_o, own_g)


def unpack_kernel(shares, *refs):
    packs, outs = refs[: len(refs) - 3], refs[len(refs) - 3 :]
    for local, pack in enumerate(packs):
        start = 0
        for out, rows in zip(outs, shares):
            for p in range(out.shape[2] // LANES):
                out[local, :, p * LANES : (p + 1) * LANES] = pack[0, start : start + rows, :].astype(f32)
                start += rows


def unpack(packs, wide_share, tall_share, width, hidden):
    count = len(packs)
    vmem = pl.BlockSpec(memory_space=pltpu.VMEM)
    return pl.pallas_call(
        functools.partial(unpack_kernel, (wide_share, wide_share, tall_share)),
        out_shape=(
            jax.ShapeDtypeStruct((count, wide_share, hidden), f32),
            jax.ShapeDtypeStruct((count, wide_share, hidden), f32),
            jax.ShapeDtypeStruct((count, tall_share, width), f32),
        ),
        in_specs=[vmem] * count,
        out_specs=(vmem,) * 3,
        compiler_params=pltpu.CompilerParams(vmem_limit_bytes=VMEM_BYTES),
        cost_estimate=pl.CostEstimate(flops=1000, bytes_accessed=1000, transcendentals=0),
        name="unpack",
    )(*packs)


class TokenSum:
    def __init__(self, count, y_ref, starts, results, scratch):
        self.bits = bits_of(count)
        self.y_ref, self.results = y_ref, results
        self.own, self.got = scratch[:2], scratch[2:4]
        self.send_sem, self.recv_sem, self.own_sem = scratch[4:7]
        self.rep, self.me = lax.axis_index("rep"), lax.axis_index("ep")
        self.orders = [list(reversed(o)) for o in gather_orders(count)]
        self.columns = [pl.ds(s, o.shape[2]) for s, o in zip(starts, self.own)]
        self.masks = [
            [list(reversed(spans(self.orders[h][k + 1 :]))) for k in range(self.bits)] for h in range(2)
        ]
        self.slots, self.seats = [], []
        for h in range(2):
            table = {}
            for stage in range(self.bits):
                for mask in self.masks[h][stage]:
                    table[(stage, mask)] = len(table)
            self.slots.append(table)
            self.seats.append({mask: i for i, mask in enumerate(self.masks[h][0])})

    @staticmethod
    def scratch(count, rows, widths):
        half = count // 2
        return [
            pltpu.VMEM((half, rows, widths[0]), bf16),
            pltpu.VMEM((half, rows, widths[1]), bf16),
            pltpu.VMEM((count - 1, rows, widths[0]), bf16),
            pltpu.VMEM((count - 1, rows, widths[1]), bf16),
            pltpu.SemaphoreType.DMA((2, count)),
            pltpu.SemaphoreType.DMA((2, count)),
            pltpu.SemaphoreType.DMA((2, half)),
        ]

    def meet(self):
        meet([(self.rep, self.me ^ (1 << b)) for b in range(self.bits)])

    def copy(self, h, stage, mask):
        bit = 1 << self.orders[h][stage]
        slot = self.slots[h][(stage, mask)]
        if stage == 0:
            source = self.y_ref.at[self.me ^ bit ^ mask, :, self.columns[h]]
        else:
            source = self.own[h].at[self.seats[h][bit | mask]]
        return pltpu.make_async_remote_copy(
            src_ref=source,
            dst_ref=self.got[h].at[slot],
            send_sem=self.send_sem.at[h, slot],
            recv_sem=self.recv_sem.at[h, slot],
            device_id=(self.rep, self.me ^ bit),
            device_id_type=MESH,
        )

    def load(self, h, mask):
        seat = self.seats[h][mask]
        return pltpu.make_async_copy(
            self.y_ref.at[self.me ^ mask, :, self.columns[h]], self.own[h].at[seat], self.own_sem.at[h, seat]
        )

    def begin(self):
        for i in range(len(self.masks[0][0])):
            for h in range(2):
                self.copy(h, 0, self.masks[h][0][i]).start()
                self.load(h, self.masks[h][0][i]).start()

    def add(self, h, stage, mask):
        slot, seat = self.slots[h][(stage, mask)], self.seats[h][mask]
        own, got = self.own[h], self.got[h]
        if stage == 0:
            self.load(h, mask).wait()
        self.copy(h, stage, mask).wait_recv()
        step = 32

        def body(i, carry):
            rows = pl.ds(pl.multiple_of(i * step, step), step)
            total = own[seat, rows, :].astype(f32) + got[slot, rows, :].astype(f32)
            if stage == self.bits - 1:
                self.results[h][rows, :] = total
            else:
                own[seat, rows, :] = total.astype(bf16)
            return carry

        lax.fori_loop(0, own.shape[1] // step, body, 0)

    def stage(self, stage):
        for i in range(len(self.masks[0][stage])):
            for h in range(2):
                mask = self.masks[h][stage][i]
                self.add(h, stage, mask)
                if stage + 1 < self.bits:
                    following = 1 << self.orders[h][stage + 1]
                    if mask & following:
                        self.copy(h, stage + 1, mask & ~following).start()

    def end(self):
        for h in range(2):
            for stage, mask in self.slots[h]:
                self.copy(h, stage, mask).wait_send()


def token_sum_kernel(count, starts, y_ref, first_ref, second_ref, *scratch):
    total = TokenSum(count, y_ref, starts, (first_ref, second_ref), scratch)
    total.meet()
    total.begin()
    for stage in range(total.bits):
        total.stage(stage)
    total.end()


def sum_tokens(y, count, starts, widths, collective_id):
    rows = y.shape[1]
    return pl.pallas_call(
        functools.partial(token_sum_kernel, count, starts),
        out_shape=tuple(jax.ShapeDtypeStruct((rows, w), f32) for w in widths),
        in_specs=[pl.BlockSpec(memory_space=pl.ANY)],
        out_specs=(pl.BlockSpec(memory_space=pltpu.VMEM),) * 2,
        scratch_shapes=TokenSum.scratch(count, rows, widths),
        compiler_params=pltpu.CompilerParams(
            collective_id=collective_id, has_side_effects=True, vmem_limit_bytes=VMEM_BYTES
        ),
        cost_estimate=pl.CostEstimate(flops=1000, bytes_accessed=1000, transcendentals=0),
        name="token_sum",
    )(y)


QUAD = 4


def attention_back_kernel(count, starts, heads_kv, groups, scale, *refs):
    (length_ref, proj_ref, gains_ref, cos_ref, sin_ref, mid_ref, wo_ref, y_ref) = refs[:8]
    right_ref, head_ref, first_ref, second_ref = refs[8:12]
    wo_buf, wo_sem, k_low, v_low, k_norm, dk_sum, dv_sum = refs[12:19]
    total = TokenSum(count, y_ref, starts, (first_ref, second_ref), refs[19:])
    size = gains_ref.shape[1]
    tokens = proj_ref.shape[0]
    heads_q = heads_kv * groups
    wide_q, wide_kv = heads_q * size, heads_kv * size
    per_group = groups // QUAD
    turns = heads_q // QUAD

    def wo_copy(i):
        rows = pl.ds(pl.multiple_of(i * QUAD * size, QUAD * size), QUAD * size)
        return pltpu.make_async_copy(wo_ref.at[rows], wo_buf.at[i % 2], wo_sem.at[i % 2])

    wo_copy(0).start()
    total.meet()
    total.begin()
    head_ref[...] = jnp.zeros_like(head_ref)
    sent = right_ref.shape[1] - wide_q - 2 * wide_kv
    for n in range(sent // mid_ref.shape[1]):
        start = wide_q + 2 * wide_kv + n * mid_ref.shape[1]
        right_ref[:, start : start + mid_ref.shape[1]] = mid_ref[...]

    def rotate(value):
        return value * cos_ref[...] + pltpu.roll(value, size // 2, 1) * sin_ref[...]

    def rotate_back(value):
        return value * cos_ref[...] - pltpu.roll(value, size // 2, 1) * sin_ref[...]

    def norm_parts(value):
        inverse = lax.rsqrt(jnp.mean(value * value, axis=-1, keepdims=True) + eps)
        return value * inverse, inverse

    def project_back(gradient, normed, inverse, row):
        scaled = rotate_back(gradient)
        head_ref[row : row + 1, :] += jnp.sum(scaled * normed, axis=0, keepdims=True)
        lifted = scaled * gains_ref[row : row + 1, :]
        mean = jnp.mean(lifted * normed, axis=-1, keepdims=True)
        return (inverse * (lifted - normed * mean)).astype(bf16)

    key_pos = lax.broadcasted_iota(jnp.int32, (tokens, tokens), 0)
    query_pos = lax.broadcasted_iota(jnp.int32, (tokens, tokens), 1)
    allowed = (key_pos <= query_pos) & (key_pos < length_ref[0])

    def lanes(start):
        return pl.ds(pl.multiple_of(start, size), size)

    def turn(i, carry):
        group = i // per_group
        for stage, when in ((0, min(1, turns - 1)), (1, turns - 2)):

            @pl.when(i == when)
            def _(stage=stage):
                if stage < total.bits - 1:
                    total.stage(stage)

        @pl.when(i % per_group == 0)
        def _():
            normed, inverse = norm_parts(proj_ref[:, lanes(wide_q + group * size)])
            k_norm[:, :size] = normed
            k_norm[:, size:] = jnp.broadcast_to(inverse, normed.shape)
            k_low[...] = rotate(normed * gains_ref[1:2, :]).astype(bf16)
            v_low[...] = proj_ref[:, lanes(wide_q + wide_kv + group * size)].astype(bf16)
            dk_sum[...] = jnp.zeros_like(dk_sum)
            dv_sum[...] = jnp.zeros_like(dv_sum)

        @pl.when(i + 1 < turns)
        def _():
            wo_copy(i + 1).start()

        wo_copy(i).wait()
        d_att = lax.dot_general(mid_ref[...], wo_buf[i % 2], NT, preferred_element_type=f32).astype(bf16)
        keys, values = k_low[...], v_low[...]
        dk, dv = dk_sum[...], dv_sum[...]
        for n in range(QUAD):
            head = i * QUAD + n
            d_out = d_att[:, n * size : (n + 1) * size]
            normed, inverse = norm_parts(proj_ref[:, lanes(head * size)])
            query = rotate(normed * gains_ref[0:1, :]).astype(bf16)
            scores = lax.dot_general(keys, query, NT, preferred_element_type=f32) * scale
            scores = jnp.where(allowed, scores, -1e30)
            raised = jnp.exp(scores - jnp.max(scores, axis=0, keepdims=True))
            probs = raised * (1.0 / jnp.sum(raised, axis=0, keepdims=True))
            dv += jnp.dot(probs.astype(bf16), d_out, preferred_element_type=f32)
            d_probs = lax.dot_general(values, d_out, NT, preferred_element_type=f32)
            weighted = probs * d_probs
            d_scores = (weighted - probs * jnp.sum(weighted, axis=0, keepdims=True)).astype(bf16)
            dk += jnp.dot(d_scores, query, preferred_element_type=f32)
            d_query = lax.dot_general(d_scores, keys, TN, preferred_element_type=f32) * scale
            right_ref[:, lanes(head * size)] = project_back(d_query, normed, inverse, 0)
        dk_sum[...] = dk
        dv_sum[...] = dv

        @pl.when(i % per_group == per_group - 1)
        def _():
            right_ref[:, lanes(wide_q + group * size)] = project_back(
                dk_sum[...] * scale, k_norm[:, :size], k_norm[:, size:], 1
            )
            right_ref[:, lanes(wide_q + wide_kv + group * size)] = dv_sum[...].astype(bf16)

        return carry

    lax.fori_loop(0, turns, turn, 0)
    for stage in range(min(2, total.bits - 1), total.bits):
        total.stage(stage)
    total.end()


def attention_back(length, proj, gains, cos, sin, d_mid, mat_o, y, count, starts, widths, heads_kv, groups, collective_id):
    tokens, width = d_mid.shape
    size = gains.shape[1]
    vmem = pl.BlockSpec(memory_space=pltpu.VMEM)
    anywhere = pl.BlockSpec(memory_space=pl.ANY)
    columns = (heads_kv * groups + 2 * heads_kv) * size + 2 * width
    return pl.pallas_call(
        functools.partial(attention_back_kernel, count, starts, heads_kv, groups, size ** (-0.5)),
        out_shape=(
            jax.ShapeDtypeStruct((tokens, columns), bf16),
            jax.ShapeDtypeStruct((8, size), f32),
        )
        + tuple(jax.ShapeDtypeStruct((tokens, w), f32) for w in widths),
        in_specs=[pl.BlockSpec(memory_space=pltpu.SMEM)] + [vmem] * 5 + [anywhere] * 2,
        out_specs=(vmem,) * 4,
        scratch_shapes=[
            pltpu.VMEM((2, QUAD * size, width), bf16),
            pltpu.SemaphoreType.DMA((2,)),
            pltpu.VMEM((tokens, size), bf16),
            pltpu.VMEM((tokens, size), bf16),
            pltpu.VMEM((tokens, 2 * size), f32),
            pltpu.VMEM((tokens, size), f32),
            pltpu.VMEM((tokens, size), f32),
        ]
        + TokenSum.scratch(count, tokens, widths),
        compiler_params=pltpu.CompilerParams(
            collective_id=collective_id, has_side_effects=True, vmem_limit_bytes=VMEM_BYTES
        ),
        cost_estimate=pl.CostEstimate(flops=1000, bytes_accessed=1000, transcendentals=0),
        name="attention_back",
    )(length, proj, gains, cos, sin, d_mid, mat_o, y)


def exchanges(n_rep, n_ep):
    near = [(0, b) for b in range(1, bits_of(n_ep))]
    far = [(1, b) for b in range(bits_of(n_rep))]
    return near + far[::-1], (near + far, near[::-1] + far), [2] * len(near) + [3] * len(far)


def dense_sum_kernel(n_rep, n_ep, rows, chunks, split, *refs):
    hidden_ref, att_ref, right_ref, small_ref, head_ref, out_ref, head_out = refs[:7]
    rest = list(refs[7:])
    bits, rep_bits = bits_of(n_ep), bits_of(n_rep)
    wide = right_ref.shape[1] // (chunks - 1)
    half = wide // 2
    rep, me = lax.axis_index("rep"), lax.axis_index("ep")
    axes, orders, depths = exchanges(n_rep, n_ep)
    count = len(axes)
    mine = {axis: lax.rem(lax.div(rep if axis[0] else me, 1 << axis[1]), 2) for axis in axes + [(0, 0)]}
    left_ref, part, got_core = rest[:3]
    acc = [None] + [rest[3 + 2 * k : 5 + 2 * k] for k in range(count)]
    rest = rest[3 + 2 * count :]
    got = [None] + [rest[2 * k : 2 * k + 2] for k in range(count)]
    rest = rest[2 * count :]
    head_own, head_got, head_rep = rest[:3]
    core_send, core_recv, step_send, step_recv, head_send, head_recv, head_rs, head_rr = rest[3:]
    left = [[[a for a in axes if a not in o[:k]] for k in range(count)] for o in orders]
    lags = [0, 1]
    for depth in depths:
        lags.append(lags[-1] + depth)
    slots = [None] + [2 * depth for depth in depths]
    others = [lax.rem(rep + d, n_rep) for d in range(1, n_rep)]
    meet([(rep, me ^ (1 << b)) for b in range(bits)] + [(other, me) for other in others])

    def core_copy(c):
        slot = lax.rem(c, 2)
        return pltpu.make_async_remote_copy(
            src_ref=part.at[slot, 1 - mine[(0, 0)]],
            dst_ref=got_core.at[slot],
            send_sem=core_send.at[slot],
            recv_sem=core_recv.at[slot],
            device_id=(rep, me ^ 1),
            device_id_type=MESH,
        )

    def pick(k, h, which):
        axis = orders[h][k - 1]
        return (slice(None),) * left[h][k - 1].index(axis) + (which(mine[axis]),)

    def bit_copy(k, h, c):
        slot = lax.rem(c, slots[k])
        on_rep, bit = orders[h][k - 1]
        return pltpu.make_async_remote_copy(
            src_ref=acc[k][h].at[(slot,) + pick(k, h, lambda m: 1 - m)],
            dst_ref=got[k][h].at[slot],
            send_sem=step_send.at[k, h, slot],
            recv_sem=step_recv.at[k, h, slot],
            device_id=(rep ^ (1 << bit), me) if on_rep else (rep, me ^ (1 << bit)),
            device_id_type=MESH,
        )

    corners = [()]
    for _ in range(bits - 1):
        corners = [c + (v,) for c in corners for v in range(2)]
    block = n_rep * rows
    side_rows = len(corners) * block
    inner = (2,) * rep_bits

    def place_rows(source, which_of):
        per = 128 // rows
        for b in range(source.shape[1] // 128):
            turned = source[:, b * 128 : (b + 1) * 128].astype(f32).T.astype(bf16)
            for q in range(per):
                which, owner = which_of(b * per + q)
                r, e = owner // n_ep, owner % n_ep
                corner = sum(((e >> bit) & 1) << (bits - 1 - bit) for bit in range(1, bits))
                start = (which * 2 + (e & 1)) * side_rows + corner * block + r * rows
                left_ref[start : start + rows, :] = turned[q * rows : (q + 1) * rows, :]

    place_rows(hidden_ref, lambda n: (0, n))
    place_rows(att_ref, lambda n: (1 + n % 2, n // 2))

    def stage_make(c):
        slot = lax.rem(c, 2)

        @pl.when(c >= 2)
        def _():
            core_copy(c - 2).wait_send()

        @pl.when(c < chunks - 1)
        def _():
            which = jnp.where(c >= split[0], 1, 0) + jnp.where(c >= split[1], 1, 0)
            columns = pl.ds(pl.multiple_of(c * wide, wide), wide)
            weights = right_ref[:, columns]
            for side in (1, 0):
                which_side = 1 - mine[(0, 0)] if side else mine[(0, 0)]
                for n, corner in enumerate(corners):
                    start = (which * 2 + which_side) * side_rows + n * block
                    value = jnp.dot(
                        left_ref[pl.ds(pl.multiple_of(start, block), block), :],
                        weights,
                        preferred_element_type=f32,
                    )
                    part[(slot, which_side) + corner] = value.astype(bf16).reshape(inner + (rows, wide))

        @pl.when(c == chunks - 1)
        def _():
            thin = small_ref.shape[1]
            lead = (slice(None),) * (rep_bits + 1)
            for side in range(2):
                for n, corner in enumerate(corners):
                    value = small_ref[pl.ds(side * side_rows + n * block, block), :].reshape(inner + (rows, thin))
                    blank = jnp.zeros(inner + (rows, wide - thin), bf16)
                    part[(slot, side) + corner + lead + (slice(0, thin),)] = value
                    part[(slot, side) + corner + lead + (slice(thin, wide),)] = blank

        core_copy(c).start()

    def stage_core(c):
        slot, put = lax.rem(c, 2), lax.rem(c, slots[1])

        @pl.when(c >= slots[1])
        def _():
            for h in range(2):
                bit_copy(1, h, c - slots[1]).wait_send()

        core_copy(c).wait_recv()
        for corner in corners:
            total = part[(slot, mine[(0, 0)]) + corner].astype(f32) + got_core[(slot,) + corner].astype(f32)
            total = total.astype(bf16)
            for h in range(2):
                acc[1][h][(put,) + corner] = total[..., h * half : (h + 1) * half]
        for h in range(2):
            bit_copy(1, h, c).start()

    def joined(k, h, c):
        slot = lax.rem(c, slots[k])
        return acc[k][h][(slot,) + pick(k, h, lambda m: m)].astype(f32) + got[k][h][slot].astype(f32)

    def stage_bit(k, c):
        for h in range(2):

            @pl.when(c >= slots[k])
            def _(h=h):
                bit_copy(k, h, c - slots[k]).wait_send()

            bit_copy(k - 1, h, c).wait_recv()
            acc[k][h][lax.rem(c, slots[k])] = joined(k - 1, h, c).astype(bf16)
            bit_copy(k, h, c).start()

    def stage_end(c):
        for h in range(2):
            bit_copy(count, h, c).wait_recv()
            out_ref[:, pl.ds(pl.multiple_of(c * wide + h * half, half), half)] = joined(count, h, c)

    def head_copy(t):
        return pltpu.make_async_remote_copy(
            src_ref=head_own.at[t],
            dst_ref=head_got.at[t],
            send_sem=head_send.at[t],
            recv_sem=head_recv.at[t],
            device_id=(rep, me ^ (1 << t)),
            device_id_type=MESH,
        )

    def head_rep_copy(d):
        return pltpu.make_async_remote_copy(
            src_ref=head_own.at[bits],
            dst_ref=head_rep.at[rep],
            send_sem=head_rs.at[d],
            recv_sem=head_rr.at[n_rep - 2 - d],
            device_id=(others[d], me),
            device_id_type=MESH,
        )

    def head_step(t):
        if t == 0:
            head_own[0] = head_ref[...]
            head_copy(0).start()
        elif t <= bits:
            head_copy(t - 1).wait_recv()
            head_own[t] = head_own[t - 1] + head_got[t - 1]
            if t < bits:
                head_copy(t).start()
            else:
                for d in range(n_rep - 1):
                    head_rep_copy(d).start()
                head_rep[rep] = head_own[bits]
        else:
            for d in range(n_rep - 1):
                head_rep_copy(d).wait_recv()
            total = head_rep[0]
            for r in range(1, n_rep):
                total = total + head_rep[r]
            head_out[...] = total

    def step(i, carry):
        for stage in reversed(range(len(lags))):
            c = i - lags[stage]

            @pl.when((c >= 0) & (c < chunks))
            def _(stage=stage, c=c):
                if stage == 0:
                    stage_make(c)
                elif stage == 1:
                    stage_core(c)
                elif stage <= count:
                    stage_bit(stage, c)
                else:
                    stage_end(c)

        for t in range(bits + 2):

            @pl.when(i == t)
            def _(t=t):
                head_step(t)

        return carry

    lax.fori_loop(0, chunks + lags[-1], step, 0)
    for c in range(chunks - 2, chunks):
        core_copy(c).wait_send()
    for k in range(1, count + 1):
        for c in range(chunks - slots[k], chunks):
            for h in range(2):
                bit_copy(k, h, c).wait_send()
    for t in range(bits):
        head_copy(t).wait_send()
    for d in range(n_rep - 1):
        head_rep_copy(d).wait_send()


def dense_sum(hidden, attended, right, small, head, n_rep, n_ep, split, collective_id):
    chunk = 512
    chunks = right.shape[1] // chunk + 1
    bits, rep_bits = bits_of(n_ep), bits_of(n_rep)
    tokens, width = hidden.shape
    rows = width // (n_rep * n_ep)
    axes, _, depths = exchanges(n_rep, n_ep)
    half = chunk // 2
    most = 2 * max(depths)
    vmem = pl.BlockSpec(memory_space=pltpu.VMEM)
    inner = (2,) * rep_bits + (rows,)
    scratch = [
        pltpu.VMEM((width + attended.shape[1], tokens), bf16),
        pltpu.VMEM((2, 2) + (2,) * (bits - 1) + inner + (chunk,), bf16),
        pltpu.VMEM((2,) + (2,) * (bits - 1) + inner + (chunk,), bf16),
    ]
    for k, depth in enumerate(depths):
        scratch += [pltpu.VMEM((2 * depth,) + (2,) * (len(axes) - k) + (rows, half), bf16)] * 2
    for k, depth in enumerate(depths):
        scratch += [pltpu.VMEM((2 * depth,) + (2,) * (len(axes) - k - 1) + (rows, half), bf16)] * 2
    scratch += [
        pltpu.VMEM((bits + 1,) + head.shape, f32),
        pltpu.VMEM((bits,) + head.shape, f32),
        pltpu.VMEM((n_rep,) + head.shape, f32),
        pltpu.SemaphoreType.DMA((2,)),
        pltpu.SemaphoreType.DMA((2,)),
        pltpu.SemaphoreType.DMA((len(axes) + 1, 2, most)),
        pltpu.SemaphoreType.DMA((len(axes) + 1, 2, most)),
        pltpu.SemaphoreType.DMA((bits,)),
        pltpu.SemaphoreType.DMA((bits,)),
        pltpu.SemaphoreType.DMA((n_rep - 1,)),
        pltpu.SemaphoreType.DMA((n_rep - 1,)),
    ]
    return pl.pallas_call(
        functools.partial(dense_sum_kernel, n_rep, n_ep, rows, chunks, split),
        out_shape=(
            jax.ShapeDtypeStruct((rows, chunks * chunk), f32),
            jax.ShapeDtypeStruct(head.shape, f32),
        ),
        in_specs=[vmem] * 5,
        out_specs=(vmem, vmem),
        scratch_shapes=scratch,
        compiler_params=pltpu.CompilerParams(
            collective_id=collective_id, has_side_effects=True, vmem_limit_bytes=VMEM_BYTES
        ),
        cost_estimate=pl.CostEstimate(flops=1000, bytes_accessed=1000, transcendentals=0),
        name="dense_sum",
    )(hidden, attended, right, small, head)


def expert_kernel(local, first, last, experts, width, hidden_of, *refs):
    (info, h_ref, g_ref, wg_all, wu_all, wd_all) = refs[:6]
    rest = list(refs[6:])
    prev_ref = None if first else rest.pop(0)
    y_ref, grad_ref = rest[:2]
    xs, gs, ds, hs, stage, prev_buf, wide, tall, in_sem, out_sem, prev_sem, grad_sem = rest[2:14]
    wg_ref, wu_ref, wd_ref, weight_sem = rest[14:]
    weights = [
        pltpu.make_async_copy(source.at[local], target, weight_sem.at[n])
        for n, (source, target) in enumerate(((wg_all, wg_ref), (wu_all, wu_ref), (wd_all, wd_ref)))
    ]
    for copy in weights:
        copy.start()
    shares = grad_ref.shape[0]
    wide_share, tall_share = width // shares, hidden_of // shares
    hidden = wg_ref.shape[1]
    units = info[0]
    expert = info[1]
    table = 8
    per_tile = TILE // UNIT
    tiles = (units + per_tile - 1) // per_tile
    most = xs.shape[0] // TILE
    floor_tiles = min(4, most)

    def unit_in(u, slot):
        source = pl.ds(pl.multiple_of(info[table + u], UNIT), UNIT)
        target = pl.ds(pl.multiple_of(u * UNIT, UNIT), UNIT)
        return (
            pltpu.make_async_copy(h_ref.at[source], xs.at[target], in_sem.at[0, slot]),
            pltpu.make_async_copy(g_ref.at[source], gs.at[target], in_sem.at[1, slot]),
        )

    def begin(u, carry):
        for copy in unit_in(u, u // per_tile):
            copy.start()
        return carry

    lax.fori_loop(0, units, begin, 0)

    def blank(u, carry):
        target = pl.ds(pl.multiple_of(u * UNIT, UNIT), UNIT)
        xs[target, :] = jnp.zeros((UNIT, xs.shape[1]), bf16)
        gs[target, :] = jnp.zeros((UNIT, gs.shape[1]), bf16)
        return carry

    lax.fori_loop(units, jnp.maximum(tiles, floor_tiles) * per_tile, blank, 0)

    def blank_tile(i, carry):
        target = pl.ds(pl.multiple_of(i * TILE, TILE), TILE)
        ds[target, :] = jnp.zeros((TILE, ds.shape[1]), bf16)
        hs[target, :] = jnp.zeros((TILE, hs.shape[1]), bf16)
        return carry

    lax.fori_loop(tiles, floor_tiles, blank_tile, 0)

    def prev_copy(i):
        rows = pl.ds(pl.multiple_of(i * TILE, TILE), TILE)
        return pltpu.make_async_copy(prev_ref.at[rows], prev_buf.at[i % 2], prev_sem.at[i % 2])

    if not first:
        prev_copy(0).start()

    def unit_out(u):
        target = pl.ds(pl.multiple_of(info[table + u], UNIT), UNIT)
        tile = u // per_tile
        source = pl.ds(pl.multiple_of((u % per_tile) * UNIT, UNIT), UNIT)
        return pltpu.make_async_copy(stage.at[tile % 2, source], y_ref.at[target], out_sem.at[tile % 2])

    def out_start(i):
        if last:
            lax.fori_loop(
                i * per_tile,
                jnp.minimum((i + 1) * per_tile, units),
                lambda u, c: (unit_out(u).start(), c)[1],
                0,
            )
        else:
            rows = pl.ds(pl.multiple_of(i * TILE, TILE), TILE)
            pltpu.make_async_copy(stage.at[i % 2], y_ref.at[rows], out_sem.at[i % 2]).start()

    def out_wait(i):
        if last:
            lax.fori_loop(
                i * per_tile,
                jnp.minimum((i + 1) * per_tile, units),
                lambda u, c: (unit_out(u).wait(), c)[1],
                0,
            )
        else:
            rows = pl.ds(pl.multiple_of(i * TILE, TILE), TILE)
            pltpu.make_async_copy(stage.at[i % 2], y_ref.at[rows], out_sem.at[i % 2]).wait()

    lane = lax.broadcasted_iota(jnp.int32, (TILE, EXT), 1)
    weight_lanes = (lane == expert) | (lane == expert + experts) | (lane == expert + 2 * experts)

    def tile_step(i, carry):
        def landed(u, c):
            for copy in unit_in(u, i):
                copy.wait()
            return c

        lax.fori_loop(i * per_tile, jnp.minimum((i + 1) * per_tile, units), landed, 0)
        rows = pl.ds(pl.multiple_of(i * TILE, TILE), TILE)
        x = xs[rows, :width]
        g = gs[rows, :]
        extra = xs[rows, width:].astype(f32)
        weight = jnp.sum(jnp.where(weight_lanes, extra, 0.0), axis=1, keepdims=True)
        gate = jnp.dot(x, wg_ref[...], preferred_element_type=f32)
        up = jnp.dot(x, wu_ref[...], preferred_element_type=f32)
        d_plain = lax.dot_general(g, wd_ref[...], NT, preferred_element_type=f32)
        sig = 1.0 / (1.0 + jnp.exp(-gate))
        silu = gate * sig
        hid = silu * up
        d_weight = jnp.sum(hid.astype(bf16).astype(f32) * d_plain, axis=1, keepdims=True)
        hs[rows, :] = (hid * weight).astype(bf16)
        d_hidden = d_plain * weight
        ds[rows, :hidden] = (d_hidden * up * sig * (1.0 + gate * (1.0 - sig))).astype(bf16)
        ds[rows, hidden:] = (d_hidden * silu).astype(bf16)

        @pl.when(i >= 2)
        def _():
            out_wait(i - 2)

        if not first:

            @pl.when(i + 1 < tiles)
            def _():
                prev_copy(i + 1).start()

            prev_copy(i).wait()
        slot = i % 2
        high = d_weight.astype(bf16).astype(f32)
        low = d_weight - high
        note = jnp.where(lane == expert, high, 0.0) + jnp.where(lane == expert + experts, low, 0.0)
        d_row = lax.dot_general(ds[rows, :hidden], wg_ref[...], NT, preferred_element_type=f32)
        d_row += lax.dot_general(ds[rows, hidden:], wu_ref[...], NT, preferred_element_type=f32)
        if not first:
            d_row += prev_buf[slot, :, :width].astype(f32)
            note += prev_buf[slot, :, width : width + EXT].astype(f32)
        stage[slot, :, :width] = d_row.astype(bf16)
        stage[slot, :, width : width + EXT] = note.astype(bf16)
        out = jnp.dot(hs[rows, :], wd_ref[...], preferred_element_type=f32)
        if not first:
            out += prev_buf[slot, :, width + EXT :].astype(f32)
        stage[slot, :, width + EXT :] = out.astype(bf16)
        out_start(i)
        return carry

    for copy in weights:
        copy.wait()
    lax.fori_loop(0, tiles, tile_step, 0)

    block = 256

    def grads(depth):
        def wide_copies(m):
            per = wide_share // block
            return tuple(
                pltpu.make_async_copy(
                    wide.at[m % 2, :, p * LANES : (p + 1) * LANES],
                    grad_ref.at[
                        m // per,
                        pl.ds(pl.multiple_of(p * wide_share + (m % per) * block, block), block),
                    ],
                    grad_sem.at[m % 2, p],
                )
                for p in range(2 * hidden // LANES)
            )

        def wide_step(m, carry):
            @pl.when(m >= 2)
            def _():
                for copy in wide_copies(m - 2):
                    copy.wait()

            columns = pl.ds(pl.multiple_of(m * block, block), block)
            wide[m % 2] = lax.dot_general(
                xs[:depth, columns], ds[:depth, :], TN, preferred_element_type=f32
            ).astype(bf16)
            for copy in wide_copies(m):
                copy.start()
            return carry

        count = width // block
        lax.fori_loop(0, count, wide_step, 0)
        for m in range(count - 2, count):
            for copy in wide_copies(m):
                copy.wait()

        piece = math.gcd(block, tall_share)
        base = 2 * hidden // LANES * wide_share

        def tall_copies(m):
            made = []
            for q in range(block // piece):
                first_row = m * block + q * piece
                share, inside = first_row // tall_share, first_row % tall_share
                for p in range(width // LANES):
                    rows = pl.ds(pl.multiple_of(base + p * tall_share + inside, piece), piece)
                    made.append(
                        pltpu.make_async_copy(
                            tall.at[m % 2, q * piece : (q + 1) * piece, p * LANES : (p + 1) * LANES],
                            grad_ref.at[share, rows],
                            grad_sem.at[m % 2, q * (width // LANES) + p],
                        )
                    )
            return made

        def tall_step(m, carry):
            @pl.when(m >= 2)
            def _():
                for copy in tall_copies(m - 2):
                    copy.wait()

            columns = pl.ds(pl.multiple_of(m * block, block), block)
            tall[m % 2] = lax.dot_general(
                hs[:depth, columns], gs[:depth, :], TN, preferred_element_type=f32
            ).astype(bf16)
            for copy in tall_copies(m):
                copy.start()
            return carry

        count = hidden // block
        lax.fori_loop(0, count, tall_step, 0)
        for m in range(count - 2, count):
            for copy in tall_copies(m):
                copy.wait()

    for choice in range(floor_tiles, most + 1):
        chosen = (tiles <= choice) if choice == floor_tiles else (tiles == choice)

        @pl.when(chosen)
        def _(choice=choice):
            grads(choice * TILE)

    @pl.when(tiles >= 2)
    def _():
        out_wait(tiles - 2)

    out_wait(tiles - 1)


def expert_pass(info, h_rows, g_rows, w_gate, w_up, w_down, local, prev, last, experts, shares):
    tokens, width = g_rows.shape
    hidden = w_gate.shape[2]
    wide_row = width + EXT + width
    any_spec = pl.BlockSpec(memory_space=pl.ANY)
    first = prev is None
    operands = [info, h_rows, g_rows, w_gate, w_up, w_down] + ([] if first else [prev])
    specs = [pl.BlockSpec(memory_space=pltpu.SMEM), any_spec, any_spec, any_spec, any_spec, any_spec]
    specs += [] if first else [any_spec]
    return pl.pallas_call(
        functools.partial(expert_kernel, local, first, last, experts, width, hidden),
        out_shape=(
            jax.ShapeDtypeStruct((tokens, wide_row), bf16),
            jax.ShapeDtypeStruct((shares, 3 * hidden * width // shares // LANES, LANES), bf16),
        ),
        in_specs=specs,
        out_specs=(any_spec,) * 2,
        scratch_shapes=[
            pltpu.VMEM((tokens, width + EXT), bf16),
            pltpu.VMEM((tokens, width), bf16),
            pltpu.VMEM((tokens, 2 * hidden), bf16),
            pltpu.VMEM((tokens, hidden), bf16),
            pltpu.VMEM((2, TILE, wide_row), bf16),
            pltpu.VMEM((2, TILE, wide_row), bf16),
            pltpu.VMEM((2, 256, 2 * hidden), bf16),
            pltpu.VMEM((2, 256, width), bf16),
            pltpu.SemaphoreType.DMA((2, tokens // TILE)),
            pltpu.SemaphoreType.DMA((2,)),
            pltpu.SemaphoreType.DMA((2,)),
            pltpu.SemaphoreType.DMA((2, max(2 * hidden // LANES, 256 // math.gcd(256, hidden // shares) * width // LANES))),
            pltpu.VMEM((width, hidden), bf16),
            pltpu.VMEM((width, hidden), bf16),
            pltpu.VMEM((hidden, width), bf16),
            pltpu.SemaphoreType.DMA((3,)),
        ],
        compiler_params=pltpu.CompilerParams(vmem_limit_bytes=VMEM_BYTES),
        cost_estimate=pl.CostEstimate(flops=1000, bytes_accessed=1000, transcendentals=0),
        name="experts",
    )(*operands)


def unit_table(lengths):
    per_sequence = TILE // UNIT
    counts = (lengths + UNIT - 1) // UNIT
    unit = jnp.arange(lengths.shape[0] * per_sequence, dtype=jnp.int32)
    live = (unit % per_sequence) < jnp.repeat(counts, per_sequence)
    place = jnp.cumsum(live.astype(jnp.int32)) - 1
    hit = (place[None, :] == unit[:, None]) & live[None, :]
    rows = jnp.sum(jnp.where(hit, unit[None, :] * UNIT, 0), axis=1)
    return (jnp.sum(counts), rows)


def split_three(value):
    high = lax.reduce_precision(value, 8, 7)
    rest = value - high
    middle = lax.reduce_precision(rest, 8, 7)
    return jnp.concatenate([high, middle, rest - middle], axis=-1)


def per_device(
    hidden_in,
    out_grad,
    attn_gain,
    w_q,
    key_weight,
    value_weight,
    w_o,
    ffn_gain,
    router_w,
    qk_gains,
    w_gate,
    w_up,
    w_down,
    lengths,
    routes,
    order,
):
    everywhere = ("rep", "ep")
    rep_count, ep_count = (lax.axis_size("rep"), lax.axis_size("ep"))
    rep_index, ep_index = (lax.axis_index("rep"), lax.axis_index("ep"))
    inputs = hidden_in[0].astype(f32)
    sequence_length, model_width = inputs.shape
    head_size = qk_gains.shape[1]
    wide_q, wide_kv = (w_q.shape[1], key_weight.shape[1])
    heads_q, heads_kv = (wide_q // head_size, wide_kv // head_size)
    groups = heads_q // heads_kv
    local_experts = w_gate.shape[0]
    experts = local_experts * ep_count
    top_count = routes.shape[2]
    score_scale = head_size ** (-0.5)
    group_lengths = lax.dynamic_slice_in_dim(lengths, rep_index * ep_count, ep_count)
    length = lax.dynamic_index_in_dim(group_lengths, ep_index, keepdims=False)
    positions = jnp.arange(sequence_length, dtype=jnp.int32)
    live = positions < length
    live_rows = live.astype(f32)

    expert_iota = jnp.arange(experts, dtype=jnp.int32)
    route_hot = routes[0][..., None] == expert_iota
    routed = jnp.any(route_hot, axis=1) & live[:, None]
    order_of = jnp.sum(
        jnp.where(route_hot, order[0].reshape(sequence_length, top_count)[..., None], 0), axis=1
    )
    sort_key = jnp.where(routed, order_of, sequence_length * top_count)
    loads = jnp.sum(routed.astype(jnp.int32), axis=0)

    own_rows = w_q.shape[0]
    load_columns = -(-experts // own_rows)
    load_block = jnp.pad(loads, (0, load_columns * own_rows - experts)).reshape(load_columns, own_rows).T
    small = jnp.concatenate(
        [router_w, attn_gain[:, None], ffn_gain[:, None], load_block.astype(bf16)], axis=1
    )
    small = jnp.pad(small, ((0, 0), (0, EXT - small.shape[1])))
    pack = jnp.concatenate([w_q, key_weight, value_weight, small], axis=1)
    mat_qkv = gather_weights(pack, rep_count, ep_count, 4).reshape(-1, pack.shape[1])

    wide_all = wide_q + 2 * wide_kv
    small_all = mat_qkv[:, wide_all:]
    mat_router = small_all[:, :experts]
    loads_all = (
        small_all[:, experts + 2 : experts + 2 + load_columns]
        .reshape(rep_count, ep_count, own_rows, load_columns)
        .transpose(0, 1, 3, 2)
        .reshape(rep_count, ep_count, load_columns * own_rows)[:, :, :experts]
        .astype(jnp.int32)
    )
    group_loads = lax.dynamic_index_in_dim(loads_all, rep_index, keepdims=False)
    earlier = (jnp.arange(ep_count) < ep_index)[:, None]
    load_prefix = jnp.sum(jnp.where(earlier, group_loads, 0), axis=0)
    capacity = 9 * top_count * jnp.sum(group_lengths) // (8 * experts)

    cosine_lookup, sine_lookup = rope_tables(sequence_length, head_size)
    sign = jnp.where(jnp.arange(head_size) < head_size // 2, -1.0, 1.0).astype(f32)
    turned_sine = sine_lookup * sign[None, :]
    (
        hidden_first,
        projected,
        attended,
        middle,
        h_two,
        logits,
        row_gain,
        rank,
        mat_o,
        grads_all,
    ) = attention_front(
        length.reshape(1),
        hidden_in[0],
        small_all,
        qk_gains.astype(f32),
        cosine_lookup,
        turned_sine,
        sort_key.astype(f32),
        mat_qkv,
        w_o,
        out_grad[0],
        rep_count,
        ep_count,
        heads_kv,
        groups,
        6,
    )
    logits = logits[:, :experts]
    gain_attn, gain_ffn = (row_gain[0], row_gain[1])
    mat_o = mat_o.reshape(-1, model_width)
    grads_all = grads_all.reshape(-1, model_width)
    norm_one, inv_one = rms_parts(inputs)
    norm_two, inv_two = rms_parts(middle)
    kept = routed & (load_prefix[None, :] + rank.T.astype(jnp.int32) < capacity)
    kept_float = kept.astype(f32)
    named = jnp.any(route_hot, axis=1)
    top_logit = jnp.max(jnp.where(named, logits, -jnp.inf), axis=1, keepdims=True)
    raised = jnp.where(named, jnp.exp(jnp.where(named, logits - top_logit, 0.0)), 0.0)
    route_gates = raised / jnp.sum(raised, axis=1, keepdims=True)
    pair_weight = route_gates * kept_float

    extra = split_three(pair_weight).astype(bf16)
    extra = jnp.pad(extra, ((0, 0), (0, EXT - extra.shape[1])))
    sent = jnp.concatenate([h_two, extra], axis=1)
    h_all = gather_tokens(sent, ep_count, 1)

    part = min(ep_count, 8)
    tokens = part * sequence_length
    sums = []
    y_parts = []
    for c in range(ep_count // part):
        live_units, unit_rows = unit_table(group_lengths[c * part : (c + 1) * part])
        h_rows = h_all[c * part : (c + 1) * part].reshape(tokens, model_width + EXT)
        g_rows = grads_all[c * tokens : (c + 1) * tokens]
        prev, found = None, []
        for local in range(local_experts):
            info = jnp.concatenate(
                [
                    jnp.stack([live_units, ep_index * local_experts + local]).astype(jnp.int32),
                    jnp.zeros((6,), jnp.int32),
                    unit_rows,
                ]
            )
            prev, weight_grads = expert_pass(
                info,
                h_rows,
                g_rows,
                w_gate,
                w_up,
                w_down,
                local,
                prev,
                local == local_experts - 1,
                experts,
                rep_count,
            )
            found.append(weight_grads)
        y_parts.append(prev.reshape(part, sequence_length, -1))
        sums.append(found)
    y_all = y_parts[0] if len(y_parts) == 1 else jnp.concatenate(y_parts, axis=0)
    hidden_units = w_gate.shape[2]
    wide_share, tall_share = model_width // rep_count, hidden_units // rep_count
    found = []
    for local in range(local_experts):
        total = sums[0][local]
        for more in sums[1:]:
            total = (total.astype(f32) + more[local].astype(f32)).astype(bf16)
        found.append(lax.psum_scatter(total, "rep", scatter_dimension=0, tiled=True))
    expert_sums = unpack(found, wide_share, tall_share, model_width, hidden_units)

    half_width = model_width // 2
    row_first, row_second = sum_tokens(
        y_all, ep_count, (0, half_width), (half_width, half_width + EXT), 2
    )
    live_column = live[:, None]
    grad_rows = out_grad[0].astype(f32) * live_rows[:, None]
    notes = row_second[:, half_width : half_width + 2 * experts]
    d_weight = jnp.where(live_column, notes[:, :experts] + notes[:, experts:], 0.0)
    d_gates = d_weight * kept_float
    d_logits = route_gates * (d_gates - jnp.sum(route_gates * d_gates, axis=-1, keepdims=True))

    router_float = mat_router.astype(f32)
    d_h_two = jnp.concatenate([row_first, row_second[:, :half_width]], axis=1)
    d_h_two = jnp.where(live_column, d_h_two, 0.0)
    d_h_two = d_h_two + jnp.dot(d_logits, router_float.T, precision=top_precision)
    grad_router = jnp.dot(h_two.astype(f32).T, d_logits, precision=top_precision)
    grad_ffn = jnp.sum(d_h_two * norm_two, axis=0)
    d_middle = grad_rows + rms_back(d_h_two * gain_ffn, norm_two, inv_two)
    d_middle_low = d_middle.astype(bf16)
    right, head, out_first, out_second = attention_back(
        length.reshape(1),
        projected,
        qk_gains.astype(f32),
        cosine_lookup,
        turned_sine,
        d_middle_low,
        mat_o,
        y_all,
        ep_count,
        (model_width + EXT, model_width + EXT + half_width),
        (half_width, half_width),
        heads_kv,
        groups,
        5,
    )
    moe_output = jnp.where(live_column, jnp.concatenate([out_first, out_second], axis=1), 0.0)
    layer_out = jnp.where(live_column, middle + moe_output, 0.0)
    d_qkv = right[:, :wide_all]
    d_h_one = jnp.einsum("tf,cf->tc", d_qkv, mat_qkv[:, :wide_all], preferred_element_type=f32)
    grad_attn = jnp.sum(d_h_one * norm_one, axis=0)
    grad_input = d_middle + rms_back(d_h_one * gain_attn, norm_one, inv_one)

    small_grads = jnp.concatenate([grad_router, grad_attn[:, None], grad_ffn[:, None]], axis=1)
    small_grads = jnp.pad(small_grads, ((0, 0), (0, EXT - small_grads.shape[1]))).astype(bf16)
    ep_bits = bits_of(ep_count)

    def owner_order(value, parts):
        shape = (rep_count,) + (2,) * ep_bits + (parts, own_rows, value.shape[1])
        axes = (ep_bits + 1,) + tuple(range(ep_bits, 0, -1)) + (0, ep_bits + 2, ep_bits + 3)
        return value.reshape(shape).transpose(axes).reshape(value.shape)

    splits = (wide_all // 512, (wide_all + model_width) // 512)
    sums_all, head_sum = dense_sum(
        hidden_first, attended, right, owner_order(small_grads, 1), head, rep_count, ep_count, splits, 3
    )
    sum_o = jnp.concatenate(
        [sums_all[:, wide_all : wide_all + model_width], sums_all[:, wide_all + model_width : wide_all + 2 * model_width]],
        axis=0,
    )
    small_sum = sums_all[:, wide_all + 2 * model_width :]
    return (
        layer_out[None],
        grad_input[None],
        small_sum[:, experts],
        sums_all[:, :wide_q],
        sums_all[:, wide_q : wide_q + wide_kv],
        sums_all[:, wide_q + wide_kv : wide_all],
        sum_o,
        small_sum[:, experts + 1],
        small_sum[:, :experts],
        head_sum[:2],
        expert_sums[0],
        expert_sums[1],
        expert_sums[2],
    )


def solution(mesh):
    both = ("rep", "ep")
    placed = (
        P(both, None, None),
        P(both, None, None),
        P(both),
        P(both, None),
        P(both, None),
        P(both, None),
        P(both, None),
        P(both),
        P(both, None),
        P(),
        P("ep", None, None),
        P("ep", None, None),
        P("ep", None, None),
        P(),
        P(both, None, None),
        P(both, None),
    )
    return jax.shard_map(
        per_device,
        mesh=mesh,
        in_specs=placed,
        out_specs=(
            P(both, None, None),
            P(both, None, None),
            P(both),
            P(both, None),
            P(both, None),
            P(both, None),
            P(both, None),
            P(both),
            P(both, None),
            P(),
            P("ep", "rep", None),
            P("ep", "rep", None),
            P("ep", "rep", None),
        ),
        check_vma=False,
    )
```

```python
import functools
import math

import jax
import jax.numpy as jnp
from jax import lax
from jax.experimental import pallas as pl
from jax.experimental.pallas import tpu as pltpu
from jax.sharding import PartitionSpec as P

eps = 1e-06
rope_base = 1000000.0
top_precision = lax.Precision.HIGHEST
MESH = pl.DeviceIdType.MESH
f32, bf16 = jnp.float32, jnp.bfloat16
EXT = 128
UNIT = 16
LANES = 256
TILE = 256
VMEM_BYTES = 58 * 1024 * 1024
NT = (((1,), (1,)), ((), ()))
TN = (((0,), (0,)), ((), ()))


def rms_parts(value_rows):
    inverse = lax.rsqrt(jnp.mean(value_rows * value_rows, axis=-1, keepdims=True) + eps)
    return (value_rows * inverse, inverse)


def rms_back(grad_norm, normed, inverse):
    return inverse * (grad_norm - normed * jnp.mean(grad_norm * normed, axis=-1, keepdims=True))


def rope_tables(count, head_size):
    half_size = head_size // 2
    freqs = rope_base ** (-2.0 * jnp.arange(half_size, dtype=f32) / head_size)
    angles = jnp.arange(count, dtype=f32)[:, None] * freqs[None, :]
    cosine_lookup = jnp.concatenate([jnp.cos(angles), jnp.cos(angles)], axis=1)
    sine_lookup = jnp.concatenate([jnp.sin(angles), jnp.sin(angles)], axis=1)
    return (cosine_lookup, sine_lookup)


def bits_of(count):
    return count.bit_length() - 1


def gather_orders(count):
    bits = bits_of(count)
    up = list(range(1, bits)) + [0]
    down = list(range(bits - 1, 0, -1)) + [0]
    return (up, down)


def spans(bits):
    masks = [0]
    for bit in bits:
        masks = masks + [m | (1 << bit) for m in masks]
    return masks


def meet(peers):
    barrier = pltpu.get_barrier_semaphore()
    for peer in peers:
        pl.semaphore_signal(barrier, inc=1, device_id=peer, device_id_type=MESH)
    pl.semaphore_wait(barrier, len(peers))


def token_gather_kernel(count, x_ref, out_ref, send_sem, recv_sem, local_sem):
    rep, me = lax.axis_index("rep"), lax.axis_index("ep")
    bits = bits_of(count)
    half = x_ref.shape[0] // 2
    meet([(rep, me ^ (1 << b)) for b in range(bits)])
    local = pltpu.make_async_copy(x_ref, out_ref.at[me], local_sem)
    local.start()
    orders = gather_orders(count)
    copies = []

    def send(h, mask, bit):
        rows = pl.ds(h * half, half)
        source = x_ref.at[rows] if mask == 0 else out_ref.at[me ^ mask, rows]
        there = mask | (1 << bit)
        copy = pltpu.make_async_remote_copy(
            src_ref=source,
            dst_ref=out_ref.at[me ^ mask, rows],
            send_sem=send_sem.at[h, there],
            recv_sem=recv_sem.at[h, there],
            device_id=(rep, me ^ (1 << bit)),
            device_id_type=MESH,
        )
        copy.start()
        copies.append(copy)

    def arrived(h, mask):
        rows = pl.ds(h * half, half)
        pltpu.make_async_copy(
            x_ref.at[rows], out_ref.at[me ^ mask, rows], recv_sem.at[h, mask]
        ).wait()

    for stage in range(bits):
        for h in range(2):
            send(h, 0, orders[h][stage])
    for stage in range(bits):
        for low in spans(orders[0][:stage]):
            index = spans(orders[0][:stage]).index(low)
            for h in range(2):
                mask = spans(orders[h][:stage])[index] | (1 << orders[h][stage])
                arrived(h, mask)
                for later in range(stage + 1, bits):
                    send(h, mask, orders[h][later])
    for copy in copies:
        copy.wait_send()
    local.wait()


def gather_tokens(x, count, collective_id):
    return pl.pallas_call(
        functools.partial(token_gather_kernel, count),
        out_shape=jax.ShapeDtypeStruct((count,) + x.shape, x.dtype),
        in_specs=[pl.BlockSpec(memory_space=pl.ANY)],
        out_specs=pl.BlockSpec(memory_space=pl.ANY),
        scratch_shapes=[
            pltpu.SemaphoreType.DMA((2, count)),
            pltpu.SemaphoreType.DMA((2, count)),
            pltpu.SemaphoreType.DMA,
        ],
        compiler_params=pltpu.CompilerParams(collective_id=collective_id, has_side_effects=True),
        name="token_gather",
    )(x)


class BlockGather:
    def __init__(self, n_rep, n_ep, x_ref, out_ref, sems):
        self.n_rep, self.bits = n_rep, bits_of(n_ep)
        self.x_ref, self.out_ref = x_ref, out_ref
        self.send_sem, self.recv_sem, self.up_sem, self.down_sem, self.local_sem = sems
        self.rep, self.me = lax.axis_index("rep"), lax.axis_index("ep")
        split = -(-x_ref.shape[1] // 256) * 128
        self.columns = (pl.ds(0, split), pl.ds(split, x_ref.shape[1] - split))
        self.orders = gather_orders(n_ep)
        self.entries = [(0, 0)]
        for s in range(1, n_rep):
            self.entries += [(s, -1), (s, 1)]

    @staticmethod
    def sems(n_rep, n_ep):
        return [
            pltpu.SemaphoreType.DMA((2 * n_rep - 1, 2, n_ep)),
            pltpu.SemaphoreType.DMA((2 * n_rep - 1, 2, n_ep)),
            pltpu.SemaphoreType.DMA((n_rep, 2)),
            pltpu.SemaphoreType.DMA((n_rep, 2)),
            pltpu.SemaphoreType.DMA,
        ]

    def meet(self):
        barrier = pltpu.get_barrier_semaphore()
        peers = [(self.rep, self.me ^ (1 << b)) for b in range(self.bits)]
        for peer in peers:
            pl.semaphore_signal(barrier, inc=1, device_id=peer, device_id_type=MESH)
        if self.n_rep > 1:
            for side in (-1, 1):

                @pl.when(self.reaches(side))
                def _(side=side):
                    pl.semaphore_signal(barrier, inc=1, device_id=(self.rep + side, self.me), device_id_type=MESH)

        count = len(peers)
        if self.n_rep > 1:
            count = count + jnp.where(self.reaches(-1), 1, 0) + jnp.where(self.reaches(1), 1, 0)
        pl.semaphore_wait(barrier, count)

    def reaches(self, side):
        return self.rep > 0 if side < 0 else self.rep < self.n_rep - 1

    def active(self, k):
        steps, side = self.entries[k]
        return self.rep >= steps if side < 0 else self.rep + steps < self.n_rep

    def guarded(self, k, action):
        if k == 0:
            action()
        else:
            pl.when(self.active(k))(action)

    def row(self, k):
        steps, side = self.entries[k]
        return 0 if self.n_rep == 1 else lax.rem(self.rep + side * steps + self.n_rep, self.n_rep)

    def place(self, k, h, mask):
        return self.out_ref.at[self.row(k), self.me ^ mask, :, self.columns[h]]

    def source(self, k, h, mask):
        return self.x_ref.at[:, self.columns[h]] if k == 0 and mask == 0 else self.place(k, h, mask)

    def hop(self, k, h, mask, bit):
        there = mask | (1 << bit)
        return pltpu.make_async_remote_copy(
            src_ref=self.source(k, h, mask),
            dst_ref=self.place(k, h, mask),
            send_sem=self.send_sem.at[k, h, there],
            recv_sem=self.recv_sem.at[k, h, there],
            device_id=(self.rep, self.me ^ (1 << bit)),
            device_id_type=MESH,
        )

    def along(self, k, h, side):
        steps = self.entries[k][0]
        lane = (steps * 2 if side > 0 else steps * 2 + 1)
        return pltpu.make_async_remote_copy(
            src_ref=self.source(k, h, 0),
            dst_ref=self.place(k, h, 0),
            send_sem=(self.up_sem if side > 0 else self.down_sem).at[steps, h],
            recv_sem=self.recv_sem.at[lane + 1, h, 0],
            device_id=(self.rep + side, self.me),
            device_id_type=MESH,
        )

    def arrived(self, k, h, mask):
        target = self.place(k, h, mask)
        pltpu.make_async_copy(target, target, self.recv_sem.at[k, h, mask]).wait()

    def local(self):
        return pltpu.make_async_copy(self.x_ref, self.out_ref.at[self.row(0), self.me], self.local_sem)

    def spread(self, k):
        for stage in range(self.bits):
            for h in range(2):
                self.hop(k, h, 0, self.orders[h][stage]).start()

    def onward(self, k, act):
        sides = (-1, 1) if k == 0 else (-self.entries[k][1],)
        if self.n_rep == 1 or self.entries[k][0] == self.n_rep - 1:
            return
        for side in sides:

            @pl.when(self.reaches(side))
            def _(side=side):
                for h in range(2):
                    act(self.along(k, h, side))

    def begin(self):
        self.local().start()
        self.onward(0, lambda copy: copy.start())
        self.spread(0)

    def from_rep(self, k):
        def action():
            for h in range(2):
                self.arrived(k, h, 0)
            self.onward(k, lambda copy: copy.start())
            self.spread(k)

        self.guarded(k, action)

    def relay(self, k, h, mask, stage):
        def action():
            self.arrived(k, h, mask)
            for later in range(stage + 1, self.bits):
                self.hop(k, h, mask, self.orders[h][later]).start()

        self.guarded(k, action)

    def tree(self):
        for stage in range(self.bits):
            for index in range(1 << stage):
                for h in range(2):
                    yield h, spans(self.orders[h][:stage])[index] | (1 << self.orders[h][stage]), stage

    def events(self):
        due = []
        for k, (steps, _) in enumerate(self.entries):
            if k:
                due.append((16 * steps, len(due), functools.partial(self.from_rep, k)))
            for h, mask, stage in self.tree():
                when = 16 * steps + 15 + 10 * stage if stage < self.bits - 1 else 1000 + steps
                due.append((when, len(due), functools.partial(self.relay, k, h, mask, stage)))
        return [step for _, _, step in sorted(due, key=lambda entry: entry[:2])]

    def end(self):
        for k in range(len(self.entries)):

            def action(k=k):
                for stage in range(self.bits):
                    for h in range(2):
                        self.hop(k, h, 0, self.orders[h][stage]).wait_send()
                for h, mask, stage in self.tree():
                    for later in range(stage + 1, self.bits):
                        self.hop(k, h, mask, self.orders[h][later]).wait_send()
                self.onward(k, lambda copy: copy.wait_send())

            self.guarded(k, action)


def weight_gather_kernel(n_rep, n_ep, x_ref, out_ref, *sems):
    gather = BlockGather(n_rep, n_ep, x_ref, out_ref, sems)
    gather.meet()
    gather.begin()
    for event in gather.events():
        event()
    gather.end()
    gather.local().wait()


def gather_weights(x, n_rep, n_ep, collective_id):
    return pl.pallas_call(
        functools.partial(weight_gather_kernel, n_rep, n_ep),
        out_shape=jax.ShapeDtypeStruct((n_rep, n_ep) + x.shape, x.dtype),
        in_specs=[pl.BlockSpec(memory_space=pl.ANY)],
        out_specs=pl.BlockSpec(memory_space=pl.ANY),
        scratch_shapes=BlockGather.sems(n_rep, n_ep),
        compiler_params=pltpu.CompilerParams(collective_id=collective_id, has_side_effects=True),
        cost_estimate=pl.CostEstimate(flops=1000, bytes_accessed=1000, transcendentals=0),
        name="weight_gather",
    )(x)


COLUMNS = 512


def attention_front_kernel(n_rep, n_ep, experts, heads_kv, groups, scale, *refs):
    (length_ref, x_ref, small_ref, gains_ref, cos_ref, sin_ref, key_ref, turned_ref) = refs[:8]
    (mat_ref, wo_ref, own_g_ref) = refs[8:11]
    h_ref, proj_ref, att_ref, middle_ref, second_ref, logit_ref, row_ref, rank_ref, wo_all, g_all = refs[11:21]
    mat_buf, mat_sem, k_low, v_low, wo_buf, wo_sem = refs[21:27]
    gather = BlockGather(n_rep, n_ep, wo_ref, wo_all, refs[27:32])
    extra = BlockGather(1, n_ep, own_g_ref, g_all, refs[32:37])
    size = gains_ref.shape[1]
    tokens, width = x_ref.shape
    wide_q, wide_kv = heads_kv * groups * size, heads_kv * size
    chunks = (wide_q + 2 * wide_kv) // COLUMNS
    pairs = heads_kv * groups // 2
    group_blocks = n_ep // 2
    block_rows = wo_ref.shape[0]
    deep = group_blocks * block_rows
    early = chunks + pairs
    turns = early + n_rep * 2

    def mat_copy(i):
        columns = pl.ds(pl.multiple_of(i * COLUMNS, COLUMNS), COLUMNS)
        return pltpu.make_async_copy(mat_ref.at[:, columns], mat_buf.at[i % 2], mat_sem.at[i % 2])

    def wo_copy(n):
        blocks = pl.ds((n % 2) * group_blocks, group_blocks)
        return pltpu.make_async_copy(wo_all.at[n // 2, blocks], wo_buf.at[n % 2], wo_sem.at[n % 2])

    mat_copy(0).start()
    gather.meet()
    gather.begin()
    pick = lax.broadcasted_iota(jnp.int32, (8, EXT), 0) + experts == lax.broadcasted_iota(jnp.int32, (8, EXT), 1)
    picks = jnp.where(pick, 1.0, 0.0).astype(bf16)
    row_ref[...] = lax.dot_general(picks, small_ref[...], NT, preferred_element_type=f32)
    x = x_ref[...].astype(f32)
    x = x * lax.rsqrt(jnp.mean(x * x, axis=-1, keepdims=True) + eps)
    h_ref[...] = (x * row_ref[0:1, :]).astype(bf16)
    for e in range(experts):
        smaller = key_ref[:, e : e + 1] < turned_ref[e : e + 1, :]
        rank_ref[e : e + 1, :] = jnp.sum(jnp.where(smaller, 1.0, 0.0), axis=0, keepdims=True)

    def rotate(value):
        return value * cos_ref[...] + pltpu.roll(value, size // 2, 1) * sin_ref[...]

    def normed(value):
        return value * lax.rsqrt(jnp.mean(value * value, axis=-1, keepdims=True) + eps)

    query_pos = lax.broadcasted_iota(jnp.int32, (tokens, tokens), 0)
    key_pos = lax.broadcasted_iota(jnp.int32, (tokens, tokens), 1)
    allowed = (key_pos <= query_pos) & (key_pos < length_ref[0])

    def lanes(start):
        return pl.ds(pl.multiple_of(start, size), size)

    first = gather.events()
    first.insert(len(first) - len(first) // 6, extra.begin)
    second = extra.events()

    def shares(events, weights, start):
        given, total, done, reached = {}, sum(weights), 0, 0.0
        for n, weight in enumerate(weights):
            reached += weight
            upto = -(-len(events) * reached // total)
            upto = len(events) if n == len(weights) - 1 else int(upto)
            given[start + n] = events[done:upto]
            done = upto
        return given

    plan = {
        **shares(first, [1.0] * chunks + [4.0] * pairs, 0),
        **shares(second, [1.0] * (turns - early), early),
    }

    def turn(i, carry):
        @pl.when(i < chunks)
        def _():
            @pl.when(i + 1 < chunks)
            def _():
                mat_copy(i + 1).start()

            mat_copy(i).wait()
            columns = pl.ds(pl.multiple_of(i * COLUMNS, COLUMNS), COLUMNS)
            proj_ref[:, columns] = jnp.dot(h_ref[...], mat_buf[i % 2], preferred_element_type=f32)

        @pl.when((i >= chunks) & (i < early))
        def _():
            pair = i - chunks
            group = pair // (groups // 2)

            @pl.when(pair % (groups // 2) == 0)
            def _():
                key = normed(proj_ref[:, lanes(wide_q + group * size)])
                k_low[...] = rotate(key * gains_ref[1:2, :]).astype(bf16)
                v_low[...] = proj_ref[:, lanes(wide_q + wide_kv + group * size)].astype(bf16)

            for n in range(2):
                head = pair * 2 + n
                query = rotate(normed(proj_ref[:, lanes(head * size)]) * gains_ref[0:1, :]).astype(bf16)
                scores = lax.dot_general(query, k_low[...], NT, preferred_element_type=f32) * scale
                scores = jnp.where(allowed, scores, -1e30)
                raised = jnp.exp(scores - jnp.max(scores, axis=1, keepdims=True))
                probs = (raised * (1.0 / jnp.sum(raised, axis=1, keepdims=True))).astype(bf16)
                att_ref[:, lanes(head * size)] = jnp.dot(
                    probs, v_low[...], preferred_element_type=f32
                ).astype(bf16)

        @pl.when(i >= early)
        def _():
            n = i - early

            @pl.when(n == 0)
            def _():
                gather.local().wait()
                wo_copy(0).start()
                middle_ref[...] = x_ref[...].astype(f32)

            @pl.when(i + 1 < turns)
            def _():
                wo_copy(n + 1).start()

            wo_copy(n).wait()
            columns = pl.ds(pl.multiple_of(n * deep, deep), deep)
            middle_ref[...] += jnp.dot(
                att_ref[:, columns], wo_buf[n % 2].reshape(deep, width), preferred_element_type=f32
            )

        for k, mine in plan.items():
            if mine:

                @pl.when(i == k)
                def _(mine=mine):
                    for event in mine:
                        event()

        return carry

    lax.fori_loop(0, turns, turn, 0)
    step = 64
    for r in range(0, tokens, step):
        low = (normed(middle_ref[r : r + step, :]) * row_ref[1:2, :]).astype(bf16)
        second_ref[r : r + step, :] = low
    logit_ref[...] = jnp.dot(second_ref[...], small_ref[...], preferred_element_type=f32)
    gather.end()
    extra.end()
    extra.local().wait()


def attention_front(
    length, x, small, gains, cos, sin, key, mat, w_o, own_g, n_rep, n_ep, heads_kv, groups, collective_id
):
    tokens, width = x.shape
    size = gains.shape[1]
    experts = key.shape[1]
    vmem = pl.BlockSpec(memory_space=pltpu.VMEM)
    anywhere = pl.BlockSpec(memory_space=pl.ANY)
    wide_q = heads_kv * groups * size
    wide_all = wide_q + 2 * heads_kv * size
    return pl.pallas_call(
        functools.partial(attention_front_kernel, n_rep, n_ep, experts, heads_kv, groups, size ** (-0.5)),
        out_shape=(
            jax.ShapeDtypeStruct((tokens, width), bf16),
            jax.ShapeDtypeStruct((tokens, wide_all), f32),
            jax.ShapeDtypeStruct((tokens, wide_q), bf16),
            jax.ShapeDtypeStruct((tokens, width), f32),
            jax.ShapeDtypeStruct((tokens, width), bf16),
            jax.ShapeDtypeStruct((tokens, EXT), f32),
            jax.ShapeDtypeStruct((8, width), f32),
            jax.ShapeDtypeStruct((experts, tokens), f32),
            jax.ShapeDtypeStruct((n_rep, n_ep) + w_o.shape, bf16),
            jax.ShapeDtypeStruct((1, n_ep) + own_g.shape, bf16),
        ),
        in_specs=[pl.BlockSpec(memory_space=pltpu.SMEM)] + [vmem] * 7 + [anywhere] * 3,
        out_specs=(vmem,) * 8 + (anywhere,) * 2,
        scratch_shapes=[
            pltpu.VMEM((2, width, COLUMNS), bf16),
            pltpu.SemaphoreType.DMA((2,)),
            pltpu.VMEM((tokens, size), bf16),
            pltpu.VMEM((tokens, size), bf16),
            pltpu.VMEM((2, n_ep // 2) + w_o.shape, bf16),
            pltpu.SemaphoreType.DMA((2,)),
        ]
        + BlockGather.sems(n_rep, n_ep)
        + BlockGather.sems(1, n_ep),
        compiler_params=pltpu.CompilerParams(
            collective_id=collective_id, has_side_effects=True, vmem_limit_bytes=VMEM_BYTES
        ),
        cost_estimate=pl.CostEstimate(flops=1000, bytes_accessed=1000, transcendentals=0),
        name="attention_front",
    )(length, x, small, gains, cos, sin, key, key.T, mat, w_o, own_g)


def unpack_kernel(shares, experts, *refs):
    (sums,) = refs[:1]
    packs, outs = refs[1:-9], refs[-9:-6]
    q_ref, k_ref, v_ref, o_ref, router_ref, rows_ref = refs[-6:]
    for local, pack in enumerate(packs):
        start = 0
        for out, rows in zip(outs, shares):
            for p in range(out.shape[2] // LANES):
                out[local, :, p * LANES : (p + 1) * LANES] = pack[0, start : start + rows, :].astype(f32)
                start += rows
    start = 0
    for out in (q_ref, k_ref, v_ref):
        out[...] = sums[:, start : start + out.shape[1]]
        start += out.shape[1]
    for n in range(2):
        rows = sums.shape[0]
        o_ref[n * rows : (n + 1) * rows, :] = sums[:, start : start + o_ref.shape[1]]
        start += o_ref.shape[1]
    small = sums[:, start : start + EXT]
    router_ref[...] = small[:, :experts]
    rows_ref[...] = small.T


def unpack(sums, packs, wide_share, tall_share, width, hidden, wide_q, wide_kv, experts):
    count, rows = len(packs), sums.shape[0]
    vmem = pl.BlockSpec(memory_space=pltpu.VMEM)
    return pl.pallas_call(
        functools.partial(unpack_kernel, (wide_share, wide_share, tall_share), experts),
        out_shape=tuple(
            jax.ShapeDtypeStruct(shape, f32)
            for shape in (
                (count, wide_share, hidden),
                (count, wide_share, hidden),
                (count, tall_share, width),
                (rows, wide_q),
                (rows, wide_kv),
                (rows, wide_kv),
                (2 * rows, width),
                (rows, experts),
                (EXT, rows),
            )
        ),
        in_specs=[vmem] * (count + 1),
        out_specs=(vmem,) * 9,
        compiler_params=pltpu.CompilerParams(vmem_limit_bytes=VMEM_BYTES),
        cost_estimate=pl.CostEstimate(flops=1000, bytes_accessed=1000, transcendentals=0),
        name="unpack",
    )(sums, *packs)


class TokenSum:
    def __init__(self, count, y_ref, starts, results, scratch):
        self.bits = bits_of(count)
        self.y_ref, self.results = y_ref, results
        self.own, self.got = scratch[:2], scratch[2:4]
        self.send_sem, self.recv_sem, self.own_sem = scratch[4:7]
        self.rep, self.me = lax.axis_index("rep"), lax.axis_index("ep")
        self.orders = [list(reversed(o)) for o in gather_orders(count)]
        self.columns = [pl.ds(s, o.shape[2]) for s, o in zip(starts, self.own)]
        self.masks = [
            [list(reversed(spans(self.orders[h][k + 1 :]))) for k in range(self.bits)] for h in range(2)
        ]
        self.slots, self.seats = [], []
        for h in range(2):
            table = {}
            for stage in range(self.bits):
                for mask in self.masks[h][stage]:
                    table[(stage, mask)] = len(table)
            self.slots.append(table)
            self.seats.append({mask: i for i, mask in enumerate(self.masks[h][0])})

    @staticmethod
    def scratch(count, rows, widths):
        half = count // 2
        return [
            pltpu.VMEM((half, rows, widths[0]), bf16),
            pltpu.VMEM((half, rows, widths[1]), bf16),
            pltpu.VMEM((count - 1, rows, widths[0]), bf16),
            pltpu.VMEM((count - 1, rows, widths[1]), bf16),
            pltpu.SemaphoreType.DMA((2, count)),
            pltpu.SemaphoreType.DMA((2, count)),
            pltpu.SemaphoreType.DMA((2, half)),
        ]

    def meet(self):
        meet([(self.rep, self.me ^ (1 << b)) for b in range(self.bits)])

    def copy(self, h, stage, mask):
        bit = 1 << self.orders[h][stage]
        slot = self.slots[h][(stage, mask)]
        if stage == 0:
            source = self.y_ref.at[self.me ^ bit ^ mask, :, self.columns[h]]
        else:
            source = self.own[h].at[self.seats[h][bit | mask]]
        return pltpu.make_async_remote_copy(
            src_ref=source,
            dst_ref=self.got[h].at[slot],
            send_sem=self.send_sem.at[h, slot],
            recv_sem=self.recv_sem.at[h, slot],
            device_id=(self.rep, self.me ^ bit),
            device_id_type=MESH,
        )

    def load(self, h, mask):
        seat = self.seats[h][mask]
        return pltpu.make_async_copy(
            self.y_ref.at[self.me ^ mask, :, self.columns[h]], self.own[h].at[seat], self.own_sem.at[h, seat]
        )

    def begin(self):
        for i in range(len(self.masks[0][0])):
            for h in range(2):
                self.copy(h, 0, self.masks[h][0][i]).start()
                self.load(h, self.masks[h][0][i]).start()

    def add(self, h, stage, mask):
        slot, seat = self.slots[h][(stage, mask)], self.seats[h][mask]
        own, got = self.own[h], self.got[h]
        if stage == 0:
            self.load(h, mask).wait()
        self.copy(h, stage, mask).wait_recv()
        step = 32

        def body(i, carry):
            rows = pl.ds(pl.multiple_of(i * step, step), step)
            total = own[seat, rows, :].astype(f32) + got[slot, rows, :].astype(f32)
            if stage == self.bits - 1:
                self.results[h][rows, :] = total
            else:
                own[seat, rows, :] = total.astype(bf16)
            return carry

        lax.fori_loop(0, own.shape[1] // step, body, 0)

    def stage(self, stage):
        for i in range(len(self.masks[0][stage])):
            for h in range(2):
                mask = self.masks[h][stage][i]
                self.add(h, stage, mask)
                if stage + 1 < self.bits:
                    following = 1 << self.orders[h][stage + 1]
                    if mask & following:
                        self.copy(h, stage + 1, mask & ~following).start()

    def end(self):
        for h in range(2):
            for stage, mask in self.slots[h]:
                self.copy(h, stage, mask).wait_send()


def token_sum_kernel(count, starts, y_ref, first_ref, second_ref, *scratch):
    total = TokenSum(count, y_ref, starts, (first_ref, second_ref), scratch)
    total.meet()
    total.begin()
    for stage in range(total.bits):
        total.stage(stage)
    total.end()


def sum_tokens(y, count, starts, widths, collective_id):
    rows = y.shape[1]
    return pl.pallas_call(
        functools.partial(token_sum_kernel, count, starts),
        out_shape=tuple(jax.ShapeDtypeStruct((rows, w), f32) for w in widths),
        in_specs=[pl.BlockSpec(memory_space=pl.ANY)],
        out_specs=(pl.BlockSpec(memory_space=pltpu.VMEM),) * 2,
        scratch_shapes=TokenSum.scratch(count, rows, widths),
        compiler_params=pltpu.CompilerParams(
            collective_id=collective_id, has_side_effects=True, vmem_limit_bytes=VMEM_BYTES
        ),
        cost_estimate=pl.CostEstimate(flops=1000, bytes_accessed=1000, transcendentals=0),
        name="token_sum",
    )(y)


QUAD = 4


def attention_back_kernel(count, starts, heads_kv, groups, scale, *refs):
    (length_ref, proj_ref, gains_ref, cos_ref, sin_ref, mid_ref, wo_ref, y_ref) = refs[:8]
    right_ref, head_ref, first_ref, second_ref = refs[8:12]
    wo_buf, wo_sem, k_low, v_low, k_norm, dk_sum, dv_sum = refs[12:19]
    total = TokenSum(count, y_ref, starts, (first_ref, second_ref), refs[19:])
    size = gains_ref.shape[1]
    tokens = proj_ref.shape[0]
    heads_q = heads_kv * groups
    wide_q, wide_kv = heads_q * size, heads_kv * size
    per_group = groups // QUAD
    turns = heads_q // QUAD

    def wo_copy(i):
        rows = pl.ds(pl.multiple_of(i * QUAD * size, QUAD * size), QUAD * size)
        return pltpu.make_async_copy(wo_ref.at[rows], wo_buf.at[i % 2], wo_sem.at[i % 2])

    wo_copy(0).start()
    total.meet()
    total.begin()
    head_ref[...] = jnp.zeros_like(head_ref)
    sent = right_ref.shape[1] - wide_q - 2 * wide_kv
    for n in range(sent // mid_ref.shape[1]):
        start = wide_q + 2 * wide_kv + n * mid_ref.shape[1]
        right_ref[:, start : start + mid_ref.shape[1]] = mid_ref[...]

    def rotate(value):
        return value * cos_ref[...] + pltpu.roll(value, size // 2, 1) * sin_ref[...]

    def rotate_back(value):
        return value * cos_ref[...] - pltpu.roll(value, size // 2, 1) * sin_ref[...]

    def norm_parts(value):
        inverse = lax.rsqrt(jnp.mean(value * value, axis=-1, keepdims=True) + eps)
        return value * inverse, inverse

    def project_back(gradient, normed, inverse, row):
        scaled = rotate_back(gradient)
        head_ref[row : row + 1, :] += jnp.sum(scaled * normed, axis=0, keepdims=True)
        lifted = scaled * gains_ref[row : row + 1, :]
        mean = jnp.mean(lifted * normed, axis=-1, keepdims=True)
        return (inverse * (lifted - normed * mean)).astype(bf16)

    key_pos = lax.broadcasted_iota(jnp.int32, (tokens, tokens), 0)
    query_pos = lax.broadcasted_iota(jnp.int32, (tokens, tokens), 1)
    allowed = (key_pos <= query_pos) & (key_pos < length_ref[0])

    def lanes(start):
        return pl.ds(pl.multiple_of(start, size), size)

    def turn(i, carry):
        group = i // per_group
        for stage, when in ((0, min(1, turns - 1)), (1, turns - 2)):

            @pl.when(i == when)
            def _(stage=stage):
                if stage < total.bits - 1:
                    total.stage(stage)

        @pl.when(i % per_group == 0)
        def _():
            normed, inverse = norm_parts(proj_ref[:, lanes(wide_q + group * size)])
            k_norm[:, :size] = normed
            k_norm[:, size:] = jnp.broadcast_to(inverse, normed.shape)
            k_low[...] = rotate(normed * gains_ref[1:2, :]).astype(bf16)
            v_low[...] = proj_ref[:, lanes(wide_q + wide_kv + group * size)].astype(bf16)
            dk_sum[...] = jnp.zeros_like(dk_sum)
            dv_sum[...] = jnp.zeros_like(dv_sum)

        @pl.when(i + 1 < turns)
        def _():
            wo_copy(i + 1).start()

        wo_copy(i).wait()
        d_att = lax.dot_general(mid_ref[...], wo_buf[i % 2], NT, preferred_element_type=f32).astype(bf16)
        keys, values = k_low[...], v_low[...]
        dk, dv = dk_sum[...], dv_sum[...]
        for n in range(QUAD):
            head = i * QUAD + n
            d_out = d_att[:, n * size : (n + 1) * size]
            normed, inverse = norm_parts(proj_ref[:, lanes(head * size)])
            query = rotate(normed * gains_ref[0:1, :]).astype(bf16)
            scores = lax.dot_general(keys, query, NT, preferred_element_type=f32) * scale
            scores = jnp.where(allowed, scores, -1e30)
            raised = jnp.exp(scores - jnp.max(scores, axis=0, keepdims=True))
            probs = raised * (1.0 / jnp.sum(raised, axis=0, keepdims=True))
            dv += jnp.dot(probs.astype(bf16), d_out, preferred_element_type=f32)
            d_probs = lax.dot_general(values, d_out, NT, preferred_element_type=f32)
            weighted = probs * d_probs
            d_scores = (weighted - probs * jnp.sum(weighted, axis=0, keepdims=True)).astype(bf16)
            dk += jnp.dot(d_scores, query, preferred_element_type=f32)
            d_query = lax.dot_general(d_scores, keys, TN, preferred_element_type=f32) * scale
            right_ref[:, lanes(head * size)] = project_back(d_query, normed, inverse, 0)
        dk_sum[...] = dk
        dv_sum[...] = dv

        @pl.when(i % per_group == per_group - 1)
        def _():
            right_ref[:, lanes(wide_q + group * size)] = project_back(
                dk_sum[...] * scale, k_norm[:, :size], k_norm[:, size:], 1
            )
            right_ref[:, lanes(wide_q + wide_kv + group * size)] = dv_sum[...].astype(bf16)

        return carry

    lax.fori_loop(0, turns, turn, 0)
    for stage in range(min(2, total.bits - 1), total.bits):
        total.stage(stage)
    total.end()


def attention_back(length, proj, gains, cos, sin, d_mid, mat_o, y, count, starts, widths, heads_kv, groups, collective_id):
    tokens, width = d_mid.shape
    size = gains.shape[1]
    vmem = pl.BlockSpec(memory_space=pltpu.VMEM)
    anywhere = pl.BlockSpec(memory_space=pl.ANY)
    columns = (heads_kv * groups + 2 * heads_kv) * size + 2 * width
    return pl.pallas_call(
        functools.partial(attention_back_kernel, count, starts, heads_kv, groups, size ** (-0.5)),
        out_shape=(
            jax.ShapeDtypeStruct((tokens, columns), bf16),
            jax.ShapeDtypeStruct((8, size), f32),
        )
        + tuple(jax.ShapeDtypeStruct((tokens, w), f32) for w in widths),
        in_specs=[pl.BlockSpec(memory_space=pltpu.SMEM)] + [vmem] * 5 + [anywhere] * 2,
        out_specs=(vmem,) * 4,
        scratch_shapes=[
            pltpu.VMEM((2, QUAD * size, width), bf16),
            pltpu.SemaphoreType.DMA((2,)),
            pltpu.VMEM((tokens, size), bf16),
            pltpu.VMEM((tokens, size), bf16),
            pltpu.VMEM((tokens, 2 * size), f32),
            pltpu.VMEM((tokens, size), f32),
            pltpu.VMEM((tokens, size), f32),
        ]
        + TokenSum.scratch(count, tokens, widths),
        compiler_params=pltpu.CompilerParams(
            collective_id=collective_id, has_side_effects=True, vmem_limit_bytes=VMEM_BYTES
        ),
        cost_estimate=pl.CostEstimate(flops=1000, bytes_accessed=1000, transcendentals=0),
        name="attention_back",
    )(length, proj, gains, cos, sin, d_mid, mat_o, y)


def exchanges(n_rep, n_ep):
    near = [(0, b) for b in range(1, bits_of(n_ep))]
    far = [(1, b) for b in range(bits_of(n_rep))]
    return near + far[::-1], (near + far, near[::-1] + far), [2] * len(near) + [3] * len(far)


def dense_sum_kernel(n_rep, n_ep, rows, chunks, split, *refs):
    hidden_ref, att_ref, right_ref, small_ref, head_ref, out_ref, head_out = refs[:7]
    rest = list(refs[7:])
    bits, rep_bits = bits_of(n_ep), bits_of(n_rep)
    wide = right_ref.shape[1] // (chunks - 1)
    half = wide // 2
    rep, me = lax.axis_index("rep"), lax.axis_index("ep")
    axes, orders, depths = exchanges(n_rep, n_ep)
    count = len(axes)
    mine = {axis: lax.rem(lax.div(rep if axis[0] else me, 1 << axis[1]), 2) for axis in axes + [(0, 0)]}
    left_ref, part, got_core = rest[:3]
    acc = [None] + [rest[3 + 2 * k : 5 + 2 * k] for k in range(count)]
    rest = rest[3 + 2 * count :]
    got = [None] + [rest[2 * k : 2 * k + 2] for k in range(count)]
    rest = rest[2 * count :]
    head_own, head_got, head_rep = rest[:3]
    core_send, core_recv, step_send, step_recv, head_send, head_recv, head_rs, head_rr = rest[3:]
    left = [[[a for a in axes if a not in o[:k]] for k in range(count)] for o in orders]
    lags = [0, 1]
    for depth in depths:
        lags.append(lags[-1] + depth)
    slots = [None] + [2 * depth for depth in depths]
    others = [lax.rem(rep + d, n_rep) for d in range(1, n_rep)]
    meet([(rep, me ^ (1 << b)) for b in range(bits)] + [(other, me) for other in others])

    def core_copy(c):
        slot = lax.rem(c, 2)
        return pltpu.make_async_remote_copy(
            src_ref=part.at[slot, 1 - mine[(0, 0)]],
            dst_ref=got_core.at[slot],
            send_sem=core_send.at[slot],
            recv_sem=core_recv.at[slot],
            device_id=(rep, me ^ 1),
            device_id_type=MESH,
        )

    def pick(k, h, which):
        axis = orders[h][k - 1]
        return (slice(None),) * left[h][k - 1].index(axis) + (which(mine[axis]),)

    def bit_copy(k, h, c):
        slot = lax.rem(c, slots[k])
        on_rep, bit = orders[h][k - 1]
        return pltpu.make_async_remote_copy(
            src_ref=acc[k][h].at[(slot,) + pick(k, h, lambda m: 1 - m)],
            dst_ref=got[k][h].at[slot],
            send_sem=step_send.at[k, h, slot],
            recv_sem=step_recv.at[k, h, slot],
            device_id=(rep ^ (1 << bit), me) if on_rep else (rep, me ^ (1 << bit)),
            device_id_type=MESH,
        )

    corners = [()]
    for _ in range(bits - 1):
        corners = [c + (v,) for c in corners for v in range(2)]
    block = n_rep * rows
    side_rows = len(corners) * block
    inner = (2,) * rep_bits

    def place_rows(source, which_of):
        per = 128 // rows
        for b in range(source.shape[1] // 128):
            turned = source[:, b * 128 : (b + 1) * 128].astype(f32).T.astype(bf16)
            for q in range(per):
                which, owner = which_of(b * per + q)
                r, e = owner // n_ep, owner % n_ep
                corner = sum(((e >> bit) & 1) << (bits - 1 - bit) for bit in range(1, bits))
                start = (which * 2 + (e & 1)) * side_rows + corner * block + r * rows
                left_ref[start : start + rows, :] = turned[q * rows : (q + 1) * rows, :]

    place_rows(hidden_ref, lambda n: (0, n))
    place_rows(att_ref, lambda n: (1 + n % 2, n // 2))

    def stage_make(c):
        slot = lax.rem(c, 2)

        @pl.when(c >= 2)
        def _():
            core_copy(c - 2).wait_send()

        @pl.when(c < chunks - 1)
        def _():
            which = jnp.where(c >= split[0], 1, 0) + jnp.where(c >= split[1], 1, 0)
            columns = pl.ds(pl.multiple_of(c * wide, wide), wide)
            weights = right_ref[:, columns]
            for side in (1, 0):
                which_side = 1 - mine[(0, 0)] if side else mine[(0, 0)]
                for n, corner in enumerate(corners):
                    start = (which * 2 + which_side) * side_rows + n * block
                    value = jnp.dot(
                        left_ref[pl.ds(pl.multiple_of(start, block), block), :],
                        weights,
                        preferred_element_type=f32,
                    )
                    part[(slot, which_side) + corner] = value.astype(bf16).reshape(inner + (rows, wide))

        @pl.when(c == chunks - 1)
        def _():
            thin = small_ref.shape[1]
            lead = (slice(None),) * (rep_bits + 1)
            for side in range(2):
                for n, corner in enumerate(corners):
                    value = small_ref[pl.ds(side * side_rows + n * block, block), :].reshape(inner + (rows, thin))
                    blank = jnp.zeros(inner + (rows, wide - thin), bf16)
                    part[(slot, side) + corner + lead + (slice(0, thin),)] = value
                    part[(slot, side) + corner + lead + (slice(thin, wide),)] = blank

        core_copy(c).start()

    def stage_core(c):
        slot, put = lax.rem(c, 2), lax.rem(c, slots[1])

        @pl.when(c >= slots[1])
        def _():
            for h in range(2):
                bit_copy(1, h, c - slots[1]).wait_send()

        core_copy(c).wait_recv()
        for corner in corners:
            total = part[(slot, mine[(0, 0)]) + corner].astype(f32) + got_core[(slot,) + corner].astype(f32)
            total = total.astype(bf16)
            for h in range(2):
                acc[1][h][(put,) + corner] = total[..., h * half : (h + 1) * half]
        for h in range(2):
            bit_copy(1, h, c).start()

    def joined(k, h, c):
        slot = lax.rem(c, slots[k])
        return acc[k][h][(slot,) + pick(k, h, lambda m: m)].astype(f32) + got[k][h][slot].astype(f32)

    def stage_bit(k, c):
        for h in range(2):

            @pl.when(c >= slots[k])
            def _(h=h):
                bit_copy(k, h, c - slots[k]).wait_send()

            bit_copy(k - 1, h, c).wait_recv()
            acc[k][h][lax.rem(c, slots[k])] = joined(k - 1, h, c).astype(bf16)
            bit_copy(k, h, c).start()

    def stage_end(c):
        for h in range(2):
            bit_copy(count, h, c).wait_recv()
            out_ref[:, pl.ds(pl.multiple_of(c * wide + h * half, half), half)] = joined(count, h, c)

    def head_copy(t):
        return pltpu.make_async_remote_copy(
            src_ref=head_own.at[t],
            dst_ref=head_got.at[t],
            send_sem=head_send.at[t],
            recv_sem=head_recv.at[t],
            device_id=(rep, me ^ (1 << t)),
            device_id_type=MESH,
        )

    def head_rep_copy(d):
        return pltpu.make_async_remote_copy(
            src_ref=head_own.at[bits],
            dst_ref=head_rep.at[rep],
            send_sem=head_rs.at[d],
            recv_sem=head_rr.at[n_rep - 2 - d],
            device_id=(others[d], me),
            device_id_type=MESH,
        )

    def head_step(t):
        if t == 0:
            head_own[0] = head_ref[...]
            head_copy(0).start()
        elif t <= bits:
            head_copy(t - 1).wait_recv()
            head_own[t] = head_own[t - 1] + head_got[t - 1]
            if t < bits:
                head_copy(t).start()
            else:
                for d in range(n_rep - 1):
                    head_rep_copy(d).start()
                head_rep[rep] = head_own[bits]
        else:
            for d in range(n_rep - 1):
                head_rep_copy(d).wait_recv()
            total = head_rep[0]
            for r in range(1, n_rep):
                total = total + head_rep[r]
            head_out[...] = total

    def step(i, carry):
        for stage in reversed(range(len(lags))):
            c = i - lags[stage]

            @pl.when((c >= 0) & (c < chunks))
            def _(stage=stage, c=c):
                if stage == 0:
                    stage_make(c)
                elif stage == 1:
                    stage_core(c)
                elif stage <= count:
                    stage_bit(stage, c)
                else:
                    stage_end(c)

        for t in range(bits + 2):

            @pl.when(i == t)
            def _(t=t):
                head_step(t)

        return carry

    lax.fori_loop(0, chunks + lags[-1], step, 0)
    for c in range(chunks - 2, chunks):
        core_copy(c).wait_send()
    for k in range(1, count + 1):
        for c in range(chunks - slots[k], chunks):
            for h in range(2):
                bit_copy(k, h, c).wait_send()
    for t in range(bits):
        head_copy(t).wait_send()
    for d in range(n_rep - 1):
        head_rep_copy(d).wait_send()


def dense_sum(hidden, attended, right, small, head, n_rep, n_ep, split, collective_id):
    chunk = 512
    chunks = right.shape[1] // chunk + 1
    bits, rep_bits = bits_of(n_ep), bits_of(n_rep)
    tokens, width = hidden.shape
    rows = width // (n_rep * n_ep)
    axes, _, depths = exchanges(n_rep, n_ep)
    half = chunk // 2
    most = 2 * max(depths)
    vmem = pl.BlockSpec(memory_space=pltpu.VMEM)
    inner = (2,) * rep_bits + (rows,)
    scratch = [
        pltpu.VMEM((width + attended.shape[1], tokens), bf16),
        pltpu.VMEM((2, 2) + (2,) * (bits - 1) + inner + (chunk,), bf16),
        pltpu.VMEM((2,) + (2,) * (bits - 1) + inner + (chunk,), bf16),
    ]
    for k, depth in enumerate(depths):
        scratch += [pltpu.VMEM((2 * depth,) + (2,) * (len(axes) - k) + (rows, half), bf16)] * 2
    for k, depth in enumerate(depths):
        scratch += [pltpu.VMEM((2 * depth,) + (2,) * (len(axes) - k - 1) + (rows, half), bf16)] * 2
    scratch += [
        pltpu.VMEM((bits + 1,) + head.shape, f32),
        pltpu.VMEM((bits,) + head.shape, f32),
        pltpu.VMEM((n_rep,) + head.shape, f32),
        pltpu.SemaphoreType.DMA((2,)),
        pltpu.SemaphoreType.DMA((2,)),
        pltpu.SemaphoreType.DMA((len(axes) + 1, 2, most)),
        pltpu.SemaphoreType.DMA((len(axes) + 1, 2, most)),
        pltpu.SemaphoreType.DMA((bits,)),
        pltpu.SemaphoreType.DMA((bits,)),
        pltpu.SemaphoreType.DMA((n_rep - 1,)),
        pltpu.SemaphoreType.DMA((n_rep - 1,)),
    ]
    return pl.pallas_call(
        functools.partial(dense_sum_kernel, n_rep, n_ep, rows, chunks, split),
        out_shape=(
            jax.ShapeDtypeStruct((rows, chunks * chunk), f32),
            jax.ShapeDtypeStruct(head.shape, f32),
        ),
        in_specs=[vmem] * 5,
        out_specs=(vmem, vmem),
        scratch_shapes=scratch,
        compiler_params=pltpu.CompilerParams(
            collective_id=collective_id, has_side_effects=True, vmem_limit_bytes=VMEM_BYTES
        ),
        cost_estimate=pl.CostEstimate(flops=1000, bytes_accessed=1000, transcendentals=0),
        name="dense_sum",
    )(hidden, attended, right, small, head)


def expert_kernel(local, first, last, experts, width, hidden_of, *refs):
    (info, h_ref, g_ref, wg_all, wu_all, wd_all) = refs[:6]
    rest = list(refs[6:])
    prev_ref = None if first else rest.pop(0)
    y_ref, grad_ref = rest[:2]
    xs, gs, ds, hs, stage, prev_buf, wide, tall, in_sem, out_sem, prev_sem, grad_sem = rest[2:14]
    wg_ref, wu_ref, wd_ref, weight_sem = rest[14:]
    weights = [
        pltpu.make_async_copy(source.at[local], target, weight_sem.at[n])
        for n, (source, target) in enumerate(((wg_all, wg_ref), (wu_all, wu_ref), (wd_all, wd_ref)))
    ]
    for copy in weights:
        copy.start()
    shares = grad_ref.shape[0]
    wide_share, tall_share = width // shares, hidden_of // shares
    hidden = wg_ref.shape[1]
    units = info[0]
    expert = info[1]
    table = 8
    per_tile = TILE // UNIT
    tiles = (units + per_tile - 1) // per_tile
    most = xs.shape[0] // TILE
    floor_tiles = min(4, most)

    def unit_in(u, slot):
        source = pl.ds(pl.multiple_of(info[table + u], UNIT), UNIT)
        target = pl.ds(pl.multiple_of(u * UNIT, UNIT), UNIT)
        return (
            pltpu.make_async_copy(h_ref.at[source], xs.at[target], in_sem.at[0, slot]),
            pltpu.make_async_copy(g_ref.at[source], gs.at[target], in_sem.at[1, slot]),
        )

    def begin(u, carry):
        for copy in unit_in(u, u // per_tile):
            copy.start()
        return carry

    lax.fori_loop(0, units, begin, 0)

    def blank(u, carry):
        target = pl.ds(pl.multiple_of(u * UNIT, UNIT), UNIT)
        xs[target, :] = jnp.zeros((UNIT, xs.shape[1]), bf16)
        gs[target, :] = jnp.zeros((UNIT, gs.shape[1]), bf16)
        return carry

    lax.fori_loop(units, jnp.maximum(tiles, floor_tiles) * per_tile, blank, 0)

    def blank_tile(i, carry):
        target = pl.ds(pl.multiple_of(i * TILE, TILE), TILE)
        ds[target, :] = jnp.zeros((TILE, ds.shape[1]), bf16)
        hs[target, :] = jnp.zeros((TILE, hs.shape[1]), bf16)
        return carry

    lax.fori_loop(tiles, floor_tiles, blank_tile, 0)

    def prev_copy(i):
        rows = pl.ds(pl.multiple_of(i * TILE, TILE), TILE)
        return pltpu.make_async_copy(prev_ref.at[rows], prev_buf.at[i % 2], prev_sem.at[i % 2])

    if not first:
        prev_copy(0).start()

    def unit_out(u):
        target = pl.ds(pl.multiple_of(info[table + u], UNIT), UNIT)
        tile = u // per_tile
        source = pl.ds(pl.multiple_of((u % per_tile) * UNIT, UNIT), UNIT)
        return pltpu.make_async_copy(stage.at[tile % 2, source], y_ref.at[target], out_sem.at[tile % 2])

    def out_start(i):
        if last:
            lax.fori_loop(
                i * per_tile,
                jnp.minimum((i + 1) * per_tile, units),
                lambda u, c: (unit_out(u).start(), c)[1],
                0,
            )
        else:
            rows = pl.ds(pl.multiple_of(i * TILE, TILE), TILE)
            pltpu.make_async_copy(stage.at[i % 2], y_ref.at[rows], out_sem.at[i % 2]).start()

    def out_wait(i):
        if last:
            lax.fori_loop(
                i * per_tile,
                jnp.minimum((i + 1) * per_tile, units),
                lambda u, c: (unit_out(u).wait(), c)[1],
                0,
            )
        else:
            rows = pl.ds(pl.multiple_of(i * TILE, TILE), TILE)
            pltpu.make_async_copy(stage.at[i % 2], y_ref.at[rows], out_sem.at[i % 2]).wait()

    lane = lax.broadcasted_iota(jnp.int32, (TILE, EXT), 1)
    weight_lanes = (lane == expert) | (lane == expert + experts) | (lane == expert + 2 * experts)

    def tile_step(i, carry):
        def landed(u, c):
            for copy in unit_in(u, i):
                copy.wait()
            return c

        lax.fori_loop(i * per_tile, jnp.minimum((i + 1) * per_tile, units), landed, 0)
        rows = pl.ds(pl.multiple_of(i * TILE, TILE), TILE)
        x = xs[rows, :width]
        g = gs[rows, :]
        extra = xs[rows, width:].astype(f32)
        weight = jnp.sum(jnp.where(weight_lanes, extra, 0.0), axis=1, keepdims=True)
        gate = jnp.dot(x, wg_ref[...], preferred_element_type=f32)
        up = jnp.dot(x, wu_ref[...], preferred_element_type=f32)
        d_plain = lax.dot_general(g, wd_ref[...], NT, preferred_element_type=f32)
        sig = 1.0 / (1.0 + jnp.exp(-gate))
        silu = gate * sig
        hid = silu * up
        d_weight = jnp.sum(hid.astype(bf16).astype(f32) * d_plain, axis=1, keepdims=True)
        hs[rows, :] = (hid * weight).astype(bf16)
        d_hidden = d_plain * weight
        ds[rows, :hidden] = (d_hidden * up * sig * (1.0 + gate * (1.0 - sig))).astype(bf16)
        ds[rows, hidden:] = (d_hidden * silu).astype(bf16)

        @pl.when(i >= 2)
        def _():
            out_wait(i - 2)

        if not first:

            @pl.when(i + 1 < tiles)
            def _():
                prev_copy(i + 1).start()

            prev_copy(i).wait()
        slot = i % 2
        high = d_weight.astype(bf16).astype(f32)
        low = d_weight - high
        note = jnp.where(lane == expert, high, 0.0) + jnp.where(lane == expert + experts, low, 0.0)
        d_row = lax.dot_general(ds[rows, :hidden], wg_ref[...], NT, preferred_element_type=f32)
        d_row += lax.dot_general(ds[rows, hidden:], wu_ref[...], NT, preferred_element_type=f32)
        if not first:
            d_row += prev_buf[slot, :, :width].astype(f32)
            note += prev_buf[slot, :, width : width + EXT].astype(f32)
        stage[slot, :, :width] = d_row.astype(bf16)
        stage[slot, :, width : width + EXT] = note.astype(bf16)
        out = jnp.dot(hs[rows, :], wd_ref[...], preferred_element_type=f32)
        if not first:
            out += prev_buf[slot, :, width + EXT :].astype(f32)
        stage[slot, :, width + EXT :] = out.astype(bf16)
        out_start(i)
        return carry

    for copy in weights:
        copy.wait()
    lax.fori_loop(0, tiles, tile_step, 0)

    block = 256

    def grads(depth):
        def wide_copies(m):
            per = wide_share // block
            return tuple(
                pltpu.make_async_copy(
                    wide.at[m % 2, :, p * LANES : (p + 1) * LANES],
                    grad_ref.at[
                        m // per,
                        pl.ds(pl.multiple_of(p * wide_share + (m % per) * block, block), block),
                    ],
                    grad_sem.at[m % 2, p],
                )
                for p in range(2 * hidden // LANES)
            )

        def wide_step(m, carry):
            @pl.when(m >= 2)
            def _():
                for copy in wide_copies(m - 2):
                    copy.wait()

            columns = pl.ds(pl.multiple_of(m * block, block), block)
            wide[m % 2] = lax.dot_general(
                xs[:depth, columns], ds[:depth, :], TN, preferred_element_type=f32
            ).astype(bf16)
            for copy in wide_copies(m):
                copy.start()
            return carry

        count = width // block
        lax.fori_loop(0, count, wide_step, 0)
        for m in range(count - 2, count):
            for copy in wide_copies(m):
                copy.wait()

        piece = math.gcd(block, tall_share)
        base = 2 * hidden // LANES * wide_share

        def tall_copies(m):
            made = []
            for q in range(block // piece):
                first_row = m * block + q * piece
                share, inside = first_row // tall_share, first_row % tall_share
                for p in range(width // LANES):
                    rows = pl.ds(pl.multiple_of(base + p * tall_share + inside, piece), piece)
                    made.append(
                        pltpu.make_async_copy(
                            tall.at[m % 2, q * piece : (q + 1) * piece, p * LANES : (p + 1) * LANES],
                            grad_ref.at[share, rows],
                            grad_sem.at[m % 2, q * (width // LANES) + p],
                        )
                    )
            return made

        def tall_step(m, carry):
            @pl.when(m >= 2)
            def _():
                for copy in tall_copies(m - 2):
                    copy.wait()

            columns = pl.ds(pl.multiple_of(m * block, block), block)
            tall[m % 2] = lax.dot_general(
                hs[:depth, columns], gs[:depth, :], TN, preferred_element_type=f32
            ).astype(bf16)
            for copy in tall_copies(m):
                copy.start()
            return carry

        count = hidden // block
        lax.fori_loop(0, count, tall_step, 0)
        for m in range(count - 2, count):
            for copy in tall_copies(m):
                copy.wait()

    for choice in range(floor_tiles, most + 1):
        chosen = (tiles <= choice) if choice == floor_tiles else (tiles == choice)

        @pl.when(chosen)
        def _(choice=choice):
            grads(choice * TILE)

    @pl.when(tiles >= 2)
    def _():
        out_wait(tiles - 2)

    out_wait(tiles - 1)


def expert_pass(info, h_rows, g_rows, w_gate, w_up, w_down, local, prev, last, experts, shares):
    tokens, width = g_rows.shape
    hidden = w_gate.shape[2]
    wide_row = width + EXT + width
    any_spec = pl.BlockSpec(memory_space=pl.ANY)
    first = prev is None
    operands = [info, h_rows, g_rows, w_gate, w_up, w_down] + ([] if first else [prev])
    specs = [pl.BlockSpec(memory_space=pltpu.SMEM), any_spec, any_spec, any_spec, any_spec, any_spec]
    specs += [] if first else [any_spec]
    return pl.pallas_call(
        functools.partial(expert_kernel, local, first, last, experts, width, hidden),
        out_shape=(
            jax.ShapeDtypeStruct((tokens, wide_row), bf16),
            jax.ShapeDtypeStruct((shares, 3 * hidden * width // shares // LANES, LANES), bf16),
        ),
        in_specs=specs,
        out_specs=(any_spec,) * 2,
        scratch_shapes=[
            pltpu.VMEM((tokens, width + EXT), bf16),
            pltpu.VMEM((tokens, width), bf16),
            pltpu.VMEM((tokens, 2 * hidden), bf16),
            pltpu.VMEM((tokens, hidden), bf16),
            pltpu.VMEM((2, TILE, wide_row), bf16),
            pltpu.VMEM((2, TILE, wide_row), bf16),
            pltpu.VMEM((2, 256, 2 * hidden), bf16),
            pltpu.VMEM((2, 256, width), bf16),
            pltpu.SemaphoreType.DMA((2, tokens // TILE)),
            pltpu.SemaphoreType.DMA((2,)),
            pltpu.SemaphoreType.DMA((2,)),
            pltpu.SemaphoreType.DMA((2, max(2 * hidden // LANES, 256 // math.gcd(256, hidden // shares) * width // LANES))),
            pltpu.VMEM((width, hidden), bf16),
            pltpu.VMEM((width, hidden), bf16),
            pltpu.VMEM((hidden, width), bf16),
            pltpu.SemaphoreType.DMA((3,)),
        ],
        compiler_params=pltpu.CompilerParams(vmem_limit_bytes=VMEM_BYTES),
        cost_estimate=pl.CostEstimate(flops=1000, bytes_accessed=1000, transcendentals=0),
        name="experts",
    )(*operands)


def unit_table(lengths):
    per_sequence = TILE // UNIT
    counts = (lengths + UNIT - 1) // UNIT
    unit = jnp.arange(lengths.shape[0] * per_sequence, dtype=jnp.int32)
    live = (unit % per_sequence) < jnp.repeat(counts, per_sequence)
    place = jnp.cumsum(live.astype(jnp.int32)) - 1
    hit = (place[None, :] == unit[:, None]) & live[None, :]
    rows = jnp.sum(jnp.where(hit, unit[None, :] * UNIT, 0), axis=1)
    return (jnp.sum(counts), rows)


def split_three(value):
    high = lax.reduce_precision(value, 8, 7)
    rest = value - high
    middle = lax.reduce_precision(rest, 8, 7)
    return jnp.concatenate([high, middle, rest - middle], axis=-1)


def per_device(
    hidden_in,
    out_grad,
    attn_gain,
    w_q,
    key_weight,
    value_weight,
    w_o,
    ffn_gain,
    router_w,
    qk_gains,
    w_gate,
    w_up,
    w_down,
    lengths,
    routes,
    order,
):
    everywhere = ("rep", "ep")
    rep_count, ep_count = (lax.axis_size("rep"), lax.axis_size("ep"))
    rep_index, ep_index = (lax.axis_index("rep"), lax.axis_index("ep"))
    inputs = hidden_in[0].astype(f32)
    sequence_length, model_width = inputs.shape
    head_size = qk_gains.shape[1]
    wide_q, wide_kv = (w_q.shape[1], key_weight.shape[1])
    heads_q, heads_kv = (wide_q // head_size, wide_kv // head_size)
    groups = heads_q // heads_kv
    local_experts = w_gate.shape[0]
    experts = local_experts * ep_count
    top_count = routes.shape[2]
    score_scale = head_size ** (-0.5)
    group_lengths = lax.dynamic_slice_in_dim(lengths, rep_index * ep_count, ep_count)
    length = lax.dynamic_index_in_dim(group_lengths, ep_index, keepdims=False)
    positions = jnp.arange(sequence_length, dtype=jnp.int32)
    live = positions < length
    live_rows = live.astype(f32)

    expert_iota = jnp.arange(experts, dtype=jnp.int32)
    route_hot = routes[0][..., None] == expert_iota
    routed = jnp.any(route_hot, axis=1) & live[:, None]
    order_of = jnp.sum(
        jnp.where(route_hot, order[0].reshape(sequence_length, top_count)[..., None], 0), axis=1
    )
    sort_key = jnp.where(routed, order_of, sequence_length * top_count)
    loads = jnp.sum(routed.astype(jnp.int32), axis=0)

    own_rows = w_q.shape[0]
    load_columns = -(-experts // own_rows)
    load_block = jnp.pad(loads, (0, load_columns * own_rows - experts)).reshape(load_columns, own_rows).T
    small = jnp.concatenate(
        [router_w, attn_gain[:, None], ffn_gain[:, None], load_block.astype(bf16)], axis=1
    )
    small = jnp.pad(small, ((0, 0), (0, EXT - small.shape[1])))
    pack = jnp.concatenate([w_q, key_weight, value_weight, small], axis=1)
    mat_qkv = gather_weights(pack, rep_count, ep_count, 4).reshape(-1, pack.shape[1])

    wide_all = wide_q + 2 * wide_kv
    small_all = mat_qkv[:, wide_all:]
    mat_router = small_all[:, :experts]
    loads_all = (
        small_all[:, experts + 2 : experts + 2 + load_columns]
        .reshape(rep_count, ep_count, own_rows, load_columns)
        .transpose(0, 1, 3, 2)
        .reshape(rep_count, ep_count, load_columns * own_rows)[:, :, :experts]
        .astype(jnp.int32)
    )
    group_loads = lax.dynamic_index_in_dim(loads_all, rep_index, keepdims=False)
    earlier = (jnp.arange(ep_count) < ep_index)[:, None]
    load_prefix = jnp.sum(jnp.where(earlier, group_loads, 0), axis=0)
    capacity = 9 * top_count * jnp.sum(group_lengths) // (8 * experts)

    cosine_lookup, sine_lookup = rope_tables(sequence_length, head_size)
    sign = jnp.where(jnp.arange(head_size) < head_size // 2, -1.0, 1.0).astype(f32)
    turned_sine = sine_lookup * sign[None, :]
    (
        hidden_first,
        projected,
        attended,
        middle,
        h_two,
        logits,
        row_gain,
        rank,
        mat_o,
        grads_all,
    ) = attention_front(
        length.reshape(1),
        hidden_in[0],
        small_all,
        qk_gains.astype(f32),
        cosine_lookup,
        turned_sine,
        sort_key.astype(f32),
        mat_qkv,
        w_o,
        out_grad[0],
        rep_count,
        ep_count,
        heads_kv,
        groups,
        6,
    )
    logits = logits[:, :experts]
    gain_attn, gain_ffn = (row_gain[0], row_gain[1])
    mat_o = mat_o.reshape(-1, model_width)
    grads_all = grads_all.reshape(-1, model_width)
    norm_one, inv_one = rms_parts(inputs)
    norm_two, inv_two = rms_parts(middle)
    kept = routed & (load_prefix[None, :] + rank.T.astype(jnp.int32) < capacity)
    kept_float = kept.astype(f32)
    named = jnp.any(route_hot, axis=1)
    top_logit = jnp.max(jnp.where(named, logits, -jnp.inf), axis=1, keepdims=True)
    raised = jnp.where(named, jnp.exp(jnp.where(named, logits - top_logit, 0.0)), 0.0)
    route_gates = raised / jnp.sum(raised, axis=1, keepdims=True)
    pair_weight = route_gates * kept_float

    extra = split_three(pair_weight).astype(bf16)
    extra = jnp.pad(extra, ((0, 0), (0, EXT - extra.shape[1])))
    sent = jnp.concatenate([h_two, extra], axis=1)
    h_all = gather_tokens(sent, ep_count, 1)

    part = min(ep_count, 8)
    tokens = part * sequence_length
    sums = []
    y_parts = []
    for c in range(ep_count // part):
        live_units, unit_rows = unit_table(group_lengths[c * part : (c + 1) * part])
        h_rows = h_all[c * part : (c + 1) * part].reshape(tokens, model_width + EXT)
        g_rows = grads_all[c * tokens : (c + 1) * tokens]
        prev, found = None, []
        for local in range(local_experts):
            info = jnp.concatenate(
                [
                    jnp.stack([live_units, ep_index * local_experts + local]).astype(jnp.int32),
                    jnp.zeros((6,), jnp.int32),
                    unit_rows,
                ]
            )
            prev, weight_grads = expert_pass(
                info,
                h_rows,
                g_rows,
                w_gate,
                w_up,
                w_down,
                local,
                prev,
                local == local_experts - 1,
                experts,
                rep_count,
            )
            found.append(weight_grads)
        y_parts.append(prev.reshape(part, sequence_length, -1))
        sums.append(found)
    y_all = y_parts[0] if len(y_parts) == 1 else jnp.concatenate(y_parts, axis=0)
    hidden_units = w_gate.shape[2]
    wide_share, tall_share = model_width // rep_count, hidden_units // rep_count
    found = []
    for local in range(local_experts):
        total = sums[0][local]
        for more in sums[1:]:
            total = (total.astype(f32) + more[local].astype(f32)).astype(bf16)
        found.append(lax.psum_scatter(total, "rep", scatter_dimension=0, tiled=True))
    half_width = model_width // 2
    row_first, row_second = sum_tokens(
        y_all, ep_count, (0, half_width), (half_width, half_width + EXT), 2
    )
    live_column = live[:, None]
    grad_rows = out_grad[0].astype(f32) * live_rows[:, None]
    notes = row_second[:, half_width : half_width + 2 * experts]
    d_weight = jnp.where(live_column, notes[:, :experts] + notes[:, experts:], 0.0)
    d_gates = d_weight * kept_float
    d_logits = route_gates * (d_gates - jnp.sum(route_gates * d_gates, axis=-1, keepdims=True))

    router_float = mat_router.astype(f32)
    d_h_two = jnp.concatenate([row_first, row_second[:, :half_width]], axis=1)
    d_h_two = jnp.where(live_column, d_h_two, 0.0)
    d_h_two = d_h_two + jnp.dot(d_logits, router_float.T, precision=top_precision)
    grad_router = jnp.dot(h_two.astype(f32).T, d_logits, precision=top_precision)
    grad_ffn = jnp.sum(d_h_two * norm_two, axis=0)
    d_middle = grad_rows + rms_back(d_h_two * gain_ffn, norm_two, inv_two)
    d_middle_low = d_middle.astype(bf16)
    right, head, out_first, out_second = attention_back(
        length.reshape(1),
        projected,
        qk_gains.astype(f32),
        cosine_lookup,
        turned_sine,
        d_middle_low,
        mat_o,
        y_all,
        ep_count,
        (model_width + EXT, model_width + EXT + half_width),
        (half_width, half_width),
        heads_kv,
        groups,
        5,
    )
    moe_output = jnp.where(live_column, jnp.concatenate([out_first, out_second], axis=1), 0.0)
    layer_out = jnp.where(live_column, middle + moe_output, 0.0)
    d_qkv = right[:, :wide_all]
    d_h_one = jnp.einsum("tf,cf->tc", d_qkv, mat_qkv[:, :wide_all], preferred_element_type=f32)
    grad_attn = jnp.sum(d_h_one * norm_one, axis=0)
    grad_input = d_middle + rms_back(d_h_one * gain_attn, norm_one, inv_one)

    small_grads = jnp.concatenate([grad_router, grad_attn[:, None], grad_ffn[:, None]], axis=1)
    small_grads = jnp.pad(small_grads, ((0, 0), (0, EXT - small_grads.shape[1]))).astype(bf16)
    ep_bits = bits_of(ep_count)

    def owner_order(value, parts):
        shape = (rep_count,) + (2,) * ep_bits + (parts, own_rows, value.shape[1])
        axes = (ep_bits + 1,) + tuple(range(ep_bits, 0, -1)) + (0, ep_bits + 2, ep_bits + 3)
        return value.reshape(shape).transpose(axes).reshape(value.shape)

    splits = (wide_all // 512, (wide_all + model_width) // 512)
    layer_out, grad_input, head = lax.optimization_barrier((layer_out, grad_input, head))
    sums_all, head_sum = dense_sum(
        hidden_first, attended, right, owner_order(small_grads, 1), head, rep_count, ep_count, splits, 3
    )
    last = unpack(
        sums_all, found, wide_share, tall_share, model_width, hidden_units, wide_q, wide_kv, experts
    )
    return (
        layer_out[None],
        grad_input[None],
        last[8][experts],
        last[3],
        last[4],
        last[5],
        last[6],
        last[8][experts + 1],
        last[7],
        head_sum[:2],
        last[0],
        last[1],
        last[2],
    )


def solution(mesh):
    both = ("rep", "ep")
    placed = (
        P(both, None, None),
        P(both, None, None),
        P(both),
        P(both, None),
        P(both, None),
        P(both, None),
        P(both, None),
        P(both),
        P(both, None),
        P(),
        P("ep", None, None),
        P("ep", None, None),
        P("ep", None, None),
        P(),
        P(both, None, None),
        P(both, None),
    )
    return jax.shard_map(
        per_device,
        mesh=mesh,
        in_specs=placed,
        out_specs=(
            P(both, None, None),
            P(both, None, None),
            P(both),
            P(both, None),
            P(both, None),
            P(both, None),
            P(both, None),
            P(both),
            P(both, None),
            P(),
            P("ep", "rep", None),
            P("ep", "rep", None),
            P("ep", "rep", None),
        ),
        check_vma=False,
    )
```

```python
import functools
import math

import jax
import jax.numpy as jnp
from jax import lax
from jax.experimental import pallas as pl
from jax.experimental.pallas import tpu as pltpu
from jax.sharding import PartitionSpec as P

eps = 1e-06
rope_base = 1000000.0
top_precision = lax.Precision.HIGHEST
MESH = pl.DeviceIdType.MESH
f32, bf16 = jnp.float32, jnp.bfloat16
EXT = 128
UNIT = 16
LANES = 256
TILE = 256
VMEM_BYTES = 58 * 1024 * 1024
NT = (((1,), (1,)), ((), ()))
TN = (((0,), (0,)), ((), ()))


def rms_parts(value_rows):
    inverse = lax.rsqrt(jnp.mean(value_rows * value_rows, axis=-1, keepdims=True) + eps)
    return (value_rows * inverse, inverse)


def rms_back(grad_norm, normed, inverse):
    return inverse * (grad_norm - normed * jnp.mean(grad_norm * normed, axis=-1, keepdims=True))


def rope_tables(count, head_size):
    half_size = head_size // 2
    freqs = rope_base ** (-2.0 * jnp.arange(half_size, dtype=f32) / head_size)
    angles = jnp.arange(count, dtype=f32)[:, None] * freqs[None, :]
    cosine_lookup = jnp.concatenate([jnp.cos(angles), jnp.cos(angles)], axis=1)
    sine_lookup = jnp.concatenate([jnp.sin(angles), jnp.sin(angles)], axis=1)
    return (cosine_lookup, sine_lookup)


def bits_of(count):
    return count.bit_length() - 1


def gather_orders(count):
    bits = bits_of(count)
    up = list(range(1, bits)) + [0]
    down = list(range(bits - 1, 0, -1)) + [0]
    return (up, down)


def spans(bits):
    masks = [0]
    for bit in bits:
        masks = masks + [m | (1 << bit) for m in masks]
    return masks


def meet(peers):
    barrier = pltpu.get_barrier_semaphore()
    for peer in peers:
        pl.semaphore_signal(barrier, inc=1, device_id=peer, device_id_type=MESH)
    pl.semaphore_wait(barrier, len(peers))


def token_gather_kernel(count, x_ref, out_ref, send_sem, recv_sem, local_sem):
    rep, me = lax.axis_index("rep"), lax.axis_index("ep")
    bits = bits_of(count)
    half = x_ref.shape[0] // 2
    meet([(rep, me ^ (1 << b)) for b in range(bits)])
    local = pltpu.make_async_copy(x_ref, out_ref.at[me], local_sem)
    local.start()
    orders = gather_orders(count)
    copies = []

    def send(h, mask, bit):
        rows = pl.ds(h * half, half)
        source = x_ref.at[rows] if mask == 0 else out_ref.at[me ^ mask, rows]
        there = mask | (1 << bit)
        copy = pltpu.make_async_remote_copy(
            src_ref=source,
            dst_ref=out_ref.at[me ^ mask, rows],
            send_sem=send_sem.at[h, there],
            recv_sem=recv_sem.at[h, there],
            device_id=(rep, me ^ (1 << bit)),
            device_id_type=MESH,
        )
        copy.start()
        copies.append(copy)

    def arrived(h, mask):
        rows = pl.ds(h * half, half)
        pltpu.make_async_copy(
            x_ref.at[rows], out_ref.at[me ^ mask, rows], recv_sem.at[h, mask]
        ).wait()

    for stage in range(bits):
        for h in range(2):
            send(h, 0, orders[h][stage])
    for stage in range(bits):
        for low in spans(orders[0][:stage]):
            index = spans(orders[0][:stage]).index(low)
            for h in range(2):
                mask = spans(orders[h][:stage])[index] | (1 << orders[h][stage])
                arrived(h, mask)
                for later in range(stage + 1, bits):
                    send(h, mask, orders[h][later])
    for copy in copies:
        copy.wait_send()
    local.wait()


def gather_tokens(x, count, collective_id):
    return pl.pallas_call(
        functools.partial(token_gather_kernel, count),
        out_shape=jax.ShapeDtypeStruct((count,) + x.shape, x.dtype),
        in_specs=[pl.BlockSpec(memory_space=pl.ANY)],
        out_specs=pl.BlockSpec(memory_space=pl.ANY),
        scratch_shapes=[
            pltpu.SemaphoreType.DMA((2, count)),
            pltpu.SemaphoreType.DMA((2, count)),
            pltpu.SemaphoreType.DMA,
        ],
        compiler_params=pltpu.CompilerParams(collective_id=collective_id, has_side_effects=True),
        name="token_gather",
    )(x)


class BlockGather:
    def __init__(self, n_rep, n_ep, x_ref, out_ref, sems):
        self.n_rep, self.bits = n_rep, bits_of(n_ep)
        self.x_ref, self.out_ref = x_ref, out_ref
        self.send_sem, self.recv_sem, self.up_sem, self.down_sem, self.local_sem = sems
        self.rep, self.me = lax.axis_index("rep"), lax.axis_index("ep")
        split = -(-x_ref.shape[1] // 256) * 128
        self.columns = (pl.ds(0, split), pl.ds(split, x_ref.shape[1] - split))
        self.orders = gather_orders(n_ep)
        self.entries = [(0, 0)]
        for s in range(1, n_rep):
            self.entries += [(s, -1), (s, 1)]

    @staticmethod
    def sems(n_rep, n_ep):
        return [
            pltpu.SemaphoreType.DMA((2 * n_rep - 1, 2, n_ep)),
            pltpu.SemaphoreType.DMA((2 * n_rep - 1, 2, n_ep)),
            pltpu.SemaphoreType.DMA((n_rep, 2)),
            pltpu.SemaphoreType.DMA((n_rep, 2)),
            pltpu.SemaphoreType.DMA,
        ]

    def meet(self):
        barrier = pltpu.get_barrier_semaphore()
        peers = [(self.rep, self.me ^ (1 << b)) for b in range(self.bits)]
        for peer in peers:
            pl.semaphore_signal(barrier, inc=1, device_id=peer, device_id_type=MESH)
        if self.n_rep > 1:
            for side in (-1, 1):

                @pl.when(self.reaches(side))
                def _(side=side):
                    pl.semaphore_signal(barrier, inc=1, device_id=(self.rep + side, self.me), device_id_type=MESH)

        count = len(peers)
        if self.n_rep > 1:
            count = count + jnp.where(self.reaches(-1), 1, 0) + jnp.where(self.reaches(1), 1, 0)
        pl.semaphore_wait(barrier, count)

    def reaches(self, side):
        return self.rep > 0 if side < 0 else self.rep < self.n_rep - 1

    def active(self, k):
        steps, side = self.entries[k]
        return self.rep >= steps if side < 0 else self.rep + steps < self.n_rep

    def guarded(self, k, action):
        if k == 0:
            action()
        else:
            pl.when(self.active(k))(action)

    def row(self, k):
        steps, side = self.entries[k]
        return 0 if self.n_rep == 1 else lax.rem(self.rep + side * steps + self.n_rep, self.n_rep)

    def place(self, k, h, mask):
        return self.out_ref.at[self.row(k), self.me ^ mask, :, self.columns[h]]

    def source(self, k, h, mask):
        return self.x_ref.at[:, self.columns[h]] if k == 0 and mask == 0 else self.place(k, h, mask)

    def hop(self, k, h, mask, bit):
        there = mask | (1 << bit)
        return pltpu.make_async_remote_copy(
            src_ref=self.source(k, h, mask),
            dst_ref=self.place(k, h, mask),
            send_sem=self.send_sem.at[k, h, there],
            recv_sem=self.recv_sem.at[k, h, there],
            device_id=(self.rep, self.me ^ (1 << bit)),
            device_id_type=MESH,
        )

    def along(self, k, h, side):
        steps = self.entries[k][0]
        lane = (steps * 2 if side > 0 else steps * 2 + 1)
        return pltpu.make_async_remote_copy(
            src_ref=self.source(k, h, 0),
            dst_ref=self.place(k, h, 0),
            send_sem=(self.up_sem if side > 0 else self.down_sem).at[steps, h],
            recv_sem=self.recv_sem.at[lane + 1, h, 0],
            device_id=(self.rep + side, self.me),
            device_id_type=MESH,
        )

    def arrived(self, k, h, mask):
        target = self.place(k, h, mask)
        pltpu.make_async_copy(target, target, self.recv_sem.at[k, h, mask]).wait()

    def local(self):
        return pltpu.make_async_copy(self.x_ref, self.out_ref.at[self.row(0), self.me], self.local_sem)

    def spread(self, k):
        for stage in range(self.bits):
            for h in range(2):
                self.hop(k, h, 0, self.orders[h][stage]).start()

    def onward(self, k, act):
        sides = (-1, 1) if k == 0 else (-self.entries[k][1],)
        if self.n_rep == 1 or self.entries[k][0] == self.n_rep - 1:
            return
        for side in sides:

            @pl.when(self.reaches(side))
            def _(side=side):
                for h in range(2):
                    act(self.along(k, h, side))

    def begin(self):
        self.local().start()
        self.onward(0, lambda copy: copy.start())
        self.spread(0)

    def from_rep(self, k):
        def action():
            for h in range(2):
                self.arrived(k, h, 0)
            self.onward(k, lambda copy: copy.start())
            self.spread(k)

        self.guarded(k, action)

    def relay(self, k, h, mask, stage):
        def action():
            self.arrived(k, h, mask)
            for later in range(stage + 1, self.bits):
                self.hop(k, h, mask, self.orders[h][later]).start()

        self.guarded(k, action)

    def tree(self):
        for stage in range(self.bits):
            for index in range(1 << stage):
                for h in range(2):
                    yield h, spans(self.orders[h][:stage])[index] | (1 << self.orders[h][stage]), stage

    def events(self):
        due = []
        for k, (steps, _) in enumerate(self.entries):
            if k:
                due.append((16 * steps, len(due), functools.partial(self.from_rep, k)))
            for h, mask, stage in self.tree():
                when = 16 * steps + 15 + 10 * stage if stage < self.bits - 1 else 1000 + steps
                due.append((when, len(due), functools.partial(self.relay, k, h, mask, stage)))
        return [step for _, _, step in sorted(due, key=lambda entry: entry[:2])]

    def end(self):
        for k in range(len(self.entries)):

            def action(k=k):
                for stage in range(self.bits):
                    for h in range(2):
                        self.hop(k, h, 0, self.orders[h][stage]).wait_send()
                for h, mask, stage in self.tree():
                    for later in range(stage + 1, self.bits):
                        self.hop(k, h, mask, self.orders[h][later]).wait_send()
                self.onward(k, lambda copy: copy.wait_send())

            self.guarded(k, action)


def weight_gather_kernel(n_rep, n_ep, x_ref, out_ref, *sems):
    gather = BlockGather(n_rep, n_ep, x_ref, out_ref, sems)
    gather.meet()
    gather.begin()
    for event in gather.events():
        event()
    gather.end()
    gather.local().wait()


def gather_weights(x, n_rep, n_ep, collective_id):
    return pl.pallas_call(
        functools.partial(weight_gather_kernel, n_rep, n_ep),
        out_shape=jax.ShapeDtypeStruct((n_rep, n_ep) + x.shape, x.dtype),
        in_specs=[pl.BlockSpec(memory_space=pl.ANY)],
        out_specs=pl.BlockSpec(memory_space=pl.ANY),
        scratch_shapes=BlockGather.sems(n_rep, n_ep),
        compiler_params=pltpu.CompilerParams(collective_id=collective_id, has_side_effects=True),
        cost_estimate=pl.CostEstimate(flops=1000, bytes_accessed=1000, transcendentals=0),
        name="weight_gather",
    )(x)


COLUMNS = 512


def attention_front_kernel(n_rep, n_ep, experts, heads_kv, groups, scale, *refs):
    (length_ref, x_ref, small_ref, gains_ref, cos_ref, sin_ref, key_ref, turned_ref) = refs[:8]
    (mat_ref, wo_ref, own_g_ref) = refs[8:11]
    h_ref, proj_ref, att_ref, middle_ref, second_ref, logit_ref, row_ref, rank_ref, wo_all, g_all = refs[11:21]
    mat_buf, mat_sem, k_low, v_low, wo_buf, wo_sem = refs[21:27]
    gather = BlockGather(n_rep, n_ep, wo_ref, wo_all, refs[27:32])
    extra = BlockGather(1, n_ep, own_g_ref, g_all, refs[32:37])
    size = gains_ref.shape[1]
    tokens, width = x_ref.shape
    wide_q, wide_kv = heads_kv * groups * size, heads_kv * size
    chunks = (wide_q + 2 * wide_kv) // COLUMNS
    pairs = heads_kv * groups // 2
    group_blocks = n_ep // 2
    block_rows = wo_ref.shape[0]
    deep = group_blocks * block_rows
    early = chunks + pairs
    turns = early + n_rep * 2

    def mat_copy(i):
        columns = pl.ds(pl.multiple_of(i * COLUMNS, COLUMNS), COLUMNS)
        return pltpu.make_async_copy(mat_ref.at[:, columns], mat_buf.at[i % 2], mat_sem.at[i % 2])

    def wo_copy(n):
        blocks = pl.ds((n % 2) * group_blocks, group_blocks)
        return pltpu.make_async_copy(wo_all.at[n // 2, blocks], wo_buf.at[n % 2], wo_sem.at[n % 2])

    mat_copy(0).start()
    gather.meet()
    gather.begin()
    pick = lax.broadcasted_iota(jnp.int32, (8, EXT), 0) + experts == lax.broadcasted_iota(jnp.int32, (8, EXT), 1)
    picks = jnp.where(pick, 1.0, 0.0).astype(bf16)
    row_ref[...] = lax.dot_general(picks, small_ref[...], NT, preferred_element_type=f32)
    x = x_ref[...].astype(f32)
    x = x * lax.rsqrt(jnp.mean(x * x, axis=-1, keepdims=True) + eps)
    h_ref[...] = (x * row_ref[0:1, :]).astype(bf16)
    for e in range(experts):
        smaller = key_ref[:, e : e + 1] < turned_ref[e : e + 1, :]
        rank_ref[e : e + 1, :] = jnp.sum(jnp.where(smaller, 1.0, 0.0), axis=0, keepdims=True)

    def rotate(value):
        return value * cos_ref[...] + pltpu.roll(value, size // 2, 1) * sin_ref[...]

    def normed(value):
        return value * lax.rsqrt(jnp.mean(value * value, axis=-1, keepdims=True) + eps)

    query_pos = lax.broadcasted_iota(jnp.int32, (tokens, tokens), 0)
    key_pos = lax.broadcasted_iota(jnp.int32, (tokens, tokens), 1)
    allowed = (key_pos <= query_pos) & (key_pos < length_ref[0])

    def lanes(start):
        return pl.ds(pl.multiple_of(start, size), size)

    first = gather.events()
    first.insert(len(first) - len(first) // 6, extra.begin)
    second = extra.events()

    def shares(events, weights, start):
        given, total, done, reached = {}, sum(weights), 0, 0.0
        for n, weight in enumerate(weights):
            reached += weight
            upto = -(-len(events) * reached // total)
            upto = len(events) if n == len(weights) - 1 else int(upto)
            given[start + n] = events[done:upto]
            done = upto
        return given

    plan = {
        **shares(first, [1.0] * chunks + [4.0] * pairs, 0),
        **shares(second, [1.0] * (turns - early), early),
    }

    def turn(i, carry):
        @pl.when(i < chunks)
        def _():
            @pl.when(i + 1 < chunks)
            def _():
                mat_copy(i + 1).start()

            mat_copy(i).wait()
            columns = pl.ds(pl.multiple_of(i * COLUMNS, COLUMNS), COLUMNS)
            proj_ref[:, columns] = jnp.dot(h_ref[...], mat_buf[i % 2], preferred_element_type=f32)

        @pl.when((i >= chunks) & (i < early))
        def _():
            pair = i - chunks
            group = pair // (groups // 2)

            @pl.when(pair % (groups // 2) == 0)
            def _():
                key = normed(proj_ref[:, lanes(wide_q + group * size)])
                k_low[...] = rotate(key * gains_ref[1:2, :]).astype(bf16)
                v_low[...] = proj_ref[:, lanes(wide_q + wide_kv + group * size)].astype(bf16)

            for n in range(2):
                head = pair * 2 + n
                query = rotate(normed(proj_ref[:, lanes(head * size)]) * gains_ref[0:1, :]).astype(bf16)
                scores = lax.dot_general(query, k_low[...], NT, preferred_element_type=f32) * scale
                scores = jnp.where(allowed, scores, -1e30)
                raised = jnp.exp(scores - jnp.max(scores, axis=1, keepdims=True))
                probs = (raised * (1.0 / jnp.sum(raised, axis=1, keepdims=True))).astype(bf16)
                att_ref[:, lanes(head * size)] = jnp.dot(
                    probs, v_low[...], preferred_element_type=f32
                ).astype(bf16)

        @pl.when(i >= early)
        def _():
            n = i - early

            @pl.when(n == 0)
            def _():
                gather.local().wait()
                wo_copy(0).start()
                middle_ref[...] = x_ref[...].astype(f32)

            @pl.when(i + 1 < turns)
            def _():
                wo_copy(n + 1).start()

            wo_copy(n).wait()
            columns = pl.ds(pl.multiple_of(n * deep, deep), deep)
            middle_ref[...] += jnp.dot(
                att_ref[:, columns], wo_buf[n % 2].reshape(deep, width), preferred_element_type=f32
            )

        for k, mine in plan.items():
            if mine:

                @pl.when(i == k)
                def _(mine=mine):
                    for event in mine:
                        event()

        return carry

    lax.fori_loop(0, turns, turn, 0)
    step = 64
    for r in range(0, tokens, step):
        low = (normed(middle_ref[r : r + step, :]) * row_ref[1:2, :]).astype(bf16)
        second_ref[r : r + step, :] = low
    logit_ref[...] = jnp.dot(second_ref[...], small_ref[...], preferred_element_type=f32)
    gather.end()
    extra.end()
    extra.local().wait()


def attention_front(
    length, x, small, gains, cos, sin, key, mat, w_o, own_g, n_rep, n_ep, heads_kv, groups, collective_id
):
    tokens, width = x.shape
    size = gains.shape[1]
    experts = key.shape[1]
    vmem = pl.BlockSpec(memory_space=pltpu.VMEM)
    anywhere = pl.BlockSpec(memory_space=pl.ANY)
    wide_q = heads_kv * groups * size
    wide_all = wide_q + 2 * heads_kv * size
    return pl.pallas_call(
        functools.partial(attention_front_kernel, n_rep, n_ep, experts, heads_kv, groups, size ** (-0.5)),
        out_shape=(
            jax.ShapeDtypeStruct((tokens, width), bf16),
            jax.ShapeDtypeStruct((tokens, wide_all), f32),
            jax.ShapeDtypeStruct((tokens, wide_q), bf16),
            jax.ShapeDtypeStruct((tokens, width), f32),
            jax.ShapeDtypeStruct((tokens, width), bf16),
            jax.ShapeDtypeStruct((tokens, EXT), f32),
            jax.ShapeDtypeStruct((8, width), f32),
            jax.ShapeDtypeStruct((experts, tokens), f32),
            jax.ShapeDtypeStruct((n_rep, n_ep) + w_o.shape, bf16),
            jax.ShapeDtypeStruct((1, n_ep) + own_g.shape, bf16),
        ),
        in_specs=[pl.BlockSpec(memory_space=pltpu.SMEM)] + [vmem] * 7 + [anywhere] * 3,
        out_specs=(vmem,) * 8 + (anywhere,) * 2,
        scratch_shapes=[
            pltpu.VMEM((2, width, COLUMNS), bf16),
            pltpu.SemaphoreType.DMA((2,)),
            pltpu.VMEM((tokens, size), bf16),
            pltpu.VMEM((tokens, size), bf16),
            pltpu.VMEM((2, n_ep // 2) + w_o.shape, bf16),
            pltpu.SemaphoreType.DMA((2,)),
        ]
        + BlockGather.sems(n_rep, n_ep)
        + BlockGather.sems(1, n_ep),
        compiler_params=pltpu.CompilerParams(
            collective_id=collective_id, has_side_effects=True, vmem_limit_bytes=VMEM_BYTES
        ),
        cost_estimate=pl.CostEstimate(flops=1000, bytes_accessed=1000, transcendentals=0),
        name="attention_front",
    )(length, x, small, gains, cos, sin, key, key.T, mat, w_o, own_g)


def unpack_kernel(shares, experts, *refs):
    (sums,) = refs[:1]
    packs, outs = refs[1:-9], refs[-9:-6]
    q_ref, k_ref, v_ref, o_ref, router_ref, rows_ref = refs[-6:]
    for local, pack in enumerate(packs):
        start = 0
        for out, rows in zip(outs, shares):
            for p in range(out.shape[2] // LANES):
                out[local, :, p * LANES : (p + 1) * LANES] = pack[0, start : start + rows, :].astype(f32)
                start += rows
    start = 0
    for out in (q_ref, k_ref, v_ref):
        out[...] = sums[:, start : start + out.shape[1]]
        start += out.shape[1]
    for n in range(2):
        rows = sums.shape[0]
        o_ref[n * rows : (n + 1) * rows, :] = sums[:, start : start + o_ref.shape[1]]
        start += o_ref.shape[1]
    small = sums[:, start : start + EXT]
    router_ref[...] = small[:, :experts]
    rows_ref[...] = small.T


def unpack(sums, packs, wide_share, tall_share, width, hidden, wide_q, wide_kv, experts):
    count, rows = len(packs), sums.shape[0]
    vmem = pl.BlockSpec(memory_space=pltpu.VMEM)
    return pl.pallas_call(
        functools.partial(unpack_kernel, (wide_share, wide_share, tall_share), experts),
        out_shape=tuple(
            jax.ShapeDtypeStruct(shape, f32)
            for shape in (
                (count, wide_share, hidden),
                (count, wide_share, hidden),
                (count, tall_share, width),
                (rows, wide_q),
                (rows, wide_kv),
                (rows, wide_kv),
                (2 * rows, width),
                (rows, experts),
                (EXT, rows),
            )
        ),
        in_specs=[vmem] * (count + 1),
        out_specs=(vmem,) * 9,
        compiler_params=pltpu.CompilerParams(vmem_limit_bytes=VMEM_BYTES),
        cost_estimate=pl.CostEstimate(flops=1000, bytes_accessed=1000, transcendentals=0),
        name="unpack",
    )(sums, *packs)


class TokenSum:
    def __init__(self, count, y_ref, starts, results, scratch):
        self.bits = bits_of(count)
        self.y_ref, self.results = y_ref, results
        self.own, self.got = scratch[:2], scratch[2:4]
        self.send_sem, self.recv_sem, self.own_sem = scratch[4:7]
        self.rep, self.me = lax.axis_index("rep"), lax.axis_index("ep")
        self.orders = [list(reversed(o)) for o in gather_orders(count)]
        self.columns = [pl.ds(s, o.shape[2]) for s, o in zip(starts, self.own)]
        self.masks = [
            [list(reversed(spans(self.orders[h][k + 1 :]))) for k in range(self.bits)] for h in range(2)
        ]
        self.slots, self.seats = [], []
        for h in range(2):
            table = {}
            for stage in range(self.bits):
                for mask in self.masks[h][stage]:
                    table[(stage, mask)] = len(table)
            self.slots.append(table)
            self.seats.append({mask: i for i, mask in enumerate(self.masks[h][0])})

    @staticmethod
    def scratch(count, rows, widths):
        half = count // 2
        return [
            pltpu.VMEM((half, rows, widths[0]), bf16),
            pltpu.VMEM((half, rows, widths[1]), bf16),
            pltpu.VMEM((count - 1, rows, widths[0]), bf16),
            pltpu.VMEM((count - 1, rows, widths[1]), bf16),
            pltpu.SemaphoreType.DMA((2, count)),
            pltpu.SemaphoreType.DMA((2, count)),
            pltpu.SemaphoreType.DMA((2, half)),
        ]

    def meet(self):
        meet([(self.rep, self.me ^ (1 << b)) for b in range(self.bits)])

    def copy(self, h, stage, mask):
        bit = 1 << self.orders[h][stage]
        slot = self.slots[h][(stage, mask)]
        if stage == 0:
            source = self.y_ref.at[self.me ^ bit ^ mask, :, self.columns[h]]
        else:
            source = self.own[h].at[self.seats[h][bit | mask]]
        return pltpu.make_async_remote_copy(
            src_ref=source,
            dst_ref=self.got[h].at[slot],
            send_sem=self.send_sem.at[h, slot],
            recv_sem=self.recv_sem.at[h, slot],
            device_id=(self.rep, self.me ^ bit),
            device_id_type=MESH,
        )

    def load(self, h, mask):
        seat = self.seats[h][mask]
        return pltpu.make_async_copy(
            self.y_ref.at[self.me ^ mask, :, self.columns[h]], self.own[h].at[seat], self.own_sem.at[h, seat]
        )

    def begin(self):
        for i in range(len(self.masks[0][0])):
            for h in range(2):
                self.copy(h, 0, self.masks[h][0][i]).start()
                self.load(h, self.masks[h][0][i]).start()

    def add(self, h, stage, mask):
        slot, seat = self.slots[h][(stage, mask)], self.seats[h][mask]
        own, got = self.own[h], self.got[h]
        if stage == 0:
            self.load(h, mask).wait()
        self.copy(h, stage, mask).wait_recv()
        step = 32

        def body(i, carry):
            rows = pl.ds(pl.multiple_of(i * step, step), step)
            total = own[seat, rows, :].astype(f32) + got[slot, rows, :].astype(f32)
            if stage == self.bits - 1:
                self.results[h][rows, :] = total
            else:
                own[seat, rows, :] = total.astype(bf16)
            return carry

        lax.fori_loop(0, own.shape[1] // step, body, 0)

    def stage(self, stage):
        for i in range(len(self.masks[0][stage])):
            for h in range(2):
                mask = self.masks[h][stage][i]
                self.add(h, stage, mask)
                if stage + 1 < self.bits:
                    following = 1 << self.orders[h][stage + 1]
                    if mask & following:
                        self.copy(h, stage + 1, mask & ~following).start()

    def end(self):
        for h in range(2):
            for stage, mask in self.slots[h]:
                self.copy(h, stage, mask).wait_send()


def token_sum_kernel(count, starts, y_ref, first_ref, second_ref, *scratch):
    total = TokenSum(count, y_ref, starts, (first_ref, second_ref), scratch)
    total.meet()
    total.begin()
    for stage in range(total.bits):
        total.stage(stage)
    total.end()


def sum_tokens(y, count, starts, widths, collective_id):
    rows = y.shape[1]
    return pl.pallas_call(
        functools.partial(token_sum_kernel, count, starts),
        out_shape=tuple(jax.ShapeDtypeStruct((rows, w), f32) for w in widths),
        in_specs=[pl.BlockSpec(memory_space=pl.ANY)],
        out_specs=(pl.BlockSpec(memory_space=pltpu.VMEM),) * 2,
        scratch_shapes=TokenSum.scratch(count, rows, widths),
        compiler_params=pltpu.CompilerParams(
            collective_id=collective_id, has_side_effects=True, vmem_limit_bytes=VMEM_BYTES
        ),
        cost_estimate=pl.CostEstimate(flops=1000, bytes_accessed=1000, transcendentals=0),
        name="token_sum",
    )(y)


QUAD = 4


def attention_back_kernel(count, starts, heads_kv, groups, scale, *refs):
    (length_ref, proj_ref, gains_ref, cos_ref, sin_ref, mid_ref, wo_ref, y_ref) = refs[:8]
    right_ref, head_ref, first_ref, second_ref = refs[8:12]
    wo_buf, wo_sem, k_low, v_low, k_norm, dk_sum, dv_sum = refs[12:19]
    total = TokenSum(count, y_ref, starts, (first_ref, second_ref), refs[19:])
    size = gains_ref.shape[1]
    tokens = proj_ref.shape[0]
    heads_q = heads_kv * groups
    wide_q, wide_kv = heads_q * size, heads_kv * size
    per_group = groups // QUAD
    turns = heads_q // QUAD

    def wo_copy(i):
        rows = pl.ds(pl.multiple_of(i * QUAD * size, QUAD * size), QUAD * size)
        return pltpu.make_async_copy(wo_ref.at[rows], wo_buf.at[i % 2], wo_sem.at[i % 2])

    wo_copy(0).start()
    total.meet()
    total.begin()
    head_ref[...] = jnp.zeros_like(head_ref)
    sent = right_ref.shape[1] - wide_q - 2 * wide_kv
    for n in range(sent // mid_ref.shape[1]):
        start = wide_q + 2 * wide_kv + n * mid_ref.shape[1]
        right_ref[:, start : start + mid_ref.shape[1]] = mid_ref[...]

    def rotate(value):
        return value * cos_ref[...] + pltpu.roll(value, size // 2, 1) * sin_ref[...]

    def rotate_back(value):
        return value * cos_ref[...] - pltpu.roll(value, size // 2, 1) * sin_ref[...]

    def norm_parts(value):
        inverse = lax.rsqrt(jnp.mean(value * value, axis=-1, keepdims=True) + eps)
        return value * inverse, inverse

    def project_back(gradient, normed, inverse, row):
        scaled = rotate_back(gradient)
        head_ref[row : row + 1, :] += jnp.sum(scaled * normed, axis=0, keepdims=True)
        lifted = scaled * gains_ref[row : row + 1, :]
        mean = jnp.mean(lifted * normed, axis=-1, keepdims=True)
        return (inverse * (lifted - normed * mean)).astype(bf16)

    key_pos = lax.broadcasted_iota(jnp.int32, (tokens, tokens), 0)
    query_pos = lax.broadcasted_iota(jnp.int32, (tokens, tokens), 1)
    allowed = (key_pos <= query_pos) & (key_pos < length_ref[0])

    def lanes(start):
        return pl.ds(pl.multiple_of(start, size), size)

    def turn(i, carry):
        group = i // per_group
        for stage, when in ((0, min(1, turns - 1)), (1, turns - 2)):

            @pl.when(i == when)
            def _(stage=stage):
                if stage < total.bits - 1:
                    total.stage(stage)

        @pl.when(i % per_group == 0)
        def _():
            normed, inverse = norm_parts(proj_ref[:, lanes(wide_q + group * size)])
            k_norm[:, :size] = normed
            k_norm[:, size:] = jnp.broadcast_to(inverse, normed.shape)
            k_low[...] = rotate(normed * gains_ref[1:2, :]).astype(bf16)
            v_low[...] = proj_ref[:, lanes(wide_q + wide_kv + group * size)].astype(bf16)
            dk_sum[...] = jnp.zeros_like(dk_sum)
            dv_sum[...] = jnp.zeros_like(dv_sum)

        @pl.when(i + 1 < turns)
        def _():
            wo_copy(i + 1).start()

        wo_copy(i).wait()
        d_att = lax.dot_general(mid_ref[...], wo_buf[i % 2], NT, preferred_element_type=f32).astype(bf16)
        keys, values = k_low[...], v_low[...]
        dk, dv = dk_sum[...], dv_sum[...]
        for n in range(QUAD):
            head = i * QUAD + n
            d_out = d_att[:, n * size : (n + 1) * size]
            normed, inverse = norm_parts(proj_ref[:, lanes(head * size)])
            query = rotate(normed * gains_ref[0:1, :]).astype(bf16)
            scores = lax.dot_general(keys, query, NT, preferred_element_type=f32) * scale
            scores = jnp.where(allowed, scores, -1e30)
            raised = jnp.exp(scores - jnp.max(scores, axis=0, keepdims=True))
            probs = raised * (1.0 / jnp.sum(raised, axis=0, keepdims=True))
            dv += jnp.dot(probs.astype(bf16), d_out, preferred_element_type=f32)
            d_probs = lax.dot_general(values, d_out, NT, preferred_element_type=f32)
            weighted = probs * d_probs
            d_scores = (weighted - probs * jnp.sum(weighted, axis=0, keepdims=True)).astype(bf16)
            dk += jnp.dot(d_scores, query, preferred_element_type=f32)
            d_query = lax.dot_general(d_scores, keys, TN, preferred_element_type=f32) * scale
            right_ref[:, lanes(head * size)] = project_back(d_query, normed, inverse, 0)
        dk_sum[...] = dk
        dv_sum[...] = dv

        @pl.when(i % per_group == per_group - 1)
        def _():
            right_ref[:, lanes(wide_q + group * size)] = project_back(
                dk_sum[...] * scale, k_norm[:, :size], k_norm[:, size:], 1
            )
            right_ref[:, lanes(wide_q + wide_kv + group * size)] = dv_sum[...].astype(bf16)

        return carry

    lax.fori_loop(0, turns, turn, 0)
    for stage in range(min(2, total.bits - 1), total.bits):
        total.stage(stage)
    total.end()


def attention_back(length, proj, gains, cos, sin, d_mid, mat_o, y, count, starts, widths, heads_kv, groups, collective_id):
    tokens, width = d_mid.shape
    size = gains.shape[1]
    vmem = pl.BlockSpec(memory_space=pltpu.VMEM)
    anywhere = pl.BlockSpec(memory_space=pl.ANY)
    columns = (heads_kv * groups + 2 * heads_kv) * size + 2 * width
    return pl.pallas_call(
        functools.partial(attention_back_kernel, count, starts, heads_kv, groups, size ** (-0.5)),
        out_shape=(
            jax.ShapeDtypeStruct((tokens, columns), bf16),
            jax.ShapeDtypeStruct((8, size), f32),
        )
        + tuple(jax.ShapeDtypeStruct((tokens, w), f32) for w in widths),
        in_specs=[pl.BlockSpec(memory_space=pltpu.SMEM)] + [vmem] * 5 + [anywhere] * 2,
        out_specs=(vmem,) * 4,
        scratch_shapes=[
            pltpu.VMEM((2, QUAD * size, width), bf16),
            pltpu.SemaphoreType.DMA((2,)),
            pltpu.VMEM((tokens, size), bf16),
            pltpu.VMEM((tokens, size), bf16),
            pltpu.VMEM((tokens, 2 * size), f32),
            pltpu.VMEM((tokens, size), f32),
            pltpu.VMEM((tokens, size), f32),
        ]
        + TokenSum.scratch(count, tokens, widths),
        compiler_params=pltpu.CompilerParams(
            collective_id=collective_id, has_side_effects=True, vmem_limit_bytes=VMEM_BYTES
        ),
        cost_estimate=pl.CostEstimate(flops=1000, bytes_accessed=1000, transcendentals=0),
        name="attention_back",
    )(length, proj, gains, cos, sin, d_mid, mat_o, y)


def exchanges(n_rep, n_ep):
    near = [(0, b) for b in range(1, bits_of(n_ep))]
    far = [(1, b) for b in range(bits_of(n_rep))]
    return near + far[::-1], (near + far, near[::-1] + far), [2] * len(near) + [3] * len(far)


def dense_sum_kernel(n_rep, n_ep, rows, chunks, split, *refs):
    hidden_ref, att_ref, right_ref, small_ref, head_ref, out_ref, head_out = refs[:7]
    rest = list(refs[7:])
    bits, rep_bits = bits_of(n_ep), bits_of(n_rep)
    wide = right_ref.shape[1] // (chunks - 1)
    half = wide // 2
    rep, me = lax.axis_index("rep"), lax.axis_index("ep")
    axes, orders, depths = exchanges(n_rep, n_ep)
    count = len(axes)
    mine = {axis: lax.rem(lax.div(rep if axis[0] else me, 1 << axis[1]), 2) for axis in axes + [(0, 0)]}
    left_ref, part, got_core = rest[:3]
    acc = [None] + [rest[3 + 2 * k : 5 + 2 * k] for k in range(count)]
    rest = rest[3 + 2 * count :]
    got = [None] + [rest[2 * k : 2 * k + 2] for k in range(count)]
    rest = rest[2 * count :]
    head_own, head_got, head_rep = rest[:3]
    core_send, core_recv, step_send, step_recv, head_send, head_recv, head_rs, head_rr = rest[3:]
    left = [[[a for a in axes if a not in o[:k]] for k in range(count)] for o in orders]
    lags = [0, 1]
    for depth in depths:
        lags.append(lags[-1] + depth)
    slots = [None] + [2 * depth for depth in depths]
    others = [lax.rem(rep + d, n_rep) for d in range(1, n_rep)]
    meet([(rep, me ^ (1 << b)) for b in range(bits)] + [(other, me) for other in others])

    def core_copy(c):
        slot = lax.rem(c, 2)
        return pltpu.make_async_remote_copy(
            src_ref=part.at[slot, 1 - mine[(0, 0)]],
            dst_ref=got_core.at[slot],
            send_sem=core_send.at[slot],
            recv_sem=core_recv.at[slot],
            device_id=(rep, me ^ 1),
            device_id_type=MESH,
        )

    def pick(k, h, which):
        axis = orders[h][k - 1]
        return (slice(None),) * left[h][k - 1].index(axis) + (which(mine[axis]),)

    def bit_copy(k, h, c):
        slot = lax.rem(c, slots[k])
        on_rep, bit = orders[h][k - 1]
        return pltpu.make_async_remote_copy(
            src_ref=acc[k][h].at[(slot,) + pick(k, h, lambda m: 1 - m)],
            dst_ref=got[k][h].at[slot],
            send_sem=step_send.at[k, h, slot],
            recv_sem=step_recv.at[k, h, slot],
            device_id=(rep ^ (1 << bit), me) if on_rep else (rep, me ^ (1 << bit)),
            device_id_type=MESH,
        )

    corners = [()]
    for _ in range(bits - 1):
        corners = [c + (v,) for c in corners for v in range(2)]
    block = n_rep * rows
    side_rows = len(corners) * block
    inner = (2,) * rep_bits

    def place_rows(source, which_of):
        per = 128 // rows
        for b in range(source.shape[1] // 128):
            turned = source[:, b * 128 : (b + 1) * 128].astype(f32).T.astype(bf16)
            for q in range(per):
                which, owner = which_of(b * per + q)
                r, e = owner // n_ep, owner % n_ep
                corner = sum(((e >> bit) & 1) << (bits - 1 - bit) for bit in range(1, bits))
                start = (which * 2 + (e & 1)) * side_rows + corner * block + r * rows
                left_ref[start : start + rows, :] = turned[q * rows : (q + 1) * rows, :]

    place_rows(hidden_ref, lambda n: (0, n))
    place_rows(att_ref, lambda n: (1 + n % 2, n // 2))

    def stage_make(c):
        slot = lax.rem(c, 2)

        @pl.when(c >= 2)
        def _():
            core_copy(c - 2).wait_send()

        @pl.when(c < chunks - 1)
        def _():
            which = jnp.where(c >= split[0], 1, 0) + jnp.where(c >= split[1], 1, 0)
            columns = pl.ds(pl.multiple_of(c * wide, wide), wide)
            weights = right_ref[:, columns]
            for side in (1, 0):
                which_side = 1 - mine[(0, 0)] if side else mine[(0, 0)]
                for n, corner in enumerate(corners):
                    start = (which * 2 + which_side) * side_rows + n * block
                    value = jnp.dot(
                        left_ref[pl.ds(pl.multiple_of(start, block), block), :],
                        weights,
                        preferred_element_type=f32,
                    )
                    part[(slot, which_side) + corner] = value.astype(bf16).reshape(inner + (rows, wide))

        @pl.when(c == chunks - 1)
        def _():
            thin = small_ref.shape[1]
            lead = (slice(None),) * (rep_bits + 1)
            for side in range(2):
                for n, corner in enumerate(corners):
                    value = small_ref[pl.ds(side * side_rows + n * block, block), :].reshape(inner + (rows, thin))
                    blank = jnp.zeros(inner + (rows, wide - thin), bf16)
                    part[(slot, side) + corner + lead + (slice(0, thin),)] = value
                    part[(slot, side) + corner + lead + (slice(thin, wide),)] = blank

        core_copy(c).start()

    def stage_core(c):
        slot, put = lax.rem(c, 2), lax.rem(c, slots[1])

        @pl.when(c >= slots[1])
        def _():
            for h in range(2):
                bit_copy(1, h, c - slots[1]).wait_send()

        core_copy(c).wait_recv()
        for corner in corners:
            total = part[(slot, mine[(0, 0)]) + corner].astype(f32) + got_core[(slot,) + corner].astype(f32)
            total = total.astype(bf16)
            for h in range(2):
                acc[1][h][(put,) + corner] = total[..., h * half : (h + 1) * half]
        for h in range(2):
            bit_copy(1, h, c).start()

    def joined(k, h, c):
        slot = lax.rem(c, slots[k])
        return acc[k][h][(slot,) + pick(k, h, lambda m: m)].astype(f32) + got[k][h][slot].astype(f32)

    def stage_bit(k, c):
        for h in range(2):

            @pl.when(c >= slots[k])
            def _(h=h):
                bit_copy(k, h, c - slots[k]).wait_send()

            bit_copy(k - 1, h, c).wait_recv()
            acc[k][h][lax.rem(c, slots[k])] = joined(k - 1, h, c).astype(bf16)
            bit_copy(k, h, c).start()

    def stage_end(c):
        for h in range(2):
            bit_copy(count, h, c).wait_recv()
            out_ref[:, pl.ds(pl.multiple_of(c * wide + h * half, half), half)] = joined(count, h, c)

    def head_copy(t):
        return pltpu.make_async_remote_copy(
            src_ref=head_own.at[t],
            dst_ref=head_got.at[t],
            send_sem=head_send.at[t],
            recv_sem=head_recv.at[t],
            device_id=(rep, me ^ (1 << t)),
            device_id_type=MESH,
        )

    def head_rep_copy(d):
        return pltpu.make_async_remote_copy(
            src_ref=head_own.at[bits],
            dst_ref=head_rep.at[rep],
            send_sem=head_rs.at[d],
            recv_sem=head_rr.at[n_rep - 2 - d],
            device_id=(others[d], me),
            device_id_type=MESH,
        )

    def head_step(t):
        if t == 0:
            head_own[0] = head_ref[...]
            head_copy(0).start()
        elif t <= bits:
            head_copy(t - 1).wait_recv()
            head_own[t] = head_own[t - 1] + head_got[t - 1]
            if t < bits:
                head_copy(t).start()
            else:
                for d in range(n_rep - 1):
                    head_rep_copy(d).start()
                head_rep[rep] = head_own[bits]
        else:
            for d in range(n_rep - 1):
                head_rep_copy(d).wait_recv()
            total = head_rep[0]
            for r in range(1, n_rep):
                total = total + head_rep[r]
            head_out[...] = total

    def step(i, carry):
        for stage in reversed(range(len(lags))):
            c = i - lags[stage]

            @pl.when((c >= 0) & (c < chunks))
            def _(stage=stage, c=c):
                if stage == 0:
                    stage_make(c)
                elif stage == 1:
                    stage_core(c)
                elif stage <= count:
                    stage_bit(stage, c)
                else:
                    stage_end(c)

        for t in range(bits + 2):

            @pl.when(i == t)
            def _(t=t):
                head_step(t)

        return carry

    lax.fori_loop(0, chunks + lags[-1], step, 0)
    for c in range(chunks - 2, chunks):
        core_copy(c).wait_send()
    for k in range(1, count + 1):
        for c in range(chunks - slots[k], chunks):
            for h in range(2):
                bit_copy(k, h, c).wait_send()
    for t in range(bits):
        head_copy(t).wait_send()
    for d in range(n_rep - 1):
        head_rep_copy(d).wait_send()


def dense_sum(hidden, attended, right, small, head, n_rep, n_ep, split, collective_id):
    chunk = 512
    chunks = right.shape[1] // chunk + 1
    bits, rep_bits = bits_of(n_ep), bits_of(n_rep)
    tokens, width = hidden.shape
    rows = width // (n_rep * n_ep)
    axes, _, depths = exchanges(n_rep, n_ep)
    half = chunk // 2
    most = 2 * max(depths)
    vmem = pl.BlockSpec(memory_space=pltpu.VMEM)
    inner = (2,) * rep_bits + (rows,)
    scratch = [
        pltpu.VMEM((width + attended.shape[1], tokens), bf16),
        pltpu.VMEM((2, 2) + (2,) * (bits - 1) + inner + (chunk,), bf16),
        pltpu.VMEM((2,) + (2,) * (bits - 1) + inner + (chunk,), bf16),
    ]
    for k, depth in enumerate(depths):
        scratch += [pltpu.VMEM((2 * depth,) + (2,) * (len(axes) - k) + (rows, half), bf16)] * 2
    for k, depth in enumerate(depths):
        scratch += [pltpu.VMEM((2 * depth,) + (2,) * (len(axes) - k - 1) + (rows, half), bf16)] * 2
    scratch += [
        pltpu.VMEM((bits + 1,) + head.shape, f32),
        pltpu.VMEM((bits,) + head.shape, f32),
        pltpu.VMEM((n_rep,) + head.shape, f32),
        pltpu.SemaphoreType.DMA((2,)),
        pltpu.SemaphoreType.DMA((2,)),
        pltpu.SemaphoreType.DMA((len(axes) + 1, 2, most)),
        pltpu.SemaphoreType.DMA((len(axes) + 1, 2, most)),
        pltpu.SemaphoreType.DMA((bits,)),
        pltpu.SemaphoreType.DMA((bits,)),
        pltpu.SemaphoreType.DMA((n_rep - 1,)),
        pltpu.SemaphoreType.DMA((n_rep - 1,)),
    ]
    return pl.pallas_call(
        functools.partial(dense_sum_kernel, n_rep, n_ep, rows, chunks, split),
        out_shape=(
            jax.ShapeDtypeStruct((rows, chunks * chunk), f32),
            jax.ShapeDtypeStruct(head.shape, f32),
        ),
        in_specs=[vmem] * 5,
        out_specs=(vmem, vmem),
        scratch_shapes=scratch,
        compiler_params=pltpu.CompilerParams(
            collective_id=collective_id, has_side_effects=True, vmem_limit_bytes=VMEM_BYTES
        ),
        cost_estimate=pl.CostEstimate(flops=1000, bytes_accessed=1000, transcendentals=0),
        name="dense_sum",
    )(hidden, attended, right, small, head)


def expert_kernel(local, experts, width, hidden_of, *refs):
    (info, h_ref, g_ref, wg_all, wu_all, wd_all) = refs[:6]
    save_ref, grad_ref = refs[6:8]
    xs, gs, ds, hs, notes, wide, tall, in_sem, save_sem, grad_sem = refs[8:18]
    wg_ref, wu_ref, wd_ref, weight_sem = refs[18:]
    weights = [
        pltpu.make_async_copy(source.at[local], target, weight_sem.at[n])
        for n, (source, target) in enumerate(((wg_all, wg_ref), (wu_all, wu_ref), (wd_all, wd_ref)))
    ]
    for copy in weights:
        copy.start()
    shares = grad_ref.shape[0]
    wide_share, tall_share = width // shares, hidden_of // shares
    hidden = wg_ref.shape[1]
    units = info[0]
    expert = info[1]
    table = 8
    per_tile = TILE // UNIT
    tiles = (units + per_tile - 1) // per_tile
    most = xs.shape[0] // TILE
    floor_tiles = min(4, most)

    def unit_in(u, slot):
        source = pl.ds(pl.multiple_of(info[table + u], UNIT), UNIT)
        target = pl.ds(pl.multiple_of(u * UNIT, UNIT), UNIT)
        return (
            pltpu.make_async_copy(h_ref.at[source], xs.at[target], in_sem.at[0, slot]),
            pltpu.make_async_copy(g_ref.at[source], gs.at[target], in_sem.at[1, slot]),
        )

    def begin(u, carry):
        for copy in unit_in(u, u // per_tile):
            copy.start()
        return carry

    lax.fori_loop(0, units, begin, 0)

    def blank(u, carry):
        target = pl.ds(pl.multiple_of(u * UNIT, UNIT), UNIT)
        xs[target, :] = jnp.zeros((UNIT, xs.shape[1]), bf16)
        gs[target, :] = jnp.zeros((UNIT, gs.shape[1]), bf16)
        return carry

    lax.fori_loop(units, jnp.maximum(tiles, floor_tiles) * per_tile, blank, 0)

    def blank_tile(i, carry):
        target = pl.ds(pl.multiple_of(i * TILE, TILE), TILE)
        ds[target, :] = jnp.zeros((TILE, ds.shape[1]), bf16)
        hs[target, :] = jnp.zeros((TILE, hs.shape[1]), bf16)
        return carry

    lax.fori_loop(tiles, floor_tiles, blank_tile, 0)

    lane = lax.broadcasted_iota(jnp.int32, (TILE, EXT), 1)
    weight_lanes = (lane == expert) | (lane == expert + experts) | (lane == expert + 2 * experts)

    def tile_step(i, carry):
        def landed(u, c):
            for copy in unit_in(u, i):
                copy.wait()
            return c

        lax.fori_loop(i * per_tile, jnp.minimum((i + 1) * per_tile, units), landed, 0)
        rows = pl.ds(pl.multiple_of(i * TILE, TILE), TILE)
        x = xs[rows, :width]
        g = gs[rows, :]
        extra = xs[rows, width:].astype(f32)
        weight = jnp.sum(jnp.where(weight_lanes, extra, 0.0), axis=1, keepdims=True)
        gate = jnp.dot(x, wg_ref[...], preferred_element_type=f32)
        up = jnp.dot(x, wu_ref[...], preferred_element_type=f32)
        d_plain = lax.dot_general(g, wd_ref[...], NT, preferred_element_type=f32)
        sig = 1.0 / (1.0 + jnp.exp(-gate))
        silu = gate * sig
        hid = silu * up
        d_weight = jnp.sum(hid.astype(bf16).astype(f32) * d_plain, axis=1, keepdims=True)
        hs[rows, :] = (hid * weight).astype(bf16)
        d_hidden = d_plain * weight
        ds[rows, :hidden] = (d_hidden * up * sig * (1.0 + gate * (1.0 - sig))).astype(bf16)
        ds[rows, hidden:] = (d_hidden * silu).astype(bf16)

        high = d_weight.astype(bf16).astype(f32)
        low = d_weight - high
        note = jnp.where(lane == expert, high, 0.0) + jnp.where(lane == expert + experts, low, 0.0)
        notes[rows, :] = note.astype(bf16)
        return carry

    for copy in weights:
        copy.wait()
    lax.fori_loop(0, tiles, tile_step, 0)
    saves = [
        pltpu.make_async_copy(source, save_ref.at[:, start : start + source.shape[1]], save_sem.at[n])
        for n, (source, start) in enumerate(((ds, 0), (hs, 2 * hidden), (notes, 3 * hidden)))
    ]
    for copy in saves:
        copy.start()

    block = 256

    def grads(depth):
        def wide_copies(m):
            per = wide_share // block
            return tuple(
                pltpu.make_async_copy(
                    wide.at[m % 2, :, p * LANES : (p + 1) * LANES],
                    grad_ref.at[
                        m // per,
                        pl.ds(pl.multiple_of(p * wide_share + (m % per) * block, block), block),
                    ],
                    grad_sem.at[m % 2, p],
                )
                for p in range(2 * hidden // LANES)
            )

        def wide_step(m, carry):
            @pl.when(m >= 2)
            def _():
                for copy in wide_copies(m - 2):
                    copy.wait()

            columns = pl.ds(pl.multiple_of(m * block, block), block)
            wide[m % 2] = lax.dot_general(
                xs[:depth, columns], ds[:depth, :], TN, preferred_element_type=f32
            ).astype(bf16)
            for copy in wide_copies(m):
                copy.start()
            return carry

        count = width // block
        lax.fori_loop(0, count, wide_step, 0)
        for m in range(count - 2, count):
            for copy in wide_copies(m):
                copy.wait()

        piece = math.gcd(block, tall_share)
        base = 2 * hidden // LANES * wide_share

        def tall_copies(m):
            made = []
            for q in range(block // piece):
                first_row = m * block + q * piece
                share, inside = first_row // tall_share, first_row % tall_share
                for p in range(width // LANES):
                    rows = pl.ds(pl.multiple_of(base + p * tall_share + inside, piece), piece)
                    made.append(
                        pltpu.make_async_copy(
                            tall.at[m % 2, q * piece : (q + 1) * piece, p * LANES : (p + 1) * LANES],
                            grad_ref.at[share, rows],
                            grad_sem.at[m % 2, q * (width // LANES) + p],
                        )
                    )
            return made

        def tall_step(m, carry):
            @pl.when(m >= 2)
            def _():
                for copy in tall_copies(m - 2):
                    copy.wait()

            columns = pl.ds(pl.multiple_of(m * block, block), block)
            tall[m % 2] = lax.dot_general(
                hs[:depth, columns], gs[:depth, :], TN, preferred_element_type=f32
            ).astype(bf16)
            for copy in tall_copies(m):
                copy.start()
            return carry

        count = hidden // block
        lax.fori_loop(0, count, tall_step, 0)
        for m in range(count - 2, count):
            for copy in tall_copies(m):
                copy.wait()

    for choice in range(floor_tiles, most + 1):
        chosen = (tiles <= choice) if choice == floor_tiles else (tiles == choice)

        @pl.when(chosen)
        def _(choice=choice):
            grads(choice * TILE)

    for copy in saves:
        copy.wait()


def expert_pass(info, h_rows, g_rows, w_gate, w_up, w_down, local, experts, shares):
    tokens, width = g_rows.shape
    hidden = w_gate.shape[2]
    any_spec = pl.BlockSpec(memory_space=pl.ANY)
    pieces = 256 // math.gcd(256, hidden // shares) * width // LANES
    return pl.pallas_call(
        functools.partial(expert_kernel, local, experts, width, hidden),
        out_shape=(
            jax.ShapeDtypeStruct((tokens, 3 * hidden + EXT), bf16),
            jax.ShapeDtypeStruct((shares, 3 * hidden * width // shares // LANES, LANES), bf16),
        ),
        in_specs=[pl.BlockSpec(memory_space=pltpu.SMEM)] + [any_spec] * 5,
        out_specs=(any_spec,) * 2,
        scratch_shapes=[
            pltpu.VMEM((tokens, width + EXT), bf16),
            pltpu.VMEM((tokens, width), bf16),
            pltpu.VMEM((tokens, 2 * hidden), bf16),
            pltpu.VMEM((tokens, hidden), bf16),
            pltpu.VMEM((tokens, EXT), bf16),
            pltpu.VMEM((2, 256, 2 * hidden), bf16),
            pltpu.VMEM((2, 256, width), bf16),
            pltpu.SemaphoreType.DMA((2, tokens // TILE)),
            pltpu.SemaphoreType.DMA((3,)),
            pltpu.SemaphoreType.DMA((2, max(2 * hidden // LANES, pieces))),
            pltpu.VMEM((width, hidden), bf16),
            pltpu.VMEM((width, hidden), bf16),
            pltpu.VMEM((hidden, width), bf16),
            pltpu.SemaphoreType.DMA((3,)),
        ],
        compiler_params=pltpu.CompilerParams(vmem_limit_bytes=VMEM_BYTES),
        cost_estimate=pl.CostEstimate(flops=1000, bytes_accessed=1000, transcendentals=0),
        name="experts",
    )(info, h_rows, g_rows, w_gate, w_up, w_down)


def returned_kernel(local_count, width, hidden, *refs):
    info, wg_all, wu_all, wd_all = refs[:4]
    saves = refs[4 : 4 + local_count]
    y_ref = refs[4 + local_count]
    wg, wu, wd, held, stage, weight_sem, held_sem, out_sem = refs[5 + local_count :]
    weights = [
        pltpu.make_async_copy(source, target, weight_sem.at[n])
        for n, (source, target) in enumerate(((wg_all, wg), (wu_all, wu), (wd_all, wd)))
    ]
    for copy in weights:
        copy.start()
    units = info[0]
    table = 8
    per_tile = TILE // UNIT
    tiles = (units + per_tile - 1) // per_tile

    def held_copies(i):
        rows = pl.ds(pl.multiple_of(i * TILE, TILE), TILE)
        return [
            pltpu.make_async_copy(save.at[rows], held.at[i % 2, n], held_sem.at[i % 2, n])
            for n, save in enumerate(saves)
        ]

    for copy in held_copies(0):
        copy.start()

    def unit_out(u):
        target = pl.ds(pl.multiple_of(info[table + u], UNIT), UNIT)
        tile = u // per_tile
        source = pl.ds(pl.multiple_of((u % per_tile) * UNIT, UNIT), UNIT)
        return pltpu.make_async_copy(stage.at[tile % 2, source], y_ref.at[target], out_sem.at[tile % 2])

    def each_unit(i, act):
        def body(u, carry):
            act(unit_out(u))
            return carry

        lax.fori_loop(i * per_tile, jnp.minimum((i + 1) * per_tile, units), body, 0)

    for copy in weights:
        copy.wait()

    def tile_step(i, carry):
        slot = i % 2

        @pl.when(i >= 2)
        def _():
            each_unit(i - 2, lambda copy: copy.wait())

        @pl.when(i + 1 < tiles)
        def _():
            for copy in held_copies(i + 1):
                copy.start()

        for copy in held_copies(i):
            copy.wait()
        d_row = jnp.zeros((TILE, width), f32)
        out = jnp.zeros((TILE, width), f32)
        note = jnp.zeros((TILE, EXT), f32)
        for n in range(local_count):
            d_row += lax.dot_general(held[slot, n, :, :hidden], wg[n], NT, preferred_element_type=f32)
            d_row += lax.dot_general(
                held[slot, n, :, hidden : 2 * hidden], wu[n], NT, preferred_element_type=f32
            )
            note += held[slot, n, :, 3 * hidden :].astype(f32)
        stage[slot, :, :width] = d_row.astype(bf16)
        stage[slot, :, width : width + EXT] = note.astype(bf16)
        for n in range(local_count):
            out += jnp.dot(held[slot, n, :, 2 * hidden : 3 * hidden], wd[n], preferred_element_type=f32)
        stage[slot, :, width + EXT :] = out.astype(bf16)
        each_unit(i, lambda copy: copy.start())
        return carry

    lax.fori_loop(0, tiles, tile_step, 0)

    @pl.when(tiles >= 2)
    def _():
        each_unit(tiles - 2, lambda copy: copy.wait())

    each_unit(tiles - 1, lambda copy: copy.wait())


def returned_rows(info, w_gate, w_up, w_down, saves):
    local_count, width, hidden = w_gate.shape
    tokens, row = saves[0].shape
    wide_row = width + EXT + width
    any_spec = pl.BlockSpec(memory_space=pl.ANY)
    return pl.pallas_call(
        functools.partial(returned_kernel, local_count, width, hidden),
        out_shape=jax.ShapeDtypeStruct((tokens, wide_row), bf16),
        in_specs=[pl.BlockSpec(memory_space=pltpu.SMEM)] + [any_spec] * (3 + local_count),
        out_specs=any_spec,
        scratch_shapes=[
            pltpu.VMEM(w_gate.shape, bf16),
            pltpu.VMEM(w_up.shape, bf16),
            pltpu.VMEM(w_down.shape, bf16),
            pltpu.VMEM((2, local_count, TILE, row), bf16),
            pltpu.VMEM((2, TILE, wide_row), bf16),
            pltpu.SemaphoreType.DMA((3,)),
            pltpu.SemaphoreType.DMA((2, local_count)),
            pltpu.SemaphoreType.DMA((2,)),
        ],
        compiler_params=pltpu.CompilerParams(vmem_limit_bytes=VMEM_BYTES),
        cost_estimate=pl.CostEstimate(flops=1000, bytes_accessed=1000, transcendentals=0),
        name="returned_rows",
    )(info, w_gate, w_up, w_down, *saves)


def unit_table(lengths):
    per_sequence = TILE // UNIT
    counts = (lengths + UNIT - 1) // UNIT
    unit = jnp.arange(lengths.shape[0] * per_sequence, dtype=jnp.int32)
    live = (unit % per_sequence) < jnp.repeat(counts, per_sequence)
    place = jnp.cumsum(live.astype(jnp.int32)) - 1
    hit = (place[None, :] == unit[:, None]) & live[None, :]
    rows = jnp.sum(jnp.where(hit, unit[None, :] * UNIT, 0), axis=1)
    return (jnp.sum(counts), rows)


def split_three(value):
    high = lax.reduce_precision(value, 8, 7)
    rest = value - high
    middle = lax.reduce_precision(rest, 8, 7)
    return jnp.concatenate([high, middle, rest - middle], axis=-1)


def per_device(
    hidden_in,
    out_grad,
    attn_gain,
    w_q,
    key_weight,
    value_weight,
    w_o,
    ffn_gain,
    router_w,
    qk_gains,
    w_gate,
    w_up,
    w_down,
    lengths,
    routes,
    order,
):
    everywhere = ("rep", "ep")
    rep_count, ep_count = (lax.axis_size("rep"), lax.axis_size("ep"))
    rep_index, ep_index = (lax.axis_index("rep"), lax.axis_index("ep"))
    inputs = hidden_in[0].astype(f32)
    sequence_length, model_width = inputs.shape
    head_size = qk_gains.shape[1]
    wide_q, wide_kv = (w_q.shape[1], key_weight.shape[1])
    heads_q, heads_kv = (wide_q // head_size, wide_kv // head_size)
    groups = heads_q // heads_kv
    local_experts = w_gate.shape[0]
    experts = local_experts * ep_count
    top_count = routes.shape[2]
    score_scale = head_size ** (-0.5)
    group_lengths = lax.dynamic_slice_in_dim(lengths, rep_index * ep_count, ep_count)
    length = lax.dynamic_index_in_dim(group_lengths, ep_index, keepdims=False)
    positions = jnp.arange(sequence_length, dtype=jnp.int32)
    live = positions < length
    live_rows = live.astype(f32)

    expert_iota = jnp.arange(experts, dtype=jnp.int32)
    route_hot = routes[0][..., None] == expert_iota
    routed = jnp.any(route_hot, axis=1) & live[:, None]
    order_of = jnp.sum(
        jnp.where(route_hot, order[0].reshape(sequence_length, top_count)[..., None], 0), axis=1
    )
    sort_key = jnp.where(routed, order_of, sequence_length * top_count)
    loads = jnp.sum(routed.astype(jnp.int32), axis=0)

    own_rows = w_q.shape[0]
    load_columns = -(-experts // own_rows)
    load_block = jnp.pad(loads, (0, load_columns * own_rows - experts)).reshape(load_columns, own_rows).T
    small = jnp.concatenate(
        [router_w, attn_gain[:, None], ffn_gain[:, None], load_block.astype(bf16)], axis=1
    )
    small = jnp.pad(small, ((0, 0), (0, EXT - small.shape[1])))
    pack = jnp.concatenate([w_q, key_weight, value_weight, small], axis=1)
    mat_qkv = gather_weights(pack, rep_count, ep_count, 4).reshape(-1, pack.shape[1])

    wide_all = wide_q + 2 * wide_kv
    small_all = mat_qkv[:, wide_all:]
    mat_router = small_all[:, :experts]
    loads_all = (
        small_all[:, experts + 2 : experts + 2 + load_columns]
        .reshape(rep_count, ep_count, own_rows, load_columns)
        .transpose(0, 1, 3, 2)
        .reshape(rep_count, ep_count, load_columns * own_rows)[:, :, :experts]
        .astype(jnp.int32)
    )
    group_loads = lax.dynamic_index_in_dim(loads_all, rep_index, keepdims=False)
    earlier = (jnp.arange(ep_count) < ep_index)[:, None]
    load_prefix = jnp.sum(jnp.where(earlier, group_loads, 0), axis=0)
    capacity = 9 * top_count * jnp.sum(group_lengths) // (8 * experts)

    cosine_lookup, sine_lookup = rope_tables(sequence_length, head_size)
    sign = jnp.where(jnp.arange(head_size) < head_size // 2, -1.0, 1.0).astype(f32)
    turned_sine = sine_lookup * sign[None, :]
    (
        hidden_first,
        projected,
        attended,
        middle,
        h_two,
        logits,
        row_gain,
        rank,
        mat_o,
        grads_all,
    ) = attention_front(
        length.reshape(1),
        hidden_in[0],
        small_all,
        qk_gains.astype(f32),
        cosine_lookup,
        turned_sine,
        sort_key.astype(f32),
        mat_qkv,
        w_o,
        out_grad[0],
        rep_count,
        ep_count,
        heads_kv,
        groups,
        6,
    )
    logits = logits[:, :experts]
    gain_attn, gain_ffn = (row_gain[0], row_gain[1])
    mat_o = mat_o.reshape(-1, model_width)
    grads_all = grads_all.reshape(-1, model_width)
    norm_one, inv_one = rms_parts(inputs)
    norm_two, inv_two = rms_parts(middle)
    kept = routed & (load_prefix[None, :] + rank.T.astype(jnp.int32) < capacity)
    kept_float = kept.astype(f32)
    named = jnp.any(route_hot, axis=1)
    top_logit = jnp.max(jnp.where(named, logits, -jnp.inf), axis=1, keepdims=True)
    raised = jnp.where(named, jnp.exp(jnp.where(named, logits - top_logit, 0.0)), 0.0)
    route_gates = raised / jnp.sum(raised, axis=1, keepdims=True)
    pair_weight = route_gates * kept_float

    extra = split_three(pair_weight).astype(bf16)
    extra = jnp.pad(extra, ((0, 0), (0, EXT - extra.shape[1])))
    sent = jnp.concatenate([h_two, extra], axis=1)
    h_all = gather_tokens(sent, ep_count, 1)

    part = min(ep_count, 8)
    tokens = part * sequence_length
    sums = []
    y_parts = []
    for c in range(ep_count // part):
        live_units, unit_rows = unit_table(group_lengths[c * part : (c + 1) * part])
        h_rows = h_all[c * part : (c + 1) * part].reshape(tokens, model_width + EXT)
        g_rows = grads_all[c * tokens : (c + 1) * tokens]
        saves, found = [], []
        for local in range(local_experts):
            info = jnp.concatenate(
                [
                    jnp.stack([live_units, ep_index * local_experts + local]).astype(jnp.int32),
                    jnp.zeros((6,), jnp.int32),
                    unit_rows,
                ]
            )
            save, weight_grads = expert_pass(
                info, h_rows, g_rows, w_gate, w_up, w_down, local, experts, rep_count
            )
            saves.append(save)
            found.append(weight_grads)
        y_parts.append(returned_rows(info, w_gate, w_up, w_down, saves).reshape(part, sequence_length, -1))
        sums.append(found)
    y_all = y_parts[0] if len(y_parts) == 1 else jnp.concatenate(y_parts, axis=0)
    hidden_units = w_gate.shape[2]
    wide_share, tall_share = model_width // rep_count, hidden_units // rep_count
    found = []
    for local in range(local_experts):
        total = sums[0][local]
        for more in sums[1:]:
            total = (total.astype(f32) + more[local].astype(f32)).astype(bf16)
        found.append(lax.psum_scatter(total, "rep", scatter_dimension=0, tiled=True))
    half_width = model_width // 2
    row_first, row_second = sum_tokens(
        y_all, ep_count, (0, half_width), (half_width, half_width + EXT), 2
    )
    live_column = live[:, None]
    grad_rows = out_grad[0].astype(f32) * live_rows[:, None]
    notes = row_second[:, half_width : half_width + 2 * experts]
    d_weight = jnp.where(live_column, notes[:, :experts] + notes[:, experts:], 0.0)
    d_gates = d_weight * kept_float
    d_logits = route_gates * (d_gates - jnp.sum(route_gates * d_gates, axis=-1, keepdims=True))

    router_float = mat_router.astype(f32)
    d_h_two = jnp.concatenate([row_first, row_second[:, :half_width]], axis=1)
    d_h_two = jnp.where(live_column, d_h_two, 0.0)
    d_h_two = d_h_two + jnp.dot(d_logits, router_float.T, precision=top_precision)
    grad_router = jnp.dot(h_two.astype(f32).T, d_logits, precision=top_precision)
    grad_ffn = jnp.sum(d_h_two * norm_two, axis=0)
    d_middle = grad_rows + rms_back(d_h_two * gain_ffn, norm_two, inv_two)
    d_middle_low = d_middle.astype(bf16)
    right, head, out_first, out_second = attention_back(
        length.reshape(1),
        projected,
        qk_gains.astype(f32),
        cosine_lookup,
        turned_sine,
        d_middle_low,
        mat_o,
        y_all,
        ep_count,
        (model_width + EXT, model_width + EXT + half_width),
        (half_width, half_width),
        heads_kv,
        groups,
        5,
    )
    moe_output = jnp.where(live_column, jnp.concatenate([out_first, out_second], axis=1), 0.0)
    layer_out = jnp.where(live_column, middle + moe_output, 0.0)
    d_qkv = right[:, :wide_all]
    d_h_one = jnp.einsum("tf,cf->tc", d_qkv, mat_qkv[:, :wide_all], preferred_element_type=f32)
    grad_attn = jnp.sum(d_h_one * norm_one, axis=0)
    grad_input = d_middle + rms_back(d_h_one * gain_attn, norm_one, inv_one)

    small_grads = jnp.concatenate([grad_router, grad_attn[:, None], grad_ffn[:, None]], axis=1)
    small_grads = jnp.pad(small_grads, ((0, 0), (0, EXT - small_grads.shape[1]))).astype(bf16)
    ep_bits = bits_of(ep_count)

    def owner_order(value, parts):
        shape = (rep_count,) + (2,) * ep_bits + (parts, own_rows, value.shape[1])
        axes = (ep_bits + 1,) + tuple(range(ep_bits, 0, -1)) + (0, ep_bits + 2, ep_bits + 3)
        return value.reshape(shape).transpose(axes).reshape(value.shape)

    splits = (wide_all // 512, (wide_all + model_width) // 512)
    layer_out, grad_input, head = lax.optimization_barrier((layer_out, grad_input, head))
    sums_all, head_sum = dense_sum(
        hidden_first, attended, right, owner_order(small_grads, 1), head, rep_count, ep_count, splits, 3
    )
    last = unpack(
        sums_all, found, wide_share, tall_share, model_width, hidden_units, wide_q, wide_kv, experts
    )
    return (
        layer_out[None],
        grad_input[None],
        last[8][experts],
        last[3],
        last[4],
        last[5],
        last[6],
        last[8][experts + 1],
        last[7],
        head_sum[:2],
        last[0],
        last[1],
        last[2],
    )


def solution(mesh):
    both = ("rep", "ep")
    placed = (
        P(both, None, None),
        P(both, None, None),
        P(both),
        P(both, None),
        P(both, None),
        P(both, None),
        P(both, None),
        P(both),
        P(both, None),
        P(),
        P("ep", None, None),
        P("ep", None, None),
        P("ep", None, None),
        P(),
        P(both, None, None),
        P(both, None),
    )
    return jax.shard_map(
        per_device,
        mesh=mesh,
        in_specs=placed,
        out_specs=(
            P(both, None, None),
            P(both, None, None),
            P(both),
            P(both, None),
            P(both, None),
            P(both, None),
            P(both, None),
            P(both),
            P(both, None),
            P(),
            P("ep", "rep", None),
            P("ep", "rep", None),
            P("ep", "rep", None),
        ),
        check_vma=False,
    )
```

```python
import functools
import math

import jax
import jax.numpy as jnp
from jax import lax
from jax.experimental import pallas as pl
from jax.experimental.pallas import tpu as pltpu
from jax.sharding import PartitionSpec as P

eps = 1e-06
rope_base = 1000000.0
top_precision = lax.Precision.HIGHEST
MESH = pl.DeviceIdType.MESH
f32, bf16 = jnp.float32, jnp.bfloat16
EXT = 128
UNIT = 16
LANES = 256
TILE = 256
VMEM_BYTES = 58 * 1024 * 1024
NT = (((1,), (1,)), ((), ()))
TN = (((0,), (0,)), ((), ()))


def rms_parts(value_rows):
    inverse = lax.rsqrt(jnp.mean(value_rows * value_rows, axis=-1, keepdims=True) + eps)
    return (value_rows * inverse, inverse)


def rms_back(grad_norm, normed, inverse):
    return inverse * (grad_norm - normed * jnp.mean(grad_norm * normed, axis=-1, keepdims=True))


def rope_tables(count, head_size):
    half_size = head_size // 2
    freqs = rope_base ** (-2.0 * jnp.arange(half_size, dtype=f32) / head_size)
    angles = jnp.arange(count, dtype=f32)[:, None] * freqs[None, :]
    cosine_lookup = jnp.concatenate([jnp.cos(angles), jnp.cos(angles)], axis=1)
    sine_lookup = jnp.concatenate([jnp.sin(angles), jnp.sin(angles)], axis=1)
    return (cosine_lookup, sine_lookup)


def bits_of(count):
    return count.bit_length() - 1


def gather_orders(count):
    bits = bits_of(count)
    up = list(range(1, bits)) + [0]
    down = list(range(bits - 1, 0, -1)) + [0]
    return (up, down)


def spans(bits):
    masks = [0]
    for bit in bits:
        masks = masks + [m | (1 << bit) for m in masks]
    return masks


def meet(peers):
    barrier = pltpu.get_barrier_semaphore()
    for peer in peers:
        pl.semaphore_signal(barrier, inc=1, device_id=peer, device_id_type=MESH)
    pl.semaphore_wait(barrier, len(peers))


def token_gather_kernel(count, x_ref, out_ref, send_sem, recv_sem, local_sem):
    rep, me = lax.axis_index("rep"), lax.axis_index("ep")
    bits = bits_of(count)
    half = x_ref.shape[0] // 2
    meet([(rep, me ^ (1 << b)) for b in range(bits)])
    local = pltpu.make_async_copy(x_ref, out_ref.at[me], local_sem)
    local.start()
    orders = gather_orders(count)
    copies = []

    def send(h, mask, bit):
        rows = pl.ds(h * half, half)
        source = x_ref.at[rows] if mask == 0 else out_ref.at[me ^ mask, rows]
        there = mask | (1 << bit)
        copy = pltpu.make_async_remote_copy(
            src_ref=source,
            dst_ref=out_ref.at[me ^ mask, rows],
            send_sem=send_sem.at[h, there],
            recv_sem=recv_sem.at[h, there],
            device_id=(rep, me ^ (1 << bit)),
            device_id_type=MESH,
        )
        copy.start()
        copies.append(copy)

    def arrived(h, mask):
        rows = pl.ds(h * half, half)
        pltpu.make_async_copy(
            x_ref.at[rows], out_ref.at[me ^ mask, rows], recv_sem.at[h, mask]
        ).wait()

    for stage in range(bits):
        for h in range(2):
            send(h, 0, orders[h][stage])
    for stage in range(bits):
        for low in spans(orders[0][:stage]):
            index = spans(orders[0][:stage]).index(low)
            for h in range(2):
                mask = spans(orders[h][:stage])[index] | (1 << orders[h][stage])
                arrived(h, mask)
                for later in range(stage + 1, bits):
                    send(h, mask, orders[h][later])
    for copy in copies:
        copy.wait_send()
    local.wait()


def gather_tokens(x, count, collective_id):
    return pl.pallas_call(
        functools.partial(token_gather_kernel, count),
        out_shape=jax.ShapeDtypeStruct((count,) + x.shape, x.dtype),
        in_specs=[pl.BlockSpec(memory_space=pl.ANY)],
        out_specs=pl.BlockSpec(memory_space=pl.ANY),
        scratch_shapes=[
            pltpu.SemaphoreType.DMA((2, count)),
            pltpu.SemaphoreType.DMA((2, count)),
            pltpu.SemaphoreType.DMA,
        ],
        compiler_params=pltpu.CompilerParams(collective_id=collective_id, has_side_effects=True),
        name="token_gather",
    )(x)


class BlockGather:
    def __init__(self, n_rep, n_ep, x_ref, out_ref, sems):
        self.n_rep, self.bits = n_rep, bits_of(n_ep)
        self.x_ref, self.out_ref = x_ref, out_ref
        self.send_sem, self.recv_sem, self.up_sem, self.down_sem, self.local_sem = sems
        self.rep, self.me = lax.axis_index("rep"), lax.axis_index("ep")
        split = -(-x_ref.shape[1] // 256) * 128
        self.columns = (pl.ds(0, split), pl.ds(split, x_ref.shape[1] - split))
        self.orders = gather_orders(n_ep)
        self.entries = [(0, 0)]
        for s in range(1, n_rep):
            self.entries += [(s, -1), (s, 1)]

    @staticmethod
    def sems(n_rep, n_ep):
        return [
            pltpu.SemaphoreType.DMA((2 * n_rep - 1, 2, n_ep)),
            pltpu.SemaphoreType.DMA((2 * n_rep - 1, 2, n_ep)),
            pltpu.SemaphoreType.DMA((n_rep, 2)),
            pltpu.SemaphoreType.DMA((n_rep, 2)),
            pltpu.SemaphoreType.DMA,
        ]

    def meet(self):
        barrier = pltpu.get_barrier_semaphore()
        peers = [(self.rep, self.me ^ (1 << b)) for b in range(self.bits)]
        for peer in peers:
            pl.semaphore_signal(barrier, inc=1, device_id=peer, device_id_type=MESH)
        if self.n_rep > 1:
            for side in (-1, 1):

                @pl.when(self.reaches(side))
                def _(side=side):
                    pl.semaphore_signal(barrier, inc=1, device_id=(self.rep + side, self.me), device_id_type=MESH)

        count = len(peers)
        if self.n_rep > 1:
            count = count + jnp.where(self.reaches(-1), 1, 0) + jnp.where(self.reaches(1), 1, 0)
        pl.semaphore_wait(barrier, count)

    def reaches(self, side):
        return self.rep > 0 if side < 0 else self.rep < self.n_rep - 1

    def active(self, k):
        steps, side = self.entries[k]
        return self.rep >= steps if side < 0 else self.rep + steps < self.n_rep

    def guarded(self, k, action):
        if k == 0:
            action()
        else:
            pl.when(self.active(k))(action)

    def row(self, k):
        steps, side = self.entries[k]
        return 0 if self.n_rep == 1 else lax.rem(self.rep + side * steps + self.n_rep, self.n_rep)

    def place(self, k, h, mask):
        return self.out_ref.at[self.row(k), self.me ^ mask, :, self.columns[h]]

    def source(self, k, h, mask):
        return self.x_ref.at[:, self.columns[h]] if k == 0 and mask == 0 else self.place(k, h, mask)

    def hop(self, k, h, mask, bit):
        there = mask | (1 << bit)
        return pltpu.make_async_remote_copy(
            src_ref=self.source(k, h, mask),
            dst_ref=self.place(k, h, mask),
            send_sem=self.send_sem.at[k, h, there],
            recv_sem=self.recv_sem.at[k, h, there],
            device_id=(self.rep, self.me ^ (1 << bit)),
            device_id_type=MESH,
        )

    def along(self, k, h, side):
        steps = self.entries[k][0]
        lane = (steps * 2 if side > 0 else steps * 2 + 1)
        return pltpu.make_async_remote_copy(
            src_ref=self.source(k, h, 0),
            dst_ref=self.place(k, h, 0),
            send_sem=(self.up_sem if side > 0 else self.down_sem).at[steps, h],
            recv_sem=self.recv_sem.at[lane + 1, h, 0],
            device_id=(self.rep + side, self.me),
            device_id_type=MESH,
        )

    def arrived(self, k, h, mask):
        target = self.place(k, h, mask)
        pltpu.make_async_copy(target, target, self.recv_sem.at[k, h, mask]).wait()

    def local(self):
        return pltpu.make_async_copy(self.x_ref, self.out_ref.at[self.row(0), self.me], self.local_sem)

    def spread(self, k):
        for stage in range(self.bits):
            for h in range(2):
                self.hop(k, h, 0, self.orders[h][stage]).start()

    def onward(self, k, act):
        sides = (-1, 1) if k == 0 else (-self.entries[k][1],)
        if self.n_rep == 1 or self.entries[k][0] == self.n_rep - 1:
            return
        for side in sides:

            @pl.when(self.reaches(side))
            def _(side=side):
                for h in range(2):
                    act(self.along(k, h, side))

    def begin(self):
        self.local().start()
        self.onward(0, lambda copy: copy.start())
        self.spread(0)

    def from_rep(self, k):
        def action():
            for h in range(2):
                self.arrived(k, h, 0)
            self.onward(k, lambda copy: copy.start())
            self.spread(k)

        self.guarded(k, action)

    def relay(self, k, h, mask, stage):
        def action():
            self.arrived(k, h, mask)
            for later in range(stage + 1, self.bits):
                self.hop(k, h, mask, self.orders[h][later]).start()

        self.guarded(k, action)

    def tree(self):
        for stage in range(self.bits):
            for index in range(1 << stage):
                for h in range(2):
                    yield h, spans(self.orders[h][:stage])[index] | (1 << self.orders[h][stage]), stage

    def events(self):
        due = []
        for k, (steps, _) in enumerate(self.entries):
            if k:
                due.append((16 * steps, len(due), functools.partial(self.from_rep, k)))
            for h, mask, stage in self.tree():
                when = 16 * steps + 15 + 10 * stage if stage < self.bits - 1 else 1000 + steps
                due.append((when, len(due), functools.partial(self.relay, k, h, mask, stage)))
        return [step for _, _, step in sorted(due, key=lambda entry: entry[:2])]

    def end(self):
        for k in range(len(self.entries)):

            def action(k=k):
                for stage in range(self.bits):
                    for h in range(2):
                        self.hop(k, h, 0, self.orders[h][stage]).wait_send()
                for h, mask, stage in self.tree():
                    for later in range(stage + 1, self.bits):
                        self.hop(k, h, mask, self.orders[h][later]).wait_send()
                self.onward(k, lambda copy: copy.wait_send())

            self.guarded(k, action)


def weight_gather_kernel(n_rep, n_ep, x_ref, out_ref, *sems):
    gather = BlockGather(n_rep, n_ep, x_ref, out_ref, sems)
    gather.meet()
    gather.begin()
    for event in gather.events():
        event()
    gather.end()
    gather.local().wait()


def gather_weights(x, n_rep, n_ep, collective_id):
    return pl.pallas_call(
        functools.partial(weight_gather_kernel, n_rep, n_ep),
        out_shape=jax.ShapeDtypeStruct((n_rep, n_ep) + x.shape, x.dtype),
        in_specs=[pl.BlockSpec(memory_space=pl.ANY)],
        out_specs=pl.BlockSpec(memory_space=pl.ANY),
        scratch_shapes=BlockGather.sems(n_rep, n_ep),
        compiler_params=pltpu.CompilerParams(collective_id=collective_id, has_side_effects=True),
        cost_estimate=pl.CostEstimate(flops=1000, bytes_accessed=1000, transcendentals=0),
        name="weight_gather",
    )(x)


COLUMNS = 512


def attention_front_kernel(n_rep, n_ep, experts, heads_kv, groups, scale, *refs):
    (lengths_ref, x_ref, gains_ref, cos_ref, sin_ref, routes_ref, order_ref) = refs[:7]
    (mat_ref, wo_ref, own_g_ref) = refs[7:10]
    h_ref, proj_ref, att_ref, middle_ref, sent_ref, gates_ref, kept_ref, row_ref, wo_all, g_all = refs[10:20]
    mat_buf, mat_sem, k_low, v_low, wo_buf, wo_sem, small_ref, ranks, loads_own, loads_all = refs[20:30]
    gather = BlockGather(n_rep, n_ep, wo_ref, wo_all, refs[30:35])
    extra = BlockGather(1, n_ep, own_g_ref, g_all, refs[35:40])
    counted = BlockGather(1, n_ep, loads_own, loads_all, refs[40:45])
    rep, me = lax.axis_index("rep"), lax.axis_index("ep")
    length = lengths_ref[rep * n_ep + me]
    group_total = lengths_ref[rep * n_ep]
    for j in range(1, n_ep):
        group_total += lengths_ref[rep * n_ep + j]
    top_count = routes_ref.shape[1]
    capacity = (9 * top_count * group_total // (8 * experts)).astype(f32)
    size = gains_ref.shape[1]
    tokens, width = x_ref.shape
    wide_q, wide_kv = heads_kv * groups * size, heads_kv * size
    chunks = (wide_q + 2 * wide_kv) // COLUMNS
    pairs = heads_kv * groups // 2
    group_blocks = n_ep // 2
    block_rows = wo_ref.shape[0]
    deep = group_blocks * block_rows
    early = chunks + pairs
    turns = early + n_rep * 2

    def mat_copy(i):
        columns = pl.ds(pl.multiple_of(i * COLUMNS, COLUMNS), COLUMNS)
        return pltpu.make_async_copy(mat_ref.at[:, columns], mat_buf.at[i % 2], mat_sem.at[i % 2])

    def wo_copy(n):
        blocks = pl.ds((n % 2) * group_blocks, group_blocks)
        return pltpu.make_async_copy(wo_all.at[n // 2, blocks], wo_buf.at[n % 2], wo_sem.at[n % 2])

    small_copy = pltpu.make_async_copy(
        mat_ref.at[:, pl.ds(wide_q + 2 * wide_kv, EXT)], small_ref, wo_sem.at[0]
    )
    small_copy.start()
    mat_copy(0).start()
    gather.meet()
    gather.begin()
    lane = lax.broadcasted_iota(jnp.int32, (tokens, EXT), 1)
    named = lane < 0
    sort_key = jnp.zeros((tokens, EXT), jnp.int32)
    for n in range(top_count):
        hit = routes_ref[:, n : n + 1] == lane
        named = named | hit
        sort_key = jnp.where(hit, order_ref[:, n : n + 1], sort_key)
    routed = named & (lax.broadcasted_iota(jnp.int32, (tokens, EXT), 0) < length)
    sort_key = jnp.where(routed, sort_key, tokens * top_count).astype(f32)
    loads = jnp.sum(jnp.where(routed, 1.0, 0.0), axis=0, keepdims=True)
    loads_own[...] = jnp.broadcast_to(jnp.concatenate([loads, loads], axis=1), loads_own.shape)
    counted.begin()
    turned = sort_key.T
    ranks[...] = jnp.zeros_like(ranks)
    for e in range(experts):
        smaller = sort_key[:, e : e + 1] < turned[e : e + 1, :]
        ranks[e : e + 1, :] = jnp.sum(jnp.where(smaller, 1.0, 0.0), axis=0, keepdims=True)
    gates_ref[...] = jnp.where(named, 1.0, 0.0)
    small_copy.wait()
    pick = lax.broadcasted_iota(jnp.int32, (8, EXT), 0) + experts == lax.broadcasted_iota(jnp.int32, (8, EXT), 1)
    picks = jnp.where(pick, 1.0, 0.0).astype(bf16)
    row_ref[...] = lax.dot_general(picks, small_ref[...], NT, preferred_element_type=f32)
    x = x_ref[...].astype(f32)
    x = x * lax.rsqrt(jnp.mean(x * x, axis=-1, keepdims=True) + eps)
    h_ref[...] = (x * row_ref[0:1, :]).astype(bf16)

    def rotate(value):
        return value * cos_ref[...] + pltpu.roll(value, size // 2, 1) * sin_ref[...]

    def normed(value):
        return value * lax.rsqrt(jnp.mean(value * value, axis=-1, keepdims=True) + eps)

    query_pos = lax.broadcasted_iota(jnp.int32, (tokens, tokens), 0)
    key_pos = lax.broadcasted_iota(jnp.int32, (tokens, tokens), 1)
    allowed = (key_pos <= query_pos) & (key_pos < length)

    def lanes(start):
        return pl.ds(pl.multiple_of(start, size), size)

    first = gather.events()
    first = first[: len(first) // 4] + counted.events() + first[len(first) // 4 :]
    first.insert(len(first) // 2, extra.begin)
    second = extra.events()

    def shares(events, weights, start):
        given, total, done, reached = {}, sum(weights), 0, 0.0
        for n, weight in enumerate(weights):
            reached += weight
            upto = -(-len(events) * reached // total)
            upto = len(events) if n == len(weights) - 1 else int(upto)
            given[start + n] = events[done:upto]
            done = upto
        return given

    plan = {
        **shares(first, [1.0] * chunks + [4.0] * pairs, 0),
        **shares(second, [1.0] * (turns - early), early),
    }

    def turn(i, carry):
        @pl.when(i < chunks)
        def _():
            @pl.when(i + 1 < chunks)
            def _():
                mat_copy(i + 1).start()

            mat_copy(i).wait()
            columns = pl.ds(pl.multiple_of(i * COLUMNS, COLUMNS), COLUMNS)
            proj_ref[:, columns] = jnp.dot(h_ref[...], mat_buf[i % 2], preferred_element_type=f32)

        @pl.when((i >= chunks) & (i < early))
        def _():
            pair = i - chunks
            group = pair // (groups // 2)

            @pl.when(pair % (groups // 2) == 0)
            def _():
                key = normed(proj_ref[:, lanes(wide_q + group * size)])
                k_low[...] = rotate(key * gains_ref[1:2, :]).astype(bf16)
                v_low[...] = proj_ref[:, lanes(wide_q + wide_kv + group * size)].astype(bf16)

            for n in range(2):
                head = pair * 2 + n
                query = rotate(normed(proj_ref[:, lanes(head * size)]) * gains_ref[0:1, :]).astype(bf16)
                scores = lax.dot_general(query, k_low[...], NT, preferred_element_type=f32) * scale
                scores = jnp.where(allowed, scores, -1e30)
                raised = jnp.exp(scores - jnp.max(scores, axis=1, keepdims=True))
                probs = (raised * (1.0 / jnp.sum(raised, axis=1, keepdims=True))).astype(bf16)
                att_ref[:, lanes(head * size)] = jnp.dot(
                    probs, v_low[...], preferred_element_type=f32
                ).astype(bf16)

        @pl.when(i >= early)
        def _():
            n = i - early

            @pl.when(n == 0)
            def _():
                gather.local().wait()
                wo_copy(0).start()
                middle_ref[...] = x_ref[...].astype(f32)

            @pl.when(i + 1 < turns)
            def _():
                wo_copy(n + 1).start()

            wo_copy(n).wait()
            columns = pl.ds(pl.multiple_of(n * deep, deep), deep)
            middle_ref[...] += jnp.dot(
                att_ref[:, columns], wo_buf[n % 2].reshape(deep, width), preferred_element_type=f32
            )

        for k, mine in plan.items():
            if mine:

                @pl.when(i == k)
                def _(mine=mine):
                    for event in mine:
                        event()

        return carry

    lax.fori_loop(0, turns, turn, 0)
    step = 64
    for r in range(0, tokens, step):
        low = (normed(middle_ref[r : r + step, :]) * row_ref[1:2, :]).astype(bf16)
        sent_ref[r : r + step, :width] = low
    logits = jnp.dot(sent_ref[:, :width], small_ref[...], preferred_element_type=f32)
    counted.local().wait()
    earlier = jnp.zeros((1, EXT), f32)
    for j in range(n_ep):
        earlier += jnp.where(j < me, loads_all[0, j, 0:1, :EXT], 0.0)
    named = gates_ref[...] > 0.0
    routed = named & (lax.broadcasted_iota(jnp.int32, (tokens, EXT), 0) < length)
    kept = jnp.where(routed & (earlier + ranks[...].T < capacity), 1.0, 0.0)
    kept_ref[...] = kept
    top = jnp.max(jnp.where(named, logits, -jnp.inf), axis=1, keepdims=True)
    raised = jnp.where(named, jnp.exp(jnp.where(named, logits - top, 0.0)), 0.0)
    gates = raised / jnp.sum(raised, axis=1, keepdims=True)
    gates_ref[...] = gates
    weight = gates * kept
    high = weight.astype(bf16).astype(f32)
    middle = (weight - high).astype(bf16).astype(f32)
    low = weight - high - middle
    spread = high + pltpu.roll(middle, experts, 1) + pltpu.roll(low, 2 * experts, 1)
    sent_ref[:, width:] = spread.astype(bf16)
    counted.end()
    gather.end()
    extra.end()
    extra.local().wait()


def attention_front(
    lengths, x, gains, cos, sin, routes, order, mat, w_o, own_g, n_rep, n_ep, experts, heads_kv, groups, collective_id
):
    tokens, width = x.shape
    size = gains.shape[1]
    vmem = pl.BlockSpec(memory_space=pltpu.VMEM)
    anywhere = pl.BlockSpec(memory_space=pl.ANY)
    wide_q = heads_kv * groups * size
    wide_all = wide_q + 2 * heads_kv * size
    return pl.pallas_call(
        functools.partial(attention_front_kernel, n_rep, n_ep, experts, heads_kv, groups, size ** (-0.5)),
        out_shape=(
            jax.ShapeDtypeStruct((tokens, width), bf16),
            jax.ShapeDtypeStruct((tokens, wide_all), f32),
            jax.ShapeDtypeStruct((tokens, wide_q), bf16),
            jax.ShapeDtypeStruct((tokens, width), f32),
            jax.ShapeDtypeStruct((tokens, width + EXT), bf16),
            jax.ShapeDtypeStruct((tokens, EXT), f32),
            jax.ShapeDtypeStruct((tokens, EXT), f32),
            jax.ShapeDtypeStruct((8, width), f32),
            jax.ShapeDtypeStruct((n_rep, n_ep) + w_o.shape, bf16),
            jax.ShapeDtypeStruct((1, n_ep) + own_g.shape, bf16),
        ),
        in_specs=[pl.BlockSpec(memory_space=pltpu.SMEM)] + [vmem] * 6 + [anywhere] * 3,
        out_specs=(vmem,) * 8 + (anywhere,) * 2,
        scratch_shapes=[
            pltpu.VMEM((2, width, COLUMNS), bf16),
            pltpu.SemaphoreType.DMA((2,)),
            pltpu.VMEM((tokens, size), bf16),
            pltpu.VMEM((tokens, size), bf16),
            pltpu.VMEM((2, n_ep // 2) + w_o.shape, bf16),
            pltpu.SemaphoreType.DMA((2,)),
            pltpu.VMEM((width, EXT), bf16),
            pltpu.VMEM((EXT, tokens), f32),
            pltpu.VMEM((8, 2 * EXT), f32),
            pltpu.VMEM((1, n_ep, 8, 2 * EXT), f32),
        ]
        + BlockGather.sems(n_rep, n_ep)
        + BlockGather.sems(1, n_ep)
        + BlockGather.sems(1, n_ep),
        compiler_params=pltpu.CompilerParams(
            collective_id=collective_id, has_side_effects=True, vmem_limit_bytes=VMEM_BYTES
        ),
        cost_estimate=pl.CostEstimate(flops=1000, bytes_accessed=1000, transcendentals=0),
        name="attention_front",
    )(lengths, x, gains, cos, sin, routes, order, mat, w_o, own_g)


def unpack_kernel(shares, experts, *refs):
    (sums,) = refs[:1]
    packs, outs = refs[1:-9], refs[-9:-6]
    q_ref, k_ref, v_ref, o_ref, router_ref, rows_ref = refs[-6:]
    for local, pack in enumerate(packs):
        start = 0
        for out, rows in zip(outs, shares):
            for p in range(out.shape[2] // LANES):
                out[local, :, p * LANES : (p + 1) * LANES] = pack[0, start : start + rows, :].astype(f32)
                start += rows
    start = 0
    for out in (q_ref, k_ref, v_ref):
        out[...] = sums[:, start : start + out.shape[1]]
        start += out.shape[1]
    for n in range(2):
        rows = sums.shape[0]
        o_ref[n * rows : (n + 1) * rows, :] = sums[:, start : start + o_ref.shape[1]]
        start += o_ref.shape[1]
    small = sums[:, start : start + EXT]
    router_ref[...] = small[:, :experts]
    rows_ref[...] = small.T


def unpack(sums, packs, wide_share, tall_share, width, hidden, wide_q, wide_kv, experts):
    count, rows = len(packs), sums.shape[0]
    vmem = pl.BlockSpec(memory_space=pltpu.VMEM)
    return pl.pallas_call(
        functools.partial(unpack_kernel, (wide_share, wide_share, tall_share), experts),
        out_shape=tuple(
            jax.ShapeDtypeStruct(shape, f32)
            for shape in (
                (count, wide_share, hidden),
                (count, wide_share, hidden),
                (count, tall_share, width),
                (rows, wide_q),
                (rows, wide_kv),
                (rows, wide_kv),
                (2 * rows, width),
                (rows, experts),
                (EXT, rows),
            )
        ),
        in_specs=[vmem] * (count + 1),
        out_specs=(vmem,) * 9,
        compiler_params=pltpu.CompilerParams(vmem_limit_bytes=VMEM_BYTES),
        cost_estimate=pl.CostEstimate(flops=1000, bytes_accessed=1000, transcendentals=0),
        name="unpack",
    )(sums, *packs)


class TokenSum:
    def __init__(self, count, y_ref, starts, results, scratch):
        self.bits = bits_of(count)
        self.y_ref, self.results = y_ref, results
        self.own, self.got = scratch[:2], scratch[2:4]
        self.send_sem, self.recv_sem, self.own_sem = scratch[4:7]
        self.rep, self.me = lax.axis_index("rep"), lax.axis_index("ep")
        self.orders = [list(reversed(o)) for o in gather_orders(count)]
        self.columns = [pl.ds(s, o.shape[2]) for s, o in zip(starts, self.own)]
        self.masks = [
            [list(reversed(spans(self.orders[h][k + 1 :]))) for k in range(self.bits)] for h in range(2)
        ]
        self.slots, self.seats = [], []
        for h in range(2):
            table = {}
            for stage in range(self.bits):
                for mask in self.masks[h][stage]:
                    table[(stage, mask)] = len(table)
            self.slots.append(table)
            self.seats.append({mask: i for i, mask in enumerate(self.masks[h][0])})

    @staticmethod
    def scratch(count, rows, widths):
        half = count // 2
        return [
            pltpu.VMEM((half, rows, widths[0]), bf16),
            pltpu.VMEM((half, rows, widths[1]), bf16),
            pltpu.VMEM((count - 1, rows, widths[0]), bf16),
            pltpu.VMEM((count - 1, rows, widths[1]), bf16),
            pltpu.SemaphoreType.DMA((2, count)),
            pltpu.SemaphoreType.DMA((2, count)),
            pltpu.SemaphoreType.DMA((2, half)),
        ]

    def meet(self):
        meet([(self.rep, self.me ^ (1 << b)) for b in range(self.bits)])

    def copy(self, h, stage, mask):
        bit = 1 << self.orders[h][stage]
        slot = self.slots[h][(stage, mask)]
        if stage == 0:
            source = self.y_ref.at[self.me ^ bit ^ mask, :, self.columns[h]]
        else:
            source = self.own[h].at[self.seats[h][bit | mask]]
        return pltpu.make_async_remote_copy(
            src_ref=source,
            dst_ref=self.got[h].at[slot],
            send_sem=self.send_sem.at[h, slot],
            recv_sem=self.recv_sem.at[h, slot],
            device_id=(self.rep, self.me ^ bit),
            device_id_type=MESH,
        )

    def load(self, h, mask):
        seat = self.seats[h][mask]
        return pltpu.make_async_copy(
            self.y_ref.at[self.me ^ mask, :, self.columns[h]], self.own[h].at[seat], self.own_sem.at[h, seat]
        )

    def begin(self):
        for i in range(len(self.masks[0][0])):
            for h in range(2):
                self.copy(h, 0, self.masks[h][0][i]).start()
                self.load(h, self.masks[h][0][i]).start()

    def add(self, h, stage, mask):
        slot, seat = self.slots[h][(stage, mask)], self.seats[h][mask]
        own, got = self.own[h], self.got[h]
        if stage == 0:
            self.load(h, mask).wait()
        self.copy(h, stage, mask).wait_recv()
        step = 32

        def body(i, carry):
            rows = pl.ds(pl.multiple_of(i * step, step), step)
            total = own[seat, rows, :].astype(f32) + got[slot, rows, :].astype(f32)
            if stage == self.bits - 1:
                self.results[h][rows, :] = total
            else:
                own[seat, rows, :] = total.astype(bf16)
            return carry

        lax.fori_loop(0, own.shape[1] // step, body, 0)

    def stage(self, stage):
        for i in range(len(self.masks[0][stage])):
            for h in range(2):
                mask = self.masks[h][stage][i]
                self.add(h, stage, mask)
                if stage + 1 < self.bits:
                    following = 1 << self.orders[h][stage + 1]
                    if mask & following:
                        self.copy(h, stage + 1, mask & ~following).start()

    def end(self):
        for h in range(2):
            for stage, mask in self.slots[h]:
                self.copy(h, stage, mask).wait_send()


def token_sum_kernel(count, starts, y_ref, first_ref, second_ref, *scratch):
    total = TokenSum(count, y_ref, starts, (first_ref, second_ref), scratch)
    total.meet()
    total.begin()
    for stage in range(total.bits):
        total.stage(stage)
    total.end()


def sum_tokens(y, count, starts, widths, collective_id):
    rows = y.shape[1]
    return pl.pallas_call(
        functools.partial(token_sum_kernel, count, starts),
        out_shape=tuple(jax.ShapeDtypeStruct((rows, w), f32) for w in widths),
        in_specs=[pl.BlockSpec(memory_space=pl.ANY)],
        out_specs=(pl.BlockSpec(memory_space=pltpu.VMEM),) * 2,
        scratch_shapes=TokenSum.scratch(count, rows, widths),
        compiler_params=pltpu.CompilerParams(
            collective_id=collective_id, has_side_effects=True, vmem_limit_bytes=VMEM_BYTES
        ),
        cost_estimate=pl.CostEstimate(flops=1000, bytes_accessed=1000, transcendentals=0),
        name="token_sum",
    )(y)


QUAD = 4


def attention_back_kernel(count, starts, heads_kv, groups, scale, *refs):
    (length_ref, proj_ref, gains_ref, cos_ref, sin_ref, mid_ref, wo_ref, y_ref) = refs[:8]
    right_ref, head_ref, first_ref, second_ref = refs[8:12]
    wo_buf, wo_sem, k_low, v_low, k_norm, dk_sum, dv_sum = refs[12:19]
    total = TokenSum(count, y_ref, starts, (first_ref, second_ref), refs[19:])
    size = gains_ref.shape[1]
    tokens = proj_ref.shape[0]
    heads_q = heads_kv * groups
    wide_q, wide_kv = heads_q * size, heads_kv * size
    per_group = groups // QUAD
    turns = heads_q // QUAD

    def wo_copy(i):
        rows = pl.ds(pl.multiple_of(i * QUAD * size, QUAD * size), QUAD * size)
        return pltpu.make_async_copy(wo_ref.at[rows], wo_buf.at[i % 2], wo_sem.at[i % 2])

    wo_copy(0).start()
    total.meet()
    total.begin()
    head_ref[...] = jnp.zeros_like(head_ref)
    sent = right_ref.shape[1] - wide_q - 2 * wide_kv
    for n in range(sent // mid_ref.shape[1]):
        start = wide_q + 2 * wide_kv + n * mid_ref.shape[1]
        right_ref[:, start : start + mid_ref.shape[1]] = mid_ref[...]

    def rotate(value):
        return value * cos_ref[...] + pltpu.roll(value, size // 2, 1) * sin_ref[...]

    def rotate_back(value):
        return value * cos_ref[...] - pltpu.roll(value, size // 2, 1) * sin_ref[...]

    def norm_parts(value):
        inverse = lax.rsqrt(jnp.mean(value * value, axis=-1, keepdims=True) + eps)
        return value * inverse, inverse

    def project_back(gradient, normed, inverse, row):
        scaled = rotate_back(gradient)
        head_ref[row : row + 1, :] += jnp.sum(scaled * normed, axis=0, keepdims=True)
        lifted = scaled * gains_ref[row : row + 1, :]
        mean = jnp.mean(lifted * normed, axis=-1, keepdims=True)
        return (inverse * (lifted - normed * mean)).astype(bf16)

    key_pos = lax.broadcasted_iota(jnp.int32, (tokens, tokens), 0)
    query_pos = lax.broadcasted_iota(jnp.int32, (tokens, tokens), 1)
    allowed = (key_pos <= query_pos) & (key_pos < length_ref[0])

    def lanes(start):
        return pl.ds(pl.multiple_of(start, size), size)

    def turn(i, carry):
        group = i // per_group
        for stage, when in ((0, min(1, turns - 1)), (1, turns - 2)):

            @pl.when(i == when)
            def _(stage=stage):
                if stage < total.bits - 1:
                    total.stage(stage)

        @pl.when(i % per_group == 0)
        def _():
            normed, inverse = norm_parts(proj_ref[:, lanes(wide_q + group * size)])
            k_norm[:, :size] = normed
            k_norm[:, size:] = jnp.broadcast_to(inverse, normed.shape)
            k_low[...] = rotate(normed * gains_ref[1:2, :]).astype(bf16)
            v_low[...] = proj_ref[:, lanes(wide_q + wide_kv + group * size)].astype(bf16)
            dk_sum[...] = jnp.zeros_like(dk_sum)
            dv_sum[...] = jnp.zeros_like(dv_sum)

        @pl.when(i + 1 < turns)
        def _():
            wo_copy(i + 1).start()

        wo_copy(i).wait()
        d_att = lax.dot_general(mid_ref[...], wo_buf[i % 2], NT, preferred_element_type=f32).astype(bf16)
        keys, values = k_low[...], v_low[...]
        dk, dv = dk_sum[...], dv_sum[...]
        for n in range(QUAD):
            head = i * QUAD + n
            d_out = d_att[:, n * size : (n + 1) * size]
            normed, inverse = norm_parts(proj_ref[:, lanes(head * size)])
            query = rotate(normed * gains_ref[0:1, :]).astype(bf16)
            scores = lax.dot_general(keys, query, NT, preferred_element_type=f32) * scale
            scores = jnp.where(allowed, scores, -1e30)
            raised = jnp.exp(scores - jnp.max(scores, axis=0, keepdims=True))
            probs = raised * (1.0 / jnp.sum(raised, axis=0, keepdims=True))
            dv += jnp.dot(probs.astype(bf16), d_out, preferred_element_type=f32)
            d_probs = lax.dot_general(values, d_out, NT, preferred_element_type=f32)
            weighted = probs * d_probs
            d_scores = (weighted - probs * jnp.sum(weighted, axis=0, keepdims=True)).astype(bf16)
            dk += jnp.dot(d_scores, query, preferred_element_type=f32)
            d_query = lax.dot_general(d_scores, keys, TN, preferred_element_type=f32) * scale
            right_ref[:, lanes(head * size)] = project_back(d_query, normed, inverse, 0)
        dk_sum[...] = dk
        dv_sum[...] = dv

        @pl.when(i % per_group == per_group - 1)
        def _():
            right_ref[:, lanes(wide_q + group * size)] = project_back(
                dk_sum[...] * scale, k_norm[:, :size], k_norm[:, size:], 1
            )
            right_ref[:, lanes(wide_q + wide_kv + group * size)] = dv_sum[...].astype(bf16)

        return carry

    lax.fori_loop(0, turns, turn, 0)
    for stage in range(min(2, total.bits - 1), total.bits):
        total.stage(stage)
    total.end()


def attention_back(length, proj, gains, cos, sin, d_mid, mat_o, y, count, starts, widths, heads_kv, groups, collective_id):
    tokens, width = d_mid.shape
    size = gains.shape[1]
    vmem = pl.BlockSpec(memory_space=pltpu.VMEM)
    anywhere = pl.BlockSpec(memory_space=pl.ANY)
    columns = (heads_kv * groups + 2 * heads_kv) * size + 2 * width
    return pl.pallas_call(
        functools.partial(attention_back_kernel, count, starts, heads_kv, groups, size ** (-0.5)),
        out_shape=(
            jax.ShapeDtypeStruct((tokens, columns), bf16),
            jax.ShapeDtypeStruct((8, size), f32),
        )
        + tuple(jax.ShapeDtypeStruct((tokens, w), f32) for w in widths),
        in_specs=[pl.BlockSpec(memory_space=pltpu.SMEM)] + [vmem] * 5 + [anywhere] * 2,
        out_specs=(vmem,) * 4,
        scratch_shapes=[
            pltpu.VMEM((2, QUAD * size, width), bf16),
            pltpu.SemaphoreType.DMA((2,)),
            pltpu.VMEM((tokens, size), bf16),
            pltpu.VMEM((tokens, size), bf16),
            pltpu.VMEM((tokens, 2 * size), f32),
            pltpu.VMEM((tokens, size), f32),
            pltpu.VMEM((tokens, size), f32),
        ]
        + TokenSum.scratch(count, tokens, widths),
        compiler_params=pltpu.CompilerParams(
            collective_id=collective_id, has_side_effects=True, vmem_limit_bytes=VMEM_BYTES
        ),
        cost_estimate=pl.CostEstimate(flops=1000, bytes_accessed=1000, transcendentals=0),
        name="attention_back",
    )(length, proj, gains, cos, sin, d_mid, mat_o, y)


def exchanges(n_rep, n_ep):
    near = [(0, b) for b in range(1, bits_of(n_ep))]
    far = [(1, b) for b in range(bits_of(n_rep))]
    return near + far[::-1], (near + far, near[::-1] + far), [2] * len(near) + [3] * len(far)


def dense_sum_kernel(n_rep, n_ep, rows, chunks, split, *refs):
    hidden_ref, att_ref, right_ref, small_ref, head_ref, out_ref, head_out = refs[:7]
    rest = list(refs[7:])
    bits, rep_bits = bits_of(n_ep), bits_of(n_rep)
    wide = right_ref.shape[1] // (chunks - 1)
    half = wide // 2
    rep, me = lax.axis_index("rep"), lax.axis_index("ep")
    axes, orders, depths = exchanges(n_rep, n_ep)
    count = len(axes)
    mine = {axis: lax.rem(lax.div(rep if axis[0] else me, 1 << axis[1]), 2) for axis in axes + [(0, 0)]}
    left_ref, part, got_core = rest[:3]
    acc = [None] + [rest[3 + 2 * k : 5 + 2 * k] for k in range(count)]
    rest = rest[3 + 2 * count :]
    got = [None] + [rest[2 * k : 2 * k + 2] for k in range(count)]
    rest = rest[2 * count :]
    head_own, head_got, head_rep = rest[:3]
    core_send, core_recv, step_send, step_recv, head_send, head_recv, head_rs, head_rr = rest[3:]
    left = [[[a for a in axes if a not in o[:k]] for k in range(count)] for o in orders]
    lags = [0, 1]
    for depth in depths:
        lags.append(lags[-1] + depth)
    slots = [None] + [2 * depth for depth in depths]
    others = [lax.rem(rep + d, n_rep) for d in range(1, n_rep)]
    meet([(rep, me ^ (1 << b)) for b in range(bits)] + [(other, me) for other in others])

    def core_copy(c):
        slot = lax.rem(c, 2)
        return pltpu.make_async_remote_copy(
            src_ref=part.at[slot, 1 - mine[(0, 0)]],
            dst_ref=got_core.at[slot],
            send_sem=core_send.at[slot],
            recv_sem=core_recv.at[slot],
            device_id=(rep, me ^ 1),
            device_id_type=MESH,
        )

    def pick(k, h, which):
        axis = orders[h][k - 1]
        return (slice(None),) * left[h][k - 1].index(axis) + (which(mine[axis]),)

    def bit_copy(k, h, c):
        slot = lax.rem(c, slots[k])
        on_rep, bit = orders[h][k - 1]
        return pltpu.make_async_remote_copy(
            src_ref=acc[k][h].at[(slot,) + pick(k, h, lambda m: 1 - m)],
            dst_ref=got[k][h].at[slot],
            send_sem=step_send.at[k, h, slot],
            recv_sem=step_recv.at[k, h, slot],
            device_id=(rep ^ (1 << bit), me) if on_rep else (rep, me ^ (1 << bit)),
            device_id_type=MESH,
        )

    corners = [()]
    for _ in range(bits - 1):
        corners = [c + (v,) for c in corners for v in range(2)]
    block = n_rep * rows
    side_rows = len(corners) * block
    inner = (2,) * rep_bits

    def place_rows(source, which_of):
        per = 128 // rows
        for b in range(source.shape[1] // 128):
            turned = source[:, b * 128 : (b + 1) * 128].astype(f32).T.astype(bf16)
            for q in range(per):
                which, owner = which_of(b * per + q)
                r, e = owner // n_ep, owner % n_ep
                corner = sum(((e >> bit) & 1) << (bits - 1 - bit) for bit in range(1, bits))
                start = (which * 2 + (e & 1)) * side_rows + corner * block + r * rows
                left_ref[start : start + rows, :] = turned[q * rows : (q + 1) * rows, :]

    place_rows(hidden_ref, lambda n: (0, n))
    place_rows(att_ref, lambda n: (1 + n % 2, n // 2))

    def stage_make(c):
        slot = lax.rem(c, 2)

        @pl.when(c >= 2)
        def _():
            core_copy(c - 2).wait_send()

        @pl.when(c < chunks - 1)
        def _():
            which = jnp.where(c >= split[0], 1, 0) + jnp.where(c >= split[1], 1, 0)
            columns = pl.ds(pl.multiple_of(c * wide, wide), wide)
            weights = right_ref[:, columns]
            for side in (1, 0):
                which_side = 1 - mine[(0, 0)] if side else mine[(0, 0)]
                for n, corner in enumerate(corners):
                    start = (which * 2 + which_side) * side_rows + n * block
                    value = jnp.dot(
                        left_ref[pl.ds(pl.multiple_of(start, block), block), :],
                        weights,
                        preferred_element_type=f32,
                    )
                    part[(slot, which_side) + corner] = value.astype(bf16).reshape(inner + (rows, wide))

        @pl.when(c == chunks - 1)
        def _():
            thin = small_ref.shape[1]
            lead = (slice(None),) * (rep_bits + 1)
            for side in range(2):
                for n, corner in enumerate(corners):
                    value = small_ref[pl.ds(side * side_rows + n * block, block), :].reshape(inner + (rows, thin))
                    blank = jnp.zeros(inner + (rows, wide - thin), bf16)
                    part[(slot, side) + corner + lead + (slice(0, thin),)] = value
                    part[(slot, side) + corner + lead + (slice(thin, wide),)] = blank

        core_copy(c).start()

    def stage_core(c):
        slot, put = lax.rem(c, 2), lax.rem(c, slots[1])

        @pl.when(c >= slots[1])
        def _():
            for h in range(2):
                bit_copy(1, h, c - slots[1]).wait_send()

        core_copy(c).wait_recv()
        for corner in corners:
            total = part[(slot, mine[(0, 0)]) + corner].astype(f32) + got_core[(slot,) + corner].astype(f32)
            total = total.astype(bf16)
            for h in range(2):
                acc[1][h][(put,) + corner] = total[..., h * half : (h + 1) * half]
        for h in range(2):
            bit_copy(1, h, c).start()

    def joined(k, h, c):
        slot = lax.rem(c, slots[k])
        return acc[k][h][(slot,) + pick(k, h, lambda m: m)].astype(f32) + got[k][h][slot].astype(f32)

    def stage_bit(k, c):
        for h in range(2):

            @pl.when(c >= slots[k])
            def _(h=h):
                bit_copy(k, h, c - slots[k]).wait_send()

            bit_copy(k - 1, h, c).wait_recv()
            acc[k][h][lax.rem(c, slots[k])] = joined(k - 1, h, c).astype(bf16)
            bit_copy(k, h, c).start()

    def stage_end(c):
        for h in range(2):
            bit_copy(count, h, c).wait_recv()
            out_ref[:, pl.ds(pl.multiple_of(c * wide + h * half, half), half)] = joined(count, h, c)

    def head_copy(t):
        return pltpu.make_async_remote_copy(
            src_ref=head_own.at[t],
            dst_ref=head_got.at[t],
            send_sem=head_send.at[t],
            recv_sem=head_recv.at[t],
            device_id=(rep, me ^ (1 << t)),
            device_id_type=MESH,
        )

    def head_rep_copy(d):
        return pltpu.make_async_remote_copy(
            src_ref=head_own.at[bits],
            dst_ref=head_rep.at[rep],
            send_sem=head_rs.at[d],
            recv_sem=head_rr.at[n_rep - 2 - d],
            device_id=(others[d], me),
            device_id_type=MESH,
        )

    def head_step(t):
        if t == 0:
            head_own[0] = head_ref[...]
            head_copy(0).start()
        elif t <= bits:
            head_copy(t - 1).wait_recv()
            head_own[t] = head_own[t - 1] + head_got[t - 1]
            if t < bits:
                head_copy(t).start()
            else:
                for d in range(n_rep - 1):
                    head_rep_copy(d).start()
                head_rep[rep] = head_own[bits]
        else:
            for d in range(n_rep - 1):
                head_rep_copy(d).wait_recv()
            total = head_rep[0]
            for r in range(1, n_rep):
                total = total + head_rep[r]
            head_out[...] = total

    def step(i, carry):
        for stage in reversed(range(len(lags))):
            c = i - lags[stage]

            @pl.when((c >= 0) & (c < chunks))
            def _(stage=stage, c=c):
                if stage == 0:
                    stage_make(c)
                elif stage == 1:
                    stage_core(c)
                elif stage <= count:
                    stage_bit(stage, c)
                else:
                    stage_end(c)

        for t in range(bits + 2):

            @pl.when(i == t)
            def _(t=t):
                head_step(t)

        return carry

    lax.fori_loop(0, chunks + lags[-1], step, 0)
    for c in range(chunks - 2, chunks):
        core_copy(c).wait_send()
    for k in range(1, count + 1):
        for c in range(chunks - slots[k], chunks):
            for h in range(2):
                bit_copy(k, h, c).wait_send()
    for t in range(bits):
        head_copy(t).wait_send()
    for d in range(n_rep - 1):
        head_rep_copy(d).wait_send()


def dense_sum(hidden, attended, right, small, head, n_rep, n_ep, split, collective_id):
    chunk = 512
    chunks = right.shape[1] // chunk + 1
    bits, rep_bits = bits_of(n_ep), bits_of(n_rep)
    tokens, width = hidden.shape
    rows = width // (n_rep * n_ep)
    axes, _, depths = exchanges(n_rep, n_ep)
    half = chunk // 2
    most = 2 * max(depths)
    vmem = pl.BlockSpec(memory_space=pltpu.VMEM)
    inner = (2,) * rep_bits + (rows,)
    scratch = [
        pltpu.VMEM((width + attended.shape[1], tokens), bf16),
        pltpu.VMEM((2, 2) + (2,) * (bits - 1) + inner + (chunk,), bf16),
        pltpu.VMEM((2,) + (2,) * (bits - 1) + inner + (chunk,), bf16),
    ]
    for k, depth in enumerate(depths):
        scratch += [pltpu.VMEM((2 * depth,) + (2,) * (len(axes) - k) + (rows, half), bf16)] * 2
    for k, depth in enumerate(depths):
        scratch += [pltpu.VMEM((2 * depth,) + (2,) * (len(axes) - k - 1) + (rows, half), bf16)] * 2
    scratch += [
        pltpu.VMEM((bits + 1,) + head.shape, f32),
        pltpu.VMEM((bits,) + head.shape, f32),
        pltpu.VMEM((n_rep,) + head.shape, f32),
        pltpu.SemaphoreType.DMA((2,)),
        pltpu.SemaphoreType.DMA((2,)),
        pltpu.SemaphoreType.DMA((len(axes) + 1, 2, most)),
        pltpu.SemaphoreType.DMA((len(axes) + 1, 2, most)),
        pltpu.SemaphoreType.DMA((bits,)),
        pltpu.SemaphoreType.DMA((bits,)),
        pltpu.SemaphoreType.DMA((n_rep - 1,)),
        pltpu.SemaphoreType.DMA((n_rep - 1,)),
    ]
    return pl.pallas_call(
        functools.partial(dense_sum_kernel, n_rep, n_ep, rows, chunks, split),
        out_shape=(
            jax.ShapeDtypeStruct((rows, chunks * chunk), f32),
            jax.ShapeDtypeStruct(head.shape, f32),
        ),
        in_specs=[vmem] * 5,
        out_specs=(vmem, vmem),
        scratch_shapes=scratch,
        compiler_params=pltpu.CompilerParams(
            collective_id=collective_id, has_side_effects=True, vmem_limit_bytes=VMEM_BYTES
        ),
        cost_estimate=pl.CostEstimate(flops=1000, bytes_accessed=1000, transcendentals=0),
        name="dense_sum",
    )(hidden, attended, right, small, head)


def expert_kernel(local, experts, width, hidden_of, *refs):
    (info, h_ref, g_ref, wg_all, wu_all, wd_all) = refs[:6]
    save_ref, grad_ref = refs[6:8]
    xs, gs, ds, hs, notes, wide, tall, in_sem, save_sem, grad_sem = refs[8:18]
    wg_ref, wu_ref, wd_ref, weight_sem = refs[18:]
    weights = [
        pltpu.make_async_copy(source.at[local], target, weight_sem.at[n])
        for n, (source, target) in enumerate(((wg_all, wg_ref), (wu_all, wu_ref), (wd_all, wd_ref)))
    ]
    for copy in weights:
        copy.start()
    shares = grad_ref.shape[0]
    wide_share, tall_share = width // shares, hidden_of // shares
    hidden = wg_ref.shape[1]
    units = info[0]
    expert = info[1]
    table = 8
    per_tile = TILE // UNIT
    tiles = (units + per_tile - 1) // per_tile
    most = xs.shape[0] // TILE
    floor_tiles = min(4, most)

    def unit_in(u, slot):
        source = pl.ds(pl.multiple_of(info[table + u], UNIT), UNIT)
        target = pl.ds(pl.multiple_of(u * UNIT, UNIT), UNIT)
        return (
            pltpu.make_async_copy(h_ref.at[source], xs.at[target], in_sem.at[0, slot]),
            pltpu.make_async_copy(g_ref.at[source], gs.at[target], in_sem.at[1, slot]),
        )

    def begin(u, carry):
        for copy in unit_in(u, u // per_tile):
            copy.start()
        return carry

    lax.fori_loop(0, units, begin, 0)

    def blank(u, carry):
        target = pl.ds(pl.multiple_of(u * UNIT, UNIT), UNIT)
        xs[target, :] = jnp.zeros((UNIT, xs.shape[1]), bf16)
        gs[target, :] = jnp.zeros((UNIT, gs.shape[1]), bf16)
        return carry

    lax.fori_loop(units, jnp.maximum(tiles, floor_tiles) * per_tile, blank, 0)

    def blank_tile(i, carry):
        target = pl.ds(pl.multiple_of(i * TILE, TILE), TILE)
        ds[target, :] = jnp.zeros((TILE, ds.shape[1]), bf16)
        hs[target, :] = jnp.zeros((TILE, hs.shape[1]), bf16)
        return carry

    lax.fori_loop(tiles, floor_tiles, blank_tile, 0)

    lane = lax.broadcasted_iota(jnp.int32, (TILE, EXT), 1)
    weight_lanes = (lane == expert) | (lane == expert + experts) | (lane == expert + 2 * experts)

    def tile_step(i, carry):
        def landed(u, c):
            for copy in unit_in(u, i):
                copy.wait()
            return c

        lax.fori_loop(i * per_tile, jnp.minimum((i + 1) * per_tile, units), landed, 0)
        rows = pl.ds(pl.multiple_of(i * TILE, TILE), TILE)
        x = xs[rows, :width]
        g = gs[rows, :]
        extra = xs[rows, width:].astype(f32)
        weight = jnp.sum(jnp.where(weight_lanes, extra, 0.0), axis=1, keepdims=True)
        gate = jnp.dot(x, wg_ref[...], preferred_element_type=f32)
        up = jnp.dot(x, wu_ref[...], preferred_element_type=f32)
        d_plain = lax.dot_general(g, wd_ref[...], NT, preferred_element_type=f32)
        sig = 1.0 / (1.0 + jnp.exp(-gate))
        silu = gate * sig
        hid = silu * up
        d_weight = jnp.sum(hid.astype(bf16).astype(f32) * d_plain, axis=1, keepdims=True)
        hs[rows, :] = (hid * weight).astype(bf16)
        d_hidden = d_plain * weight
        ds[rows, :hidden] = (d_hidden * up * sig * (1.0 + gate * (1.0 - sig))).astype(bf16)
        ds[rows, hidden:] = (d_hidden * silu).astype(bf16)

        high = d_weight.astype(bf16).astype(f32)
        low = d_weight - high
        note = jnp.where(lane == expert, high, 0.0) + jnp.where(lane == expert + experts, low, 0.0)
        notes[rows, :] = note.astype(bf16)
        return carry

    for copy in weights:
        copy.wait()
    lax.fori_loop(0, tiles, tile_step, 0)
    saves = [
        pltpu.make_async_copy(source, save_ref.at[:, start : start + source.shape[1]], save_sem.at[n])
        for n, (source, start) in enumerate(((ds, 0), (hs, 2 * hidden), (notes, 3 * hidden)))
    ]
    for copy in saves:
        copy.start()

    block = 256

    def grads(depth):
        def wide_copies(m):
            per = wide_share // block
            return tuple(
                pltpu.make_async_copy(
                    wide.at[m % 2, :, p * LANES : (p + 1) * LANES],
                    grad_ref.at[
                        m // per,
                        pl.ds(pl.multiple_of(p * wide_share + (m % per) * block, block), block),
                    ],
                    grad_sem.at[m % 2, p],
                )
                for p in range(2 * hidden // LANES)
            )

        def wide_step(m, carry):
            @pl.when(m >= 2)
            def _():
                for copy in wide_copies(m - 2):
                    copy.wait()

            columns = pl.ds(pl.multiple_of(m * block, block), block)
            wide[m % 2] = lax.dot_general(
                xs[:depth, columns], ds[:depth, :], TN, preferred_element_type=f32
            ).astype(bf16)
            for copy in wide_copies(m):
                copy.start()
            return carry

        count = width // block
        lax.fori_loop(0, count, wide_step, 0)
        for m in range(count - 2, count):
            for copy in wide_copies(m):
                copy.wait()

        piece = math.gcd(block, tall_share)
        base = 2 * hidden // LANES * wide_share

        def tall_copies(m):
            made = []
            for q in range(block // piece):
                first_row = m * block + q * piece
                share, inside = first_row // tall_share, first_row % tall_share
                for p in range(width // LANES):
                    rows = pl.ds(pl.multiple_of(base + p * tall_share + inside, piece), piece)
                    made.append(
                        pltpu.make_async_copy(
                            tall.at[m % 2, q * piece : (q + 1) * piece, p * LANES : (p + 1) * LANES],
                            grad_ref.at[share, rows],
                            grad_sem.at[m % 2, q * (width // LANES) + p],
                        )
                    )
            return made

        def tall_step(m, carry):
            @pl.when(m >= 2)
            def _():
                for copy in tall_copies(m - 2):
                    copy.wait()

            columns = pl.ds(pl.multiple_of(m * block, block), block)
            tall[m % 2] = lax.dot_general(
                hs[:depth, columns], gs[:depth, :], TN, preferred_element_type=f32
            ).astype(bf16)
            for copy in tall_copies(m):
                copy.start()
            return carry

        count = hidden // block
        lax.fori_loop(0, count, tall_step, 0)
        for m in range(count - 2, count):
            for copy in tall_copies(m):
                copy.wait()

    for choice in range(floor_tiles, most + 1):
        chosen = (tiles <= choice) if choice == floor_tiles else (tiles == choice)

        @pl.when(chosen)
        def _(choice=choice):
            grads(choice * TILE)

    for copy in saves:
        copy.wait()


def expert_pass(info, h_rows, g_rows, w_gate, w_up, w_down, local, experts, shares):
    tokens, width = g_rows.shape
    hidden = w_gate.shape[2]
    any_spec = pl.BlockSpec(memory_space=pl.ANY)
    pieces = 256 // math.gcd(256, hidden // shares) * width // LANES
    return pl.pallas_call(
        functools.partial(expert_kernel, local, experts, width, hidden),
        out_shape=(
            jax.ShapeDtypeStruct((tokens, 3 * hidden + EXT), bf16),
            jax.ShapeDtypeStruct((shares, 3 * hidden * width // shares // LANES, LANES), bf16),
        ),
        in_specs=[pl.BlockSpec(memory_space=pltpu.SMEM)] + [any_spec] * 5,
        out_specs=(any_spec,) * 2,
        scratch_shapes=[
            pltpu.VMEM((tokens, width + EXT), bf16),
            pltpu.VMEM((tokens, width), bf16),
            pltpu.VMEM((tokens, 2 * hidden), bf16),
            pltpu.VMEM((tokens, hidden), bf16),
            pltpu.VMEM((tokens, EXT), bf16),
            pltpu.VMEM((2, 256, 2 * hidden), bf16),
            pltpu.VMEM((2, 256, width), bf16),
            pltpu.SemaphoreType.DMA((2, tokens // TILE)),
            pltpu.SemaphoreType.DMA((3,)),
            pltpu.SemaphoreType.DMA((2, max(2 * hidden // LANES, pieces))),
            pltpu.VMEM((width, hidden), bf16),
            pltpu.VMEM((width, hidden), bf16),
            pltpu.VMEM((hidden, width), bf16),
            pltpu.SemaphoreType.DMA((3,)),
        ],
        compiler_params=pltpu.CompilerParams(vmem_limit_bytes=VMEM_BYTES),
        cost_estimate=pl.CostEstimate(flops=1000, bytes_accessed=1000, transcendentals=0),
        name="experts",
    )(info, h_rows, g_rows, w_gate, w_up, w_down)


def returned_kernel(local_count, width, hidden, *refs):
    info, wg_all, wu_all, wd_all = refs[:4]
    saves = refs[4 : 4 + local_count]
    y_ref = refs[4 + local_count]
    wg, wu, wd, held, stage, weight_sem, held_sem, out_sem = refs[5 + local_count :]
    weights = [
        pltpu.make_async_copy(source, target, weight_sem.at[n])
        for n, (source, target) in enumerate(((wg_all, wg), (wu_all, wu), (wd_all, wd)))
    ]
    for copy in weights:
        copy.start()
    units = info[0]
    table = 8
    per_tile = TILE // UNIT
    tiles = (units + per_tile - 1) // per_tile

    def held_copies(i):
        rows = pl.ds(pl.multiple_of(i * TILE, TILE), TILE)
        return [
            pltpu.make_async_copy(save.at[rows], held.at[i % 2, n], held_sem.at[i % 2, n])
            for n, save in enumerate(saves)
        ]

    for copy in held_copies(0):
        copy.start()

    def unit_out(u):
        target = pl.ds(pl.multiple_of(info[table + u], UNIT), UNIT)
        tile = u // per_tile
        source = pl.ds(pl.multiple_of((u % per_tile) * UNIT, UNIT), UNIT)
        return pltpu.make_async_copy(stage.at[tile % 2, source], y_ref.at[target], out_sem.at[tile % 2])

    def each_unit(i, act):
        def body(u, carry):
            act(unit_out(u))
            return carry

        lax.fori_loop(i * per_tile, jnp.minimum((i + 1) * per_tile, units), body, 0)

    for copy in weights:
        copy.wait()

    def tile_step(i, carry):
        slot = i % 2

        @pl.when(i >= 2)
        def _():
            each_unit(i - 2, lambda copy: copy.wait())

        @pl.when(i + 1 < tiles)
        def _():
            for copy in held_copies(i + 1):
                copy.start()

        for copy in held_copies(i):
            copy.wait()
        d_row = jnp.zeros((TILE, width), f32)
        out = jnp.zeros((TILE, width), f32)
        note = jnp.zeros((TILE, EXT), f32)
        for n in range(local_count):
            d_row += lax.dot_general(held[slot, n, :, :hidden], wg[n], NT, preferred_element_type=f32)
            d_row += lax.dot_general(
                held[slot, n, :, hidden : 2 * hidden], wu[n], NT, preferred_element_type=f32
            )
            note += held[slot, n, :, 3 * hidden :].astype(f32)
        stage[slot, :, :width] = d_row.astype(bf16)
        stage[slot, :, width : width + EXT] = note.astype(bf16)
        for n in range(local_count):
            out += jnp.dot(held[slot, n, :, 2 * hidden : 3 * hidden], wd[n], preferred_element_type=f32)
        stage[slot, :, width + EXT :] = out.astype(bf16)
        each_unit(i, lambda copy: copy.start())
        return carry

    lax.fori_loop(0, tiles, tile_step, 0)

    @pl.when(tiles >= 2)
    def _():
        each_unit(tiles - 2, lambda copy: copy.wait())

    each_unit(tiles - 1, lambda copy: copy.wait())


def returned_rows(info, w_gate, w_up, w_down, saves):
    local_count, width, hidden = w_gate.shape
    tokens, row = saves[0].shape
    wide_row = width + EXT + width
    any_spec = pl.BlockSpec(memory_space=pl.ANY)
    return pl.pallas_call(
        functools.partial(returned_kernel, local_count, width, hidden),
        out_shape=jax.ShapeDtypeStruct((tokens, wide_row), bf16),
        in_specs=[pl.BlockSpec(memory_space=pltpu.SMEM)] + [any_spec] * (3 + local_count),
        out_specs=any_spec,
        scratch_shapes=[
            pltpu.VMEM(w_gate.shape, bf16),
            pltpu.VMEM(w_up.shape, bf16),
            pltpu.VMEM(w_down.shape, bf16),
            pltpu.VMEM((2, local_count, TILE, row), bf16),
            pltpu.VMEM((2, TILE, wide_row), bf16),
            pltpu.SemaphoreType.DMA((3,)),
            pltpu.SemaphoreType.DMA((2, local_count)),
            pltpu.SemaphoreType.DMA((2,)),
        ],
        compiler_params=pltpu.CompilerParams(vmem_limit_bytes=VMEM_BYTES),
        cost_estimate=pl.CostEstimate(flops=1000, bytes_accessed=1000, transcendentals=0),
        name="returned_rows",
    )(info, w_gate, w_up, w_down, *saves)


def unit_table(lengths):
    per_sequence = TILE // UNIT
    counts = (lengths + UNIT - 1) // UNIT
    unit = jnp.arange(lengths.shape[0] * per_sequence, dtype=jnp.int32)
    live = (unit % per_sequence) < jnp.repeat(counts, per_sequence)
    place = jnp.cumsum(live.astype(jnp.int32)) - 1
    hit = (place[None, :] == unit[:, None]) & live[None, :]
    rows = jnp.sum(jnp.where(hit, unit[None, :] * UNIT, 0), axis=1)
    return (jnp.sum(counts), rows)


def per_device(
    hidden_in,
    out_grad,
    attn_gain,
    w_q,
    key_weight,
    value_weight,
    w_o,
    ffn_gain,
    router_w,
    qk_gains,
    w_gate,
    w_up,
    w_down,
    lengths,
    routes,
    order,
):
    everywhere = ("rep", "ep")
    rep_count, ep_count = (lax.axis_size("rep"), lax.axis_size("ep"))
    rep_index, ep_index = (lax.axis_index("rep"), lax.axis_index("ep"))
    inputs = hidden_in[0].astype(f32)
    sequence_length, model_width = inputs.shape
    head_size = qk_gains.shape[1]
    wide_q, wide_kv = (w_q.shape[1], key_weight.shape[1])
    heads_q, heads_kv = (wide_q // head_size, wide_kv // head_size)
    groups = heads_q // heads_kv
    local_experts = w_gate.shape[0]
    experts = local_experts * ep_count
    top_count = routes.shape[2]
    score_scale = head_size ** (-0.5)
    group_lengths = lax.dynamic_slice_in_dim(lengths, rep_index * ep_count, ep_count)
    length = lax.dynamic_index_in_dim(group_lengths, ep_index, keepdims=False)
    positions = jnp.arange(sequence_length, dtype=jnp.int32)
    live = positions < length
    live_rows = live.astype(f32)

    own_rows = w_q.shape[0]
    small = jnp.concatenate([router_w, attn_gain[:, None], ffn_gain[:, None]], axis=1)
    small = jnp.pad(small, ((0, 0), (0, EXT - small.shape[1])))
    pack = jnp.concatenate([w_q, key_weight, value_weight, small], axis=1)
    mat_qkv = gather_weights(pack, rep_count, ep_count, 4).reshape(-1, pack.shape[1])

    wide_all = wide_q + 2 * wide_kv
    small_all = mat_qkv[:, wide_all:]
    mat_router = small_all[:, :experts]
    cosine_lookup, sine_lookup = rope_tables(sequence_length, head_size)
    sign = jnp.where(jnp.arange(head_size) < head_size // 2, -1.0, 1.0).astype(f32)
    turned_sine = sine_lookup * sign[None, :]
    (
        hidden_first,
        projected,
        attended,
        middle,
        sent,
        route_gates,
        kept_float,
        row_gain,
        mat_o,
        grads_all,
    ) = attention_front(
        lengths,
        hidden_in[0],
        qk_gains.astype(f32),
        cosine_lookup,
        turned_sine,
        routes[0],
        order[0].reshape(sequence_length, top_count),
        mat_qkv,
        w_o,
        out_grad[0],
        rep_count,
        ep_count,
        experts,
        heads_kv,
        groups,
        6,
    )
    h_all = gather_tokens(sent, ep_count, 1)
    h_two = sent[:, :model_width]
    route_gates, kept_float = (route_gates[:, :experts], kept_float[:, :experts])
    gain_attn, gain_ffn = (row_gain[0], row_gain[1])
    mat_o = mat_o.reshape(-1, model_width)
    grads_all = grads_all.reshape(-1, model_width)
    norm_one, inv_one = rms_parts(inputs)
    norm_two, inv_two = rms_parts(middle)

    part = min(ep_count, 8)
    tokens = part * sequence_length
    sums = []
    y_parts = []
    for c in range(ep_count // part):
        live_units, unit_rows = unit_table(group_lengths[c * part : (c + 1) * part])
        h_rows = h_all[c * part : (c + 1) * part].reshape(tokens, model_width + EXT)
        g_rows = grads_all[c * tokens : (c + 1) * tokens]
        saves, found = [], []
        for local in range(local_experts):
            info = jnp.concatenate(
                [
                    jnp.stack([live_units, ep_index * local_experts + local]).astype(jnp.int32),
                    jnp.zeros((6,), jnp.int32),
                    unit_rows,
                ]
            )
            save, weight_grads = expert_pass(
                info, h_rows, g_rows, w_gate, w_up, w_down, local, experts, rep_count
            )
            saves.append(save)
            found.append(weight_grads)
        y_parts.append(returned_rows(info, w_gate, w_up, w_down, saves).reshape(part, sequence_length, -1))
        sums.append(found)
    y_all = y_parts[0] if len(y_parts) == 1 else jnp.concatenate(y_parts, axis=0)
    hidden_units = w_gate.shape[2]
    wide_share, tall_share = model_width // rep_count, hidden_units // rep_count
    found = []
    for local in range(local_experts):
        total = sums[0][local]
        for more in sums[1:]:
            total = (total.astype(f32) + more[local].astype(f32)).astype(bf16)
        found.append(lax.psum_scatter(total, "rep", scatter_dimension=0, tiled=True))
    half_width = model_width // 2
    row_first, row_second = sum_tokens(
        y_all, ep_count, (0, half_width), (half_width, half_width + EXT), 2
    )
    live_column = live[:, None]
    grad_rows = out_grad[0].astype(f32) * live_rows[:, None]
    notes = row_second[:, half_width : half_width + 2 * experts]
    d_weight = jnp.where(live_column, notes[:, :experts] + notes[:, experts:], 0.0)
    d_gates = d_weight * kept_float
    d_logits = route_gates * (d_gates - jnp.sum(route_gates * d_gates, axis=-1, keepdims=True))

    router_float = mat_router.astype(f32)
    d_h_two = jnp.concatenate([row_first, row_second[:, :half_width]], axis=1)
    d_h_two = jnp.where(live_column, d_h_two, 0.0)
    d_h_two = d_h_two + jnp.dot(d_logits, router_float.T, precision=top_precision)
    grad_router = jnp.dot(h_two.astype(f32).T, d_logits, precision=top_precision)
    grad_ffn = jnp.sum(d_h_two * norm_two, axis=0)
    d_middle = grad_rows + rms_back(d_h_two * gain_ffn, norm_two, inv_two)
    d_middle_low = d_middle.astype(bf16)
    right, head, out_first, out_second = attention_back(
        length.reshape(1),
        projected,
        qk_gains.astype(f32),
        cosine_lookup,
        turned_sine,
        d_middle_low,
        mat_o,
        y_all,
        ep_count,
        (model_width + EXT, model_width + EXT + half_width),
        (half_width, half_width),
        heads_kv,
        groups,
        5,
    )
    moe_output = jnp.where(live_column, jnp.concatenate([out_first, out_second], axis=1), 0.0)
    layer_out = jnp.where(live_column, middle + moe_output, 0.0)
    d_qkv = right[:, :wide_all]
    d_h_one = jnp.einsum("tf,cf->tc", d_qkv, mat_qkv[:, :wide_all], preferred_element_type=f32)
    grad_attn = jnp.sum(d_h_one * norm_one, axis=0)
    grad_input = d_middle + rms_back(d_h_one * gain_attn, norm_one, inv_one)

    small_grads = jnp.concatenate([grad_router, grad_attn[:, None], grad_ffn[:, None]], axis=1)
    small_grads = jnp.pad(small_grads, ((0, 0), (0, EXT - small_grads.shape[1]))).astype(bf16)
    ep_bits = bits_of(ep_count)

    def owner_order(value, parts):
        shape = (rep_count,) + (2,) * ep_bits + (parts, own_rows, value.shape[1])
        axes = (ep_bits + 1,) + tuple(range(ep_bits, 0, -1)) + (0, ep_bits + 2, ep_bits + 3)
        return value.reshape(shape).transpose(axes).reshape(value.shape)

    splits = (wide_all // 512, (wide_all + model_width) // 512)
    layer_out, grad_input, head = lax.optimization_barrier((layer_out, grad_input, head))
    sums_all, head_sum = dense_sum(
        hidden_first, attended, right, owner_order(small_grads, 1), head, rep_count, ep_count, splits, 3
    )
    last = unpack(
        sums_all, found, wide_share, tall_share, model_width, hidden_units, wide_q, wide_kv, experts
    )
    return (
        layer_out[None],
        grad_input[None],
        last[8][experts],
        last[3],
        last[4],
        last[5],
        last[6],
        last[8][experts + 1],
        last[7],
        head_sum[:2],
        last[0],
        last[1],
        last[2],
    )


def solution(mesh):
    both = ("rep", "ep")
    placed = (
        P(both, None, None),
        P(both, None, None),
        P(both),
        P(both, None),
        P(both, None),
        P(both, None),
        P(both, None),
        P(both),
        P(both, None),
        P(),
        P("ep", None, None),
        P("ep", None, None),
        P("ep", None, None),
        P(),
        P(both, None, None),
        P(both, None),
    )
    return jax.shard_map(
        per_device,
        mesh=mesh,
        in_specs=placed,
        out_specs=(
            P(both, None, None),
            P(both, None, None),
            P(both),
            P(both, None),
            P(both, None),
            P(both, None),
            P(both, None),
            P(both),
            P(both, None),
            P(),
            P("ep", "rep", None),
            P("ep", "rep", None),
            P("ep", "rep", None),
        ),
        check_vma=False,
    )
```

```python
import functools
import math

import jax
import jax.numpy as jnp
from jax import lax
from jax.experimental import pallas as pl
from jax.experimental.pallas import tpu as pltpu
from jax.sharding import PartitionSpec as P

eps = 1e-06
rope_base = 1000000.0
top_precision = lax.Precision.HIGHEST
MESH = pl.DeviceIdType.MESH
f32, bf16 = jnp.float32, jnp.bfloat16
EXT = 128
UNIT = 16
LANES = 256
TILE = 256
VMEM_BYTES = 58 * 1024 * 1024
NT = (((1,), (1,)), ((), ()))
TN = (((0,), (0,)), ((), ()))


def rms_parts(value_rows):
    inverse = lax.rsqrt(jnp.mean(value_rows * value_rows, axis=-1, keepdims=True) + eps)
    return (value_rows * inverse, inverse)


def rms_back(grad_norm, normed, inverse):
    return inverse * (grad_norm - normed * jnp.mean(grad_norm * normed, axis=-1, keepdims=True))


def rope_tables(count, head_size):
    half_size = head_size // 2
    freqs = rope_base ** (-2.0 * jnp.arange(half_size, dtype=f32) / head_size)
    angles = jnp.arange(count, dtype=f32)[:, None] * freqs[None, :]
    cosine_lookup = jnp.concatenate([jnp.cos(angles), jnp.cos(angles)], axis=1)
    sine_lookup = jnp.concatenate([jnp.sin(angles), jnp.sin(angles)], axis=1)
    return (cosine_lookup, sine_lookup)


def bits_of(count):
    return count.bit_length() - 1


def gather_orders(count):
    bits = bits_of(count)
    up = list(range(1, bits)) + [0]
    down = list(range(bits - 1, 0, -1)) + [0]
    return (up, down)


def spans(bits):
    masks = [0]
    for bit in bits:
        masks = masks + [m | (1 << bit) for m in masks]
    return masks


def meet(peers):
    barrier = pltpu.get_barrier_semaphore()
    for peer in peers:
        pl.semaphore_signal(barrier, inc=1, device_id=peer, device_id_type=MESH)
    pl.semaphore_wait(barrier, len(peers))


def token_gather_kernel(count, x_ref, out_ref, send_sem, recv_sem, local_sem):
    rep, me = lax.axis_index("rep"), lax.axis_index("ep")
    bits = bits_of(count)
    half = x_ref.shape[0] // 2
    meet([(rep, me ^ (1 << b)) for b in range(bits)])
    local = pltpu.make_async_copy(x_ref, out_ref.at[me], local_sem)
    local.start()
    orders = gather_orders(count)
    copies = []

    def send(h, mask, bit):
        rows = pl.ds(h * half, half)
        source = x_ref.at[rows] if mask == 0 else out_ref.at[me ^ mask, rows]
        there = mask | (1 << bit)
        copy = pltpu.make_async_remote_copy(
            src_ref=source,
            dst_ref=out_ref.at[me ^ mask, rows],
            send_sem=send_sem.at[h, there],
            recv_sem=recv_sem.at[h, there],
            device_id=(rep, me ^ (1 << bit)),
            device_id_type=MESH,
        )
        copy.start()
        copies.append(copy)

    def arrived(h, mask):
        rows = pl.ds(h * half, half)
        pltpu.make_async_copy(
            x_ref.at[rows], out_ref.at[me ^ mask, rows], recv_sem.at[h, mask]
        ).wait()

    for stage in range(bits):
        for h in range(2):
            send(h, 0, orders[h][stage])
    for stage in range(bits):
        for low in spans(orders[0][:stage]):
            index = spans(orders[0][:stage]).index(low)
            for h in range(2):
                mask = spans(orders[h][:stage])[index] | (1 << orders[h][stage])
                arrived(h, mask)
                for later in range(stage + 1, bits):
                    send(h, mask, orders[h][later])
    for copy in copies:
        copy.wait_send()
    local.wait()


def gather_tokens(x, count, collective_id):
    return pl.pallas_call(
        functools.partial(token_gather_kernel, count),
        out_shape=jax.ShapeDtypeStruct((count,) + x.shape, x.dtype),
        in_specs=[pl.BlockSpec(memory_space=pl.ANY)],
        out_specs=pl.BlockSpec(memory_space=pl.ANY),
        scratch_shapes=[
            pltpu.SemaphoreType.DMA((2, count)),
            pltpu.SemaphoreType.DMA((2, count)),
            pltpu.SemaphoreType.DMA,
        ],
        compiler_params=pltpu.CompilerParams(collective_id=collective_id, has_side_effects=True),
        name="token_gather",
    )(x)


class BlockGather:
    def __init__(self, n_rep, n_ep, x_ref, out_ref, sems):
        self.n_rep, self.bits = n_rep, bits_of(n_ep)
        self.x_ref, self.out_ref = x_ref, out_ref
        self.send_sem, self.recv_sem, self.up_sem, self.down_sem, self.local_sem = sems
        self.rep, self.me = lax.axis_index("rep"), lax.axis_index("ep")
        split = -(-x_ref.shape[1] // 256) * 128
        self.columns = (pl.ds(0, split), pl.ds(split, x_ref.shape[1] - split))
        self.orders = gather_orders(n_ep)
        self.entries = [(0, 0)]
        for s in range(1, n_rep):
            self.entries += [(s, -1), (s, 1)]

    @staticmethod
    def sems(n_rep, n_ep):
        return [
            pltpu.SemaphoreType.DMA((2 * n_rep - 1, 2, n_ep)),
            pltpu.SemaphoreType.DMA((2 * n_rep - 1, 2, n_ep)),
            pltpu.SemaphoreType.DMA((n_rep, 2)),
            pltpu.SemaphoreType.DMA((n_rep, 2)),
            pltpu.SemaphoreType.DMA,
        ]

    def meet(self):
        barrier = pltpu.get_barrier_semaphore()
        peers = [(self.rep, self.me ^ (1 << b)) for b in range(self.bits)]
        for peer in peers:
            pl.semaphore_signal(barrier, inc=1, device_id=peer, device_id_type=MESH)
        if self.n_rep > 1:
            for side in (-1, 1):

                @pl.when(self.reaches(side))
                def _(side=side):
                    pl.semaphore_signal(barrier, inc=1, device_id=(self.rep + side, self.me), device_id_type=MESH)

        count = len(peers)
        if self.n_rep > 1:
            count = count + jnp.where(self.reaches(-1), 1, 0) + jnp.where(self.reaches(1), 1, 0)
        pl.semaphore_wait(barrier, count)

    def reaches(self, side):
        return self.rep > 0 if side < 0 else self.rep < self.n_rep - 1

    def active(self, k):
        steps, side = self.entries[k]
        return self.rep >= steps if side < 0 else self.rep + steps < self.n_rep

    def guarded(self, k, action):
        if k == 0:
            action()
        else:
            pl.when(self.active(k))(action)

    def row(self, k):
        steps, side = self.entries[k]
        return 0 if self.n_rep == 1 else lax.rem(self.rep + side * steps + self.n_rep, self.n_rep)

    def place(self, k, h, mask):
        return self.out_ref.at[self.row(k), self.me ^ mask, :, self.columns[h]]

    def source(self, k, h, mask):
        return self.x_ref.at[:, self.columns[h]] if k == 0 and mask == 0 else self.place(k, h, mask)

    def hop(self, k, h, mask, bit):
        there = mask | (1 << bit)
        return pltpu.make_async_remote_copy(
            src_ref=self.source(k, h, mask),
            dst_ref=self.place(k, h, mask),
            send_sem=self.send_sem.at[k, h, there],
            recv_sem=self.recv_sem.at[k, h, there],
            device_id=(self.rep, self.me ^ (1 << bit)),
            device_id_type=MESH,
        )

    def along(self, k, h, side):
        steps = self.entries[k][0]
        lane = (steps * 2 if side > 0 else steps * 2 + 1)
        return pltpu.make_async_remote_copy(
            src_ref=self.source(k, h, 0),
            dst_ref=self.place(k, h, 0),
            send_sem=(self.up_sem if side > 0 else self.down_sem).at[steps, h],
            recv_sem=self.recv_sem.at[lane + 1, h, 0],
            device_id=(self.rep + side, self.me),
            device_id_type=MESH,
        )

    def arrived(self, k, h, mask):
        target = self.place(k, h, mask)
        pltpu.make_async_copy(target, target, self.recv_sem.at[k, h, mask]).wait()

    def local(self):
        return pltpu.make_async_copy(self.x_ref, self.out_ref.at[self.row(0), self.me], self.local_sem)

    def spread(self, k):
        for stage in range(self.bits):
            for h in range(2):
                self.hop(k, h, 0, self.orders[h][stage]).start()

    def onward(self, k, act):
        sides = (-1, 1) if k == 0 else (-self.entries[k][1],)
        if self.n_rep == 1 or self.entries[k][0] == self.n_rep - 1:
            return
        for side in sides:

            @pl.when(self.reaches(side))
            def _(side=side):
                for h in range(2):
                    act(self.along(k, h, side))

    def begin(self):
        self.local().start()
        self.onward(0, lambda copy: copy.start())
        self.spread(0)

    def from_rep(self, k):
        def action():
            for h in range(2):
                self.arrived(k, h, 0)
            self.onward(k, lambda copy: copy.start())
            self.spread(k)

        self.guarded(k, action)

    def relay(self, k, h, mask, stage):
        def action():
            self.arrived(k, h, mask)
            for later in range(stage + 1, self.bits):
                self.hop(k, h, mask, self.orders[h][later]).start()

        self.guarded(k, action)

    def tree(self):
        for stage in range(self.bits):
            for index in range(1 << stage):
                for h in range(2):
                    yield h, spans(self.orders[h][:stage])[index] | (1 << self.orders[h][stage]), stage

    def events(self):
        due = []
        for k, (steps, _) in enumerate(self.entries):
            if k:
                due.append((16 * steps, len(due), functools.partial(self.from_rep, k)))
            for h, mask, stage in self.tree():
                when = 16 * steps + 15 + 10 * stage if stage < self.bits - 1 else 1000 + steps
                due.append((when, len(due), functools.partial(self.relay, k, h, mask, stage)))
        return [step for _, _, step in sorted(due, key=lambda entry: entry[:2])]

    def end(self):
        for k in range(len(self.entries)):

            def action(k=k):
                for stage in range(self.bits):
                    for h in range(2):
                        self.hop(k, h, 0, self.orders[h][stage]).wait_send()
                for h, mask, stage in self.tree():
                    for later in range(stage + 1, self.bits):
                        self.hop(k, h, mask, self.orders[h][later]).wait_send()
                self.onward(k, lambda copy: copy.wait_send())

            self.guarded(k, action)


def weight_gather_kernel(n_rep, n_ep, x_ref, out_ref, *sems):
    gather = BlockGather(n_rep, n_ep, x_ref, out_ref, sems)
    gather.meet()
    gather.begin()
    for event in gather.events():
        event()
    gather.end()
    gather.local().wait()


def gather_weights(x, n_rep, n_ep, collective_id):
    return pl.pallas_call(
        functools.partial(weight_gather_kernel, n_rep, n_ep),
        out_shape=jax.ShapeDtypeStruct((n_rep, n_ep) + x.shape, x.dtype),
        in_specs=[pl.BlockSpec(memory_space=pl.ANY)],
        out_specs=pl.BlockSpec(memory_space=pl.ANY),
        scratch_shapes=BlockGather.sems(n_rep, n_ep),
        compiler_params=pltpu.CompilerParams(collective_id=collective_id, has_side_effects=True),
        cost_estimate=pl.CostEstimate(flops=1000, bytes_accessed=1000, transcendentals=0),
        name="weight_gather",
    )(x)


COLUMNS = 512


def attention_front_kernel(n_rep, n_ep, experts, heads_kv, groups, scale, *refs):
    (lengths_ref, x_ref, gains_ref, cos_ref, sin_ref, routes_ref, order_ref) = refs[:7]
    (mat_ref, wo_ref, own_g_ref) = refs[7:10]
    h_ref, proj_ref, att_ref, middle_ref, sent_ref, gates_ref, kept_ref, row_ref, wo_all, g_all = refs[10:20]
    mat_buf, mat_sem, k_low, v_low, wo_buf, wo_sem, small_ref, ranks, loads_own, loads_all = refs[20:30]
    gather = BlockGather(n_rep, n_ep, wo_ref, wo_all, refs[30:35])
    extra = BlockGather(1, n_ep, own_g_ref, g_all, refs[35:40])
    counted = BlockGather(1, n_ep, loads_own, loads_all, refs[40:45])
    rep, me = lax.axis_index("rep"), lax.axis_index("ep")
    length = lengths_ref[rep * n_ep + me]
    group_total = lengths_ref[rep * n_ep]
    for j in range(1, n_ep):
        group_total += lengths_ref[rep * n_ep + j]
    top_count = routes_ref.shape[1]
    capacity = (9 * top_count * group_total // (8 * experts)).astype(f32)
    size = gains_ref.shape[1]
    tokens, width = x_ref.shape
    wide_q, wide_kv = heads_kv * groups * size, heads_kv * size
    chunks = (wide_q + 2 * wide_kv) // COLUMNS
    pairs = heads_kv * groups // 2
    deep = n_ep * wo_ref.shape[0]
    early = chunks + pairs
    turns = early + n_rep

    def mat_copy(i):
        columns = pl.ds(pl.multiple_of(i * COLUMNS, COLUMNS), COLUMNS)
        return pltpu.make_async_copy(mat_ref.at[:, columns], mat_buf.at[i % 2], mat_sem.at[i % 2])

    def wo_copy(n):
        return pltpu.make_async_copy(wo_all.at[n], wo_buf.at[n % 2], wo_sem.at[n % 2])

    small_copy = pltpu.make_async_copy(
        mat_ref.at[:, pl.ds(wide_q + 2 * wide_kv, EXT)], small_ref, wo_sem.at[0]
    )
    small_copy.start()
    mat_copy(0).start()
    gather.meet()
    gather.begin()
    lane = lax.broadcasted_iota(jnp.int32, (tokens, EXT), 1)
    named = lane < 0
    sort_key = jnp.zeros((tokens, EXT), jnp.int32)
    for n in range(top_count):
        hit = routes_ref[:, n : n + 1] == lane
        named = named | hit
        sort_key = jnp.where(hit, order_ref[:, n : n + 1], sort_key)
    routed = named & (lax.broadcasted_iota(jnp.int32, (tokens, EXT), 0) < length)
    sort_key = jnp.where(routed, sort_key, tokens * top_count).astype(f32)
    loads = jnp.sum(jnp.where(routed, 1.0, 0.0), axis=0, keepdims=True)
    loads_own[...] = jnp.broadcast_to(jnp.concatenate([loads, loads], axis=1), loads_own.shape)
    counted.begin()
    turned = sort_key.T
    ranks[...] = jnp.zeros_like(ranks)
    for e in range(experts):
        smaller = sort_key[:, e : e + 1] < turned[e : e + 1, :]
        ranks[e : e + 1, :] = jnp.sum(jnp.where(smaller, 1.0, 0.0), axis=0, keepdims=True)
    gates_ref[...] = jnp.where(named, 1.0, 0.0)
    small_copy.wait()
    pick = lax.broadcasted_iota(jnp.int32, (8, EXT), 0) + experts == lax.broadcasted_iota(jnp.int32, (8, EXT), 1)
    picks = jnp.where(pick, 1.0, 0.0).astype(bf16)
    row_ref[...] = lax.dot_general(picks, small_ref[...], NT, preferred_element_type=f32)
    x = x_ref[...].astype(f32)
    x = x * lax.rsqrt(jnp.mean(x * x, axis=-1, keepdims=True) + eps)
    h_ref[...] = (x * row_ref[0:1, :]).astype(bf16)

    def rotate(value):
        return value * cos_ref[...] + pltpu.roll(value, size // 2, 1) * sin_ref[...]

    def normed(value):
        return value * lax.rsqrt(jnp.mean(value * value, axis=-1, keepdims=True) + eps)

    query_pos = lax.broadcasted_iota(jnp.int32, (tokens, tokens), 0)
    key_pos = lax.broadcasted_iota(jnp.int32, (tokens, tokens), 1)
    allowed = (key_pos <= query_pos) & (key_pos < length)

    def lanes(start):
        return pl.ds(pl.multiple_of(start, size), size)

    first = gather.events()
    first = first[: len(first) // 4] + counted.events() + first[len(first) // 4 :]
    first.insert(len(first) // 2, extra.begin)
    second = extra.events()

    def shares(events, weights, start):
        given, total, done, reached = {}, sum(weights), 0, 0.0
        for n, weight in enumerate(weights):
            reached += weight
            upto = -(-len(events) * reached // total)
            upto = len(events) if n == len(weights) - 1 else int(upto)
            given[start + n] = events[done:upto]
            done = upto
        return given

    plan = {
        **shares(first, [1.0] * chunks + [4.0] * pairs, 0),
        early: second[:2],
        turns - 1: second[2 : len(second) - n_ep],
    }

    def turn(i, carry):
        @pl.when(i < chunks)
        def _():
            @pl.when(i + 1 < chunks)
            def _():
                mat_copy(i + 1).start()

            mat_copy(i).wait()
            columns = pl.ds(pl.multiple_of(i * COLUMNS, COLUMNS), COLUMNS)
            proj_ref[:, columns] = jnp.dot(h_ref[...], mat_buf[i % 2], preferred_element_type=f32)

        @pl.when((i >= chunks) & (i < early))
        def _():
            pair = i - chunks
            group = pair // (groups // 2)

            @pl.when(pair % (groups // 2) == 0)
            def _():
                key = normed(proj_ref[:, lanes(wide_q + group * size)])
                k_low[...] = rotate(key * gains_ref[1:2, :]).astype(bf16)
                v_low[...] = proj_ref[:, lanes(wide_q + wide_kv + group * size)].astype(bf16)

            for n in range(2):
                head = pair * 2 + n
                query = rotate(normed(proj_ref[:, lanes(head * size)]) * gains_ref[0:1, :]).astype(bf16)
                scores = lax.dot_general(query, k_low[...], NT, preferred_element_type=f32) * scale
                scores = jnp.where(allowed, scores, -1e30)
                raised = jnp.exp(scores - jnp.max(scores, axis=1, keepdims=True))
                probs = (raised * (1.0 / jnp.sum(raised, axis=1, keepdims=True))).astype(bf16)
                att_ref[:, lanes(head * size)] = jnp.dot(
                    probs, v_low[...], preferred_element_type=f32
                ).astype(bf16)

        @pl.when(i >= early)
        def _():
            n = i - early

            @pl.when(n == 0)
            def _():
                gather.local().wait()
                wo_copy(0).start()
                middle_ref[...] = x_ref[...].astype(f32)

            @pl.when(i + 1 < turns)
            def _():
                wo_copy(n + 1).start()

            wo_copy(n).wait()
            columns = pl.ds(pl.multiple_of(n * deep, deep), deep)
            middle_ref[...] += jnp.dot(
                att_ref[:, columns], wo_buf[n % 2].reshape(deep, width), preferred_element_type=f32
            )

        for k, mine in plan.items():
            if mine:

                @pl.when(i == k)
                def _(mine=mine):
                    for event in mine:
                        event()

        return carry

    lax.fori_loop(0, turns, turn, 0)
    step = 64
    for r in range(0, tokens, step):
        low = (normed(middle_ref[r : r + step, :]) * row_ref[1:2, :]).astype(bf16)
        sent_ref[r : r + step, :width] = low
    logits = jnp.dot(sent_ref[:, :width], small_ref[...], preferred_element_type=f32)
    counted.local().wait()
    earlier = jnp.zeros((1, EXT), f32)
    for j in range(n_ep):
        earlier += jnp.where(j < me, loads_all[0, j, 0:1, :EXT], 0.0)
    named = gates_ref[...] > 0.0
    routed = named & (lax.broadcasted_iota(jnp.int32, (tokens, EXT), 0) < length)
    kept = jnp.where(routed & (earlier + ranks[...].T < capacity), 1.0, 0.0)
    kept_ref[...] = kept
    top = jnp.max(jnp.where(named, logits, -jnp.inf), axis=1, keepdims=True)
    raised = jnp.where(named, jnp.exp(jnp.where(named, logits - top, 0.0)), 0.0)
    gates = raised / jnp.sum(raised, axis=1, keepdims=True)
    gates_ref[...] = gates
    weight = gates * kept
    high = weight.astype(bf16).astype(f32)
    middle = (weight - high).astype(bf16).astype(f32)
    low = weight - high - middle
    spread = high + pltpu.roll(middle, experts, 1) + pltpu.roll(low, 2 * experts, 1)
    sent_ref[:, width:] = spread.astype(bf16)
    counted.end()
    for event in second[len(second) - n_ep :]:
        event()
    gather.end()
    extra.end()
    extra.local().wait()


def attention_front(
    lengths, x, gains, cos, sin, routes, order, mat, w_o, own_g, n_rep, n_ep, experts, heads_kv, groups, collective_id
):
    tokens, width = x.shape
    size = gains.shape[1]
    vmem = pl.BlockSpec(memory_space=pltpu.VMEM)
    anywhere = pl.BlockSpec(memory_space=pl.ANY)
    wide_q = heads_kv * groups * size
    wide_all = wide_q + 2 * heads_kv * size
    return pl.pallas_call(
        functools.partial(attention_front_kernel, n_rep, n_ep, experts, heads_kv, groups, size ** (-0.5)),
        out_shape=(
            jax.ShapeDtypeStruct((tokens, width), bf16),
            jax.ShapeDtypeStruct((tokens, wide_all), f32),
            jax.ShapeDtypeStruct((tokens, wide_q), bf16),
            jax.ShapeDtypeStruct((tokens, width), f32),
            jax.ShapeDtypeStruct((tokens, width + EXT), bf16),
            jax.ShapeDtypeStruct((tokens, EXT), f32),
            jax.ShapeDtypeStruct((tokens, EXT), f32),
            jax.ShapeDtypeStruct((8, width), f32),
            jax.ShapeDtypeStruct((n_rep, n_ep) + w_o.shape, bf16),
            jax.ShapeDtypeStruct((1, n_ep) + own_g.shape, bf16),
        ),
        in_specs=[pl.BlockSpec(memory_space=pltpu.SMEM)] + [vmem] * 6 + [anywhere] * 3,
        out_specs=(vmem,) * 8 + (anywhere,) * 2,
        scratch_shapes=[
            pltpu.VMEM((2, width, COLUMNS), bf16),
            pltpu.SemaphoreType.DMA((2,)),
            pltpu.VMEM((tokens, size), bf16),
            pltpu.VMEM((tokens, size), bf16),
            pltpu.VMEM((2, n_ep) + w_o.shape, bf16),
            pltpu.SemaphoreType.DMA((2,)),
            pltpu.VMEM((width, EXT), bf16),
            pltpu.VMEM((EXT, tokens), f32),
            pltpu.VMEM((8, 2 * EXT), f32),
            pltpu.VMEM((1, n_ep, 8, 2 * EXT), f32),
        ]
        + BlockGather.sems(n_rep, n_ep)
        + BlockGather.sems(1, n_ep)
        + BlockGather.sems(1, n_ep),
        compiler_params=pltpu.CompilerParams(
            collective_id=collective_id, has_side_effects=True, vmem_limit_bytes=VMEM_BYTES
        ),
        cost_estimate=pl.CostEstimate(flops=1000, bytes_accessed=1000, transcendentals=0),
        name="attention_front",
    )(lengths, x, gains, cos, sin, routes, order, mat, w_o, own_g)


def unpack_kernel(shares, experts, *refs):
    (sums,) = refs[:1]
    packs, outs = refs[1:-9], refs[-9:-6]
    q_ref, k_ref, v_ref, o_ref, router_ref, rows_ref = refs[-6:]
    for local, pack in enumerate(packs):
        start = 0
        for out, rows in zip(outs, shares):
            for p in range(out.shape[2] // LANES):
                out[local, :, p * LANES : (p + 1) * LANES] = pack[0, start : start + rows, :].astype(f32)
                start += rows
    start = 0
    for out in (q_ref, k_ref, v_ref):
        out[...] = sums[:, start : start + out.shape[1]]
        start += out.shape[1]
    for n in range(2):
        rows = sums.shape[0]
        o_ref[n * rows : (n + 1) * rows, :] = sums[:, start : start + o_ref.shape[1]]
        start += o_ref.shape[1]
    small = sums[:, start : start + EXT]
    router_ref[...] = small[:, :experts]
    rows_ref[...] = small.T


def unpack(sums, packs, wide_share, tall_share, width, hidden, wide_q, wide_kv, experts):
    count, rows = len(packs), sums.shape[0]
    vmem = pl.BlockSpec(memory_space=pltpu.VMEM)
    return pl.pallas_call(
        functools.partial(unpack_kernel, (wide_share, wide_share, tall_share), experts),
        out_shape=tuple(
            jax.ShapeDtypeStruct(shape, f32)
            for shape in (
                (count, wide_share, hidden),
                (count, wide_share, hidden),
                (count, tall_share, width),
                (rows, wide_q),
                (rows, wide_kv),
                (rows, wide_kv),
                (2 * rows, width),
                (rows, experts),
                (EXT, rows),
            )
        ),
        in_specs=[vmem] * (count + 1),
        out_specs=(vmem,) * 9,
        compiler_params=pltpu.CompilerParams(vmem_limit_bytes=VMEM_BYTES),
        cost_estimate=pl.CostEstimate(flops=1000, bytes_accessed=1000, transcendentals=0),
        name="unpack",
    )(sums, *packs)


class TokenSum:
    def __init__(self, count, y_ref, starts, results, scratch):
        self.bits = bits_of(count)
        self.y_ref, self.results = y_ref, results
        self.own, self.got = scratch[:2], scratch[2:4]
        self.send_sem, self.recv_sem, self.own_sem = scratch[4:7]
        self.rep, self.me = lax.axis_index("rep"), lax.axis_index("ep")
        self.orders = [list(reversed(o)) for o in gather_orders(count)]
        self.columns = [pl.ds(s, o.shape[2]) for s, o in zip(starts, self.own)]
        self.masks = [
            [list(reversed(spans(self.orders[h][k + 1 :]))) for k in range(self.bits)] for h in range(2)
        ]
        self.slots, self.seats = [], []
        for h in range(2):
            table = {}
            for stage in range(self.bits):
                for mask in self.masks[h][stage]:
                    table[(stage, mask)] = len(table)
            self.slots.append(table)
            self.seats.append({mask: i for i, mask in enumerate(self.masks[h][0])})

    @staticmethod
    def scratch(count, rows, widths):
        half = count // 2
        return [
            pltpu.VMEM((half, rows, widths[0]), bf16),
            pltpu.VMEM((half, rows, widths[1]), bf16),
            pltpu.VMEM((count - 1, rows, widths[0]), bf16),
            pltpu.VMEM((count - 1, rows, widths[1]), bf16),
            pltpu.SemaphoreType.DMA((2, count)),
            pltpu.SemaphoreType.DMA((2, count)),
            pltpu.SemaphoreType.DMA((2, half)),
        ]

    def meet(self):
        meet([(self.rep, self.me ^ (1 << b)) for b in range(self.bits)])

    def copy(self, h, stage, mask):
        bit = 1 << self.orders[h][stage]
        slot = self.slots[h][(stage, mask)]
        if stage == 0:
            source = self.y_ref.at[self.me ^ bit ^ mask, :, self.columns[h]]
        else:
            source = self.own[h].at[self.seats[h][bit | mask]]
        return pltpu.make_async_remote_copy(
            src_ref=source,
            dst_ref=self.got[h].at[slot],
            send_sem=self.send_sem.at[h, slot],
            recv_sem=self.recv_sem.at[h, slot],
            device_id=(self.rep, self.me ^ bit),
            device_id_type=MESH,
        )

    def load(self, h, mask):
        seat = self.seats[h][mask]
        return pltpu.make_async_copy(
            self.y_ref.at[self.me ^ mask, :, self.columns[h]], self.own[h].at[seat], self.own_sem.at[h, seat]
        )

    def begin(self):
        for i in range(len(self.masks[0][0])):
            for h in range(2):
                self.copy(h, 0, self.masks[h][0][i]).start()
                self.load(h, self.masks[h][0][i]).start()

    def add(self, h, stage, mask):
        slot, seat = self.slots[h][(stage, mask)], self.seats[h][mask]
        own, got = self.own[h], self.got[h]
        if stage == 0:
            self.load(h, mask).wait()
        self.copy(h, stage, mask).wait_recv()
        step = 32

        def body(i, carry):
            rows = pl.ds(pl.multiple_of(i * step, step), step)
            total = own[seat, rows, :].astype(f32) + got[slot, rows, :].astype(f32)
            if stage == self.bits - 1:
                self.results[h][rows, :] = total
            else:
                own[seat, rows, :] = total.astype(bf16)
            return carry

        lax.fori_loop(0, own.shape[1] // step, body, 0)

    def stage(self, stage):
        for i in range(len(self.masks[0][stage])):
            for h in range(2):
                mask = self.masks[h][stage][i]
                self.add(h, stage, mask)
                if stage + 1 < self.bits:
                    following = 1 << self.orders[h][stage + 1]
                    if mask & following:
                        self.copy(h, stage + 1, mask & ~following).start()

    def end(self):
        for h in range(2):
            for stage, mask in self.slots[h]:
                self.copy(h, stage, mask).wait_send()


def token_sum_kernel(count, starts, y_ref, first_ref, second_ref, *scratch):
    total = TokenSum(count, y_ref, starts, (first_ref, second_ref), scratch)
    total.meet()
    total.begin()
    for stage in range(total.bits):
        total.stage(stage)
    total.end()


def sum_tokens(y, count, starts, widths, collective_id):
    rows = y.shape[1]
    return pl.pallas_call(
        functools.partial(token_sum_kernel, count, starts),
        out_shape=tuple(jax.ShapeDtypeStruct((rows, w), f32) for w in widths),
        in_specs=[pl.BlockSpec(memory_space=pl.ANY)],
        out_specs=(pl.BlockSpec(memory_space=pltpu.VMEM),) * 2,
        scratch_shapes=TokenSum.scratch(count, rows, widths),
        compiler_params=pltpu.CompilerParams(
            collective_id=collective_id, has_side_effects=True, vmem_limit_bytes=VMEM_BYTES
        ),
        cost_estimate=pl.CostEstimate(flops=1000, bytes_accessed=1000, transcendentals=0),
        name="token_sum",
    )(y)


QUAD = 4


def attention_back_kernel(count, starts, heads_kv, groups, scale, *refs):
    (length_ref, proj_ref, gains_ref, cos_ref, sin_ref, mid_ref, wo_ref, y_ref) = refs[:8]
    right_ref, head_ref, first_ref, second_ref = refs[8:12]
    wo_buf, wo_sem, k_low, v_low, k_norm, dk_sum, dv_sum = refs[12:19]
    total = TokenSum(count, y_ref, starts, (first_ref, second_ref), refs[19:])
    size = gains_ref.shape[1]
    tokens = proj_ref.shape[0]
    heads_q = heads_kv * groups
    wide_q, wide_kv = heads_q * size, heads_kv * size
    per_group = groups // QUAD
    turns = heads_q // QUAD

    def wo_copy(i):
        rows = pl.ds(pl.multiple_of(i * QUAD * size, QUAD * size), QUAD * size)
        return pltpu.make_async_copy(wo_ref.at[rows], wo_buf.at[i % 2], wo_sem.at[i % 2])

    wo_copy(0).start()
    total.meet()
    total.begin()
    head_ref[...] = jnp.zeros_like(head_ref)
    sent = right_ref.shape[1] - wide_q - 2 * wide_kv
    for n in range(sent // mid_ref.shape[1]):
        start = wide_q + 2 * wide_kv + n * mid_ref.shape[1]
        right_ref[:, start : start + mid_ref.shape[1]] = mid_ref[...]

    def rotate(value):
        return value * cos_ref[...] + pltpu.roll(value, size // 2, 1) * sin_ref[...]

    def rotate_back(value):
        return value * cos_ref[...] - pltpu.roll(value, size // 2, 1) * sin_ref[...]

    def norm_parts(value):
        inverse = lax.rsqrt(jnp.mean(value * value, axis=-1, keepdims=True) + eps)
        return value * inverse, inverse

    def project_back(gradient, normed, inverse, row):
        scaled = rotate_back(gradient)
        head_ref[row : row + 1, :] += jnp.sum(scaled * normed, axis=0, keepdims=True)
        lifted = scaled * gains_ref[row : row + 1, :]
        mean = jnp.mean(lifted * normed, axis=-1, keepdims=True)
        return (inverse * (lifted - normed * mean)).astype(bf16)

    key_pos = lax.broadcasted_iota(jnp.int32, (tokens, tokens), 0)
    query_pos = lax.broadcasted_iota(jnp.int32, (tokens, tokens), 1)
    allowed = (key_pos <= query_pos) & (key_pos < length_ref[0])

    def lanes(start):
        return pl.ds(pl.multiple_of(start, size), size)

    def turn(i, carry):
        group = i // per_group
        for stage, when in ((0, min(1, turns - 1)), (1, turns - 2)):

            @pl.when(i == when)
            def _(stage=stage):
                if stage < total.bits - 1:
                    total.stage(stage)

        @pl.when(i % per_group == 0)
        def _():
            normed, inverse = norm_parts(proj_ref[:, lanes(wide_q + group * size)])
            k_norm[:, :size] = normed
            k_norm[:, size:] = jnp.broadcast_to(inverse, normed.shape)
            k_low[...] = rotate(normed * gains_ref[1:2, :]).astype(bf16)
            v_low[...] = proj_ref[:, lanes(wide_q + wide_kv + group * size)].astype(bf16)
            dk_sum[...] = jnp.zeros_like(dk_sum)
            dv_sum[...] = jnp.zeros_like(dv_sum)

        @pl.when(i + 1 < turns)
        def _():
            wo_copy(i + 1).start()

        wo_copy(i).wait()
        d_att = lax.dot_general(mid_ref[...], wo_buf[i % 2], NT, preferred_element_type=f32).astype(bf16)
        keys, values = k_low[...], v_low[...]
        dk, dv = dk_sum[...], dv_sum[...]
        for n in range(QUAD):
            head = i * QUAD + n
            d_out = d_att[:, n * size : (n + 1) * size]
            normed, inverse = norm_parts(proj_ref[:, lanes(head * size)])
            query = rotate(normed * gains_ref[0:1, :]).astype(bf16)
            scores = lax.dot_general(keys, query, NT, preferred_element_type=f32) * scale
            scores = jnp.where(allowed, scores, -1e30)
            raised = jnp.exp(scores - jnp.max(scores, axis=0, keepdims=True))
            probs = raised * (1.0 / jnp.sum(raised, axis=0, keepdims=True))
            dv += jnp.dot(probs.astype(bf16), d_out, preferred_element_type=f32)
            d_probs = lax.dot_general(values, d_out, NT, preferred_element_type=f32)
            weighted = probs * d_probs
            d_scores = (weighted - probs * jnp.sum(weighted, axis=0, keepdims=True)).astype(bf16)
            dk += jnp.dot(d_scores, query, preferred_element_type=f32)
            d_query = lax.dot_general(d_scores, keys, TN, preferred_element_type=f32) * scale
            right_ref[:, lanes(head * size)] = project_back(d_query, normed, inverse, 0)
        dk_sum[...] = dk
        dv_sum[...] = dv

        @pl.when(i % per_group == per_group - 1)
        def _():
            right_ref[:, lanes(wide_q + group * size)] = project_back(
                dk_sum[...] * scale, k_norm[:, :size], k_norm[:, size:], 1
            )
            right_ref[:, lanes(wide_q + wide_kv + group * size)] = dv_sum[...].astype(bf16)

        return carry

    lax.fori_loop(0, turns, turn, 0)
    for stage in range(min(2, total.bits - 1), total.bits):
        total.stage(stage)
    total.end()


def attention_back(length, proj, gains, cos, sin, d_mid, mat_o, y, count, starts, widths, heads_kv, groups, collective_id):
    tokens, width = d_mid.shape
    size = gains.shape[1]
    vmem = pl.BlockSpec(memory_space=pltpu.VMEM)
    anywhere = pl.BlockSpec(memory_space=pl.ANY)
    columns = (heads_kv * groups + 2 * heads_kv) * size + 2 * width
    return pl.pallas_call(
        functools.partial(attention_back_kernel, count, starts, heads_kv, groups, size ** (-0.5)),
        out_shape=(
            jax.ShapeDtypeStruct((tokens, columns), bf16),
            jax.ShapeDtypeStruct((8, size), f32),
        )
        + tuple(jax.ShapeDtypeStruct((tokens, w), f32) for w in widths),
        in_specs=[pl.BlockSpec(memory_space=pltpu.SMEM)] + [vmem] * 5 + [anywhere] * 2,
        out_specs=(vmem,) * 4,
        scratch_shapes=[
            pltpu.VMEM((2, QUAD * size, width), bf16),
            pltpu.SemaphoreType.DMA((2,)),
            pltpu.VMEM((tokens, size), bf16),
            pltpu.VMEM((tokens, size), bf16),
            pltpu.VMEM((tokens, 2 * size), f32),
            pltpu.VMEM((tokens, size), f32),
            pltpu.VMEM((tokens, size), f32),
        ]
        + TokenSum.scratch(count, tokens, widths),
        compiler_params=pltpu.CompilerParams(
            collective_id=collective_id, has_side_effects=True, vmem_limit_bytes=VMEM_BYTES
        ),
        cost_estimate=pl.CostEstimate(flops=1000, bytes_accessed=1000, transcendentals=0),
        name="attention_back",
    )(length, proj, gains, cos, sin, d_mid, mat_o, y)


def exchanges(n_rep, n_ep):
    near = [(0, b) for b in range(1, bits_of(n_ep))]
    far = [(1, b) for b in range(bits_of(n_rep))]
    return near + far[::-1], (near + far, near[::-1] + far), [2] * len(near) + [3] * len(far)


def dense_sum_kernel(n_rep, n_ep, rows, chunks, split, *refs):
    hidden_ref, att_ref, right_ref, small_ref, head_ref, out_ref, head_out = refs[:7]
    rest = list(refs[7:])
    bits, rep_bits = bits_of(n_ep), bits_of(n_rep)
    wide = right_ref.shape[1] // (chunks - 1)
    half = wide // 2
    rep, me = lax.axis_index("rep"), lax.axis_index("ep")
    axes, orders, depths = exchanges(n_rep, n_ep)
    count = len(axes)
    mine = {axis: lax.rem(lax.div(rep if axis[0] else me, 1 << axis[1]), 2) for axis in axes + [(0, 0)]}
    left_ref, part, got_core = rest[:3]
    acc = [None] + [rest[3 + 2 * k : 5 + 2 * k] for k in range(count)]
    rest = rest[3 + 2 * count :]
    got = [None] + [rest[2 * k : 2 * k + 2] for k in range(count)]
    rest = rest[2 * count :]
    head_own, head_got, head_rep = rest[:3]
    core_send, core_recv, step_send, step_recv, head_send, head_recv, head_rs, head_rr = rest[3:]
    left = [[[a for a in axes if a not in o[:k]] for k in range(count)] for o in orders]
    lags = [0, 1]
    for depth in depths:
        lags.append(lags[-1] + depth)
    slots = [None] + [2 * depth for depth in depths]
    others = [lax.rem(rep + d, n_rep) for d in range(1, n_rep)]
    meet([(rep, me ^ (1 << b)) for b in range(bits)] + [(other, me) for other in others])

    def core_copy(c):
        slot = lax.rem(c, 2)
        return pltpu.make_async_remote_copy(
            src_ref=part.at[slot, 1 - mine[(0, 0)]],
            dst_ref=got_core.at[slot],
            send_sem=core_send.at[slot],
            recv_sem=core_recv.at[slot],
            device_id=(rep, me ^ 1),
            device_id_type=MESH,
        )

    def pick(k, h, which):
        axis = orders[h][k - 1]
        return (slice(None),) * left[h][k - 1].index(axis) + (which(mine[axis]),)

    def bit_copy(k, h, c):
        slot = lax.rem(c, slots[k])
        on_rep, bit = orders[h][k - 1]
        return pltpu.make_async_remote_copy(
            src_ref=acc[k][h].at[(slot,) + pick(k, h, lambda m: 1 - m)],
            dst_ref=got[k][h].at[slot],
            send_sem=step_send.at[k, h, slot],
            recv_sem=step_recv.at[k, h, slot],
            device_id=(rep ^ (1 << bit), me) if on_rep else (rep, me ^ (1 << bit)),
            device_id_type=MESH,
        )

    corners = [()]
    for _ in range(bits - 1):
        corners = [c + (v,) for c in corners for v in range(2)]
    block = n_rep * rows
    side_rows = len(corners) * block
    inner = (2,) * rep_bits

    def place_rows(source, which_of):
        per = 128 // rows
        for b in range(source.shape[1] // 128):
            turned = source[:, b * 128 : (b + 1) * 128].astype(f32).T.astype(bf16)
            for q in range(per):
                which, owner = which_of(b * per + q)
                r, e = owner // n_ep, owner % n_ep
                corner = sum(((e >> bit) & 1) << (bits - 1 - bit) for bit in range(1, bits))
                start = (which * 2 + (e & 1)) * side_rows + corner * block + r * rows
                left_ref[start : start + rows, :] = turned[q * rows : (q + 1) * rows, :]

    place_rows(hidden_ref, lambda n: (0, n))
    place_rows(att_ref, lambda n: (1 + n % 2, n // 2))

    def stage_make(c):
        slot = lax.rem(c, 2)

        @pl.when(c >= 2)
        def _():
            core_copy(c - 2).wait_send()

        @pl.when(c < chunks - 1)
        def _():
            which = jnp.where(c >= split[0], 1, 0) + jnp.where(c >= split[1], 1, 0)
            columns = pl.ds(pl.multiple_of(c * wide, wide), wide)
            weights = right_ref[:, columns]
            for side in (1, 0):
                which_side = 1 - mine[(0, 0)] if side else mine[(0, 0)]
                for n, corner in enumerate(corners):
                    start = (which * 2 + which_side) * side_rows + n * block
                    value = jnp.dot(
                        left_ref[pl.ds(pl.multiple_of(start, block), block), :],
                        weights,
                        preferred_element_type=f32,
                    )
                    part[(slot, which_side) + corner] = value.astype(bf16).reshape(inner + (rows, wide))

        @pl.when(c == chunks - 1)
        def _():
            thin = small_ref.shape[1]
            lead = (slice(None),) * (rep_bits + 1)
            for side in range(2):
                for n, corner in enumerate(corners):
                    value = small_ref[pl.ds(side * side_rows + n * block, block), :].reshape(inner + (rows, thin))
                    blank = jnp.zeros(inner + (rows, wide - thin), bf16)
                    part[(slot, side) + corner + lead + (slice(0, thin),)] = value
                    part[(slot, side) + corner + lead + (slice(thin, wide),)] = blank

        core_copy(c).start()

    def stage_core(c):
        slot, put = lax.rem(c, 2), lax.rem(c, slots[1])

        @pl.when(c >= slots[1])
        def _():
            for h in range(2):
                bit_copy(1, h, c - slots[1]).wait_send()

        core_copy(c).wait_recv()
        for corner in corners:
            total = part[(slot, mine[(0, 0)]) + corner].astype(f32) + got_core[(slot,) + corner].astype(f32)
            total = total.astype(bf16)
            for h in range(2):
                acc[1][h][(put,) + corner] = total[..., h * half : (h + 1) * half]
        for h in range(2):
            bit_copy(1, h, c).start()

    def joined(k, h, c):
        slot = lax.rem(c, slots[k])
        return acc[k][h][(slot,) + pick(k, h, lambda m: m)].astype(f32) + got[k][h][slot].astype(f32)

    def stage_bit(k, c):
        for h in range(2):

            @pl.when(c >= slots[k])
            def _(h=h):
                bit_copy(k, h, c - slots[k]).wait_send()

            bit_copy(k - 1, h, c).wait_recv()
            acc[k][h][lax.rem(c, slots[k])] = joined(k - 1, h, c).astype(bf16)
            bit_copy(k, h, c).start()

    def stage_end(c):
        for h in range(2):
            bit_copy(count, h, c).wait_recv()
            out_ref[:, pl.ds(pl.multiple_of(c * wide + h * half, half), half)] = joined(count, h, c)

    def head_copy(t):
        return pltpu.make_async_remote_copy(
            src_ref=head_own.at[t],
            dst_ref=head_got.at[t],
            send_sem=head_send.at[t],
            recv_sem=head_recv.at[t],
            device_id=(rep, me ^ (1 << t)),
            device_id_type=MESH,
        )

    def head_rep_copy(d):
        return pltpu.make_async_remote_copy(
            src_ref=head_own.at[bits],
            dst_ref=head_rep.at[rep],
            send_sem=head_rs.at[d],
            recv_sem=head_rr.at[n_rep - 2 - d],
            device_id=(others[d], me),
            device_id_type=MESH,
        )

    def head_step(t):
        if t == 0:
            head_own[0] = head_ref[...]
            head_copy(0).start()
        elif t <= bits:
            head_copy(t - 1).wait_recv()
            head_own[t] = head_own[t - 1] + head_got[t - 1]
            if t < bits:
                head_copy(t).start()
            else:
                for d in range(n_rep - 1):
                    head_rep_copy(d).start()
                head_rep[rep] = head_own[bits]
        else:
            for d in range(n_rep - 1):
                head_rep_copy(d).wait_recv()
            total = head_rep[0]
            for r in range(1, n_rep):
                total = total + head_rep[r]
            head_out[...] = total

    def step(i, carry):
        for stage in reversed(range(len(lags))):
            c = i - lags[stage]

            @pl.when((c >= 0) & (c < chunks))
            def _(stage=stage, c=c):
                if stage == 0:
                    stage_make(c)
                elif stage == 1:
                    stage_core(c)
                elif stage <= count:
                    stage_bit(stage, c)
                else:
                    stage_end(c)

        for t in range(bits + 2):

            @pl.when(i == t)
            def _(t=t):
                head_step(t)

        return carry

    lax.fori_loop(0, chunks + lags[-1], step, 0)
    for c in range(chunks - 2, chunks):
        core_copy(c).wait_send()
    for k in range(1, count + 1):
        for c in range(chunks - slots[k], chunks):
            for h in range(2):
                bit_copy(k, h, c).wait_send()
    for t in range(bits):
        head_copy(t).wait_send()
    for d in range(n_rep - 1):
        head_rep_copy(d).wait_send()


def dense_sum(hidden, attended, right, small, head, n_rep, n_ep, split, collective_id):
    chunk = 512
    chunks = right.shape[1] // chunk + 1
    bits, rep_bits = bits_of(n_ep), bits_of(n_rep)
    tokens, width = hidden.shape
    rows = width // (n_rep * n_ep)
    axes, _, depths = exchanges(n_rep, n_ep)
    half = chunk // 2
    most = 2 * max(depths)
    vmem = pl.BlockSpec(memory_space=pltpu.VMEM)
    inner = (2,) * rep_bits + (rows,)
    scratch = [
        pltpu.VMEM((width + attended.shape[1], tokens), bf16),
        pltpu.VMEM((2, 2) + (2,) * (bits - 1) + inner + (chunk,), bf16),
        pltpu.VMEM((2,) + (2,) * (bits - 1) + inner + (chunk,), bf16),
    ]
    for k, depth in enumerate(depths):
        scratch += [pltpu.VMEM((2 * depth,) + (2,) * (len(axes) - k) + (rows, half), bf16)] * 2
    for k, depth in enumerate(depths):
        scratch += [pltpu.VMEM((2 * depth,) + (2,) * (len(axes) - k - 1) + (rows, half), bf16)] * 2
    scratch += [
        pltpu.VMEM((bits + 1,) + head.shape, f32),
        pltpu.VMEM((bits,) + head.shape, f32),
        pltpu.VMEM((n_rep,) + head.shape, f32),
        pltpu.SemaphoreType.DMA((2,)),
        pltpu.SemaphoreType.DMA((2,)),
        pltpu.SemaphoreType.DMA((len(axes) + 1, 2, most)),
        pltpu.SemaphoreType.DMA((len(axes) + 1, 2, most)),
        pltpu.SemaphoreType.DMA((bits,)),
        pltpu.SemaphoreType.DMA((bits,)),
        pltpu.SemaphoreType.DMA((n_rep - 1,)),
        pltpu.SemaphoreType.DMA((n_rep - 1,)),
    ]
    return pl.pallas_call(
        functools.partial(dense_sum_kernel, n_rep, n_ep, rows, chunks, split),
        out_shape=(
            jax.ShapeDtypeStruct((rows, chunks * chunk), f32),
            jax.ShapeDtypeStruct(head.shape, f32),
        ),
        in_specs=[vmem] * 5,
        out_specs=(vmem, vmem),
        scratch_shapes=scratch,
        compiler_params=pltpu.CompilerParams(
            collective_id=collective_id, has_side_effects=True, vmem_limit_bytes=VMEM_BYTES
        ),
        cost_estimate=pl.CostEstimate(flops=1000, bytes_accessed=1000, transcendentals=0),
        name="dense_sum",
    )(hidden, attended, right, small, head)


def expert_kernel(local, experts, width, hidden_of, *refs):
    (info, h_ref, g_ref, wg_all, wu_all, wd_all) = refs[:6]
    save_ref, grad_ref = refs[6:8]
    xs, gs, ds, hs, notes, wide, tall, in_sem, save_sem, grad_sem = refs[8:18]
    wg_ref, wu_ref, wd_ref, weight_sem = refs[18:]
    weights = [
        pltpu.make_async_copy(source.at[local], target, weight_sem.at[n])
        for n, (source, target) in enumerate(((wg_all, wg_ref), (wu_all, wu_ref), (wd_all, wd_ref)))
    ]
    for copy in weights:
        copy.start()
    shares = grad_ref.shape[0]
    wide_share, tall_share = width // shares, hidden_of // shares
    hidden = wg_ref.shape[1]
    units = info[0]
    expert = info[1]
    table = 8
    per_tile = TILE // UNIT
    tiles = (units + per_tile - 1) // per_tile
    most = xs.shape[0] // TILE
    floor_tiles = min(4, most)

    def unit_in(u, slot):
        source = pl.ds(pl.multiple_of(info[table + u], UNIT), UNIT)
        target = pl.ds(pl.multiple_of(u * UNIT, UNIT), UNIT)
        return (
            pltpu.make_async_copy(h_ref.at[source], xs.at[target], in_sem.at[0, slot]),
            pltpu.make_async_copy(g_ref.at[source], gs.at[target], in_sem.at[1, slot]),
        )

    def begin(u, carry):
        for copy in unit_in(u, u // per_tile):
            copy.start()
        return carry

    def begin_tile(i):
        lax.fori_loop(
            jnp.minimum(i * per_tile, units), jnp.minimum((i + 1) * per_tile, units), begin, 0
        )

    begin_tile(0)
    begin_tile(1)

    def blank(u, carry):
        target = pl.ds(pl.multiple_of(u * UNIT, UNIT), UNIT)
        xs[target, :] = jnp.zeros((UNIT, xs.shape[1]), bf16)
        gs[target, :] = jnp.zeros((UNIT, gs.shape[1]), bf16)
        return carry

    lax.fori_loop(units, jnp.maximum(tiles, floor_tiles) * per_tile, blank, 0)

    def blank_tile(i, carry):
        target = pl.ds(pl.multiple_of(i * TILE, TILE), TILE)
        ds[target, :] = jnp.zeros((TILE, ds.shape[1]), bf16)
        hs[target, :] = jnp.zeros((TILE, hs.shape[1]), bf16)
        return carry

    lax.fori_loop(tiles, floor_tiles, blank_tile, 0)

    lane = lax.broadcasted_iota(jnp.int32, (TILE, EXT), 1)
    weight_lanes = (lane == expert) | (lane == expert + experts) | (lane == expert + 2 * experts)

    def tile_step(i, carry):
        def landed(u, c):
            for copy in unit_in(u, i):
                copy.wait()
            return c

        begin_tile(i + 2)
        lax.fori_loop(i * per_tile, jnp.minimum((i + 1) * per_tile, units), landed, 0)
        rows = pl.ds(pl.multiple_of(i * TILE, TILE), TILE)
        x = xs[rows, :width]
        g = gs[rows, :]
        extra = xs[rows, width:].astype(f32)
        weight = jnp.sum(jnp.where(weight_lanes, extra, 0.0), axis=1, keepdims=True)
        gate = jnp.dot(x, wg_ref[...], preferred_element_type=f32)
        up = jnp.dot(x, wu_ref[...], preferred_element_type=f32)
        d_plain = lax.dot_general(g, wd_ref[...], NT, preferred_element_type=f32)
        sig = 1.0 / (1.0 + jnp.exp(-gate))
        silu = gate * sig
        hid = silu * up
        d_weight = jnp.sum(hid.astype(bf16).astype(f32) * d_plain, axis=1, keepdims=True)
        hs[rows, :] = (hid * weight).astype(bf16)
        d_hidden = d_plain * weight
        ds[rows, :hidden] = (d_hidden * up * sig * (1.0 + gate * (1.0 - sig))).astype(bf16)
        ds[rows, hidden:] = (d_hidden * silu).astype(bf16)

        high = d_weight.astype(bf16).astype(f32)
        low = d_weight - high
        note = jnp.where(lane == expert, high, 0.0) + jnp.where(lane == expert + experts, low, 0.0)
        notes[rows, :] = note.astype(bf16)
        return carry

    for copy in weights:
        copy.wait()
    lax.fori_loop(0, tiles, tile_step, 0)
    saves = [
        pltpu.make_async_copy(source, save_ref.at[:, start : start + source.shape[1]], save_sem.at[n])
        for n, (source, start) in enumerate(((ds, 0), (hs, 2 * hidden), (notes, 3 * hidden)))
    ]
    for copy in saves:
        copy.start()

    block = 256

    def grads(depth):
        def wide_copies(m):
            per = wide_share // block
            return tuple(
                pltpu.make_async_copy(
                    wide.at[m % 2, :, p * LANES : (p + 1) * LANES],
                    grad_ref.at[
                        m // per,
                        pl.ds(pl.multiple_of(p * wide_share + (m % per) * block, block), block),
                    ],
                    grad_sem.at[m % 2, p],
                )
                for p in range(2 * hidden // LANES)
            )

        def wide_step(m, carry):
            @pl.when(m >= 2)
            def _():
                for copy in wide_copies(m - 2):
                    copy.wait()

            columns = pl.ds(pl.multiple_of(m * block, block), block)
            wide[m % 2] = lax.dot_general(
                xs[:depth, columns], ds[:depth, :], TN, preferred_element_type=f32
            ).astype(bf16)
            for copy in wide_copies(m):
                copy.start()
            return carry

        count = width // block
        lax.fori_loop(0, count, wide_step, 0)
        for m in range(count - 2, count):
            for copy in wide_copies(m):
                copy.wait()

        piece = math.gcd(block, tall_share)
        base = 2 * hidden // LANES * wide_share

        def tall_copies(m):
            made = []
            for q in range(block // piece):
                first_row = m * block + q * piece
                share, inside = first_row // tall_share, first_row % tall_share
                for p in range(width // LANES):
                    rows = pl.ds(pl.multiple_of(base + p * tall_share + inside, piece), piece)
                    made.append(
                        pltpu.make_async_copy(
                            tall.at[m % 2, q * piece : (q + 1) * piece, p * LANES : (p + 1) * LANES],
                            grad_ref.at[share, rows],
                            grad_sem.at[m % 2, q * (width // LANES) + p],
                        )
                    )
            return made

        def tall_step(m, carry):
            @pl.when(m >= 2)
            def _():
                for copy in tall_copies(m - 2):
                    copy.wait()

            columns = pl.ds(pl.multiple_of(m * block, block), block)
            tall[m % 2] = lax.dot_general(
                hs[:depth, columns], gs[:depth, :], TN, preferred_element_type=f32
            ).astype(bf16)
            for copy in tall_copies(m):
                copy.start()
            return carry

        count = hidden // block
        lax.fori_loop(0, count, tall_step, 0)
        for m in range(count - 2, count):
            for copy in tall_copies(m):
                copy.wait()

    for choice in range(floor_tiles, most + 1):
        chosen = (tiles <= choice) if choice == floor_tiles else (tiles == choice)

        @pl.when(chosen)
        def _(choice=choice):
            grads(choice * TILE)

    for copy in saves:
        copy.wait()


def expert_pass(info, h_rows, g_rows, w_gate, w_up, w_down, local, experts, shares):
    tokens, width = g_rows.shape
    hidden = w_gate.shape[2]
    any_spec = pl.BlockSpec(memory_space=pl.ANY)
    pieces = 256 // math.gcd(256, hidden // shares) * width // LANES
    return pl.pallas_call(
        functools.partial(expert_kernel, local, experts, width, hidden),
        out_shape=(
            jax.ShapeDtypeStruct((tokens, 3 * hidden + EXT), bf16),
            jax.ShapeDtypeStruct((shares, 3 * hidden * width // shares // LANES, LANES), bf16),
        ),
        in_specs=[pl.BlockSpec(memory_space=pltpu.SMEM)] + [any_spec] * 5,
        out_specs=(any_spec,) * 2,
        scratch_shapes=[
            pltpu.VMEM((tokens, width + EXT), bf16),
            pltpu.VMEM((tokens, width), bf16),
            pltpu.VMEM((tokens, 2 * hidden), bf16),
            pltpu.VMEM((tokens, hidden), bf16),
            pltpu.VMEM((tokens, EXT), bf16),
            pltpu.VMEM((2, 256, 2 * hidden), bf16),
            pltpu.VMEM((2, 256, width), bf16),
            pltpu.SemaphoreType.DMA((2, tokens // TILE)),
            pltpu.SemaphoreType.DMA((3,)),
            pltpu.SemaphoreType.DMA((2, max(2 * hidden // LANES, pieces))),
            pltpu.VMEM((width, hidden), bf16),
            pltpu.VMEM((width, hidden), bf16),
            pltpu.VMEM((hidden, width), bf16),
            pltpu.SemaphoreType.DMA((3,)),
        ],
        compiler_params=pltpu.CompilerParams(vmem_limit_bytes=VMEM_BYTES),
        cost_estimate=pl.CostEstimate(flops=1000, bytes_accessed=1000, transcendentals=0),
        name="experts",
    )(info, h_rows, g_rows, w_gate, w_up, w_down)


def returned_kernel(local_count, width, hidden, *refs):
    info, wg_all, wu_all, wd_all = refs[:4]
    saves = refs[4 : 4 + local_count]
    y_ref = refs[4 + local_count]
    wg, wu, wd, held, stage, weight_sem, held_sem, out_sem = refs[5 + local_count :]
    weights = [
        pltpu.make_async_copy(source, target, weight_sem.at[n])
        for n, (source, target) in enumerate(((wg_all, wg), (wu_all, wu), (wd_all, wd)))
    ]
    for copy in weights:
        copy.start()
    units = info[0]
    table = 8
    per_tile = TILE // UNIT
    tiles = (units + per_tile - 1) // per_tile

    def held_copies(i):
        rows = pl.ds(pl.multiple_of(i * TILE, TILE), TILE)
        return [
            pltpu.make_async_copy(save.at[rows], held.at[i % 2, n], held_sem.at[i % 2, n])
            for n, save in enumerate(saves)
        ]

    for copy in held_copies(0):
        copy.start()

    def unit_out(u):
        target = pl.ds(pl.multiple_of(info[table + u], UNIT), UNIT)
        tile = u // per_tile
        source = pl.ds(pl.multiple_of((u % per_tile) * UNIT, UNIT), UNIT)
        return pltpu.make_async_copy(stage.at[tile % 2, source], y_ref.at[target], out_sem.at[tile % 2])

    def each_unit(i, act):
        def body(u, carry):
            act(unit_out(u))
            return carry

        lax.fori_loop(i * per_tile, jnp.minimum((i + 1) * per_tile, units), body, 0)

    for copy in weights:
        copy.wait()

    def tile_step(i, carry):
        slot = i % 2

        @pl.when(i >= 2)
        def _():
            each_unit(i - 2, lambda copy: copy.wait())

        @pl.when(i + 1 < tiles)
        def _():
            for copy in held_copies(i + 1):
                copy.start()

        for copy in held_copies(i):
            copy.wait()
        d_row = jnp.zeros((TILE, width), f32)
        out = jnp.zeros((TILE, width), f32)
        note = jnp.zeros((TILE, EXT), f32)
        for n in range(local_count):
            d_row += lax.dot_general(held[slot, n, :, :hidden], wg[n], NT, preferred_element_type=f32)
            d_row += lax.dot_general(
                held[slot, n, :, hidden : 2 * hidden], wu[n], NT, preferred_element_type=f32
            )
            note += held[slot, n, :, 3 * hidden :].astype(f32)
        stage[slot, :, :width] = d_row.astype(bf16)
        stage[slot, :, width : width + EXT] = note.astype(bf16)
        for n in range(local_count):
            out += jnp.dot(held[slot, n, :, 2 * hidden : 3 * hidden], wd[n], preferred_element_type=f32)
        stage[slot, :, width + EXT :] = out.astype(bf16)
        each_unit(i, lambda copy: copy.start())
        return carry

    lax.fori_loop(0, tiles, tile_step, 0)

    @pl.when(tiles >= 2)
    def _():
        each_unit(tiles - 2, lambda copy: copy.wait())

    each_unit(tiles - 1, lambda copy: copy.wait())


def returned_rows(info, w_gate, w_up, w_down, saves):
    local_count, width, hidden = w_gate.shape
    tokens, row = saves[0].shape
    wide_row = width + EXT + width
    any_spec = pl.BlockSpec(memory_space=pl.ANY)
    return pl.pallas_call(
        functools.partial(returned_kernel, local_count, width, hidden),
        out_shape=jax.ShapeDtypeStruct((tokens, wide_row), bf16),
        in_specs=[pl.BlockSpec(memory_space=pltpu.SMEM)] + [any_spec] * (3 + local_count),
        out_specs=any_spec,
        scratch_shapes=[
            pltpu.VMEM(w_gate.shape, bf16),
            pltpu.VMEM(w_up.shape, bf16),
            pltpu.VMEM(w_down.shape, bf16),
            pltpu.VMEM((2, local_count, TILE, row), bf16),
            pltpu.VMEM((2, TILE, wide_row), bf16),
            pltpu.SemaphoreType.DMA((3,)),
            pltpu.SemaphoreType.DMA((2, local_count)),
            pltpu.SemaphoreType.DMA((2,)),
        ],
        compiler_params=pltpu.CompilerParams(vmem_limit_bytes=VMEM_BYTES),
        cost_estimate=pl.CostEstimate(flops=1000, bytes_accessed=1000, transcendentals=0),
        name="returned_rows",
    )(info, w_gate, w_up, w_down, *saves)


def unit_table(lengths):
    per_sequence = TILE // UNIT
    counts = (lengths + UNIT - 1) // UNIT
    unit = jnp.arange(lengths.shape[0] * per_sequence, dtype=jnp.int32)
    live = (unit % per_sequence) < jnp.repeat(counts, per_sequence)
    place = jnp.cumsum(live.astype(jnp.int32)) - 1
    hit = (place[None, :] == unit[:, None]) & live[None, :]
    rows = jnp.sum(jnp.where(hit, unit[None, :] * UNIT, 0), axis=1)
    return (jnp.sum(counts), rows)


def per_device(
    hidden_in,
    out_grad,
    attn_gain,
    w_q,
    key_weight,
    value_weight,
    w_o,
    ffn_gain,
    router_w,
    qk_gains,
    w_gate,
    w_up,
    w_down,
    lengths,
    routes,
    order,
):
    everywhere = ("rep", "ep")
    rep_count, ep_count = (lax.axis_size("rep"), lax.axis_size("ep"))
    rep_index, ep_index = (lax.axis_index("rep"), lax.axis_index("ep"))
    inputs = hidden_in[0].astype(f32)
    sequence_length, model_width = inputs.shape
    head_size = qk_gains.shape[1]
    wide_q, wide_kv = (w_q.shape[1], key_weight.shape[1])
    heads_q, heads_kv = (wide_q // head_size, wide_kv // head_size)
    groups = heads_q // heads_kv
    local_experts = w_gate.shape[0]
    experts = local_experts * ep_count
    top_count = routes.shape[2]
    score_scale = head_size ** (-0.5)
    group_lengths = lax.dynamic_slice_in_dim(lengths, rep_index * ep_count, ep_count)
    length = lax.dynamic_index_in_dim(group_lengths, ep_index, keepdims=False)
    positions = jnp.arange(sequence_length, dtype=jnp.int32)
    live = positions < length
    live_rows = live.astype(f32)

    own_rows = w_q.shape[0]
    small = jnp.concatenate([router_w, attn_gain[:, None], ffn_gain[:, None]], axis=1)
    small = jnp.pad(small, ((0, 0), (0, EXT - small.shape[1])))
    pack = jnp.concatenate([w_q, key_weight, value_weight, small], axis=1)
    mat_qkv = gather_weights(pack, rep_count, ep_count, 4).reshape(-1, pack.shape[1])

    wide_all = wide_q + 2 * wide_kv
    small_all = mat_qkv[:, wide_all:]
    mat_router = small_all[:, :experts]
    cosine_lookup, sine_lookup = rope_tables(sequence_length, head_size)
    sign = jnp.where(jnp.arange(head_size) < head_size // 2, -1.0, 1.0).astype(f32)
    turned_sine = sine_lookup * sign[None, :]
    (
        hidden_first,
        projected,
        attended,
        middle,
        sent,
        route_gates,
        kept_float,
        row_gain,
        mat_o,
        grads_all,
    ) = attention_front(
        lengths,
        hidden_in[0],
        qk_gains.astype(f32),
        cosine_lookup,
        turned_sine,
        routes[0],
        order[0].reshape(sequence_length, top_count),
        mat_qkv,
        w_o,
        out_grad[0],
        rep_count,
        ep_count,
        experts,
        heads_kv,
        groups,
        6,
    )
    h_all = gather_tokens(sent, ep_count, 1)
    h_two = sent[:, :model_width]
    route_gates, kept_float = (route_gates[:, :experts], kept_float[:, :experts])
    gain_attn, gain_ffn = (row_gain[0], row_gain[1])
    mat_o = mat_o.reshape(-1, model_width)
    grads_all = grads_all.reshape(-1, model_width)
    norm_one, inv_one = rms_parts(inputs)
    norm_two, inv_two = rms_parts(middle)

    part = min(ep_count, 8)
    tokens = part * sequence_length
    sums = []
    y_parts = []
    for c in range(ep_count // part):
        live_units, unit_rows = unit_table(group_lengths[c * part : (c + 1) * part])
        h_rows = h_all[c * part : (c + 1) * part].reshape(tokens, model_width + EXT)
        g_rows = grads_all[c * tokens : (c + 1) * tokens]
        saves, found = [], []
        for local in range(local_experts):
            info = jnp.concatenate(
                [
                    jnp.stack([live_units, ep_index * local_experts + local]).astype(jnp.int32),
                    jnp.zeros((6,), jnp.int32),
                    unit_rows,
                ]
            )
            save, weight_grads = expert_pass(
                info, h_rows, g_rows, w_gate, w_up, w_down, local, experts, rep_count
            )
            saves.append(save)
            found.append(weight_grads)
        y_parts.append(returned_rows(info, w_gate, w_up, w_down, saves).reshape(part, sequence_length, -1))
        sums.append(found)
    y_all = y_parts[0] if len(y_parts) == 1 else jnp.concatenate(y_parts, axis=0)
    hidden_units = w_gate.shape[2]
    wide_share, tall_share = model_width // rep_count, hidden_units // rep_count
    found = []
    for local in range(local_experts):
        total = sums[0][local]
        for more in sums[1:]:
            total = (total.astype(f32) + more[local].astype(f32)).astype(bf16)
        found.append(lax.psum_scatter(total, "rep", scatter_dimension=0, tiled=True))
    half_width = model_width // 2
    row_first, row_second = sum_tokens(
        y_all, ep_count, (0, half_width), (half_width, half_width + EXT), 2
    )
    live_column = live[:, None]
    grad_rows = out_grad[0].astype(f32) * live_rows[:, None]
    notes = row_second[:, half_width : half_width + 2 * experts]
    d_weight = jnp.where(live_column, notes[:, :experts] + notes[:, experts:], 0.0)
    d_gates = d_weight * kept_float
    d_logits = route_gates * (d_gates - jnp.sum(route_gates * d_gates, axis=-1, keepdims=True))

    router_float = mat_router.astype(f32)
    d_h_two = jnp.concatenate([row_first, row_second[:, :half_width]], axis=1)
    d_h_two = jnp.where(live_column, d_h_two, 0.0)
    d_h_two = d_h_two + jnp.dot(d_logits, router_float.T, precision=top_precision)
    grad_router = jnp.dot(h_two.astype(f32).T, d_logits, precision=top_precision)
    grad_ffn = jnp.sum(d_h_two * norm_two, axis=0)
    d_middle = grad_rows + rms_back(d_h_two * gain_ffn, norm_two, inv_two)
    d_middle_low = d_middle.astype(bf16)
    right, head, out_first, out_second = attention_back(
        length.reshape(1),
        projected,
        qk_gains.astype(f32),
        cosine_lookup,
        turned_sine,
        d_middle_low,
        mat_o,
        y_all,
        ep_count,
        (model_width + EXT, model_width + EXT + half_width),
        (half_width, half_width),
        heads_kv,
        groups,
        5,
    )
    moe_output = jnp.where(live_column, jnp.concatenate([out_first, out_second], axis=1), 0.0)
    layer_out = jnp.where(live_column, middle + moe_output, 0.0)
    d_qkv = right[:, :wide_all]
    d_h_one = jnp.einsum("tf,cf->tc", d_qkv, mat_qkv[:, :wide_all], preferred_element_type=f32)
    grad_attn = jnp.sum(d_h_one * norm_one, axis=0)
    grad_input = d_middle + rms_back(d_h_one * gain_attn, norm_one, inv_one)

    small_grads = jnp.concatenate([grad_router, grad_attn[:, None], grad_ffn[:, None]], axis=1)
    small_grads = jnp.pad(small_grads, ((0, 0), (0, EXT - small_grads.shape[1]))).astype(bf16)
    ep_bits = bits_of(ep_count)

    def owner_order(value, parts):
        shape = (rep_count,) + (2,) * ep_bits + (parts, own_rows, value.shape[1])
        axes = (ep_bits + 1,) + tuple(range(ep_bits, 0, -1)) + (0, ep_bits + 2, ep_bits + 3)
        return value.reshape(shape).transpose(axes).reshape(value.shape)

    splits = (wide_all // 512, (wide_all + model_width) // 512)
    layer_out, grad_input, head = lax.optimization_barrier((layer_out, grad_input, head))
    sums_all, head_sum = dense_sum(
        hidden_first, attended, right, owner_order(small_grads, 1), head, rep_count, ep_count, splits, 3
    )
    last = unpack(
        sums_all, found, wide_share, tall_share, model_width, hidden_units, wide_q, wide_kv, experts
    )
    return (
        layer_out[None],
        grad_input[None],
        last[8][experts],
        last[3],
        last[4],
        last[5],
        last[6],
        last[8][experts + 1],
        last[7],
        head_sum[:2],
        last[0],
        last[1],
        last[2],
    )


def solution(mesh):
    both = ("rep", "ep")
    placed = (
        P(both, None, None),
        P(both, None, None),
        P(both),
        P(both, None),
        P(both, None),
        P(both, None),
        P(both, None),
        P(both),
        P(both, None),
        P(),
        P("ep", None, None),
        P("ep", None, None),
        P("ep", None, None),
        P(),
        P(both, None, None),
        P(both, None),
    )
    return jax.shard_map(
        per_device,
        mesh=mesh,
        in_specs=placed,
        out_specs=(
            P(both, None, None),
            P(both, None, None),
            P(both),
            P(both, None),
            P(both, None),
            P(both, None),
            P(both, None),
            P(both),
            P(both, None),
            P(),
            P("ep", "rep", None),
            P("ep", "rep", None),
            P("ep", "rep", None),
        ),
        check_vma=False,
    )
```

```python
import functools
import math

import jax
import jax.numpy as jnp
from jax import lax
from jax.experimental import pallas as pl
from jax.experimental.pallas import tpu as pltpu
from jax.sharding import PartitionSpec as P

eps = 1e-06
rope_base = 1000000.0
top_precision = lax.Precision.HIGHEST
MESH = pl.DeviceIdType.MESH
f32, bf16 = jnp.float32, jnp.bfloat16
EXT = 128
UNIT = 16
LANES = 256
TILE = 256
VMEM_BYTES = 58 * 1024 * 1024
NT = (((1,), (1,)), ((), ()))
TN = (((0,), (0,)), ((), ()))


def rms_parts(value_rows):
    inverse = lax.rsqrt(jnp.mean(value_rows * value_rows, axis=-1, keepdims=True) + eps)
    return (value_rows * inverse, inverse)


def rms_back(grad_norm, normed, inverse):
    return inverse * (grad_norm - normed * jnp.mean(grad_norm * normed, axis=-1, keepdims=True))


def rope_tables(count, head_size):
    half_size = head_size // 2
    freqs = rope_base ** (-2.0 * jnp.arange(half_size, dtype=f32) / head_size)
    angles = jnp.arange(count, dtype=f32)[:, None] * freqs[None, :]
    cosine_lookup = jnp.concatenate([jnp.cos(angles), jnp.cos(angles)], axis=1)
    sine_lookup = jnp.concatenate([jnp.sin(angles), jnp.sin(angles)], axis=1)
    return (cosine_lookup, sine_lookup)


def bits_of(count):
    return count.bit_length() - 1


def gather_orders(count):
    bits = bits_of(count)
    up = list(range(1, bits)) + [0]
    down = list(range(bits - 1, 0, -1)) + [0]
    return (up, down)


def spans(bits):
    masks = [0]
    for bit in bits:
        masks = masks + [m | (1 << bit) for m in masks]
    return masks


def meet(peers):
    barrier = pltpu.get_barrier_semaphore()
    for peer in peers:
        pl.semaphore_signal(barrier, inc=1, device_id=peer, device_id_type=MESH)
    pl.semaphore_wait(barrier, len(peers))


def token_gather_kernel(count, x_ref, out_ref, send_sem, recv_sem, local_sem):
    rep, me = lax.axis_index("rep"), lax.axis_index("ep")
    bits = bits_of(count)
    half = x_ref.shape[0] // 2
    meet([(rep, me ^ (1 << b)) for b in range(bits)])
    local = pltpu.make_async_copy(x_ref, out_ref.at[me], local_sem)
    local.start()
    orders = gather_orders(count)
    copies = []

    def send(h, mask, bit):
        rows = pl.ds(h * half, half)
        source = x_ref.at[rows] if mask == 0 else out_ref.at[me ^ mask, rows]
        there = mask | (1 << bit)
        copy = pltpu.make_async_remote_copy(
            src_ref=source,
            dst_ref=out_ref.at[me ^ mask, rows],
            send_sem=send_sem.at[h, there],
            recv_sem=recv_sem.at[h, there],
            device_id=(rep, me ^ (1 << bit)),
            device_id_type=MESH,
        )
        copy.start()
        copies.append(copy)

    def arrived(h, mask):
        rows = pl.ds(h * half, half)
        pltpu.make_async_copy(
            x_ref.at[rows], out_ref.at[me ^ mask, rows], recv_sem.at[h, mask]
        ).wait()

    for stage in range(bits):
        for h in range(2):
            send(h, 0, orders[h][stage])
    for stage in range(bits):
        for low in spans(orders[0][:stage]):
            index = spans(orders[0][:stage]).index(low)
            for h in range(2):
                mask = spans(orders[h][:stage])[index] | (1 << orders[h][stage])
                arrived(h, mask)
                for later in range(stage + 1, bits):
                    send(h, mask, orders[h][later])
    for copy in copies:
        copy.wait_send()
    local.wait()


def gather_tokens(x, count, collective_id):
    return pl.pallas_call(
        functools.partial(token_gather_kernel, count),
        out_shape=jax.ShapeDtypeStruct((count,) + x.shape, x.dtype),
        in_specs=[pl.BlockSpec(memory_space=pl.ANY)],
        out_specs=pl.BlockSpec(memory_space=pl.ANY),
        scratch_shapes=[
            pltpu.SemaphoreType.DMA((2, count)),
            pltpu.SemaphoreType.DMA((2, count)),
            pltpu.SemaphoreType.DMA,
        ],
        compiler_params=pltpu.CompilerParams(collective_id=collective_id, has_side_effects=True),
        name="token_gather",
    )(x)


class BlockGather:
    def __init__(self, n_rep, n_ep, x_ref, out_ref, sems):
        self.n_rep, self.bits = n_rep, bits_of(n_ep)
        self.x_ref, self.out_ref = x_ref, out_ref
        self.send_sem, self.recv_sem, self.up_sem, self.down_sem, self.local_sem = sems
        self.rep, self.me = lax.axis_index("rep"), lax.axis_index("ep")
        split = -(-x_ref.shape[1] // 256) * 128
        self.columns = (pl.ds(0, split), pl.ds(split, x_ref.shape[1] - split))
        self.orders = gather_orders(n_ep)
        self.entries = [(0, 0)]
        for s in range(1, n_rep):
            self.entries += [(s, -1), (s, 1)]

    @staticmethod
    def sems(n_rep, n_ep):
        return [
            pltpu.SemaphoreType.DMA((2 * n_rep - 1, 2, n_ep)),
            pltpu.SemaphoreType.DMA((2 * n_rep - 1, 2, n_ep)),
            pltpu.SemaphoreType.DMA((n_rep, 2)),
            pltpu.SemaphoreType.DMA((n_rep, 2)),
            pltpu.SemaphoreType.DMA,
        ]

    def meet(self):
        barrier = pltpu.get_barrier_semaphore()
        peers = [(self.rep, self.me ^ (1 << b)) for b in range(self.bits)]
        for peer in peers:
            pl.semaphore_signal(barrier, inc=1, device_id=peer, device_id_type=MESH)
        if self.n_rep > 1:
            for side in (-1, 1):

                @pl.when(self.reaches(side))
                def _(side=side):
                    pl.semaphore_signal(barrier, inc=1, device_id=(self.rep + side, self.me), device_id_type=MESH)

        count = len(peers)
        if self.n_rep > 1:
            count = count + jnp.where(self.reaches(-1), 1, 0) + jnp.where(self.reaches(1), 1, 0)
        pl.semaphore_wait(barrier, count)

    def reaches(self, side):
        return self.rep > 0 if side < 0 else self.rep < self.n_rep - 1

    def active(self, k):
        steps, side = self.entries[k]
        return self.rep >= steps if side < 0 else self.rep + steps < self.n_rep

    def guarded(self, k, action):
        if k == 0:
            action()
        else:
            pl.when(self.active(k))(action)

    def row(self, k):
        steps, side = self.entries[k]
        return 0 if self.n_rep == 1 else lax.rem(self.rep + side * steps + self.n_rep, self.n_rep)

    def place(self, k, h, mask):
        return self.out_ref.at[self.row(k), self.me ^ mask, :, self.columns[h]]

    def source(self, k, h, mask):
        return self.x_ref.at[:, self.columns[h]] if k == 0 and mask == 0 else self.place(k, h, mask)

    def hop(self, k, h, mask, bit):
        there = mask | (1 << bit)
        return pltpu.make_async_remote_copy(
            src_ref=self.source(k, h, mask),
            dst_ref=self.place(k, h, mask),
            send_sem=self.send_sem.at[k, h, there],
            recv_sem=self.recv_sem.at[k, h, there],
            device_id=(self.rep, self.me ^ (1 << bit)),
            device_id_type=MESH,
        )

    def along(self, k, h, side):
        steps = self.entries[k][0]
        lane = (steps * 2 if side > 0 else steps * 2 + 1)
        return pltpu.make_async_remote_copy(
            src_ref=self.source(k, h, 0),
            dst_ref=self.place(k, h, 0),
            send_sem=(self.up_sem if side > 0 else self.down_sem).at[steps, h],
            recv_sem=self.recv_sem.at[lane + 1, h, 0],
            device_id=(self.rep + side, self.me),
            device_id_type=MESH,
        )

    def arrived(self, k, h, mask):
        target = self.place(k, h, mask)
        pltpu.make_async_copy(target, target, self.recv_sem.at[k, h, mask]).wait()

    def local(self):
        return pltpu.make_async_copy(self.x_ref, self.out_ref.at[self.row(0), self.me], self.local_sem)

    def spread(self, k):
        for stage in range(self.bits):
            for h in range(2):
                self.hop(k, h, 0, self.orders[h][stage]).start()

    def onward(self, k, act):
        sides = (-1, 1) if k == 0 else (-self.entries[k][1],)
        if self.n_rep == 1 or self.entries[k][0] == self.n_rep - 1:
            return
        for side in sides:

            @pl.when(self.reaches(side))
            def _(side=side):
                for h in range(2):
                    act(self.along(k, h, side))

    def begin(self):
        self.local().start()
        self.onward(0, lambda copy: copy.start())
        self.spread(0)

    def from_rep(self, k):
        def action():
            for h in range(2):
                self.arrived(k, h, 0)
            self.onward(k, lambda copy: copy.start())
            self.spread(k)

        self.guarded(k, action)

    def relay(self, k, h, mask, stage):
        def action():
            self.arrived(k, h, mask)
            for later in range(stage + 1, self.bits):
                self.hop(k, h, mask, self.orders[h][later]).start()

        self.guarded(k, action)

    def tree(self):
        for stage in range(self.bits):
            for index in range(1 << stage):
                for h in range(2):
                    yield h, spans(self.orders[h][:stage])[index] | (1 << self.orders[h][stage]), stage

    def events(self):
        due = []
        for k, (steps, _) in enumerate(self.entries):
            if k:
                due.append((16 * steps, len(due), functools.partial(self.from_rep, k)))
            for h, mask, stage in self.tree():
                when = 16 * steps + 15 + 10 * stage if stage < self.bits - 1 else 1000 + steps
                due.append((when, len(due), functools.partial(self.relay, k, h, mask, stage)))
        return [step for _, _, step in sorted(due, key=lambda entry: entry[:2])]

    def end(self):
        for k in range(len(self.entries)):

            def action(k=k):
                for stage in range(self.bits):
                    for h in range(2):
                        self.hop(k, h, 0, self.orders[h][stage]).wait_send()
                for h, mask, stage in self.tree():
                    for later in range(stage + 1, self.bits):
                        self.hop(k, h, mask, self.orders[h][later]).wait_send()
                self.onward(k, lambda copy: copy.wait_send())

            self.guarded(k, action)


def weight_gather_kernel(n_rep, n_ep, x_ref, out_ref, *sems):
    gather = BlockGather(n_rep, n_ep, x_ref, out_ref, sems)
    gather.meet()
    gather.begin()
    for event in gather.events():
        event()
    gather.end()
    gather.local().wait()


def gather_weights(x, n_rep, n_ep, collective_id):
    return pl.pallas_call(
        functools.partial(weight_gather_kernel, n_rep, n_ep),
        out_shape=jax.ShapeDtypeStruct((n_rep, n_ep) + x.shape, x.dtype),
        in_specs=[pl.BlockSpec(memory_space=pl.ANY)],
        out_specs=pl.BlockSpec(memory_space=pl.ANY),
        scratch_shapes=BlockGather.sems(n_rep, n_ep),
        compiler_params=pltpu.CompilerParams(collective_id=collective_id, has_side_effects=True),
        cost_estimate=pl.CostEstimate(flops=1000, bytes_accessed=1000, transcendentals=0),
        name="weight_gather",
    )(x)


COLUMNS = 512


def attention_front_kernel(n_rep, n_ep, experts, heads_kv, groups, scale, *refs):
    (lengths_ref, x_ref, gains_ref, cos_ref, sin_ref, routes_ref, order_ref) = refs[:7]
    (mat_ref, wo_ref, own_g_ref) = refs[7:10]
    h_ref, proj_ref, att_ref, middle_ref, sent_ref, gates_ref, kept_ref, row_ref, wo_all, g_all = refs[10:20]
    mat_buf, mat_sem, k_low, v_low, wo_buf, wo_sem, small_ref, ranks, loads_own, loads_all = refs[20:30]
    gather = BlockGather(n_rep, n_ep, wo_ref, wo_all, refs[30:35])
    extra = BlockGather(1, n_ep, own_g_ref, g_all, refs[35:40])
    counted = BlockGather(1, n_ep, loads_own, loads_all, refs[40:45])
    rep, me = lax.axis_index("rep"), lax.axis_index("ep")
    length = lengths_ref[rep * n_ep + me]
    group_total = lengths_ref[rep * n_ep]
    for j in range(1, n_ep):
        group_total += lengths_ref[rep * n_ep + j]
    top_count = routes_ref.shape[1]
    capacity = (9 * top_count * group_total // (8 * experts)).astype(f32)
    size = gains_ref.shape[1]
    tokens, width = x_ref.shape
    wide_q, wide_kv = heads_kv * groups * size, heads_kv * size
    chunks = (wide_q + 2 * wide_kv) // COLUMNS
    pairs = heads_kv * groups // 2
    deep = n_ep * wo_ref.shape[0]
    early = chunks + pairs
    turns = early + n_rep

    def mat_copy(i):
        columns = pl.ds(pl.multiple_of(i * COLUMNS, COLUMNS), COLUMNS)
        return pltpu.make_async_copy(mat_ref.at[:, columns], mat_buf.at[i % 2], mat_sem.at[i % 2])

    def wo_copy(n):
        return pltpu.make_async_copy(wo_all.at[n], wo_buf.at[n % 2], wo_sem.at[n % 2])

    small_copy = pltpu.make_async_copy(
        mat_ref.at[:, pl.ds(wide_q + 2 * wide_kv, EXT)], small_ref, wo_sem.at[0]
    )
    small_copy.start()
    mat_copy(0).start()
    gather.meet()
    gather.begin()
    lane = lax.broadcasted_iota(jnp.int32, (tokens, EXT), 1)
    named = lane < 0
    sort_key = jnp.zeros((tokens, EXT), jnp.int32)
    for n in range(top_count):
        hit = routes_ref[:, n : n + 1] == lane
        named = named | hit
        sort_key = jnp.where(hit, order_ref[:, n : n + 1], sort_key)
    routed = named & (lax.broadcasted_iota(jnp.int32, (tokens, EXT), 0) < length)
    sort_key = jnp.where(routed, sort_key, tokens * top_count).astype(f32)
    loads = jnp.sum(jnp.where(routed, 1.0, 0.0), axis=0, keepdims=True)
    loads_own[...] = jnp.broadcast_to(jnp.concatenate([loads, loads], axis=1), loads_own.shape)
    counted.begin()
    turned = sort_key.T
    ranks[...] = jnp.zeros_like(ranks)
    for e in range(experts):
        smaller = sort_key[:, e : e + 1] < turned[e : e + 1, :]
        ranks[e : e + 1, :] = jnp.sum(jnp.where(smaller, 1.0, 0.0), axis=0, keepdims=True)
    gates_ref[...] = jnp.where(named, 1.0, 0.0)
    small_copy.wait()
    pick = lax.broadcasted_iota(jnp.int32, (8, EXT), 0) + experts == lax.broadcasted_iota(jnp.int32, (8, EXT), 1)
    picks = jnp.where(pick, 1.0, 0.0).astype(bf16)
    row_ref[...] = lax.dot_general(picks, small_ref[...], NT, preferred_element_type=f32)
    x = x_ref[...].astype(f32)
    x = x * lax.rsqrt(jnp.mean(x * x, axis=-1, keepdims=True) + eps)
    h_ref[...] = (x * row_ref[0:1, :]).astype(bf16)

    def rotate(value):
        return value * cos_ref[...] + pltpu.roll(value, size // 2, 1) * sin_ref[...]

    def normed(value):
        return value * lax.rsqrt(jnp.mean(value * value, axis=-1, keepdims=True) + eps)

    query_pos = lax.broadcasted_iota(jnp.int32, (tokens, tokens), 0)
    key_pos = lax.broadcasted_iota(jnp.int32, (tokens, tokens), 1)
    allowed = (key_pos <= query_pos) & (key_pos < length)

    def lanes(start):
        return pl.ds(pl.multiple_of(start, size), size)

    first = gather.events()
    first = first[: len(first) // 4] + counted.events() + first[len(first) // 4 :]
    first.insert(len(first) // 2, extra.begin)
    second = extra.events()

    def shares(events, weights, start):
        given, total, done, reached = {}, sum(weights), 0, 0.0
        for n, weight in enumerate(weights):
            reached += weight
            upto = -(-len(events) * reached // total)
            upto = len(events) if n == len(weights) - 1 else int(upto)
            given[start + n] = events[done:upto]
            done = upto
        return given

    plan = {
        **shares(first, [1.0] * chunks + [4.0] * pairs, 0),
        early: second[:2],
        turns - 1: second[2 : len(second) - n_ep],
    }

    def turn(i, carry):
        @pl.when(i < chunks)
        def _():
            @pl.when(i + 1 < chunks)
            def _():
                mat_copy(i + 1).start()

            mat_copy(i).wait()
            columns = pl.ds(pl.multiple_of(i * COLUMNS, COLUMNS), COLUMNS)
            proj_ref[:, columns] = jnp.dot(h_ref[...], mat_buf[i % 2], preferred_element_type=f32)

        @pl.when((i >= chunks) & (i < early))
        def _():
            pair = i - chunks
            group = pair // (groups // 2)

            @pl.when(pair % (groups // 2) == 0)
            def _():
                key = normed(proj_ref[:, lanes(wide_q + group * size)])
                k_low[...] = rotate(key * gains_ref[1:2, :]).astype(bf16)
                v_low[...] = proj_ref[:, lanes(wide_q + wide_kv + group * size)].astype(bf16)

            for n in range(2):
                head = pair * 2 + n
                query = rotate(normed(proj_ref[:, lanes(head * size)]) * gains_ref[0:1, :]).astype(bf16)
                scores = lax.dot_general(query, k_low[...], NT, preferred_element_type=f32) * scale
                scores = jnp.where(allowed, scores, -1e30)
                raised = jnp.exp(scores - jnp.max(scores, axis=1, keepdims=True))
                probs = (raised * (1.0 / jnp.sum(raised, axis=1, keepdims=True))).astype(bf16)
                att_ref[:, lanes(head * size)] = jnp.dot(
                    probs, v_low[...], preferred_element_type=f32
                ).astype(bf16)

        @pl.when(i >= early)
        def _():
            n = i - early

            @pl.when(n == 0)
            def _():
                gather.local().wait()
                wo_copy(0).start()
                middle_ref[...] = x_ref[...].astype(f32)

            @pl.when(i + 1 < turns)
            def _():
                wo_copy(n + 1).start()

            wo_copy(n).wait()
            columns = pl.ds(pl.multiple_of(n * deep, deep), deep)
            middle_ref[...] += jnp.dot(
                att_ref[:, columns], wo_buf[n % 2].reshape(deep, width), preferred_element_type=f32
            )

        for k, mine in plan.items():
            if mine:

                @pl.when(i == k)
                def _(mine=mine):
                    for event in mine:
                        event()

        return carry

    lax.fori_loop(0, turns, turn, 0)
    step = 64
    for r in range(0, tokens, step):
        low = (normed(middle_ref[r : r + step, :]) * row_ref[1:2, :]).astype(bf16)
        sent_ref[r : r + step, :width] = low
    logits = jnp.dot(sent_ref[:, :width], small_ref[...], preferred_element_type=f32)
    counted.local().wait()
    earlier = jnp.zeros((1, EXT), f32)
    for j in range(n_ep):
        earlier += jnp.where(j < me, loads_all[0, j, 0:1, :EXT], 0.0)
    named = gates_ref[...] > 0.0
    routed = named & (lax.broadcasted_iota(jnp.int32, (tokens, EXT), 0) < length)
    kept = jnp.where(routed & (earlier + ranks[...].T < capacity), 1.0, 0.0)
    kept_ref[...] = kept
    top = jnp.max(jnp.where(named, logits, -jnp.inf), axis=1, keepdims=True)
    raised = jnp.where(named, jnp.exp(jnp.where(named, logits - top, 0.0)), 0.0)
    gates = raised / jnp.sum(raised, axis=1, keepdims=True)
    gates_ref[...] = gates
    weight = gates * kept
    high = weight.astype(bf16).astype(f32)
    middle = (weight - high).astype(bf16).astype(f32)
    low = weight - high - middle
    spread = high + pltpu.roll(middle, experts, 1) + pltpu.roll(low, 2 * experts, 1)
    sent_ref[:, width:] = spread.astype(bf16)
    counted.end()
    for event in second[len(second) - n_ep :]:
        event()
    gather.end()
    extra.end()
    extra.local().wait()


def attention_front(
    lengths, x, gains, cos, sin, routes, order, mat, w_o, own_g, n_rep, n_ep, experts, heads_kv, groups, collective_id
):
    tokens, width = x.shape
    size = gains.shape[1]
    vmem = pl.BlockSpec(memory_space=pltpu.VMEM)
    anywhere = pl.BlockSpec(memory_space=pl.ANY)
    wide_q = heads_kv * groups * size
    wide_all = wide_q + 2 * heads_kv * size
    return pl.pallas_call(
        functools.partial(attention_front_kernel, n_rep, n_ep, experts, heads_kv, groups, size ** (-0.5)),
        out_shape=(
            jax.ShapeDtypeStruct((tokens, width), bf16),
            jax.ShapeDtypeStruct((tokens, wide_all), f32),
            jax.ShapeDtypeStruct((tokens, wide_q), bf16),
            jax.ShapeDtypeStruct((tokens, width), f32),
            jax.ShapeDtypeStruct((tokens, width + EXT), bf16),
            jax.ShapeDtypeStruct((tokens, EXT), f32),
            jax.ShapeDtypeStruct((tokens, EXT), f32),
            jax.ShapeDtypeStruct((8, width), f32),
            jax.ShapeDtypeStruct((n_rep, n_ep) + w_o.shape, bf16),
            jax.ShapeDtypeStruct((1, n_ep) + own_g.shape, bf16),
        ),
        in_specs=[pl.BlockSpec(memory_space=pltpu.SMEM)] + [vmem] * 6 + [anywhere] * 3,
        out_specs=(vmem,) * 8 + (anywhere,) * 2,
        scratch_shapes=[
            pltpu.VMEM((2, width, COLUMNS), bf16),
            pltpu.SemaphoreType.DMA((2,)),
            pltpu.VMEM((tokens, size), bf16),
            pltpu.VMEM((tokens, size), bf16),
            pltpu.VMEM((2, n_ep) + w_o.shape, bf16),
            pltpu.SemaphoreType.DMA((2,)),
            pltpu.VMEM((width, EXT), bf16),
            pltpu.VMEM((EXT, tokens), f32),
            pltpu.VMEM((8, 2 * EXT), f32),
            pltpu.VMEM((1, n_ep, 8, 2 * EXT), f32),
        ]
        + BlockGather.sems(n_rep, n_ep)
        + BlockGather.sems(1, n_ep)
        + BlockGather.sems(1, n_ep),
        compiler_params=pltpu.CompilerParams(
            collective_id=collective_id, has_side_effects=True, vmem_limit_bytes=VMEM_BYTES
        ),
        cost_estimate=pl.CostEstimate(flops=1000, bytes_accessed=1000, transcendentals=0),
        name="attention_front",
    )(lengths, x, gains, cos, sin, routes, order, mat, w_o, own_g)


def unpack_kernel(shares, experts, *refs):
    (sums,) = refs[:1]
    packs, outs = refs[1:-9], refs[-9:-6]
    q_ref, k_ref, v_ref, o_ref, router_ref, rows_ref = refs[-6:]
    for local, pack in enumerate(packs):
        start = 0
        for out, rows in zip(outs, shares):
            for p in range(out.shape[2] // LANES):
                out[local, :, p * LANES : (p + 1) * LANES] = pack[0, start : start + rows, :].astype(f32)
                start += rows
    start = 0
    for out in (q_ref, k_ref, v_ref):
        out[...] = sums[:, start : start + out.shape[1]]
        start += out.shape[1]
    for n in range(2):
        rows = sums.shape[0]
        o_ref[n * rows : (n + 1) * rows, :] = sums[:, start : start + o_ref.shape[1]]
        start += o_ref.shape[1]
    small = sums[:, start : start + EXT]
    router_ref[...] = small[:, :experts]
    rows_ref[...] = small.T


def unpack(sums, packs, wide_share, tall_share, width, hidden, wide_q, wide_kv, experts):
    count, rows = len(packs), sums.shape[0]
    vmem = pl.BlockSpec(memory_space=pltpu.VMEM)
    return pl.pallas_call(
        functools.partial(unpack_kernel, (wide_share, wide_share, tall_share), experts),
        out_shape=tuple(
            jax.ShapeDtypeStruct(shape, f32)
            for shape in (
                (count, wide_share, hidden),
                (count, wide_share, hidden),
                (count, tall_share, width),
                (rows, wide_q),
                (rows, wide_kv),
                (rows, wide_kv),
                (2 * rows, width),
                (rows, experts),
                (EXT, rows),
            )
        ),
        in_specs=[vmem] * (count + 1),
        out_specs=(vmem,) * 9,
        compiler_params=pltpu.CompilerParams(vmem_limit_bytes=VMEM_BYTES),
        cost_estimate=pl.CostEstimate(flops=1000, bytes_accessed=1000, transcendentals=0),
        name="unpack",
    )(sums, *packs)


class TokenSum:
    def __init__(self, count, y_ref, starts, results, scratch):
        self.bits = bits_of(count)
        self.y_ref, self.results = y_ref, results
        self.own, self.got = scratch[:2], scratch[2:4]
        self.send_sem, self.recv_sem, self.own_sem = scratch[4:7]
        self.rep, self.me = lax.axis_index("rep"), lax.axis_index("ep")
        self.orders = [list(reversed(o)) for o in gather_orders(count)]
        self.columns = [pl.ds(s, o.shape[2]) for s, o in zip(starts, self.own)]
        self.masks = [
            [list(reversed(spans(self.orders[h][k + 1 :]))) for k in range(self.bits)] for h in range(2)
        ]
        self.slots, self.seats = [], []
        for h in range(2):
            table = {}
            for stage in range(self.bits):
                for mask in self.masks[h][stage]:
                    table[(stage, mask)] = len(table)
            self.slots.append(table)
            self.seats.append({mask: i for i, mask in enumerate(self.masks[h][0])})

    @staticmethod
    def scratch(count, rows, widths):
        half = count // 2
        return [
            pltpu.VMEM((half, rows, widths[0]), bf16),
            pltpu.VMEM((half, rows, widths[1]), bf16),
            pltpu.VMEM((count - 1, rows, widths[0]), bf16),
            pltpu.VMEM((count - 1, rows, widths[1]), bf16),
            pltpu.SemaphoreType.DMA((2, count)),
            pltpu.SemaphoreType.DMA((2, count)),
            pltpu.SemaphoreType.DMA((2, half)),
        ]

    def meet(self):
        meet([(self.rep, self.me ^ (1 << b)) for b in range(self.bits)])

    def copy(self, h, stage, mask):
        bit = 1 << self.orders[h][stage]
        slot = self.slots[h][(stage, mask)]
        if stage == 0:
            source = self.y_ref.at[self.me ^ bit ^ mask, :, self.columns[h]]
        else:
            source = self.own[h].at[self.seats[h][bit | mask]]
        return pltpu.make_async_remote_copy(
            src_ref=source,
            dst_ref=self.got[h].at[slot],
            send_sem=self.send_sem.at[h, slot],
            recv_sem=self.recv_sem.at[h, slot],
            device_id=(self.rep, self.me ^ bit),
            device_id_type=MESH,
        )

    def load(self, h, mask):
        seat = self.seats[h][mask]
        return pltpu.make_async_copy(
            self.y_ref.at[self.me ^ mask, :, self.columns[h]], self.own[h].at[seat], self.own_sem.at[h, seat]
        )

    def begin(self):
        for i in range(len(self.masks[0][0])):
            for h in range(2):
                self.copy(h, 0, self.masks[h][0][i]).start()
                self.load(h, self.masks[h][0][i]).start()

    def add(self, h, stage, mask):
        slot, seat = self.slots[h][(stage, mask)], self.seats[h][mask]
        own, got = self.own[h], self.got[h]
        if stage == 0:
            self.load(h, mask).wait()
        self.copy(h, stage, mask).wait_recv()
        step = 32

        def body(i, carry):
            rows = pl.ds(pl.multiple_of(i * step, step), step)
            total = own[seat, rows, :].astype(f32) + got[slot, rows, :].astype(f32)
            if stage == self.bits - 1:
                self.results[h][rows, :] = total
            else:
                own[seat, rows, :] = total.astype(bf16)
            return carry

        lax.fori_loop(0, own.shape[1] // step, body, 0)

    def stage(self, stage):
        for i in range(len(self.masks[0][stage])):
            for h in range(2):
                mask = self.masks[h][stage][i]
                self.add(h, stage, mask)
                if stage + 1 < self.bits:
                    following = 1 << self.orders[h][stage + 1]
                    if mask & following:
                        self.copy(h, stage + 1, mask & ~following).start()

    def end(self):
        for h in range(2):
            for stage, mask in self.slots[h]:
                self.copy(h, stage, mask).wait_send()


def token_sum_kernel(count, starts, y_ref, first_ref, second_ref, *scratch):
    total = TokenSum(count, y_ref, starts, (first_ref, second_ref), scratch)
    total.meet()
    total.begin()
    for stage in range(total.bits):
        total.stage(stage)
    total.end()


def sum_tokens(y, count, starts, widths, collective_id):
    rows = y.shape[1]
    return pl.pallas_call(
        functools.partial(token_sum_kernel, count, starts),
        out_shape=tuple(jax.ShapeDtypeStruct((rows, w), f32) for w in widths),
        in_specs=[pl.BlockSpec(memory_space=pl.ANY)],
        out_specs=(pl.BlockSpec(memory_space=pltpu.VMEM),) * 2,
        scratch_shapes=TokenSum.scratch(count, rows, widths),
        compiler_params=pltpu.CompilerParams(
            collective_id=collective_id, has_side_effects=True, vmem_limit_bytes=VMEM_BYTES
        ),
        cost_estimate=pl.CostEstimate(flops=1000, bytes_accessed=1000, transcendentals=0),
        name="token_sum",
    )(y)


QUAD = 4


def attention_back_kernel(count, starts, heads_kv, groups, scale, *refs):
    (length_ref, proj_ref, gains_ref, cos_ref, sin_ref, mid_ref, wo_ref, y_ref) = refs[:8]
    right_ref, head_ref, first_ref, second_ref = refs[8:12]
    wo_buf, wo_sem, k_low, v_low, k_norm, dk_sum, dv_sum = refs[12:19]
    total = TokenSum(count, y_ref, starts, (first_ref, second_ref), refs[19:])
    size = gains_ref.shape[1]
    tokens = proj_ref.shape[0]
    heads_q = heads_kv * groups
    wide_q, wide_kv = heads_q * size, heads_kv * size
    per_group = groups // QUAD
    turns = heads_q // QUAD

    def wo_copy(i):
        rows = pl.ds(pl.multiple_of(i * QUAD * size, QUAD * size), QUAD * size)
        return pltpu.make_async_copy(wo_ref.at[rows], wo_buf.at[i % 2], wo_sem.at[i % 2])

    wo_copy(0).start()
    total.meet()
    total.begin()
    head_ref[...] = jnp.zeros_like(head_ref)
    sent = right_ref.shape[1] - wide_q - 2 * wide_kv
    for n in range(sent // mid_ref.shape[1]):
        start = wide_q + 2 * wide_kv + n * mid_ref.shape[1]
        right_ref[:, start : start + mid_ref.shape[1]] = mid_ref[...]

    def rotate(value):
        return value * cos_ref[...] + pltpu.roll(value, size // 2, 1) * sin_ref[...]

    def rotate_back(value):
        return value * cos_ref[...] - pltpu.roll(value, size // 2, 1) * sin_ref[...]

    def norm_parts(value):
        inverse = lax.rsqrt(jnp.mean(value * value, axis=-1, keepdims=True) + eps)
        return value * inverse, inverse

    def project_back(gradient, normed, inverse, row):
        scaled = rotate_back(gradient)
        head_ref[row : row + 1, :] += jnp.sum(scaled * normed, axis=0, keepdims=True)
        lifted = scaled * gains_ref[row : row + 1, :]
        mean = jnp.mean(lifted * normed, axis=-1, keepdims=True)
        return (inverse * (lifted - normed * mean)).astype(bf16)

    key_pos = lax.broadcasted_iota(jnp.int32, (tokens, tokens), 0)
    query_pos = lax.broadcasted_iota(jnp.int32, (tokens, tokens), 1)
    allowed = (key_pos <= query_pos) & (key_pos < length_ref[0])

    def lanes(start):
        return pl.ds(pl.multiple_of(start, size), size)

    def turn(i, carry):
        group = i // per_group
        for stage, when in ((0, min(1, turns - 1)), (1, turns - 2)):

            @pl.when(i == when)
            def _(stage=stage):
                if stage < total.bits - 1:
                    total.stage(stage)

        @pl.when(i % per_group == 0)
        def _():
            normed, inverse = norm_parts(proj_ref[:, lanes(wide_q + group * size)])
            k_norm[:, :size] = normed
            k_norm[:, size:] = jnp.broadcast_to(inverse, normed.shape)
            k_low[...] = rotate(normed * gains_ref[1:2, :]).astype(bf16)
            v_low[...] = proj_ref[:, lanes(wide_q + wide_kv + group * size)].astype(bf16)
            dk_sum[...] = jnp.zeros_like(dk_sum)
            dv_sum[...] = jnp.zeros_like(dv_sum)

        @pl.when(i + 1 < turns)
        def _():
            wo_copy(i + 1).start()

        wo_copy(i).wait()
        d_att = lax.dot_general(mid_ref[...], wo_buf[i % 2], NT, preferred_element_type=f32).astype(bf16)
        keys, values = k_low[...], v_low[...]
        dk, dv = dk_sum[...], dv_sum[...]
        for n in range(QUAD):
            head = i * QUAD + n
            d_out = d_att[:, n * size : (n + 1) * size]
            normed, inverse = norm_parts(proj_ref[:, lanes(head * size)])
            query = rotate(normed * gains_ref[0:1, :]).astype(bf16)
            scores = lax.dot_general(keys, query, NT, preferred_element_type=f32) * scale
            scores = jnp.where(allowed, scores, -1e30)
            raised = jnp.exp(scores - jnp.max(scores, axis=0, keepdims=True))
            probs = raised * (1.0 / jnp.sum(raised, axis=0, keepdims=True))
            dv += jnp.dot(probs.astype(bf16), d_out, preferred_element_type=f32)
            d_probs = lax.dot_general(values, d_out, NT, preferred_element_type=f32)
            weighted = probs * d_probs
            d_scores = (weighted - probs * jnp.sum(weighted, axis=0, keepdims=True)).astype(bf16)
            dk += jnp.dot(d_scores, query, preferred_element_type=f32)
            d_query = lax.dot_general(d_scores, keys, TN, preferred_element_type=f32) * scale
            right_ref[:, lanes(head * size)] = project_back(d_query, normed, inverse, 0)
        dk_sum[...] = dk
        dv_sum[...] = dv

        @pl.when(i % per_group == per_group - 1)
        def _():
            right_ref[:, lanes(wide_q + group * size)] = project_back(
                dk_sum[...] * scale, k_norm[:, :size], k_norm[:, size:], 1
            )
            right_ref[:, lanes(wide_q + wide_kv + group * size)] = dv_sum[...].astype(bf16)

        return carry

    lax.fori_loop(0, turns, turn, 0)
    for stage in range(min(2, total.bits - 1), total.bits):
        total.stage(stage)
    total.end()


def attention_back(length, proj, gains, cos, sin, d_mid, mat_o, y, count, starts, widths, heads_kv, groups, collective_id):
    tokens, width = d_mid.shape
    size = gains.shape[1]
    vmem = pl.BlockSpec(memory_space=pltpu.VMEM)
    anywhere = pl.BlockSpec(memory_space=pl.ANY)
    columns = (heads_kv * groups + 2 * heads_kv) * size + 2 * width
    return pl.pallas_call(
        functools.partial(attention_back_kernel, count, starts, heads_kv, groups, size ** (-0.5)),
        out_shape=(
            jax.ShapeDtypeStruct((tokens, columns), bf16),
            jax.ShapeDtypeStruct((8, size), f32),
        )
        + tuple(jax.ShapeDtypeStruct((tokens, w), f32) for w in widths),
        in_specs=[pl.BlockSpec(memory_space=pltpu.SMEM)] + [vmem] * 5 + [anywhere] * 2,
        out_specs=(vmem,) * 4,
        scratch_shapes=[
            pltpu.VMEM((2, QUAD * size, width), bf16),
            pltpu.SemaphoreType.DMA((2,)),
            pltpu.VMEM((tokens, size), bf16),
            pltpu.VMEM((tokens, size), bf16),
            pltpu.VMEM((tokens, 2 * size), f32),
            pltpu.VMEM((tokens, size), f32),
            pltpu.VMEM((tokens, size), f32),
        ]
        + TokenSum.scratch(count, tokens, widths),
        compiler_params=pltpu.CompilerParams(
            collective_id=collective_id, has_side_effects=True, vmem_limit_bytes=VMEM_BYTES
        ),
        cost_estimate=pl.CostEstimate(flops=1000, bytes_accessed=1000, transcendentals=0),
        name="attention_back",
    )(length, proj, gains, cos, sin, d_mid, mat_o, y)


def exchanges(n_rep, n_ep):
    near = [(0, b) for b in range(1, bits_of(n_ep))]
    far = [(1, b) for b in range(bits_of(n_rep))]
    return near + far[::-1], (near + far, near[::-1] + far), [2] * len(near) + [3] * len(far)


def dense_sum_kernel(n_rep, n_ep, rows, chunks, split, *refs):
    hidden_ref, att_ref, right_ref, small_ref, head_ref, out_ref, head_out = refs[:7]
    rest = list(refs[7:])
    bits, rep_bits = bits_of(n_ep), bits_of(n_rep)
    wide = right_ref.shape[1] // (chunks - 1)
    half = wide // 2
    rep, me = lax.axis_index("rep"), lax.axis_index("ep")
    axes, orders, depths = exchanges(n_rep, n_ep)
    count = len(axes)
    mine = {axis: lax.rem(lax.div(rep if axis[0] else me, 1 << axis[1]), 2) for axis in axes + [(0, 0)]}
    left_ref, part, got_core = rest[:3]
    acc = [None] + [rest[3 + 2 * k : 5 + 2 * k] for k in range(count)]
    rest = rest[3 + 2 * count :]
    got = [None] + [rest[2 * k : 2 * k + 2] for k in range(count)]
    rest = rest[2 * count :]
    head_own, head_got, head_rep = rest[:3]
    core_send, core_recv, step_send, step_recv, head_send, head_recv, head_rs, head_rr = rest[3:]
    left = [[[a for a in axes if a not in o[:k]] for k in range(count)] for o in orders]
    lags = [0, 1]
    for depth in depths:
        lags.append(lags[-1] + depth)
    slots = [None] + [2 * depth for depth in depths]
    others = [lax.rem(rep + d, n_rep) for d in range(1, n_rep)]
    meet([(rep, me ^ (1 << b)) for b in range(bits)] + [(other, me) for other in others])

    def core_copy(c):
        slot = lax.rem(c, 2)
        return pltpu.make_async_remote_copy(
            src_ref=part.at[slot, 1 - mine[(0, 0)]],
            dst_ref=got_core.at[slot],
            send_sem=core_send.at[slot],
            recv_sem=core_recv.at[slot],
            device_id=(rep, me ^ 1),
            device_id_type=MESH,
        )

    def pick(k, h, which):
        axis = orders[h][k - 1]
        return (slice(None),) * left[h][k - 1].index(axis) + (which(mine[axis]),)

    def bit_copy(k, h, c):
        slot = lax.rem(c, slots[k])
        on_rep, bit = orders[h][k - 1]
        return pltpu.make_async_remote_copy(
            src_ref=acc[k][h].at[(slot,) + pick(k, h, lambda m: 1 - m)],
            dst_ref=got[k][h].at[slot],
            send_sem=step_send.at[k, h, slot],
            recv_sem=step_recv.at[k, h, slot],
            device_id=(rep ^ (1 << bit), me) if on_rep else (rep, me ^ (1 << bit)),
            device_id_type=MESH,
        )

    corners = [()]
    for _ in range(bits - 1):
        corners = [c + (v,) for c in corners for v in range(2)]
    block = n_rep * rows
    side_rows = len(corners) * block
    inner = (2,) * rep_bits

    def place_rows(source, which_of):
        per = 128 // rows
        for b in range(source.shape[1] // 128):
            turned = source[:, b * 128 : (b + 1) * 128].astype(f32).T.astype(bf16)
            for q in range(per):
                which, owner = which_of(b * per + q)
                r, e = owner // n_ep, owner % n_ep
                corner = sum(((e >> bit) & 1) << (bits - 1 - bit) for bit in range(1, bits))
                start = (which * 2 + (e & 1)) * side_rows + corner * block + r * rows
                left_ref[start : start + rows, :] = turned[q * rows : (q + 1) * rows, :]

    place_rows(hidden_ref, lambda n: (0, n))
    place_rows(att_ref, lambda n: (1 + n % 2, n // 2))

    def stage_make(c):
        slot = lax.rem(c, 2)

        @pl.when(c >= 2)
        def _():
            core_copy(c - 2).wait_send()

        @pl.when(c < chunks - 1)
        def _():
            which = jnp.where(c >= split[0], 1, 0) + jnp.where(c >= split[1], 1, 0)
            columns = pl.ds(pl.multiple_of(c * wide, wide), wide)
            weights = right_ref[:, columns]
            for side in (1, 0):
                which_side = 1 - mine[(0, 0)] if side else mine[(0, 0)]
                for n, corner in enumerate(corners):
                    start = (which * 2 + which_side) * side_rows + n * block
                    value = jnp.dot(
                        left_ref[pl.ds(pl.multiple_of(start, block), block), :],
                        weights,
                        preferred_element_type=f32,
                    )
                    part[(slot, which_side) + corner] = value.astype(bf16).reshape(inner + (rows, wide))

        @pl.when(c == chunks - 1)
        def _():
            thin = small_ref.shape[1]
            lead = (slice(None),) * (rep_bits + 1)
            for side in range(2):
                for n, corner in enumerate(corners):
                    value = small_ref[pl.ds(side * side_rows + n * block, block), :].reshape(inner + (rows, thin))
                    blank = jnp.zeros(inner + (rows, wide - thin), bf16)
                    part[(slot, side) + corner + lead + (slice(0, thin),)] = value
                    part[(slot, side) + corner + lead + (slice(thin, wide),)] = blank

        core_copy(c).start()

    def stage_core(c):
        slot, put = lax.rem(c, 2), lax.rem(c, slots[1])

        @pl.when(c >= slots[1])
        def _():
            for h in range(2):
                bit_copy(1, h, c - slots[1]).wait_send()

        core_copy(c).wait_recv()
        for corner in corners:
            total = part[(slot, mine[(0, 0)]) + corner].astype(f32) + got_core[(slot,) + corner].astype(f32)
            total = total.astype(bf16)
            for h in range(2):
                acc[1][h][(put,) + corner] = total[..., h * half : (h + 1) * half]
        for h in range(2):
            bit_copy(1, h, c).start()

    def joined(k, h, c):
        slot = lax.rem(c, slots[k])
        return acc[k][h][(slot,) + pick(k, h, lambda m: m)].astype(f32) + got[k][h][slot].astype(f32)

    def stage_bit(k, c):
        for h in range(2):

            @pl.when(c >= slots[k])
            def _(h=h):
                bit_copy(k, h, c - slots[k]).wait_send()

            bit_copy(k - 1, h, c).wait_recv()
            acc[k][h][lax.rem(c, slots[k])] = joined(k - 1, h, c).astype(bf16)
            bit_copy(k, h, c).start()

    def stage_end(c):
        for h in range(2):
            bit_copy(count, h, c).wait_recv()
            out_ref[:, pl.ds(pl.multiple_of(c * wide + h * half, half), half)] = joined(count, h, c)

    def head_copy(t):
        return pltpu.make_async_remote_copy(
            src_ref=head_own.at[t],
            dst_ref=head_got.at[t],
            send_sem=head_send.at[t],
            recv_sem=head_recv.at[t],
            device_id=(rep, me ^ (1 << t)),
            device_id_type=MESH,
        )

    def head_rep_copy(d):
        return pltpu.make_async_remote_copy(
            src_ref=head_own.at[bits],
            dst_ref=head_rep.at[rep],
            send_sem=head_rs.at[d],
            recv_sem=head_rr.at[n_rep - 2 - d],
            device_id=(others[d], me),
            device_id_type=MESH,
        )

    def head_step(t):
        if t == 0:
            head_own[0] = head_ref[...]
            head_copy(0).start()
        elif t <= bits:
            head_copy(t - 1).wait_recv()
            head_own[t] = head_own[t - 1] + head_got[t - 1]
            if t < bits:
                head_copy(t).start()
            else:
                for d in range(n_rep - 1):
                    head_rep_copy(d).start()
                head_rep[rep] = head_own[bits]
        else:
            for d in range(n_rep - 1):
                head_rep_copy(d).wait_recv()
            total = head_rep[0]
            for r in range(1, n_rep):
                total = total + head_rep[r]
            head_out[...] = total

    def step(i, carry):
        for stage in reversed(range(len(lags))):
            c = i - lags[stage]

            @pl.when((c >= 0) & (c < chunks))
            def _(stage=stage, c=c):
                if stage == 0:
                    stage_make(c)
                elif stage == 1:
                    stage_core(c)
                elif stage <= count:
                    stage_bit(stage, c)
                else:
                    stage_end(c)

        for t in range(bits + 2):

            @pl.when(i == t)
            def _(t=t):
                head_step(t)

        return carry

    lax.fori_loop(0, chunks + lags[-1], step, 0)
    for c in range(chunks - 2, chunks):
        core_copy(c).wait_send()
    for k in range(1, count + 1):
        for c in range(chunks - slots[k], chunks):
            for h in range(2):
                bit_copy(k, h, c).wait_send()
    for t in range(bits):
        head_copy(t).wait_send()
    for d in range(n_rep - 1):
        head_rep_copy(d).wait_send()


def dense_sum(hidden, attended, right, small, head, n_rep, n_ep, split, collective_id):
    chunk = 512
    chunks = right.shape[1] // chunk + 1
    bits, rep_bits = bits_of(n_ep), bits_of(n_rep)
    tokens, width = hidden.shape
    rows = width // (n_rep * n_ep)
    axes, _, depths = exchanges(n_rep, n_ep)
    half = chunk // 2
    most = 2 * max(depths)
    vmem = pl.BlockSpec(memory_space=pltpu.VMEM)
    inner = (2,) * rep_bits + (rows,)
    scratch = [
        pltpu.VMEM((width + attended.shape[1], tokens), bf16),
        pltpu.VMEM((2, 2) + (2,) * (bits - 1) + inner + (chunk,), bf16),
        pltpu.VMEM((2,) + (2,) * (bits - 1) + inner + (chunk,), bf16),
    ]
    for k, depth in enumerate(depths):
        scratch += [pltpu.VMEM((2 * depth,) + (2,) * (len(axes) - k) + (rows, half), bf16)] * 2
    for k, depth in enumerate(depths):
        scratch += [pltpu.VMEM((2 * depth,) + (2,) * (len(axes) - k - 1) + (rows, half), bf16)] * 2
    scratch += [
        pltpu.VMEM((bits + 1,) + head.shape, f32),
        pltpu.VMEM((bits,) + head.shape, f32),
        pltpu.VMEM((n_rep,) + head.shape, f32),
        pltpu.SemaphoreType.DMA((2,)),
        pltpu.SemaphoreType.DMA((2,)),
        pltpu.SemaphoreType.DMA((len(axes) + 1, 2, most)),
        pltpu.SemaphoreType.DMA((len(axes) + 1, 2, most)),
        pltpu.SemaphoreType.DMA((bits,)),
        pltpu.SemaphoreType.DMA((bits,)),
        pltpu.SemaphoreType.DMA((n_rep - 1,)),
        pltpu.SemaphoreType.DMA((n_rep - 1,)),
    ]
    return pl.pallas_call(
        functools.partial(dense_sum_kernel, n_rep, n_ep, rows, chunks, split),
        out_shape=(
            jax.ShapeDtypeStruct((rows, chunks * chunk), f32),
            jax.ShapeDtypeStruct(head.shape, f32),
        ),
        in_specs=[vmem] * 5,
        out_specs=(vmem, vmem),
        scratch_shapes=scratch,
        compiler_params=pltpu.CompilerParams(
            collective_id=collective_id, has_side_effects=True, vmem_limit_bytes=VMEM_BYTES
        ),
        cost_estimate=pl.CostEstimate(flops=1000, bytes_accessed=1000, transcendentals=0),
        name="dense_sum",
    )(hidden, attended, right, small, head)


def expert_kernel(local, experts, width, hidden_of, *refs):
    (info, h_ref, g_ref, wg_all, wu_all, wd_all) = refs[:6]
    save_ref, grad_ref = refs[6:8]
    xs, gs, ds, hs, notes, wide, tall, in_sem, save_sem, grad_sem = refs[8:18]
    wg_ref, wu_ref, wd_ref, weight_sem = refs[18:]
    weights = [
        pltpu.make_async_copy(source.at[local], target, weight_sem.at[n])
        for n, (source, target) in enumerate(((wg_all, wg_ref), (wu_all, wu_ref), (wd_all, wd_ref)))
    ]
    weights[0].start()
    shares = grad_ref.shape[0]
    wide_share, tall_share = width // shares, hidden_of // shares
    hidden = wg_ref.shape[1]
    units = info[0]
    expert = info[1]
    table = 8
    per_tile = TILE // UNIT
    tiles = (units + per_tile - 1) // per_tile
    most = xs.shape[0] // TILE
    floor_tiles = min(4, most)

    def unit_in(u, slot):
        source = pl.ds(pl.multiple_of(info[table + u], UNIT), UNIT)
        target = pl.ds(pl.multiple_of(u * UNIT, UNIT), UNIT)
        return (
            pltpu.make_async_copy(h_ref.at[source], xs.at[target], in_sem.at[0, slot]),
            pltpu.make_async_copy(g_ref.at[source], gs.at[target], in_sem.at[1, slot]),
        )

    def begin(u, carry):
        for copy in unit_in(u, u // per_tile):
            copy.start()
        return carry

    def begin_tile(i):
        lax.fori_loop(
            jnp.minimum(i * per_tile, units), jnp.minimum((i + 1) * per_tile, units), begin, 0
        )

    begin_tile(0)
    for copy in weights[1:]:
        copy.start()
    begin_tile(1)

    def blank(u, carry):
        target = pl.ds(pl.multiple_of(u * UNIT, UNIT), UNIT)
        xs[target, :] = jnp.zeros((UNIT, xs.shape[1]), bf16)
        gs[target, :] = jnp.zeros((UNIT, gs.shape[1]), bf16)
        return carry

    lax.fori_loop(units, jnp.maximum(tiles, floor_tiles) * per_tile, blank, 0)

    def blank_tile(i, carry):
        target = pl.ds(pl.multiple_of(i * TILE, TILE), TILE)
        ds[target, :] = jnp.zeros((TILE, ds.shape[1]), bf16)
        hs[target, :] = jnp.zeros((TILE, hs.shape[1]), bf16)
        return carry

    lax.fori_loop(tiles, floor_tiles, blank_tile, 0)

    lane = lax.broadcasted_iota(jnp.int32, (TILE, EXT), 1)
    weight_lanes = (lane == expert) | (lane == expert + experts) | (lane == expert + 2 * experts)

    def tile_step(i, carry):
        def landed(u, c):
            for copy in unit_in(u, i):
                copy.wait()
            return c

        begin_tile(i + 2)
        lax.fori_loop(i * per_tile, jnp.minimum((i + 1) * per_tile, units), landed, 0)
        rows = pl.ds(pl.multiple_of(i * TILE, TILE), TILE)
        x = xs[rows, :width]
        g = gs[rows, :]
        extra = xs[rows, width:].astype(f32)
        weight = jnp.sum(jnp.where(weight_lanes, extra, 0.0), axis=1, keepdims=True)

        def loaded(n):
            @pl.when(i == 0)
            def _():
                weights[n].wait()

        loaded(0)
        gate = jnp.dot(x, wg_ref[...], preferred_element_type=f32)
        loaded(1)
        up = jnp.dot(x, wu_ref[...], preferred_element_type=f32)
        loaded(2)
        d_plain = lax.dot_general(g, wd_ref[...], NT, preferred_element_type=f32)
        sig = 1.0 / (1.0 + jnp.exp(-gate))
        silu = gate * sig
        hid = silu * up
        d_weight = jnp.sum(hid.astype(bf16).astype(f32) * d_plain, axis=1, keepdims=True)
        hs[rows, :] = (hid * weight).astype(bf16)
        d_hidden = d_plain * weight
        ds[rows, :hidden] = (d_hidden * up * sig * (1.0 + gate * (1.0 - sig))).astype(bf16)
        ds[rows, hidden:] = (d_hidden * silu).astype(bf16)

        high = d_weight.astype(bf16).astype(f32)
        low = d_weight - high
        note = jnp.where(lane == expert, high, 0.0) + jnp.where(lane == expert + experts, low, 0.0)
        notes[rows, :] = note.astype(bf16)
        return carry

    lax.fori_loop(0, tiles, tile_step, 0)
    saves = [
        pltpu.make_async_copy(source, save_ref.at[:, start : start + source.shape[1]], save_sem.at[n])
        for n, (source, start) in enumerate(((ds, 0), (hs, 2 * hidden), (notes, 3 * hidden)))
    ]
    for copy in saves:
        copy.start()

    block = 256

    def grads(depth):
        def wide_copies(m):
            per = wide_share // block
            return tuple(
                pltpu.make_async_copy(
                    wide.at[m % 2, :, p * LANES : (p + 1) * LANES],
                    grad_ref.at[
                        m // per,
                        pl.ds(pl.multiple_of(p * wide_share + (m % per) * block, block), block),
                    ],
                    grad_sem.at[m % 2, p],
                )
                for p in range(2 * hidden // LANES)
            )

        def wide_step(m, carry):
            @pl.when(m >= 2)
            def _():
                for copy in wide_copies(m - 2):
                    copy.wait()

            columns = pl.ds(pl.multiple_of(m * block, block), block)
            wide[m % 2] = lax.dot_general(
                xs[:depth, columns], ds[:depth, :], TN, preferred_element_type=f32
            ).astype(bf16)
            for copy in wide_copies(m):
                copy.start()
            return carry

        count = width // block
        lax.fori_loop(0, count, wide_step, 0)
        for m in range(count - 2, count):
            for copy in wide_copies(m):
                copy.wait()

        piece = math.gcd(block, tall_share)
        base = 2 * hidden // LANES * wide_share

        def tall_copies(m):
            made = []
            for q in range(block // piece):
                first_row = m * block + q * piece
                share, inside = first_row // tall_share, first_row % tall_share
                for p in range(width // LANES):
                    rows = pl.ds(pl.multiple_of(base + p * tall_share + inside, piece), piece)
                    made.append(
                        pltpu.make_async_copy(
                            tall.at[m % 2, q * piece : (q + 1) * piece, p * LANES : (p + 1) * LANES],
                            grad_ref.at[share, rows],
                            grad_sem.at[m % 2, q * (width // LANES) + p],
                        )
                    )
            return made

        def tall_step(m, carry):
            @pl.when(m >= 2)
            def _():
                for copy in tall_copies(m - 2):
                    copy.wait()

            columns = pl.ds(pl.multiple_of(m * block, block), block)
            tall[m % 2] = lax.dot_general(
                hs[:depth, columns], gs[:depth, :], TN, preferred_element_type=f32
            ).astype(bf16)
            for copy in tall_copies(m):
                copy.start()
            return carry

        count = hidden // block
        lax.fori_loop(0, count, tall_step, 0)
        for m in range(count - 2, count):
            for copy in tall_copies(m):
                copy.wait()

    for choice in range(floor_tiles, most + 1):
        chosen = (tiles <= choice) if choice == floor_tiles else (tiles == choice)

        @pl.when(chosen)
        def _(choice=choice):
            grads(choice * TILE)

    for copy in saves:
        copy.wait()


def expert_pass(info, h_rows, g_rows, w_gate, w_up, w_down, local, experts, shares):
    tokens, width = g_rows.shape
    hidden = w_gate.shape[2]
    any_spec = pl.BlockSpec(memory_space=pl.ANY)
    pieces = 256 // math.gcd(256, hidden // shares) * width // LANES
    return pl.pallas_call(
        functools.partial(expert_kernel, local, experts, width, hidden),
        out_shape=(
            jax.ShapeDtypeStruct((tokens, 3 * hidden + EXT), bf16),
            jax.ShapeDtypeStruct((shares, 3 * hidden * width // shares // LANES, LANES), bf16),
        ),
        in_specs=[pl.BlockSpec(memory_space=pltpu.SMEM)] + [any_spec] * 5,
        out_specs=(any_spec,) * 2,
        scratch_shapes=[
            pltpu.VMEM((tokens, width + EXT), bf16),
            pltpu.VMEM((tokens, width), bf16),
            pltpu.VMEM((tokens, 2 * hidden), bf16),
            pltpu.VMEM((tokens, hidden), bf16),
            pltpu.VMEM((tokens, EXT), bf16),
            pltpu.VMEM((2, 256, 2 * hidden), bf16),
            pltpu.VMEM((2, 256, width), bf16),
            pltpu.SemaphoreType.DMA((2, tokens // TILE)),
            pltpu.SemaphoreType.DMA((3,)),
            pltpu.SemaphoreType.DMA((2, max(2 * hidden // LANES, pieces))),
            pltpu.VMEM((width, hidden), bf16),
            pltpu.VMEM((width, hidden), bf16),
            pltpu.VMEM((hidden, width), bf16),
            pltpu.SemaphoreType.DMA((3,)),
        ],
        compiler_params=pltpu.CompilerParams(vmem_limit_bytes=VMEM_BYTES),
        cost_estimate=pl.CostEstimate(flops=1000, bytes_accessed=1000, transcendentals=0),
        name="experts",
    )(info, h_rows, g_rows, w_gate, w_up, w_down)


def returned_kernel(local_count, width, hidden, *refs):
    info, wg_all, wu_all, wd_all = refs[:4]
    saves = refs[4 : 4 + local_count]
    y_ref = refs[4 + local_count]
    wg, wu, wd, held, stage, weight_sem, held_sem, out_sem = refs[5 + local_count :]
    weights = [
        pltpu.make_async_copy(source, target, weight_sem.at[n])
        for n, (source, target) in enumerate(((wg_all, wg), (wu_all, wu), (wd_all, wd)))
    ]
    units = info[0]
    table = 8
    per_tile = TILE // UNIT
    tiles = (units + per_tile - 1) // per_tile

    def held_copies(i):
        rows = pl.ds(pl.multiple_of(i * TILE, TILE), TILE)
        return [
            pltpu.make_async_copy(save.at[rows], held.at[i % 2, n], held_sem.at[i % 2, n])
            for n, save in enumerate(saves)
        ]

    for copy in held_copies(0) + weights:
        copy.start()

    def unit_out(u):
        target = pl.ds(pl.multiple_of(info[table + u], UNIT), UNIT)
        tile = u // per_tile
        source = pl.ds(pl.multiple_of((u % per_tile) * UNIT, UNIT), UNIT)
        return pltpu.make_async_copy(stage.at[tile % 2, source], y_ref.at[target], out_sem.at[tile % 2])

    def each_unit(i, act):
        def body(u, carry):
            act(unit_out(u))
            return carry

        lax.fori_loop(i * per_tile, jnp.minimum((i + 1) * per_tile, units), body, 0)

    def tile_step(i, carry):
        slot = i % 2

        def loaded(n):
            @pl.when(i == 0)
            def _():
                weights[n].wait()


        @pl.when(i >= 2)
        def _():
            each_unit(i - 2, lambda copy: copy.wait())

        @pl.when(i + 1 < tiles)
        def _():
            for copy in held_copies(i + 1):
                copy.start()

        for copy in held_copies(i):
            copy.wait()
        d_row = jnp.zeros((TILE, width), f32)
        out = jnp.zeros((TILE, width), f32)
        note = jnp.zeros((TILE, EXT), f32)
        loaded(0)
        loaded(1)
        for n in range(local_count):
            d_row += lax.dot_general(held[slot, n, :, :hidden], wg[n], NT, preferred_element_type=f32)
            d_row += lax.dot_general(
                held[slot, n, :, hidden : 2 * hidden], wu[n], NT, preferred_element_type=f32
            )
            note += held[slot, n, :, 3 * hidden :].astype(f32)
        stage[slot, :, :width] = d_row.astype(bf16)
        stage[slot, :, width : width + EXT] = note.astype(bf16)
        loaded(2)
        for n in range(local_count):
            out += jnp.dot(held[slot, n, :, 2 * hidden : 3 * hidden], wd[n], preferred_element_type=f32)
        stage[slot, :, width + EXT :] = out.astype(bf16)
        each_unit(i, lambda copy: copy.start())
        return carry

    lax.fori_loop(0, tiles, tile_step, 0)

    @pl.when(tiles >= 2)
    def _():
        each_unit(tiles - 2, lambda copy: copy.wait())

    each_unit(tiles - 1, lambda copy: copy.wait())


def returned_rows(info, w_gate, w_up, w_down, saves):
    local_count, width, hidden = w_gate.shape
    tokens, row = saves[0].shape
    wide_row = width + EXT + width
    any_spec = pl.BlockSpec(memory_space=pl.ANY)
    return pl.pallas_call(
        functools.partial(returned_kernel, local_count, width, hidden),
        out_shape=jax.ShapeDtypeStruct((tokens, wide_row), bf16),
        in_specs=[pl.BlockSpec(memory_space=pltpu.SMEM)] + [any_spec] * (3 + local_count),
        out_specs=any_spec,
        scratch_shapes=[
            pltpu.VMEM(w_gate.shape, bf16),
            pltpu.VMEM(w_up.shape, bf16),
            pltpu.VMEM(w_down.shape, bf16),
            pltpu.VMEM((2, local_count, TILE, row), bf16),
            pltpu.VMEM((2, TILE, wide_row), bf16),
            pltpu.SemaphoreType.DMA((3,)),
            pltpu.SemaphoreType.DMA((2, local_count)),
            pltpu.SemaphoreType.DMA((2,)),
        ],
        compiler_params=pltpu.CompilerParams(vmem_limit_bytes=VMEM_BYTES),
        cost_estimate=pl.CostEstimate(flops=1000, bytes_accessed=1000, transcendentals=0),
        name="returned_rows",
    )(info, w_gate, w_up, w_down, *saves)


def unit_table(lengths):
    per_sequence = TILE // UNIT
    counts = (lengths + UNIT - 1) // UNIT
    unit = jnp.arange(lengths.shape[0] * per_sequence, dtype=jnp.int32)
    live = (unit % per_sequence) < jnp.repeat(counts, per_sequence)
    place = jnp.cumsum(live.astype(jnp.int32)) - 1
    hit = (place[None, :] == unit[:, None]) & live[None, :]
    rows = jnp.sum(jnp.where(hit, unit[None, :] * UNIT, 0), axis=1)
    return (jnp.sum(counts), rows)


def per_device(
    hidden_in,
    out_grad,
    attn_gain,
    w_q,
    key_weight,
    value_weight,
    w_o,
    ffn_gain,
    router_w,
    qk_gains,
    w_gate,
    w_up,
    w_down,
    lengths,
    routes,
    order,
):
    everywhere = ("rep", "ep")
    rep_count, ep_count = (lax.axis_size("rep"), lax.axis_size("ep"))
    rep_index, ep_index = (lax.axis_index("rep"), lax.axis_index("ep"))
    inputs = hidden_in[0].astype(f32)
    sequence_length, model_width = inputs.shape
    head_size = qk_gains.shape[1]
    wide_q, wide_kv = (w_q.shape[1], key_weight.shape[1])
    heads_q, heads_kv = (wide_q // head_size, wide_kv // head_size)
    groups = heads_q // heads_kv
    local_experts = w_gate.shape[0]
    experts = local_experts * ep_count
    top_count = routes.shape[2]
    score_scale = head_size ** (-0.5)
    group_lengths = lax.dynamic_slice_in_dim(lengths, rep_index * ep_count, ep_count)
    length = lax.dynamic_index_in_dim(group_lengths, ep_index, keepdims=False)
    positions = jnp.arange(sequence_length, dtype=jnp.int32)
    live = positions < length
    live_rows = live.astype(f32)

    own_rows = w_q.shape[0]
    small = jnp.concatenate([router_w, attn_gain[:, None], ffn_gain[:, None]], axis=1)
    small = jnp.pad(small, ((0, 0), (0, EXT - small.shape[1])))
    pack = jnp.concatenate([w_q, key_weight, value_weight, small], axis=1)
    mat_qkv = gather_weights(pack, rep_count, ep_count, 4).reshape(-1, pack.shape[1])

    wide_all = wide_q + 2 * wide_kv
    small_all = mat_qkv[:, wide_all:]
    mat_router = small_all[:, :experts]
    cosine_lookup, sine_lookup = rope_tables(sequence_length, head_size)
    sign = jnp.where(jnp.arange(head_size) < head_size // 2, -1.0, 1.0).astype(f32)
    turned_sine = sine_lookup * sign[None, :]
    (
        hidden_first,
        projected,
        attended,
        middle,
        sent,
        route_gates,
        kept_float,
        row_gain,
        mat_o,
        grads_all,
    ) = attention_front(
        lengths,
        hidden_in[0],
        qk_gains.astype(f32),
        cosine_lookup,
        turned_sine,
        routes[0],
        order[0].reshape(sequence_length, top_count),
        mat_qkv,
        w_o,
        out_grad[0],
        rep_count,
        ep_count,
        experts,
        heads_kv,
        groups,
        6,
    )
    h_all = gather_tokens(sent, ep_count, 1)
    h_two = sent[:, :model_width]
    route_gates, kept_float = (route_gates[:, :experts], kept_float[:, :experts])
    gain_attn, gain_ffn = (row_gain[0], row_gain[1])
    mat_o = mat_o.reshape(-1, model_width)
    grads_all = grads_all.reshape(-1, model_width)
    norm_one, inv_one = rms_parts(inputs)
    norm_two, inv_two = rms_parts(middle)

    part = min(ep_count, 8)
    tokens = part * sequence_length
    sums = []
    y_parts = []
    for c in range(ep_count // part):
        live_units, unit_rows = unit_table(group_lengths[c * part : (c + 1) * part])
        h_rows = h_all[c * part : (c + 1) * part].reshape(tokens, model_width + EXT)
        g_rows = grads_all[c * tokens : (c + 1) * tokens]
        saves, found = [], []
        for local in range(local_experts):
            info = jnp.concatenate(
                [
                    jnp.stack([live_units, ep_index * local_experts + local]).astype(jnp.int32),
                    jnp.zeros((6,), jnp.int32),
                    unit_rows,
                ]
            )
            save, weight_grads = expert_pass(
                info, h_rows, g_rows, w_gate, w_up, w_down, local, experts, rep_count
            )
            saves.append(save)
            found.append(weight_grads)
        y_parts.append(returned_rows(info, w_gate, w_up, w_down, saves).reshape(part, sequence_length, -1))
        sums.append(found)
    y_all = y_parts[0] if len(y_parts) == 1 else jnp.concatenate(y_parts, axis=0)
    hidden_units = w_gate.shape[2]
    wide_share, tall_share = model_width // rep_count, hidden_units // rep_count
    found = []
    for local in range(local_experts):
        total = sums[0][local]
        for more in sums[1:]:
            total = (total.astype(f32) + more[local].astype(f32)).astype(bf16)
        found.append(lax.psum_scatter(total, "rep", scatter_dimension=0, tiled=True))
    half_width = model_width // 2
    row_first, row_second = sum_tokens(
        y_all, ep_count, (0, half_width), (half_width, half_width + EXT), 2
    )
    live_column = live[:, None]
    grad_rows = out_grad[0].astype(f32) * live_rows[:, None]
    notes = row_second[:, half_width : half_width + 2 * experts]
    d_weight = jnp.where(live_column, notes[:, :experts] + notes[:, experts:], 0.0)
    d_gates = d_weight * kept_float
    d_logits = route_gates * (d_gates - jnp.sum(route_gates * d_gates, axis=-1, keepdims=True))

    router_float = mat_router.astype(f32)
    d_h_two = jnp.concatenate([row_first, row_second[:, :half_width]], axis=1)
    d_h_two = jnp.where(live_column, d_h_two, 0.0)
    d_h_two = d_h_two + jnp.dot(d_logits, router_float.T, precision=top_precision)
    grad_router = jnp.dot(h_two.astype(f32).T, d_logits, precision=top_precision)
    grad_ffn = jnp.sum(d_h_two * norm_two, axis=0)
    d_middle = grad_rows + rms_back(d_h_two * gain_ffn, norm_two, inv_two)
    d_middle_low = d_middle.astype(bf16)
    right, head, out_first, out_second = attention_back(
        length.reshape(1),
        projected,
        qk_gains.astype(f32),
        cosine_lookup,
        turned_sine,
        d_middle_low,
        mat_o,
        y_all,
        ep_count,
        (model_width + EXT, model_width + EXT + half_width),
        (half_width, half_width),
        heads_kv,
        groups,
        5,
    )
    moe_output = jnp.where(live_column, jnp.concatenate([out_first, out_second], axis=1), 0.0)
    layer_out = jnp.where(live_column, middle + moe_output, 0.0)
    d_qkv = right[:, :wide_all]
    d_h_one = jnp.einsum("tf,cf->tc", d_qkv, mat_qkv[:, :wide_all], preferred_element_type=f32)
    grad_attn = jnp.sum(d_h_one * norm_one, axis=0)
    grad_input = d_middle + rms_back(d_h_one * gain_attn, norm_one, inv_one)

    small_grads = jnp.concatenate([grad_router, grad_attn[:, None], grad_ffn[:, None]], axis=1)
    small_grads = jnp.pad(small_grads, ((0, 0), (0, EXT - small_grads.shape[1]))).astype(bf16)
    ep_bits = bits_of(ep_count)

    def owner_order(value, parts):
        shape = (rep_count,) + (2,) * ep_bits + (parts, own_rows, value.shape[1])
        axes = (ep_bits + 1,) + tuple(range(ep_bits, 0, -1)) + (0, ep_bits + 2, ep_bits + 3)
        return value.reshape(shape).transpose(axes).reshape(value.shape)

    splits = (wide_all // 512, (wide_all + model_width) // 512)
    layer_out, grad_input, head = lax.optimization_barrier((layer_out, grad_input, head))
    sums_all, head_sum = dense_sum(
        hidden_first, attended, right, owner_order(small_grads, 1), head, rep_count, ep_count, splits, 3
    )
    last = unpack(
        sums_all, found, wide_share, tall_share, model_width, hidden_units, wide_q, wide_kv, experts
    )
    return (
        layer_out[None],
        grad_input[None],
        last[8][experts],
        last[3],
        last[4],
        last[5],
        last[6],
        last[8][experts + 1],
        last[7],
        head_sum[:2],
        last[0],
        last[1],
        last[2],
    )


def solution(mesh):
    both = ("rep", "ep")
    placed = (
        P(both, None, None),
        P(both, None, None),
        P(both),
        P(both, None),
        P(both, None),
        P(both, None),
        P(both, None),
        P(both),
        P(both, None),
        P(),
        P("ep", None, None),
        P("ep", None, None),
        P("ep", None, None),
        P(),
        P(both, None, None),
        P(both, None),
    )
    return jax.shard_map(
        per_device,
        mesh=mesh,
        in_specs=placed,
        out_specs=(
            P(both, None, None),
            P(both, None, None),
            P(both),
            P(both, None),
            P(both, None),
            P(both, None),
            P(both, None),
            P(both),
            P(both, None),
            P(),
            P("ep", "rep", None),
            P("ep", "rep", None),
            P("ep", "rep", None),
        ),
        check_vma=False,
    )
```
